32 devices in a mesh: dp: 8 (over y, x, core), tensor: 4 (over z).
Axes of the slice: x: 2, y: 2, z: 4, core: 2. Of those that a mesh axis runs over, the one named last changes fastest.
Arguments:
- tokens: bfloat16 [1024, 8, 1024], P('tensor', 'dp'), may hold values from -6 to 6
- lengths: int32 [8], replicated, may hold values from 1 to 1024, 5120 in all
- order: int32 [8], replicated, may hold values from 0 to 7, each once
- norm_mix: bfloat16 [2, 1024], replicated, may hold values from 0.5 to 1.5
- w_query: bfloat16 [2, 1024, 1024], P(None, 'dp', 'tensor'), may hold values from -0.1875 to 0.1875
- w_key: bfloat16 [2, 1024, 1024], P(None, 'dp', 'tensor'), may hold values from -0.1875 to 0.1875
- w_value: bfloat16 [2, 1024, 2048], P(None, 'dp', 'tensor'), may hold values from -0.1875 to 0.1875
- w_gate: bfloat16 [2, 1024, 2048], P(None, 'dp', 'tensor'), may hold values from -0.1875 to 0.1875
- w_decay: bfloat16 [2, 1024, 4, 2], P(None, 'dp', 'tensor'), may hold values from -0.1875 to 0.1875
- conv_filter: bfloat16 [2, 4, 4, 1024], P(None, None, 'tensor', 'dp'), may hold values from -3 to 3
- log_rate: bfloat16 [2, 4], replicated, may hold values from 0 to 2.6875
- step_bias: bfloat16 [2, 4], replicated, may hold values from -6 to -2
- norm_heads: bfloat16 [2, 512], replicated, may hold values from 0.5 to 1.5
- w_out: bfloat16 [2, 2048, 1024], P(None, 'tensor', 'dp'), may hold values from -0.25 to 0.25
- norm_ffn: bfloat16 [2, 1024], replicated, may hold values from 0.5 to 1.5
- w_ffn_gate: bfloat16 [2, 1024, 2816], P(None, 'dp', 'tensor'), may hold values from -0.1875 to 0.1875
- w_ffn_up: bfloat16 [2, 1024, 2816], P(None, 'dp', 'tensor'), may hold values from -0.1875 to 0.1875
- w_ffn_down: bfloat16 [2, 2816, 1024], P(None, 'tensor', 'dp'), may hold values from -0.109375 to 0.109375
- cotangent: bfloat16 [1024, 8, 1024], P('tensor', 'dp'), may hold values from -6 to 6
Outputs:
- mixed: bfloat16 [1024, 8, 1024], P('tensor', 'dp')
- grad_tokens: float32 [1024, 8, 1024], P('tensor', 'dp')
- grad_norm_mix: float32 [2, 1024], replicated
- grad_w_query: float32 [2, 1024, 1024], P(None, 'dp', 'tensor')
- grad_w_key: float32 [2, 1024, 1024], P(None, 'dp', 'tensor')
- grad_w_value: float32 [2, 1024, 2048], P(None, 'dp', 'tensor')
- grad_w_gate: float32 [2, 1024, 2048], P(None, 'dp', 'tensor')
- grad_w_decay: float32 [2, 1024, 4, 2], P(None, 'dp', 'tensor')
- grad_conv_filter: float32 [2, 4, 4, 1024], P(None, None, 'tensor', 'dp')
- grad_log_rate: float32 [2, 4], replicated
- grad_step_bias: float32 [2, 4], replicated
- grad_norm_heads: float32 [2, 512], replicated
- grad_w_out: float32 [2, 2048, 1024], P(None, 'tensor', 'dp')
- grad_norm_ffn: float32 [2, 1024], replicated
- feedforward_gate_weight_gradient: float32 [2, 1024, 2816], P(None, 'dp', 'tensor')
- grad_w_ffn_up: float32 [2, 1024, 2816], P(None, 'dp', 'tensor')
- grad_w_ffn_down: float32 [2, 2816, 1024], P(None, 'tensor', 'dp')
The draws below stay inside these ranges and needn't reach their ends.
Inputs may be any that keep to these rules, and one draw needn't show every extreme that they name: lengths sum to 5120 and one slot is full; a slot's sequence takes its first time positions. `order`: each slot appears once.
All inputs are finite; a program needn't handle non-finite values.
Results may differ from the reference program's by a relative error of at most 0.035.
Values may be sent and summed in bfloat16 or wider, within the bound.
A program may use at most 320 MiB of HBM per device.

```python
import math
import jax
import jax.numpy as jnp
import numpy as np
from jax import lax

D = 1024
HEADS = 4
KEY_DIM = 256
VAL_DIM = 512
FF = 2816
CONV = 4
GROUP = 64
LAYERS = 2
SEQ_LEN = 1024
SLOTS = 8


def steps_of(stream_key, extent, pieces, smallest, top_value):
    factor_of = 1.0
    for axis_at, blocks in pieces:
        steps = jax.random.uniform(jax.random.fold_in(jax.random.fold_in(stream_key, 6), axis_at), (blocks,), jnp.float32, smallest / len(pieces), top_value / len(pieces))
        factor_of = factor_of * jnp.repeat(jnp.exp(steps), extent[axis_at] // blocks).reshape((-1,) + (1,) * (len(extent) - 1 - axis_at))
    return factor_of


def split_up(count, total, reach, lean):
    portions = [(1 << 20) // math.isqrt(standing ** lean) + 1 for standing in range(2, count + 1)]
    surplus, given = total - reach - (count - 1), [1] * (count - 1)
    while surplus > 0:
        free = [i for i in range(count - 1) if given[i] < reach]
        mass, left = sum([portions[i] for i in free]), surplus
        for i in free:
            extra = min(reach - given[i], max(1, left * portions[i] // mass), surplus)
            given[i] = given[i] + extra
            surplus = surplus - extra
    return np.array([reach] + given)


def ragged(stream_key, count, total, bound, skew):
    if count == 2:
        one = jax.random.randint(stream_key, (), max(1, total - bound), min(bound, total - 1) + 1)
        return jnp.stack([one, total - one])
    sizes = jnp.asarray(split_up(count, total, bound, skew), jnp.int32)
    pairs = (count - 1) // 2
    giver, taker = sizes[1:1 + 2 * pairs:2], sizes[2:2 + 2 * pairs:2]
    slack = jnp.minimum(giver - 1, bound - taker)
    passed = jax.random.randint(jax.random.fold_in(stream_key, 1), (pairs,), 0, 1 << 20) % (slack + 1)
    sizes = sizes.at[1:1 + 2 * pairs:2].set(giver - passed).at[2:2 + 2 * pairs:2].set(taker + passed)
    return sizes[jax.random.permutation(jax.random.fold_in(stream_key, 2), count)]


def centred(own_key, shape, scale, most, cuts=(), kind=jnp.bfloat16):
    factor_of = steps_of(own_key, shape, cuts, -0.22, 0.18) if cuts else 1.0
    array = jax.random.normal(own_key, shape, jnp.float32) * scale * factor_of
    return jnp.minimum(jnp.maximum(array, -most), most).astype(kind)


def setup_inputs(seed: int = 0) -> dict:
    key_list = jax.random.split(jax.random.key(seed), 20)
    tokens = centred(key_list[0], (SEQ_LEN, SLOTS, D), 1.0, 6.0, ((0, 4), (1, 8)))
    lengths = ragged(key_list[1], SLOTS, 5 * SLOTS * SEQ_LEN // 8, SEQ_LEN, 2).astype(jnp.int32)
    order = jax.random.permutation(key_list[2], SLOTS).astype(jnp.int32)
    norm_mix = jnp.clip(1.0 + 0.1 * jax.random.normal(key_list[3], (LAYERS, D), jnp.float32), 0.5, 1.5).astype(jnp.bfloat16)
    w_query = centred(key_list[4], (LAYERS, D, HEADS * KEY_DIM), D ** -0.5, 0.1875, ((1, 8), (2, 4)))
    w_key = centred(key_list[5], (LAYERS, D, HEADS * KEY_DIM), D ** -0.5, 0.1875, ((1, 8), (2, 4)))
    w_value = centred(key_list[6], (LAYERS, D, HEADS * VAL_DIM), D ** -0.5, 0.1875, ((1, 8), (2, 4)))
    w_gate = centred(key_list[7], (LAYERS, D, HEADS * VAL_DIM), D ** -0.5, 0.1875, ((1, 8), (2, 4)))
    w_decay = centred(key_list[8], (LAYERS, D, HEADS, 2), D ** -0.5, 0.1875, ((1, 8), (2, 4)))
    conv_filter = centred(key_list[9], (LAYERS, CONV, HEADS, 2 * KEY_DIM + VAL_DIM), CONV ** -0.5, 3.0, ((2, 4), (3, 8)))
    log_rate = jnp.clip(jax.random.uniform(key_list[10], (LAYERS, HEADS), jnp.float32, 0.0, 2.6875), 0.0, 2.6875).astype(jnp.bfloat16)
    step_bias = jnp.clip(jax.random.uniform(key_list[11], (LAYERS, HEADS), jnp.float32, -6.0, -2.0), -6.0, -2.0).astype(jnp.bfloat16)
    norm_heads = jnp.clip(1.0 + 0.1 * jax.random.normal(key_list[12], (LAYERS, VAL_DIM), jnp.float32), 0.5, 1.5).astype(jnp.bfloat16)
    w_out = centred(key_list[13], (LAYERS, HEADS * VAL_DIM, D), VAL_DIM ** -0.5, 0.25, ((1, 4), (2, 8)))
    norm_ffn = jnp.clip(1.0 + 0.1 * jax.random.normal(key_list[14], (LAYERS, D), jnp.float32), 0.5, 1.5).astype(jnp.bfloat16)
    w_ffn_gate = centred(key_list[15], (LAYERS, D, FF), D ** -0.5, 0.1875, ((1, 8), (2, 4)))
    w_ffn_up = centred(key_list[16], (LAYERS, D, FF), D ** -0.5, 0.1875, ((1, 8), (2, 4)))
    w_ffn_down = centred(key_list[17], (LAYERS, FF, D), FF ** -0.5, 0.109375, ((1, 4), (2, 8)))
    cotangent = centred(key_list[18], (SEQ_LEN, SLOTS, D), 1.0, 6.0, ((0, 4), (1, 8)))
    return dict(tokens=tokens, lengths=lengths, order=order, norm_mix=norm_mix, w_query=w_query, w_key=w_key, w_value=w_value, w_gate=w_gate, w_decay=w_decay, conv_filter=conv_filter, log_rate=log_rate, step_bias=step_bias, norm_heads=norm_heads, w_out=w_out, norm_ffn=norm_ffn, w_ffn_gate=w_ffn_gate, w_ffn_up=w_ffn_up, w_ffn_down=w_ffn_down, cotangent=cotangent)


@jax.custom_vjp
def low(v):
    return lax.optimization_barrier(v.astype(jnp.bfloat16)).astype(jnp.float32)

@jax.custom_vjp
def low_back(v):
    return v

def low_keep(v):
    return (low(v), None)

def low_pass(kept, grad):
    return (grad,)

def back_keep(v):
    return (v, None)

def back_low(kept, grad):
    return (low(grad),)
low.defvjp(low_keep, low_pass)
low_back.defvjp(back_keep, back_low)

def precise_product(left_side, right_side):
    return jnp.dot(left_side, right_side, precision=lax.Precision.HIGHEST)

def block_step(memory, inputs):
    queries, key_rows, values, write_rate, log_decay = inputs
    length = queries.shape[0]
    row_ids = jnp.arange(length)
    strictly = row_ids[:, None] > row_ids[None, :]
    inclusive = row_ids[:, None] >= row_ids[None, :]
    spread = log_decay[:, None] - log_decay[None, :]
    below_decay = jnp.exp(jnp.where(strictly, spread, 0.0)) * strictly.astype(jnp.float32)
    within = jnp.exp(jnp.where(inclusive, spread, 0.0)) * inclusive.astype(jnp.float32)
    coupling = write_rate[:, None] * precise_product(key_rows, key_rows.T) * below_decay
    unit_lower = jnp.eye(length, dtype=jnp.float32) + coupling
    growth = jnp.exp(log_decay)[:, None]
    key_terms = jax.scipy.linalg.solve_triangular(unit_lower, write_rate[:, None] * key_rows * growth, lower=True, unit_diagonal=True)
    value_terms = jax.scipy.linalg.solve_triangular(unit_lower, write_rate[:, None] * values, lower=True, unit_diagonal=True)
    corrected = value_terms - precise_product(key_terms, memory)
    output = precise_product(queries * growth, memory) + precise_product(precise_product(queries, key_rows.T) * within, corrected)
    final_decay = log_decay[-1]
    memory = jnp.exp(final_decay) * memory + precise_product((key_rows * jnp.exp(final_decay - log_decay)[:, None]).T, corrected)
    return (memory, output)

def delta_sequence(queries, key_rows, values, write_rate, log_step):
    length = queries.shape[0]
    blocks = length // GROUP
    key_size = key_rows.shape[1]
    value_size = values.shape[1]
    inputs = (queries.reshape(blocks, GROUP, key_size), key_rows.reshape(blocks, GROUP, key_size), values.reshape(blocks, GROUP, value_size), write_rate.reshape(blocks, GROUP), jnp.cumsum(log_step.reshape(blocks, GROUP), axis=1))
    initial = jnp.zeros((key_size, value_size), jnp.float32)
    final_memory, outputs = lax.scan(jax.checkpoint(block_step), initial, inputs)
    return outputs.reshape(length, value_size)

def causal_filter(signal, filter_taps):
    tap_count = filter_taps.shape[0]
    length = signal.shape[0]
    padded = jnp.pad(signal, ((tap_count - 1, 0), (0, 0), (0, 0), (0, 0)))
    result = jnp.zeros_like(signal)
    for tap_index in range(tap_count):
        result = result + padded[tap_index:tap_index + length] * filter_taps[tap_index]
    return result

def unit_rows(vector):
    return vector * lax.rsqrt(lax.optimization_barrier(jnp.sum(vector * vector, axis=-1, keepdims=True)) + 1e-06)

def norm_rows(values, gain_row):
    return values * lax.rsqrt(lax.optimization_barrier(jnp.mean(values * values, axis=-1, keepdims=True)) + 1e-06) * gain_row

def delta_mixer(query_in, key_in, value_in, gate_in, rate_in, filter_taps, rate_param, bias_param, gain_row):
    length, slot_count = (query_in.shape[0], query_in.shape[1])
    head_count = filter_taps.shape[1]
    key_size = query_in.shape[2] // head_count
    value_size = value_in.shape[2] // head_count
    joined = jnp.concatenate([query_in.reshape(length, slot_count, head_count, key_size), key_in.reshape(length, slot_count, head_count, key_size), value_in.reshape(length, slot_count, head_count, value_size)], axis=3)
    filtered = jax.nn.silu(causal_filter(joined, filter_taps))
    queries = unit_rows(filtered[..., :key_size]) * key_size ** (-0.5)
    key_rows = unit_rows(filtered[..., key_size:2 * key_size])
    values = filtered[..., 2 * key_size:]
    rate_pairs = rate_in.reshape(length, slot_count, head_count, 2)
    write_rate = jax.nn.sigmoid(rate_pairs[..., 0])
    log_step = -jnp.exp(rate_param) * jax.nn.softplus(rate_pairs[..., 1] + bias_param)
    axes_order = (1, 2, 0, 3)
    outputs = jax.vmap(jax.vmap(delta_sequence))(queries.transpose(axes_order), key_rows.transpose(axes_order), values.transpose(axes_order), write_rate.transpose((1, 2, 0)), log_step.transpose((1, 2, 0)))
    outputs = outputs.transpose((2, 0, 1, 3))
    scaled = outputs * lax.rsqrt(lax.optimization_barrier(jnp.mean(outputs * outputs, axis=-1, keepdims=True)) + 1e-05) * gain_row
    gated_rows = scaled * jax.nn.silu(gate_in.reshape(length, slot_count, head_count, value_size))
    return gated_rows.reshape(length, slot_count, head_count * value_size)

def exact_project(values, weight):
    return jnp.einsum('lsd,dc->lsc', values, weight, precision=lax.Precision.HIGHEST)

def residual_block(residual, layer_params):
    gain_mix, weight_query, weight_key, weight_value, weight_gate, weight_decay, filter_taps, rate_param, bias_param, gain_heads, weight_out, gain_ffn, weight_up_gate, weight_up, down_projection_weight = layer_params
    width_model = weight_decay.shape[0]
    normed = low(norm_rows(residual, gain_mix))
    query_in = low_back(exact_project(normed, weight_query))
    key_in = low_back(exact_project(normed, weight_key))
    value_in = low_back(exact_project(normed, weight_value))
    gate_in = low_back(exact_project(normed, weight_gate))
    rate_in = low_back(exact_project(normed, weight_decay.reshape(width_model, -1)))
    mixer_output = delta_mixer(query_in, key_in, value_in, gate_in, rate_in, filter_taps, rate_param, bias_param, gain_heads)
    residual = residual + low_back(exact_project(low(mixer_output), weight_out))
    normed_ffn = low(norm_rows(residual, gain_ffn))
    gate_act = low_back(exact_project(normed_ffn, weight_up_gate))
    up_act = low_back(exact_project(normed_ffn, weight_up))
    hidden = low(jax.nn.silu(gate_act) * up_act)
    return residual + low_back(exact_project(hidden, down_projection_weight))

def reference(tokens, lengths, order, norm_mix, w_query, w_key, w_value, w_gate, w_decay, conv_filter, log_rate, step_bias, norm_heads, w_out, norm_ffn, w_ffn_gate, w_ffn_up, w_ffn_down, cotangent):
    weights = tuple((argument.astype(jnp.float32) for argument in (norm_mix, w_query, w_key, w_value, w_gate, w_decay, conv_filter, log_rate, step_bias, norm_heads, w_out, norm_ffn, w_ffn_gate, w_ffn_up, w_ffn_down)))
    order_ids = order.astype(jnp.int32)

    def forward(slot_inputs, *weight_sets):
        residual = jnp.take(slot_inputs, order_ids, axis=1)
        for layer_index in range(LAYERS):
            residual = residual_block(residual, [weight_set[layer_index] for weight_set in weight_sets])
        return residual
    output, backward = jax.vjp(forward, tokens.astype(jnp.float32), *weights)
    dealt_lengths = jnp.take(lengths, order_ids)
    valid_mask = (jnp.arange(SEQ_LEN)[:, None] < dealt_lengths[None, :]).astype(jnp.float32)
    gradients = backward(cotangent.astype(jnp.float32) * valid_mask[:, :, None])
    return (output.astype(jnp.bfloat16), gradients[0], gradients[1], gradients[2], gradients[3], gradients[4], gradients[5], gradients[6], gradients[7], gradients[8], gradients[9], gradients[10], gradients[11], gradients[12], gradients[13], gradients[14], gradients[15])
```

```python
import functools
import jax
import jax.numpy as jnp
from jax import lax
from jax.experimental import pallas as pl
from jax.experimental.pallas import tpu as pltpu
from jax.sharding import PartitionSpec as P

CHUNK = 256
LANES = 128
KEY = 256
VAL = 512
CONV_CH = 2 * KEY + VAL
F32 = jnp.float32
BF16 = jnp.bfloat16
NN = (((1,), (0,)), ((), ()))
NT = (((1,), (1,)), ((), ()))
TN = (((0,), (0,)), ((), ()))


def mm(a, b, dims=NN):
    return lax.dot_general(
        a.astype(BF16), b.astype(BF16), dims, preferred_element_type=F32
    )


def split_low(a):
    high = a.astype(BF16)
    return high, (a - high.astype(F32)).astype(BF16)


def mm3(a, b, dims=NN):
    a_high, a_low = split_low(a)
    b_high, b_low = split_low(b)
    dot = functools.partial(
        lax.dot_general, dimension_numbers=dims, preferred_element_type=F32
    )
    return dot(a_high, b_high) + (dot(a_high, b_low) + dot(a_low, b_high))


def mm_exact_left(a, b, dims=NN):
    a = a.astype(BF16)
    high = b.astype(BF16)
    rest = b - high.astype(F32)
    mid = rest.astype(BF16)
    low = (rest - mid.astype(F32)).astype(BF16)
    dot = functools.partial(
        lax.dot_general, dimension_numbers=dims, preferred_element_type=F32
    )
    return dot(a, high) + (dot(a, mid) + dot(a, low))


def iotas():
    rows = lax.broadcasted_iota(jnp.int32, (CHUNK, CHUNK), 0)
    cols = lax.broadcasted_iota(jnp.int32, (CHUNK, CHUNK), 1)
    return rows, cols


def wide(col_block, width):
    return jnp.concatenate([col_block] * (width // LANES), axis=1)


def rates_of(rates, rate, bias):
    write = jax.nn.sigmoid(jnp.broadcast_to(rates[:, 0:1], (CHUNK, LANES)))
    logit = jnp.broadcast_to(rates[:, 1:2], (CHUNK, LANES)) + bias
    soft = jnp.maximum(logit, 0.0) + jnp.log1p(jnp.exp(-jnp.abs(logit)))
    return write, -rate * soft, jax.nn.sigmoid(logit)


def decay_terms(step, rows, cols):
    inclusive = (rows >= cols).astype(BF16)
    total = mm_exact_left(inclusive, step)
    spread = wide(total, CHUNK) - jnp.concatenate([total.T] * (CHUNK // LANES), axis=0)
    decay = jnp.where(rows >= cols, jnp.exp(jnp.minimum(spread, 0.0)), 0.0)
    last = jnp.broadcast_to(total[CHUNK - 1 : CHUNK, :], (CHUNK, LANES))
    return decay, jnp.exp(total), jnp.exp(last - total), jnp.exp(last)


def solve_unit(coupling, rows, cols, product):
    same = ((rows >> 1) == (cols >> 1)) & (rows != cols)
    inverse = jnp.where(rows == cols, 1.0, 0.0) - jnp.where(same, coupling, 0.0)
    for level in range(1, CHUNK.bit_length() - 1):
        between = ((rows >> (level + 1)) == (cols >> (level + 1))) & (
            (rows >> level) != (cols >> level)
        )
        part = jnp.where(between, coupling, 0.0)
        inverse = inverse - product(product(inverse, part), inverse)
    return inverse


def silu_of(x):
    gate = jax.nn.sigmoid(x)
    return x * gate, gate


def conv_rows(padded_ref, taps_ref, start):
    result = padded_ref[pl.ds(start, CHUNK), :] * taps_ref[0:1, :]
    for j in range(1, 4):
        result = result + padded_ref[pl.ds(start + j, CHUNK), :] * taps_ref[j : j + 1, :]
    return result


def forward_kernel(
    scalars_ref, x_ref, w_in_ref, w_aux_ref, w_out_ref, taps_ref, gain_ref,
    part_ref, heads_ref, proj_ref, gate_ref, rates_ref, inverse_ref, fresh_ref, o_ref, state_ref,
    padded, memory,
):
    @pl.when(pl.program_id(0) == 0)
    def _():
        memory[...] = jnp.zeros_like(memory)
        padded[0:8, :] = jnp.zeros((8, CONV_CH), F32)

    x = x_ref[...]
    proj = mm(x, w_in_ref[...])
    rates = mm(x, w_aux_ref[...])
    rates_ref[...] = rates
    qkv = proj[:, :CONV_CH]
    proj_ref[...] = qkv
    gate_in = proj[:, CONV_CH:]
    gate_ref[...] = gate_in
    padded[8 : 8 + CHUNK, :] = qkv
    conv = conv_rows(padded, taps_ref, 5)
    padded[0:8, :] = qkv[CHUNK - 8 :, :]
    act, _ = silu_of(conv)
    q, k, v = act[:, :KEY], act[:, KEY : 2 * KEY], act[:, 2 * KEY :]
    q = q * (lax.rsqrt(jnp.sum(q * q, axis=1, keepdims=True) + 1e-6) * KEY**-0.5)
    k = k * lax.rsqrt(jnp.sum(k * k, axis=1, keepdims=True) + 1e-6)
    rows, cols = iotas()
    write, step, _ = rates_of(rates, scalars_ref[0], scalars_ref[1])
    decay, growth, rest, final = decay_terms(step, rows, cols)
    coupling = jnp.where(rows > cols, wide(write, CHUNK) * mm3(k, k, NT) * decay, 0.0)
    inverse = solve_unit(coupling, rows, cols, mm3)
    inverse_ref[...] = inverse.astype(BF16)
    within = mm(q, k, NT) * decay
    state = memory[...]
    state_ref[...] = state
    low_state = state.astype(BF16)
    source = wide(write, VAL) * (v - wide(growth, VAL) * mm(k, low_state))
    fresh = mm3(inverse, source)
    fresh_ref[...] = fresh
    o = wide(growth, VAL) * mm(q, low_state) + mm(within, fresh)
    o_ref[...] = o
    memory[...] = wide(final, VAL) * state + mm(k * wide(rest, KEY), fresh, TN)
    scaled = o * lax.rsqrt(jnp.mean(o * o, axis=1, keepdims=True) + 1e-5) * gain_ref[...]
    heads = (scaled * silu_of(gate_in)[0]).astype(BF16)
    heads_ref[...] = heads
    part_ref[...] = mm(heads, w_out_ref[...], NT).astype(BF16)


def mixer_forward(x, pack, taps, gain, scalars):
    length, width = x.shape
    chunks = length // CHUNK
    row = lambda cols: pl.BlockSpec((CHUNK, cols), lambda i: (i, 0))
    fixed = lambda shape, at: pl.BlockSpec(shape, lambda i: (0, at), pipeline_mode=pl.Buffered(1))
    out = lambda cols, kind: jax.ShapeDtypeStruct((length, cols), kind)
    return pl.pallas_call(
        forward_kernel,
        grid=(chunks,),
        in_specs=[
            pl.BlockSpec(memory_space=pltpu.SMEM),
            row(width),
            fixed((width, 1536), 0),
            fixed((width, LANES), 16),
            fixed((width, VAL), 3),
            fixed((4, CONV_CH), 0),
            fixed((1, VAL), 0),
        ],
        out_specs=[
            row(width), row(VAL), row(CONV_CH), row(VAL), row(LANES), row(CHUNK), row(VAL), row(VAL),
            pl.BlockSpec((None, KEY, VAL), lambda i: (i, 0, 0)),
        ],
        out_shape=[
            out(width, BF16), out(VAL, BF16), out(CONV_CH, F32), out(VAL, F32), out(LANES, F32),
            out(CHUNK, BF16), out(VAL, F32), out(VAL, F32),
            jax.ShapeDtypeStruct((chunks, KEY, VAL), F32),
        ],
        scratch_shapes=[pltpu.VMEM((CHUNK + 8, CONV_CH), F32), pltpu.VMEM((KEY, VAL), F32)],
        compiler_params=pltpu.CompilerParams(
            dimension_semantics=("arbitrary",), vmem_limit_bytes=56 * 1024 * 1024
        ),
        name="mixer_forward",
    )(scalars, x, pack, pack, pack, taps, gain)


def unit_back(grad, vector, scale):
    inv = lax.rsqrt(jnp.sum(vector * vector, axis=1, keepdims=True) + 1e-6)
    dot = jnp.sum(grad * vector, axis=1, keepdims=True)
    return (grad - vector * (inv * inv * dot)) * (inv * scale)


def backward_kernel(
    scalars_ref, g_ref, w_in_ref, w_aux_ref, w_out_ref, taps_ref, gain_ref,
    proj_ref, halo_ref, gate_ref, rates_ref, inverse_ref, fresh_ref, o_ref, state_ref,
    part_ref, dproj_ref, drates_ref, dtaps_ref, dgain_ref, dscalars_ref,
    padded, dpadded, dmemory,
):
    at = pl.program_id(0)
    last = pl.num_programs(0) - 1

    @pl.when(at == 0)
    def _():
        dmemory[...] = jnp.zeros_like(dmemory)
        dpadded[CHUNK : CHUNK + 8, :] = jnp.zeros((8, CONV_CH), F32)
        dtaps_ref[...] = jnp.zeros_like(dtaps_ref)
        dgain_ref[...] = jnp.zeros_like(dgain_ref)
        dscalars_ref[...] = jnp.zeros_like(dscalars_ref)

    rows, cols = iotas()
    padded[8 : 8 + CHUNK, :] = proj_ref[...]
    padded[0:8, :] = jnp.where(at == last, 0.0, halo_ref[...])
    conv = conv_rows(padded, taps_ref, 5)
    act, sig = silu_of(conv)
    act_q, act_k, v = act[:, :KEY], act[:, KEY : 2 * KEY], act[:, 2 * KEY :]
    q = act_q * (lax.rsqrt(jnp.sum(act_q * act_q, axis=1, keepdims=True) + 1e-6) * KEY**-0.5)
    k = act_k * lax.rsqrt(jnp.sum(act_k * act_k, axis=1, keepdims=True) + 1e-6)
    rates = rates_ref[...]
    write, step, sig_decay = rates_of(rates, scalars_ref[0], scalars_ref[1])
    decay, growth, rest, final = decay_terms(step, rows, cols)
    growth_v = wide(growth, VAL)
    write_v = wide(write, VAL)
    low_q, low_k = q.astype(BF16), k.astype(BF16)
    below = rows > cols
    strict_decay = jnp.where(below, decay, 0.0)
    keys = mm(low_k, low_k, NT) * strict_decay * wide(write, CHUNK)
    within = mm(low_q, low_k, NT) * decay
    dheads = mm(g_ref[...], w_out_ref[...])
    o = o_ref[...]
    gate_in = gate_ref[...]
    gate, gate_sig = silu_of(gate_in)
    inv = lax.rsqrt(jnp.mean(o * o, axis=1, keepdims=True) + 1e-5)
    normal = o * inv
    gain = gain_ref[...]
    dgate = dheads * normal * gain * (gate_sig * (1.0 + gate_in * (1.0 - gate_sig)))
    dscaled = dheads * gate
    dgain_ref[...] += jnp.sum(dscaled * normal, axis=0, keepdims=True)
    dnormal = dscaled * gain
    do = inv * (dnormal - normal * jnp.mean(dnormal * normal, axis=1, keepdims=True))
    state = state_ref[...]
    low_state = state.astype(BF16)
    fresh = fresh_ref[...]
    low_fresh = fresh.astype(BF16)
    dstate = dmemory[...]
    low_dstate = dstate.astype(BF16)
    low_do = do.astype(BF16)
    k_rest = k * wide(rest, KEY)
    rest_dstate = mm(k_rest, low_dstate)
    dfresh = mm(within, low_do, TN) + rest_dstate
    dsource = mm(inverse_ref[...], dfresh, TN)
    low_dsource = dsource.astype(BF16)
    dv = write_v * dsource
    dread = -(growth_v * dv)
    low_dread = dread.astype(BF16)
    do_growth = growth_v * do
    low_do_growth = do_growth.astype(BF16)
    dwithin = mm(low_do, low_fresh, NT)
    dcoupling = -mm(low_dsource, low_fresh, NT)
    dkeys = dcoupling * strict_decay * wide(write, CHUNK)
    dpairs = dwithin * decay
    dq = mm(low_do_growth, low_state, NT) + mm(dpairs, low_k)
    dk = (
        mm(low_dread, low_state, NT)
        + mm(dpairs, low_q, TN)
        + mm(dkeys + dkeys.T, low_k)
        + wide(rest, KEY) * mm(low_fresh, low_dstate, NT)
    )
    dmemory[...] = (
        wide(final, VAL) * dstate + mm(low_q, low_do_growth, TN) + mm(low_k, low_dread, TN)
    )
    spread = dwithin * within + dcoupling * keys
    straddle = jnp.where(below, mm_exact_left((rows <= cols).astype(BF16), spread), 0.0)
    read_rows = jnp.sum(
        do_growth * mm(low_q, low_state) + dread * mm(low_k, low_state), axis=1, keepdims=True
    )
    rest_rows = jnp.sum(fresh * rest_dstate, axis=1, keepdims=True)
    carried = jnp.sum(dstate * state) * final[0:1, 0:1]
    suffix = mm_exact_left(
        (rows <= cols).astype(BF16), jnp.broadcast_to(read_rows, (CHUNK, LANES))
    ) + mm_exact_left((rows > cols).astype(BF16), jnp.broadcast_to(rest_rows, (CHUNK, LANES)))
    dstep = suffix + jnp.sum(straddle, axis=1, keepdims=True) + carried
    dlogit = dstep * (-scalars_ref[0]) * sig_decay
    dwrite = (1.0 - write) * jnp.sum(dsource * fresh, axis=1, keepdims=True)
    lane = lax.broadcasted_iota(jnp.int32, (CHUNK, LANES), 1)
    drates = jnp.where(lane == 0, dwrite, jnp.where(lane == 1, dlogit, 0.0))
    low_drates = drates.astype(BF16)
    drates_ref[...] = low_drates
    dscalars_ref[0:1, :] += jnp.sum(dstep * step, axis=0, keepdims=True)
    dscalars_ref[1:2, :] += jnp.sum(dlogit, axis=0, keepdims=True)
    dact = jnp.concatenate(
        [unit_back(dq, act_q, KEY**-0.5), unit_back(dk, act_k, 1.0), dv], axis=1
    )
    dconv = dact * (sig * (1.0 + conv * (1.0 - sig)))
    dpadded[0:CHUNK, :] = dconv
    dtaps_ref[...] += jnp.concatenate(
        [
            jnp.sum(dconv * padded[5 + j : 5 + j + CHUNK, :], axis=0, keepdims=True)
            for j in range(4)
        ],
        axis=0,
    )
    dqkv = dconv * taps_ref[3:4, :]
    for j in range(3):
        dqkv = dqkv + dpadded[pl.ds(3 - j, CHUNK), :] * taps_ref[j : j + 1, :]
    dpadded[CHUNK : CHUNK + 8, :] = dconv[0:8, :]
    low_dproj = jnp.concatenate([dqkv, dgate], axis=1).astype(BF16)
    dproj_ref[...] = low_dproj
    part_ref[...] = (
        mm(low_dproj, w_in_ref[...], NT) + mm(low_drates, w_aux_ref[...], NT)
    ).astype(BF16)


def mixer_backward(g, pack, taps, gain, scalars, saved):
    proj, gate_in, rates, inverse, fresh, o, states = saved
    length, width = g.shape
    chunks = length // CHUNK
    back = chunks - 1
    row = lambda cols: pl.BlockSpec((CHUNK, cols), lambda i: (back - i, 0))
    fixed = lambda shape, at: pl.BlockSpec(shape, lambda i: (0, at), pipeline_mode=pl.Buffered(1))
    out = lambda cols, kind: jax.ShapeDtypeStruct((length, cols), kind)
    steps = CHUNK // 8
    return pl.pallas_call(
        backward_kernel,
        grid=(chunks,),
        in_specs=[
            pl.BlockSpec(memory_space=pltpu.SMEM),
            row(width),
            fixed((width, 1536), 0),
            fixed((width, LANES), 16),
            fixed((width, VAL), 3),
            fixed((4, CONV_CH), 0),
            fixed((1, VAL), 0),
            row(CONV_CH),
            pl.BlockSpec((8, CONV_CH), lambda i: (jnp.maximum((back - i) * steps - 1, 0), 0)),
            row(VAL), row(LANES), row(CHUNK), row(VAL), row(VAL),
            pl.BlockSpec((None, KEY, VAL), lambda i: (back - i, 0, 0)),
        ],
        out_specs=[
            row(width), row(1536), row(LANES),
            pl.BlockSpec((4, CONV_CH), lambda i: (0, 0)),
            pl.BlockSpec((1, VAL), lambda i: (0, 0)),
            pl.BlockSpec((8, LANES), lambda i: (0, 0)),
        ],
        out_shape=[
            out(width, BF16), out(1536, BF16), out(LANES, BF16),
            jax.ShapeDtypeStruct((4, CONV_CH), F32),
            jax.ShapeDtypeStruct((1, VAL), F32),
            jax.ShapeDtypeStruct((8, LANES), F32),
        ],
        scratch_shapes=[
            pltpu.VMEM((CHUNK + 8, CONV_CH), F32),
            pltpu.VMEM((CHUNK + 8, CONV_CH), F32),
            pltpu.VMEM((KEY, VAL), F32),
        ],
        compiler_params=pltpu.CompilerParams(
            dimension_semantics=("arbitrary",), vmem_limit_bytes=56 * 1024 * 1024
        ),
        name="mixer_backward",
    )(scalars, g, pack, pack, pack, taps, gain, proj, proj, gate_in, rates, inverse, fresh, o, states)


def norm_rows(values, gain_row):
    return values * lax.rsqrt(jnp.mean(values * values, axis=-1, keepdims=True) + 1e-06) * gain_row


def swiglu_rows(paired):
    gate_part, up_part = jnp.split(paired, 2, axis=1)
    return jax.nn.silu(gate_part) * up_part


def gather_rows(values):
    return lax.all_gather(values, "tensor", axis=0, tiled=True)


def scatter_sum(partial):
    return lax.psum_scatter(partial, "tensor", scatter_dimension=0, tiled=True).astype(F32)


def dot32(a, b, dims):
    return lax.dot_general(a, b, dims, preferred_element_type=F32)


def shards(
    tokens, lengths, order, norm_mix, w_query, w_key, w_value, w_gate, w_decay, conv_filter,
    log_rate, step_bias, norm_heads, w_out, norm_ffn, w_ffn_gate, w_ffn_up, w_ffn_down, cotangent,
):
    layer_count = w_query.shape[0]
    heads_total = log_rate.shape[1]
    device_part = lax.axis_index("tensor")
    dp_place = lax.axis_index("dp")
    rows_local, slots_local, width = tokens.shape
    assert slots_local == 1 and w_decay.shape[2] == 1
    slot_total = order.shape[0]
    units = w_ffn_gate.shape[2]
    rows_part = w_query.shape[1]

    packs = []
    for layer in range(layer_count):
        aux = jnp.concatenate([w_decay[layer, :, 0, :], conv_filter[layer, :, 0, :].T], axis=1)
        aux = jnp.pad(aux, ((0, 0), (0, LANES - aux.shape[1])))
        mix = jnp.concatenate(
            [w_query[layer], w_key[layer], w_value[layer], w_gate[layer], w_out[layer].T, aux], axis=1
        )
        ffn = jnp.concatenate([w_ffn_gate[layer], w_ffn_up[layer], w_ffn_down[layer].T], axis=1)
        packs.append(
            (
                lax.all_gather(mix, "dp", axis=0, tiled=True),
                lax.all_gather(ffn, "dp", axis=0, tiled=True),
            )
        )

    spread_in = lax.all_to_all(tokens, "dp", split_axis=2, concat_axis=1, tiled=True)
    picked = jnp.take(spread_in, order, axis=1)
    dealt = lax.all_to_all(picked, "dp", split_axis=1, concat_axis=2, tiled=True)
    residual = dealt[:, 0, :].astype(F32)

    saved = []
    for layer in range(layer_count):
        mix, ffn = packs[layer]
        taps = mix[:, 2050:2054].T.astype(F32)
        gain_heads = norm_heads[layer].astype(F32)[None]
        scalars = jnp.concatenate(
            [
                jnp.exp(lax.dynamic_slice_in_dim(log_rate[layer].astype(F32), device_part, 1)),
                lax.dynamic_slice_in_dim(step_bias[layer].astype(F32), device_part, 1),
            ]
        )
        normed, norm_back = jax.vjp(norm_rows, residual, norm_mix[layer].astype(F32))
        rows_in = gather_rows(normed.astype(BF16))
        part, heads, *kept = mixer_forward(rows_in, mix, taps, gain_heads, scalars)
        residual = residual + scatter_sum(part)
        normed_ffn, ffn_norm_back = jax.vjp(norm_rows, residual, norm_ffn[layer].astype(F32))
        rows_ffn = gather_rows(normed_ffn.astype(BF16))
        paired = dot32(rows_ffn, ffn[:, : 2 * units], NN)
        hidden, swiglu_back = jax.vjp(swiglu_rows, paired)
        hidden = hidden.astype(BF16)
        residual = residual + scatter_sum(dot32(hidden, ffn[:, 2 * units :], NT).astype(BF16))
        saved.append(
            (norm_back, rows_in, taps, gain_heads, scalars, kept, heads, ffn_norm_back, rows_ffn,
             swiglu_back, hidden)
        )

    my_length = lengths[order[dp_place]]
    positions = device_part * rows_local + jnp.arange(rows_local)
    gradient = cotangent[:, 0, :].astype(F32) * (positions < my_length).astype(F32)[:, None]
    weight_grads = [None] * layer_count
    small_terms = [None] * layer_count
    for layer in reversed(range(layer_count)):
        mix, ffn = packs[layer]
        (norm_back, rows_in, taps, gain_heads, scalars, kept, heads, ffn_norm_back, rows_ffn,
         swiglu_back, hidden) = saved[layer]
        grad_rows = gather_rows(gradient.astype(BF16))
        (grad_paired,) = swiglu_back(dot32(grad_rows, ffn[:, 2 * units :], NN))
        paired_low = grad_paired.astype(BF16)
        grad_normed = scatter_sum(dot32(paired_low, ffn[:, : 2 * units], NT).astype(BF16))
        ffn_grads = jnp.concatenate(
            [dot32(rows_ffn, paired_low, TN).astype(BF16), dot32(grad_rows, hidden, TN).astype(BF16)],
            axis=1,
        )
        ffn_grads = lax.psum_scatter(ffn_grads, "dp", scatter_dimension=0, tiled=True)
        grad_residual, grad_gain_ffn = ffn_norm_back(grad_normed)
        gradient = gradient + grad_residual
        grad_rows = gather_rows(gradient.astype(BF16))
        part, dproj, drates, dtaps, dgain, dscalars = mixer_backward(
            grad_rows, mix, taps, gain_heads, scalars, kept
        )
        grad_normed = scatter_sum(part)
        aux = dot32(rows_in, drates, TN) + jnp.pad(dtaps.T, ((0, 0), (2, LANES - 6)))
        mix_grads = jnp.concatenate(
            [
                dot32(rows_in, dproj, TN).astype(BF16),
                dot32(grad_rows, heads, TN).astype(BF16),
                aux.astype(BF16),
            ],
            axis=1,
        )
        mix_grads = lax.psum_scatter(mix_grads, "dp", scatter_dimension=0, tiled=True)
        grad_residual, grad_gain_mix = norm_back(grad_normed)
        gradient = gradient + grad_residual
        weight_grads[layer] = (
            mix_grads[:, :256].astype(F32),
            mix_grads[:, 256:512].astype(F32),
            mix_grads[:, 512:1024].astype(F32),
            mix_grads[:, 1024:1536].astype(F32),
            mix_grads[:, 2048:2050].astype(F32).reshape(rows_part, 1, 2),
            mix_grads[:, 2050:2054].astype(F32).T.reshape(4, 1, rows_part),
            mix_grads[:, 1536:2048].astype(F32).T,
            ffn_grads[:, :units].astype(F32),
            ffn_grads[:, units : 2 * units].astype(F32),
            ffn_grads[:, 2 * units :].astype(F32).T,
        )
        mine = (jnp.arange(heads_total) == device_part).astype(F32)
        small_terms[layer] = jnp.concatenate(
            [grad_gain_mix, grad_gain_ffn, dgain[0], mine * dscalars[0, 0], mine * dscalars[1, 0]]
        )
    small = lax.psum(jnp.stack(small_terms), ("dp", "tensor"))
    spread_back = lax.all_to_all(
        gradient.astype(BF16)[:, None, :], "dp", split_axis=2, concat_axis=1, tiled=True
    )
    inverse_order = (
        jnp.zeros((slot_total,), jnp.int32).at[order].set(jnp.arange(slot_total, dtype=jnp.int32))
    )
    homed = jnp.take(spread_back, inverse_order, axis=1)
    grad_home = lax.all_to_all(homed, "dp", split_axis=1, concat_axis=2, tiled=True).astype(F32)
    members = [jnp.stack([grads[m] for grads in weight_grads]) for m in range(10)]
    ends = 2 * width + VAL
    return (
        residual.astype(BF16)[:, None, :],
        grad_home,
        small[:, :width],
        members[0], members[1], members[2], members[3], members[4], members[5],
        small[:, ends : ends + heads_total],
        small[:, ends + heads_total :],
        small[:, 2 * width : ends],
        members[6],
        small[:, width : 2 * width],
        members[7], members[8], members[9],
    )


def solution(mesh):
    return jax.shard_map(
        shards,
        mesh=mesh,
        in_specs=(
            P("tensor", "dp", None), P(), P(), P(),
            P(None, "dp", "tensor"), P(None, "dp", "tensor"), P(None, "dp", "tensor"),
            P(None, "dp", "tensor"), P(None, "dp", "tensor", None), P(None, None, "tensor", "dp"),
            P(), P(), P(), P(None, "tensor", "dp"), P(),
            P(None, "dp", "tensor"), P(None, "dp", "tensor"), P(None, "tensor", "dp"),
            P("tensor", "dp", None),
        ),
        out_specs=(
            P("tensor", "dp", None), P("tensor", "dp", None), P(),
            P(None, "dp", "tensor"), P(None, "dp", "tensor"), P(None, "dp", "tensor"),
            P(None, "dp", "tensor"), P(None, "dp", "tensor", None), P(None, None, "tensor", "dp"),
            P(), P(), P(), P(None, "tensor", "dp"), P(),
            P(None, "dp", "tensor"), P(None, "dp", "tensor"), P(None, "tensor", "dp"),
        ),
        check_vma=False,
    )
```

```python
import functools
import jax
import jax.numpy as jnp
from jax import lax
from jax.experimental import pallas as pl
from jax.experimental.layout import Layout, with_layout_constraint
from jax.experimental.pallas import tpu as pltpu
from jax.sharding import Mesh, PartitionSpec as P

CHUNK = 256
LANES = 128
KEY = 256
VAL = 512
CONV_CH = 2 * KEY + VAL
F32 = jnp.float32
BF16 = jnp.bfloat16
NN = (((1,), (0,)), ((), ()))
NT = (((1,), (1,)), ((), ()))
TN = (((0,), (0,)), ((), ()))


def mm(a, b, dims=NN):
    return lax.dot_general(
        a.astype(BF16), b.astype(BF16), dims, preferred_element_type=F32
    )


def split_low(a):
    high = a.astype(BF16)
    return high, (a - high.astype(F32)).astype(BF16)


def mm3(a, b, dims=NN):
    a_high, a_low = split_low(a)
    b_high, b_low = split_low(b)
    dot = functools.partial(
        lax.dot_general, dimension_numbers=dims, preferred_element_type=F32
    )
    return dot(a_high, b_high) + (dot(a_high, b_low) + dot(a_low, b_high))


def mm_exact_left(a, b, dims=NN):
    a = a.astype(BF16)
    high = b.astype(BF16)
    rest = b - high.astype(F32)
    mid = rest.astype(BF16)
    low = (rest - mid.astype(F32)).astype(BF16)
    dot = functools.partial(
        lax.dot_general, dimension_numbers=dims, preferred_element_type=F32
    )
    return dot(a, high) + (dot(a, mid) + dot(a, low))


def iotas():
    rows = lax.broadcasted_iota(jnp.int32, (CHUNK, CHUNK), 0)
    cols = lax.broadcasted_iota(jnp.int32, (CHUNK, CHUNK), 1)
    return rows, cols


def wide(col_block, width):
    return jnp.concatenate([col_block] * (width // LANES), axis=1)


def rates_of(rates, rate, bias):
    write = jax.nn.sigmoid(jnp.broadcast_to(rates[:, 0:1], (CHUNK, LANES)))
    logit = jnp.broadcast_to(rates[:, 1:2], (CHUNK, LANES)) + bias
    soft = jnp.maximum(logit, 0.0) + jnp.log1p(jnp.exp(-jnp.abs(logit)))
    return write, -rate * soft, jax.nn.sigmoid(logit)


def decay_terms(step, rows, cols):
    inclusive = (rows >= cols).astype(BF16)
    total = mm_exact_left(inclusive, step)
    spread = wide(total, CHUNK) - jnp.concatenate([total.T] * (CHUNK // LANES), axis=0)
    decay = jnp.where(rows >= cols, jnp.exp(jnp.minimum(spread, 0.0)), 0.0)
    last = jnp.broadcast_to(total[CHUNK - 1 : CHUNK, :], (CHUNK, LANES))
    return decay, jnp.exp(total), jnp.exp(last - total), jnp.exp(last)


def solve_unit(coupling, rows, cols, product):
    same = ((rows >> 1) == (cols >> 1)) & (rows != cols)
    inverse = jnp.where(rows == cols, 1.0, 0.0) - jnp.where(same, coupling, 0.0)
    for level in range(1, CHUNK.bit_length() - 1):
        between = ((rows >> (level + 1)) == (cols >> (level + 1))) & (
            (rows >> level) != (cols >> level)
        )
        part = jnp.where(between, coupling, 0.0)
        inverse = inverse - product(product(inverse, part), inverse)
    return inverse


def silu_of(x):
    gate = jax.nn.sigmoid(x)
    return x * gate, gate


def conv_rows(padded_ref, taps_ref, start):
    result = padded_ref[pl.ds(start, CHUNK), :] * taps_ref[0:1, :]
    for j in range(1, 4):
        result = result + padded_ref[pl.ds(start + j, CHUNK), :] * taps_ref[j : j + 1, :]
    return result


def forward_kernel(
    scalars_ref, x_ref, w_in_ref, w_aux_ref, w_out_ref, taps_ref, gain_ref,
    part_ref, heads_ref, proj_ref, gate_ref, rates_ref, inverse_ref, fresh_ref, o_ref, state_ref,
    padded, memory,
):
    @pl.when(pl.program_id(0) == 0)
    def _():
        memory[...] = jnp.zeros_like(memory)
        padded[0:8, :] = jnp.zeros((8, CONV_CH), F32)

    x = x_ref[...]
    proj = mm(x, w_in_ref[...])
    rates = mm(x, w_aux_ref[...])
    rates_ref[...] = rates
    qkv = proj[:, :CONV_CH]
    proj_ref[...] = qkv
    gate_in = proj[:, CONV_CH:]
    gate_ref[...] = gate_in
    padded[8 : 8 + CHUNK, :] = qkv
    conv = conv_rows(padded, taps_ref, 5)
    padded[0:8, :] = qkv[CHUNK - 8 :, :]
    act, _ = silu_of(conv)
    q, k, v = act[:, :KEY], act[:, KEY : 2 * KEY], act[:, 2 * KEY :]
    q = q * (lax.rsqrt(jnp.sum(q * q, axis=1, keepdims=True) + 1e-6) * KEY**-0.5)
    k = k * lax.rsqrt(jnp.sum(k * k, axis=1, keepdims=True) + 1e-6)
    rows, cols = iotas()
    write, step, _ = rates_of(rates, scalars_ref[0], scalars_ref[1])
    decay, growth, rest, final = decay_terms(step, rows, cols)
    coupling = jnp.where(rows > cols, wide(write, CHUNK) * mm3(k, k, NT) * decay, 0.0)
    inverse = solve_unit(coupling, rows, cols, mm3)
    inverse_ref[...] = inverse.astype(BF16)
    within = mm(q, k, NT) * decay
    state = memory[...]
    state_ref[...] = state
    low_state = state.astype(BF16)
    source = wide(write, VAL) * (v - wide(growth, VAL) * mm(k, low_state))
    fresh = mm3(inverse, source)
    fresh_ref[...] = fresh
    o = wide(growth, VAL) * mm(q, low_state) + mm(within, fresh)
    o_ref[...] = o
    memory[...] = wide(final, VAL) * state + mm(k * wide(rest, KEY), fresh, TN)
    scaled = o * lax.rsqrt(jnp.mean(o * o, axis=1, keepdims=True) + 1e-5) * gain_ref[...]
    heads = (scaled * silu_of(gate_in)[0]).astype(BF16)
    heads_ref[...] = heads
    part_ref[...] = mm(heads, w_out_ref[...], NT).astype(BF16)


def mixer_forward(x, pack, taps, gain, scalars):
    length, width = x.shape
    chunks = length // CHUNK
    row = lambda cols: pl.BlockSpec((CHUNK, cols), lambda i: (i, 0))
    fixed = lambda shape, at: pl.BlockSpec(shape, lambda i: (0, at), pipeline_mode=pl.Buffered(1))
    out = lambda cols, kind: jax.ShapeDtypeStruct((length, cols), kind)
    return pl.pallas_call(
        forward_kernel,
        grid=(chunks,),
        in_specs=[
            pl.BlockSpec(memory_space=pltpu.SMEM),
            row(width),
            fixed((width, 1536), 0),
            fixed((width, LANES), 16),
            fixed((width, VAL), 3),
            fixed((4, CONV_CH), 0),
            fixed((1, VAL), 0),
        ],
        out_specs=[
            row(width), row(VAL), row(CONV_CH), row(VAL), row(LANES), row(CHUNK), row(VAL), row(VAL),
            pl.BlockSpec((None, KEY, VAL), lambda i: (i, 0, 0)),
        ],
        out_shape=[
            out(width, BF16), out(VAL, BF16), out(CONV_CH, F32), out(VAL, F32), out(LANES, F32),
            out(CHUNK, BF16), out(VAL, F32), out(VAL, F32),
            jax.ShapeDtypeStruct((chunks, KEY, VAL), F32),
        ],
        scratch_shapes=[pltpu.VMEM((CHUNK + 8, CONV_CH), F32), pltpu.VMEM((KEY, VAL), F32)],
        compiler_params=pltpu.CompilerParams(
            dimension_semantics=("arbitrary",), vmem_limit_bytes=56 * 1024 * 1024
        ),
        cost_estimate=pl.CostEstimate(
            flops=16 * 10**9, bytes_accessed=80 * 10**6, transcendentals=4 * 10**6
        ),
        name="mixer_forward",
    )(scalars, x, pack, pack, pack, taps, gain)


def unit_back(grad, vector, scale):
    inv = lax.rsqrt(jnp.sum(vector * vector, axis=1, keepdims=True) + 1e-6)
    dot = jnp.sum(grad * vector, axis=1, keepdims=True)
    return (grad - vector * (inv * inv * dot)) * (inv * scale)


def backward_kernel(
    scalars_ref, g_ref, w_in_ref, w_aux_ref, w_out_ref, taps_ref, gain_ref,
    proj_ref, halo_ref, gate_ref, rates_ref, inverse_ref, fresh_ref, o_ref, state_ref,
    part_ref, dproj_ref, drates_ref, dtaps_ref, dgain_ref, dscalars_ref,
    padded, dpadded, dmemory,
):
    at = pl.program_id(0)
    last = pl.num_programs(0) - 1

    @pl.when(at == 0)
    def _():
        dmemory[...] = jnp.zeros_like(dmemory)
        dpadded[CHUNK : CHUNK + 8, :] = jnp.zeros((8, CONV_CH), F32)
        dtaps_ref[...] = jnp.zeros_like(dtaps_ref)
        dgain_ref[...] = jnp.zeros_like(dgain_ref)
        dscalars_ref[...] = jnp.zeros_like(dscalars_ref)

    rows, cols = iotas()
    padded[8 : 8 + CHUNK, :] = proj_ref[...]
    padded[0:8, :] = jnp.where(at == last, 0.0, halo_ref[...])
    conv = conv_rows(padded, taps_ref, 5)
    act, sig = silu_of(conv)
    act_q, act_k, v = act[:, :KEY], act[:, KEY : 2 * KEY], act[:, 2 * KEY :]
    q = act_q * (lax.rsqrt(jnp.sum(act_q * act_q, axis=1, keepdims=True) + 1e-6) * KEY**-0.5)
    k = act_k * lax.rsqrt(jnp.sum(act_k * act_k, axis=1, keepdims=True) + 1e-6)
    rates = rates_ref[...]
    write, step, sig_decay = rates_of(rates, scalars_ref[0], scalars_ref[1])
    decay, growth, rest, final = decay_terms(step, rows, cols)
    growth_v = wide(growth, VAL)
    write_v = wide(write, VAL)
    low_q, low_k = q.astype(BF16), k.astype(BF16)
    below = rows > cols
    strict_decay = jnp.where(below, decay, 0.0)
    keys = mm(low_k, low_k, NT) * strict_decay * wide(write, CHUNK)
    within = mm(low_q, low_k, NT) * decay
    dheads = mm(g_ref[...], w_out_ref[...])
    o = o_ref[...]
    gate_in = gate_ref[...]
    gate, gate_sig = silu_of(gate_in)
    inv = lax.rsqrt(jnp.mean(o * o, axis=1, keepdims=True) + 1e-5)
    normal = o * inv
    gain = gain_ref[...]
    dgate = dheads * normal * gain * (gate_sig * (1.0 + gate_in * (1.0 - gate_sig)))
    dscaled = dheads * gate
    dgain_ref[...] += jnp.sum(dscaled * normal, axis=0, keepdims=True)
    dnormal = dscaled * gain
    do = inv * (dnormal - normal * jnp.mean(dnormal * normal, axis=1, keepdims=True))
    state = state_ref[...]
    low_state = state.astype(BF16)
    fresh = fresh_ref[...]
    low_fresh = fresh.astype(BF16)
    dstate = dmemory[...]
    low_dstate = dstate.astype(BF16)
    low_do = do.astype(BF16)
    k_rest = k * wide(rest, KEY)
    rest_dstate = mm(k_rest, low_dstate)
    dfresh = mm(within, low_do, TN) + rest_dstate
    dsource = mm(inverse_ref[...], dfresh, TN)
    low_dsource = dsource.astype(BF16)
    dv = write_v * dsource
    dread = -(growth_v * dv)
    low_dread = dread.astype(BF16)
    do_growth = growth_v * do
    low_do_growth = do_growth.astype(BF16)
    dwithin = mm(low_do, low_fresh, NT)
    dcoupling = -mm(low_dsource, low_fresh, NT)
    dkeys = dcoupling * strict_decay * wide(write, CHUNK)
    dpairs = dwithin * decay
    dq = mm(low_do_growth, low_state, NT) + mm(dpairs, low_k)
    dk = (
        mm(low_dread, low_state, NT)
        + mm(dpairs, low_q, TN)
        + mm(dkeys + dkeys.T, low_k)
        + wide(rest, KEY) * mm(low_fresh, low_dstate, NT)
    )
    dmemory[...] = (
        wide(final, VAL) * dstate + mm(low_q, low_do_growth, TN) + mm(low_k, low_dread, TN)
    )
    spread = dwithin * within + dcoupling * keys
    straddle = jnp.where(below, mm_exact_left((rows <= cols).astype(BF16), spread), 0.0)
    read_rows = jnp.sum(
        do_growth * mm(low_q, low_state) + dread * mm(low_k, low_state), axis=1, keepdims=True
    )
    rest_rows = jnp.sum(fresh * rest_dstate, axis=1, keepdims=True)
    carried = jnp.sum(dstate * state) * final[0:1, 0:1]
    suffix = mm_exact_left(
        (rows <= cols).astype(BF16), jnp.broadcast_to(read_rows, (CHUNK, LANES))
    ) + mm_exact_left((rows > cols).astype(BF16), jnp.broadcast_to(rest_rows, (CHUNK, LANES)))
    dstep = suffix + jnp.sum(straddle, axis=1, keepdims=True) + carried
    dlogit = dstep * (-scalars_ref[0]) * sig_decay
    dwrite = (1.0 - write) * jnp.sum(dsource * fresh, axis=1, keepdims=True)
    lane = lax.broadcasted_iota(jnp.int32, (CHUNK, LANES), 1)
    drates = jnp.where(lane == 0, dwrite, jnp.where(lane == 1, dlogit, 0.0))
    low_drates = drates.astype(BF16)
    drates_ref[...] = low_drates
    dscalars_ref[0:1, :] += jnp.sum(dstep * step, axis=0, keepdims=True)
    dscalars_ref[1:2, :] += jnp.sum(dlogit, axis=0, keepdims=True)
    dact = jnp.concatenate(
        [unit_back(dq, act_q, KEY**-0.5), unit_back(dk, act_k, 1.0), dv], axis=1
    )
    dconv = dact * (sig * (1.0 + conv * (1.0 - sig)))
    dpadded[0:CHUNK, :] = dconv
    dtaps_ref[...] += jnp.concatenate(
        [
            jnp.sum(dconv * padded[5 + j : 5 + j + CHUNK, :], axis=0, keepdims=True)
            for j in range(4)
        ],
        axis=0,
    )
    dqkv = dconv * taps_ref[3:4, :]
    for j in range(3):
        dqkv = dqkv + dpadded[pl.ds(3 - j, CHUNK), :] * taps_ref[j : j + 1, :]
    dpadded[CHUNK : CHUNK + 8, :] = dconv[0:8, :]
    low_dproj = jnp.concatenate([dqkv, dgate], axis=1).astype(BF16)
    dproj_ref[...] = low_dproj
    part_ref[...] = (
        mm(low_dproj, w_in_ref[...], NT) + mm(low_drates, w_aux_ref[...], NT)
    ).astype(BF16)


def mixer_backward(g, pack, taps, gain, scalars, saved):
    proj, gate_in, rates, inverse, fresh, o, states = saved
    length, width = g.shape
    chunks = length // CHUNK
    back = chunks - 1
    row = lambda cols: pl.BlockSpec((CHUNK, cols), lambda i: (back - i, 0))
    fixed = lambda shape, at: pl.BlockSpec(shape, lambda i: (0, at), pipeline_mode=pl.Buffered(1))
    out = lambda cols, kind: jax.ShapeDtypeStruct((length, cols), kind)
    steps = CHUNK // 8
    return pl.pallas_call(
        backward_kernel,
        grid=(chunks,),
        in_specs=[
            pl.BlockSpec(memory_space=pltpu.SMEM),
            row(width),
            fixed((width, 1536), 0),
            fixed((width, LANES), 16),
            fixed((width, VAL), 3),
            fixed((4, CONV_CH), 0),
            fixed((1, VAL), 0),
            row(CONV_CH),
            pl.BlockSpec((8, CONV_CH), lambda i: (jnp.maximum((back - i) * steps - 1, 0), 0)),
            row(VAL), row(LANES), row(CHUNK), row(VAL), row(VAL),
            pl.BlockSpec((None, KEY, VAL), lambda i: (back - i, 0, 0)),
        ],
        out_specs=[
            row(width), row(1536), row(LANES),
            pl.BlockSpec((4, CONV_CH), lambda i: (0, 0)),
            pl.BlockSpec((1, VAL), lambda i: (0, 0)),
            pl.BlockSpec((8, LANES), lambda i: (0, 0)),
        ],
        out_shape=[
            out(width, BF16), out(1536, BF16), out(LANES, BF16),
            jax.ShapeDtypeStruct((4, CONV_CH), F32),
            jax.ShapeDtypeStruct((1, VAL), F32),
            jax.ShapeDtypeStruct((8, LANES), F32),
        ],
        scratch_shapes=[
            pltpu.VMEM((CHUNK + 8, CONV_CH), F32),
            pltpu.VMEM((CHUNK + 8, CONV_CH), F32),
            pltpu.VMEM((KEY, VAL), F32),
        ],
        compiler_params=pltpu.CompilerParams(
            dimension_semantics=("arbitrary",), vmem_limit_bytes=56 * 1024 * 1024
        ),
        cost_estimate=pl.CostEstimate(
            flops=16 * 10**9, bytes_accessed=80 * 10**6, transcendentals=4 * 10**6
        ),
        name="mixer_backward",
    )(scalars, g, pack, pack, pack, taps, gain, proj, proj, gate_in, rates, inverse, fresh, o, states)


PIECES = 4
AXES = ("chip", "core", "zp", "zl")


def partners():
    core, zl = lax.axis_index("core"), lax.axis_index("zl")
    return core, zl, {"core": 1 - core}, {"zl": 1 - zl}


def greet():
    _, _, beside, across = partners()
    barrier = pltpu.get_barrier_semaphore()
    for device in (beside, across):
        pl.semaphore_signal(
            barrier, inc=1, device_id=device, device_id_type=pl.DeviceIdType.MESH
        )
    pl.semaphore_wait(barrier, 2)


class Block:
    def __init__(self, zl, core, rows):
        self.first = (zl * 2 + core) * rows
        self.size = rows // PIECES

    def piece(self, p):
        return pl.ds(pl.multiple_of(self.first + p * self.size, self.size), self.size)


def remote(src, dst, send, recv, device):
    return pltpu.make_async_remote_copy(
        src_ref=src, dst_ref=dst, send_sem=send, recv_sem=recv,
        device_id=device, device_id_type=pl.DeviceIdType.MESH,
    )


class Scatter:
    def __init__(self, partial, beside_far, beside_own, sums, far, send, recv):
        core, zl, beside, across = partners()
        rows = far.shape[0]
        self.partial, self.beside_far, self.beside_own = partial, beside_far, beside_own
        self.sums, self.far = sums, far
        self.size = rows // PIECES
        self.own = Block(zl, core, rows)
        self.away = Block(1 - zl, core, rows)
        own_beside, away_beside = Block(zl, 1 - core, rows), Block(1 - zl, 1 - core, rows)
        self.to_far = [
            remote(partial.at[away_beside.piece(p)], beside_far.at[self.local(p)],
                   send.at[0, p], recv.at[0, p], beside)
            for p in range(PIECES)
        ]
        self.to_own = [
            remote(partial.at[own_beside.piece(p)], beside_own.at[self.local(p)],
                   send.at[1, p], recv.at[1, p], beside)
            for p in range(PIECES)
        ]
        self.cross = [
            remote(sums.at[self.local(p)], far.at[self.local(p)],
                   send.at[2, p], recv.at[2, p], across)
            for p in range(PIECES)
        ]

    def local(self, p):
        return pl.ds(p * self.size, self.size)

    def start(self):
        for copy in self.to_far:
            copy.start()
        for copy in self.to_own:
            copy.start()
        for p in range(PIECES):
            self.to_far[p].wait_recv()
            at = self.local(p)
            self.sums[at, :] = (
                self.partial[self.away.piece(p), :].astype(F32) + self.beside_far[at, :].astype(F32)
            ).astype(BF16)
            self.cross[p].start()

    def total(self, p):
        self.to_own[p].wait_recv()
        self.cross[p].wait_recv()
        at = self.local(p)
        return (
            self.partial[self.own.piece(p), :].astype(F32)
            + self.beside_own[at, :].astype(F32)
            + self.far[at, :].astype(F32)
        )

    def finish(self):
        for copies in (self.to_far, self.to_own, self.cross):
            for copy in copies:
                copy.wait_send()


class Gather:
    def __init__(self, gathered, send, recv, first):
        core, zl, beside, across = partners()
        rows = gathered.shape[0] // 4
        self.gathered = gathered
        self.own = Block(zl, core, rows)
        other = Block(1 - zl, core, rows)
        make = lambda block, at, device: [
            remote(gathered.at[block.piece(p)], gathered.at[block.piece(p)],
                   send.at[first + at, p], recv.at[first + at, p], device)
            for p in range(PIECES)
        ]
        self.across = make(self.own, 0, across)
        self.beside = make(self.own, 1, beside)
        self.forward = make(other, 2, beside)

    def put(self, p, rows):
        self.gathered[self.own.piece(p), :] = rows
        self.across[p].start()
        self.beside[p].start()

    def finish(self):
        for p in range(PIECES):
            self.across[p].wait_recv()
            self.forward[p].start()
        for p in range(PIECES):
            self.beside[p].wait_recv()
            self.forward[p].wait_recv()
        for copies in (self.across, self.beside, self.forward):
            for copy in copies:
                copy.wait_send()


def normed_of(x, gain):
    return x * lax.rsqrt(jnp.mean(x * x, axis=1, keepdims=True) + 1e-6) * gain


def first_kernel(x_ref, gain_ref, out_ref, send, recv):
    greet()
    gather = Gather(out_ref, send, recv, 0)
    size = x_ref.shape[0] // PIECES
    for p in range(PIECES):
        x = x_ref[p * size : (p + 1) * size, :].astype(F32)
        gather.put(p, normed_of(x, gain_ref[...]).astype(BF16))
    gather.finish()


def forward_bridge_kernel(
    partial, x_ref, gain_ref, new_ref, out_ref, beside_far, beside_own, sums, far, send, recv
):
    greet()
    scatter = Scatter(partial, beside_far, beside_own, sums, far, send, recv)
    gather = Gather(out_ref, send, recv, 3)
    scatter.start()
    for p in range(PIECES):
        at = scatter.local(p)
        x = x_ref[at, :].astype(F32) + scatter.total(p)
        new_ref[at, :] = x
        gather.put(p, normed_of(x, gain_ref[...]).astype(BF16))
    scatter.finish()
    gather.finish()


def norm_back(total, x, gain):
    inv = lax.rsqrt(jnp.mean(x * x, axis=1, keepdims=True) + 1e-6)
    unit = x * inv
    scaled = total * gain
    grad = inv * (scaled - unit * jnp.mean(scaled * unit, axis=1, keepdims=True))
    return grad, jnp.sum(total * unit, axis=0, keepdims=True)


def backward_bridge_kernel(
    partial, x_ref, gain_ref, grad_ref, new_ref, out_ref, dgain_ref,
    beside_far, beside_own, sums, far, send, recv
):
    greet()
    scatter = Scatter(partial, beside_far, beside_own, sums, far, send, recv)
    gather = Gather(out_ref, send, recv, 3)
    scatter.start()
    dgain = jnp.zeros_like(dgain_ref)
    for p in range(PIECES):
        at = scatter.local(p)
        grad, part = norm_back(scatter.total(p), x_ref[at, :].astype(F32), gain_ref[...])
        dgain = dgain + part
        grad = grad + grad_ref[at, :].astype(F32)
        new_ref[at, :] = grad
        gather.put(p, grad.astype(BF16))
    dgain_ref[...] = dgain
    scatter.finish()
    gather.finish()


def forward_last_kernel(partial, x_ref, new_ref, beside_far, beside_own, sums, far, send, recv):
    greet()
    scatter = Scatter(partial, beside_far, beside_own, sums, far, send, recv)
    scatter.start()
    for p in range(PIECES):
        at = scatter.local(p)
        new_ref[at, :] = (x_ref[at, :] + scatter.total(p)).astype(BF16)
    scatter.finish()


def backward_last_kernel(
    partial, x_ref, gain_ref, grad_ref, new_ref, dgain_ref,
    beside_far, beside_own, sums, far, send, recv
):
    greet()
    scatter = Scatter(partial, beside_far, beside_own, sums, far, send, recv)
    scatter.start()
    dgain = jnp.zeros_like(dgain_ref)
    for p in range(PIECES):
        at = scatter.local(p)
        grad, part = norm_back(scatter.total(p), x_ref[at, :].astype(F32), gain_ref[...])
        dgain = dgain + part
        new_ref[at, :] = (grad + grad_ref[at, :]).astype(BF16)
    dgain_ref[...] = dgain
    scatter.finish()


def comm_call(kernel, number, outs, args, scatters, gathers):
    rows = args[1].shape[0] if scatters else args[0].shape[0]
    width = args[0].shape[1]
    vmem = pl.BlockSpec(memory_space=pltpu.VMEM)
    block = lambda: pltpu.VMEM((rows, width), BF16)
    hops = 3 * scatters + 3 * gathers
    kinds = sum(1 << at for at, arg in enumerate(args[1:]) if arg.dtype == BF16)
    return pl.pallas_call(
        kernel,
        in_specs=[vmem] * len(args),
        out_specs=[vmem] * len(outs),
        out_shape=[jax.ShapeDtypeStruct(shape, kind) for shape, kind in outs],
        scratch_shapes=[block() for _ in range(4 * scatters)]
        + [pltpu.SemaphoreType.DMA((hops, PIECES)), pltpu.SemaphoreType.DMA((hops, PIECES))],
        compiler_params=pltpu.CompilerParams(
            collective_id=number + 6 * min(kinds, 2), has_side_effects=True, vmem_limit_bytes=48 * 1024 * 1024
        ),
        cost_estimate=pl.CostEstimate(
            flops=rows * width * 20, bytes_accessed=40 * 1024 * 1024, transcendentals=0
        ),
        name=kernel.__name__.replace("_kernel", ""),
    )(*args)


def first_gather(x, gain):
    rows, width = x.shape
    return comm_call(first_kernel, 0, [((4 * rows, width), BF16)], (x, gain), 0, 1)[0]


def forward_bridge(partial, x, gain):
    rows, width = x.shape
    return comm_call(
        forward_bridge_kernel, 1, [((rows, width), F32), ((4 * rows, width), BF16)],
        (partial, x, gain), 1, 1,
    )


def backward_bridge(partial, x, gain, grad):
    rows, width = x.shape
    return comm_call(
        backward_bridge_kernel, 2,
        [((rows, width), F32), ((4 * rows, width), BF16), ((1, width), F32)],
        (partial, x, gain, grad), 1, 1,
    )


def forward_last(partial, x):
    rows, width = x.shape
    return comm_call(forward_last_kernel, 3, [((rows, width), BF16)], (partial, x), 1, 0)[0]


def backward_last(partial, x, gain, grad):
    rows, width = x.shape
    return comm_call(
        backward_last_kernel, 4, [((rows, width), BF16), ((1, width), F32)],
        (partial, x, gain, grad), 1, 0,
    )


def gather_plain_kernel(x_ref, out_ref, send, recv):
    greet()
    gather = Gather(out_ref, send, recv, 0)
    size = x_ref.shape[0] // PIECES
    for p in range(PIECES):
        gather.put(p, x_ref[p * size : (p + 1) * size, :])
    gather.finish()


def gather_plain(x):
    rows, width = x.shape
    return comm_call(gather_plain_kernel, 5, [((4 * rows, width), BF16)], (x,), 0, 1)[0]


def swiglu_rows(paired):
    gate_part, up_part = jnp.split(paired, 2, axis=1)
    return jax.nn.silu(gate_part) * up_part


def dot32(a, b, dims):
    return lax.dot_general(a, b, dims, preferred_element_type=F32)


def row_major(x):
    return with_layout_constraint(x, Layout(major_to_minor=tuple(range(x.ndim))))


def linear(sizes, index):
    place = 0
    for size, at in zip(sizes, index):
        place = place * size + at
    return place


class Roles:
    def __init__(self):
        self.sizes = tuple(lax.axis_size(name) for name in AXES)
        self.chips, self.cores, self.zps, self.zls = self.sizes
        assert self.cores == 2 and self.zps == 2 and self.zls == 2

    def every(self):
        for chip in range(self.chips):
            for core in range(2):
                for zp in range(2):
                    for zl in range(2):
                        yield chip, core, zp, zl

    def rows_pairs(self):
        pairs = []
        for chip, core, zp, zl in self.every():
            slot, part = zp * self.chips + chip, zl * 2 + core
            source = linear(self.sizes, (slot // 2, slot % 2, part // 2, part % 2))
            pairs.append((source, linear(self.sizes, (chip, core, zp, zl))))
        return pairs

    def weight_pairs(self, which):
        pairs = []
        for chip, core, zp, zl in self.every():
            head = zp * 2 + zl
            to = (chip, head % 2, core ^ which, head // 2)
            pairs.append(
                (linear(self.sizes, (chip, core, zp, zl)), linear(self.sizes, to))
            )
        return pairs


def flipped(pairs):
    return [(b, a) for a, b in pairs]


def weights_in(pack, roles):
    halves = [lax.ppermute(pack, AXES, roles.weight_pairs(which)) for which in range(2)]
    swap = lax.axis_index("zp") == 1
    ordered = jnp.concatenate(
        [jnp.where(swap, halves[1], halves[0]), jnp.where(swap, halves[0], halves[1])], axis=0
    )
    return row_major(lax.all_gather(row_major(ordered), "chip", axis=0, tiled=True))


def weights_out(grads, roles):
    mine = lax.psum_scatter(grads, "chip", scatter_dimension=0, tiled=True)
    rows = mine.shape[0] // 2
    swap = lax.axis_index("zp") == 1
    low, high = mine[:rows], mine[rows:]
    halves = [jnp.where(swap, high, low), jnp.where(swap, low, high)]
    back = [
        lax.ppermute(half, AXES, flipped(roles.weight_pairs(which)))
        for which, half in enumerate(halves)
    ]
    return back[0].astype(F32) + back[1].astype(F32)


def deal(values, order):
    spread = lax.all_to_all(values, ("chip", "core"), split_axis=2, concat_axis=1, tiled=True)
    picked = jnp.take(spread, order, axis=1)
    return lax.all_to_all(picked, ("chip", "core"), split_axis=1, concat_axis=2, tiled=True)


def shards(
    tokens, lengths, order, norm_mix, w_query, w_key, w_value, w_gate, w_decay, conv_filter,
    log_rate, step_bias, norm_heads, w_out, norm_ffn, w_ffn_gate, w_ffn_up, w_ffn_down, cotangent,
):
    roles = Roles()
    layer_count = w_query.shape[0]
    heads_total = log_rate.shape[1]
    chip, core, zp, zl = (lax.axis_index(name) for name in AXES)
    head = zl * 2 + core
    rows_local, slots_local, width = tokens.shape
    assert slots_local == 1 and w_decay.shape[2] == 1
    slot_total = order.shape[0]
    units = w_ffn_gate.shape[2]
    rows_part = w_query.shape[1]
    to_roles = roles.rows_pairs()

    packs = []
    for layer in range(layer_count):
        aux = jnp.concatenate([w_decay[layer, :, 0, :], conv_filter[layer, :, 0, :].T], axis=1)
        aux = jnp.pad(aux, ((0, 0), (0, LANES - aux.shape[1])))
        mix = jnp.concatenate(
            [w_query[layer], w_key[layer], w_value[layer], w_gate[layer], w_out[layer].T, aux], axis=1
        )
        ffn = jnp.concatenate([w_ffn_gate[layer], w_ffn_up[layer], w_ffn_down[layer].T], axis=1)
        packs.append((weights_in(row_major(mix), roles), weights_in(row_major(ffn), roles)))

    dealt = deal(tokens, order)[:, 0, :]
    residual = lax.ppermute(dealt, AXES, to_roles)

    positions = (zp * 2 + zl) * rows_local + jnp.arange(rows_local)
    my_length = lengths[order[chip * 2 + core]]
    start = cotangent[:, 0, :] * (positions < my_length).astype(BF16)[:, None]
    gradient = lax.ppermute(start, AXES, to_roles)
    grad_rows = gather_plain(gradient)

    saved = []
    gains = [
        (norm_mix[layer].astype(F32)[None], norm_ffn[layer].astype(F32)[None])
        for layer in range(layer_count)
    ]
    rows_in = first_gather(residual, gains[0][0])
    for layer in range(layer_count):
        mix, ffn = packs[layer]
        taps = mix[:, 2050:2054].T.astype(F32)
        gain_heads = norm_heads[layer].astype(F32)[None]
        scalars = jnp.concatenate(
            [
                jnp.exp(lax.dynamic_slice_in_dim(log_rate[layer].astype(F32), head, 1)),
                lax.dynamic_slice_in_dim(step_bias[layer].astype(F32), head, 1),
            ]
        )
        part, heads, *kept = mixer_forward(rows_in, mix, taps, gain_heads, scalars)
        middle, rows_ffn = forward_bridge(part, residual, gains[layer][1])
        paired = dot32(rows_ffn, ffn[:, : 2 * units], NN)
        hidden, swiglu_back = jax.vjp(swiglu_rows, paired)
        hidden = hidden.astype(BF16)
        part = dot32(hidden, ffn[:, 2 * units :], NT).astype(BF16)
        saved.append(
            (residual, rows_in, taps, gain_heads, scalars, kept, heads, middle, rows_ffn,
             swiglu_back, hidden)
        )
        if layer + 1 < layer_count:
            residual, rows_in = forward_bridge(part, middle, gains[layer + 1][0])
        else:
            mixed = forward_last(part, middle)
    mixed = lax.ppermute(mixed, AXES, flipped(to_roles))

    weight_grads = [None] * layer_count
    small_terms = [None] * layer_count
    for layer in reversed(range(layer_count)):
        mix, ffn = packs[layer]
        (residual, rows_in, taps, gain_heads, scalars, kept, heads, middle, rows_ffn,
         swiglu_back, hidden) = saved[layer]
        (grad_paired,) = swiglu_back(dot32(grad_rows, ffn[:, 2 * units :], NN))
        paired_low = grad_paired.astype(BF16)
        part = dot32(paired_low, ffn[:, : 2 * units], NT).astype(BF16)
        ffn_grads = jnp.concatenate(
            [dot32(rows_ffn, paired_low, TN).astype(BF16), dot32(grad_rows, hidden, TN).astype(BF16)],
            axis=1,
        )
        ffn_grads = weights_out(ffn_grads, roles)
        gradient, grad_rows, dgain_ffn = backward_bridge(part, middle, gains[layer][1], gradient)
        part, dproj, drates, dtaps, dgain, dscalars = mixer_backward(
            grad_rows, mix, taps, gain_heads, scalars, kept
        )
        aux = dot32(rows_in, drates, TN) + jnp.pad(dtaps.T, ((0, 0), (2, LANES - 6)))
        mix_grads = jnp.concatenate(
            [
                dot32(rows_in, dproj, TN).astype(BF16),
                dot32(grad_rows, heads, TN).astype(BF16),
                aux.astype(BF16),
            ],
            axis=1,
        )
        mix_grads = weights_out(mix_grads, roles)
        if layer:
            gradient, grad_rows, dgain_mix = backward_bridge(part, residual, gains[layer][0], gradient)
        else:
            gradient, dgain_mix = backward_last(part, residual, gains[layer][0], gradient)
        weight_grads[layer] = (
            mix_grads[:, :256],
            mix_grads[:, 256:512],
            mix_grads[:, 512:1024],
            mix_grads[:, 1024:1536],
            mix_grads[:, 2048:2050].reshape(rows_part, 1, 2),
            mix_grads[:, 2050:2054].T.reshape(4, 1, rows_part),
            mix_grads[:, 1536:2048].T,
            ffn_grads[:, :units],
            ffn_grads[:, units : 2 * units],
            ffn_grads[:, 2 * units :].T,
        )
        mine = (jnp.arange(heads_total) == head).astype(F32)
        small_terms[layer] = jnp.concatenate(
            [dgain_mix[0], dgain_ffn[0], dgain[0], mine * dscalars[0, 0], mine * dscalars[1, 0]]
        )
    small = lax.psum(jnp.stack(small_terms), AXES)
    dealt_grad = lax.ppermute(gradient, AXES, flipped(to_roles))
    inverse_order = (
        jnp.zeros((slot_total,), jnp.int32).at[order].set(jnp.arange(slot_total, dtype=jnp.int32))
    )
    grad_home = deal(dealt_grad[:, None, :], inverse_order).astype(F32)
    members = [jnp.stack([grads[m] for grads in weight_grads]) for m in range(10)]
    ends = 2 * width + VAL
    return (
        mixed[:, None, :],
        grad_home,
        small[:, :width],
        members[0], members[1], members[2], members[3], members[4], members[5],
        small[:, ends : ends + heads_total],
        small[:, ends + heads_total :],
        small[:, 2 * width : ends],
        members[6],
        small[:, width : 2 * width],
        members[7], members[8], members[9],
    )


def solution(mesh):
    dp, tensor = mesh.devices.shape
    mesh = Mesh(mesh.devices.reshape(dp // 2, 2, tensor // 2, 2), AXES)
    d, t = ("chip", "core"), ("zp", "zl")
    rows = P(t, d, None)
    by_rows, by_columns = P(None, d, t), P(None, t, d)
    heads, filters = P(None, d, t, None), P(None, None, t, d)
    return jax.shard_map(
        shards,
        mesh=mesh,
        in_specs=(
            rows, P(), P(), P(), by_rows, by_rows, by_rows, by_rows, heads, filters,
            P(), P(), P(), by_columns, P(), by_rows, by_rows, by_columns, rows,
        ),
        out_specs=(
            rows, rows, P(), by_rows, by_rows, by_rows, by_rows, heads, filters,
            P(), P(), P(), by_columns, P(), by_rows, by_rows, by_columns,
        ),
        check_vma=False,
    )
```

```python
import functools
import jax
import jax.numpy as jnp
from jax import lax
from jax.experimental import pallas as pl
from jax.experimental.layout import Layout, with_layout_constraint
from jax.experimental.pallas import tpu as pltpu
from jax.sharding import Mesh, PartitionSpec as P

CHUNK = 256
LANES = 128
KEY = 256
VAL = 512
CONV_CH = 2 * KEY + VAL
F32 = jnp.float32
BF16 = jnp.bfloat16
NN = (((1,), (0,)), ((), ()))
NT = (((1,), (1,)), ((), ()))
TN = (((0,), (0,)), ((), ()))


def mm(a, b, dims=NN):
    return lax.dot_general(
        a.astype(BF16), b.astype(BF16), dims, preferred_element_type=F32
    )


def split_low(a):
    high = a.astype(BF16)
    return high, (a - high.astype(F32)).astype(BF16)


def mm3(a, b, dims=NN):
    a_high, a_low = split_low(a)
    b_high, b_low = split_low(b)
    dot = functools.partial(
        lax.dot_general, dimension_numbers=dims, preferred_element_type=F32
    )
    return dot(a_high, b_high) + (dot(a_high, b_low) + dot(a_low, b_high))


def mm_exact_left(a, b, dims=NN):
    a = a.astype(BF16)
    high = b.astype(BF16)
    rest = b - high.astype(F32)
    mid = rest.astype(BF16)
    low = (rest - mid.astype(F32)).astype(BF16)
    dot = functools.partial(
        lax.dot_general, dimension_numbers=dims, preferred_element_type=F32
    )
    return dot(a, high) + (dot(a, mid) + dot(a, low))


def iotas():
    rows = lax.broadcasted_iota(jnp.int32, (CHUNK, CHUNK), 0)
    cols = lax.broadcasted_iota(jnp.int32, (CHUNK, CHUNK), 1)
    return rows, cols


def wide(col_block, width):
    return jnp.concatenate([col_block] * (width // LANES), axis=1)


def rates_of(rates, rate, bias):
    write = jax.nn.sigmoid(jnp.broadcast_to(rates[:, 0:1], (CHUNK, LANES)))
    logit = jnp.broadcast_to(rates[:, 1:2], (CHUNK, LANES)) + bias
    soft = jnp.maximum(logit, 0.0) + jnp.log1p(jnp.exp(-jnp.abs(logit)))
    return write, -rate * soft, jax.nn.sigmoid(logit)


def decay_terms(step, rows, cols):
    inclusive = (rows >= cols).astype(BF16)
    total = mm_exact_left(inclusive, step)
    spread = wide(total, CHUNK) - jnp.concatenate([total.T] * (CHUNK // LANES), axis=0)
    decay = jnp.where(rows >= cols, jnp.exp(jnp.minimum(spread, 0.0)), 0.0)
    last = jnp.broadcast_to(total[CHUNK - 1 : CHUNK, :], (CHUNK, LANES))
    return decay, jnp.exp(total), jnp.exp(last - total), jnp.exp(last)


def solve_unit(coupling, rows, cols, product):
    same = ((rows >> 1) == (cols >> 1)) & (rows != cols)
    inverse = jnp.where(rows == cols, 1.0, 0.0) - jnp.where(same, coupling, 0.0)
    for level in range(1, CHUNK.bit_length() - 1):
        between = ((rows >> (level + 1)) == (cols >> (level + 1))) & (
            (rows >> level) != (cols >> level)
        )
        part = jnp.where(between, coupling, 0.0)
        inverse = inverse - product(product(inverse, part), inverse)
    return inverse


def silu_of(x):
    gate = jax.nn.sigmoid(x)
    return x * gate, gate


def conv_rows(padded_ref, taps_ref, start):
    result = padded_ref[pl.ds(start, CHUNK), :] * taps_ref[0:1, :]
    for j in range(1, 4):
        result = result + padded_ref[pl.ds(start + j, CHUNK), :] * taps_ref[j : j + 1, :]
    return result


def forward_kernel(
    chips, scalars_ref, x_ref, w_in_ref, w_aux_ref, w_out_ref, taps_ref, gain_ref, pack_ref,
    part_ref, heads_ref, proj_ref, gate_ref, rates_ref, inverse_ref, fresh_ref, o_ref, state_ref,
    wide_ref, padded, memory, send, recv,
):
    weights = Weights(pack_ref, wide_ref, send, recv, chips)

    @pl.when(pl.program_id(0) == 0)
    def _():
        wait_greetings(weights.greet())
        weights.start()
        memory[...] = jnp.zeros_like(memory)
        padded[0:8, :] = jnp.zeros((8, CONV_CH), F32)

    x = x_ref[...]
    proj = mm(x, w_in_ref[...])
    rates = mm(x, w_aux_ref[...])
    rates_ref[...] = rates
    qkv = proj[:, :CONV_CH]
    proj_ref[...] = qkv
    gate_in = proj[:, CONV_CH:]
    gate_ref[...] = gate_in
    padded[8 : 8 + CHUNK, :] = qkv
    conv = conv_rows(padded, taps_ref, 5)
    padded[0:8, :] = qkv[CHUNK - 8 :, :]
    act, _ = silu_of(conv)
    q, k, v = act[:, :KEY], act[:, KEY : 2 * KEY], act[:, 2 * KEY :]
    q = q * (lax.rsqrt(jnp.sum(q * q, axis=1, keepdims=True) + 1e-6) * KEY**-0.5)
    k = k * lax.rsqrt(jnp.sum(k * k, axis=1, keepdims=True) + 1e-6)
    rows, cols = iotas()
    write, step, _ = rates_of(rates, scalars_ref[0], scalars_ref[1])
    decay, growth, rest, final = decay_terms(step, rows, cols)
    coupling = jnp.where(rows > cols, wide(write, CHUNK) * mm3(k, k, NT) * decay, 0.0)
    inverse = solve_unit(coupling, rows, cols, mm3)
    inverse_ref[...] = inverse.astype(BF16)
    within = mm(q, k, NT) * decay
    state = memory[...]
    state_ref[...] = state
    low_state = state.astype(BF16)
    source = wide(write, VAL) * (v - wide(growth, VAL) * mm(k, low_state))
    fresh = mm3(inverse, source)
    fresh_ref[...] = fresh
    o = wide(growth, VAL) * mm(q, low_state) + mm(within, fresh)
    o_ref[...] = o
    memory[...] = wide(final, VAL) * state + mm(k * wide(rest, KEY), fresh, TN)
    scaled = o * lax.rsqrt(jnp.mean(o * o, axis=1, keepdims=True) + 1e-5) * gain_ref[...]
    heads = (scaled * silu_of(gate_in)[0]).astype(BF16)
    heads_ref[...] = heads
    part_ref[...] = mm(heads, w_out_ref[...], NT).astype(BF16)

    @pl.when(pl.program_id(0) == pl.num_programs(0) - 1)
    def _():
        weights.finish()


def mixer_forward(x, pack, taps, gain, scalars, moved, chips, number):
    length, width = x.shape
    chunks = length // CHUNK
    row = lambda cols: pl.BlockSpec((CHUNK, cols), lambda i: (i, 0))
    fixed = lambda shape, at: pl.BlockSpec(shape, lambda i: (0, at), pipeline_mode=pl.Buffered(1))
    out = lambda cols, kind: jax.ShapeDtypeStruct((length, cols), kind)
    return pl.pallas_call(
        functools.partial(forward_kernel, chips),
        grid=(chunks,),
        in_specs=[
            pl.BlockSpec(memory_space=pltpu.SMEM),
            row(width),
            fixed((width, 1536), 0),
            fixed((width, LANES), 16),
            fixed((width, VAL), 3),
            fixed((4, CONV_CH), 0),
            fixed((1, VAL), 0),
            pl.BlockSpec(memory_space=pl.ANY),
        ],
        out_specs=[
            row(width), row(VAL), row(CONV_CH), row(VAL), row(LANES), row(CHUNK), row(VAL), row(VAL),
            pl.BlockSpec((None, KEY, VAL), lambda i: (i, 0, 0)),
            pl.BlockSpec(memory_space=pl.ANY),
        ],
        out_shape=[
            out(width, BF16), out(VAL, BF16), out(CONV_CH, F32), out(VAL, F32), out(LANES, F32),
            out(CHUNK, BF16), out(VAL, F32), out(VAL, F32),
            jax.ShapeDtypeStruct((chunks, KEY, VAL), F32),
            jax.ShapeDtypeStruct((2 * moved.shape[0], moved.shape[1]), BF16),
        ],
        scratch_shapes=[
            pltpu.VMEM((CHUNK + 8, CONV_CH), F32), pltpu.VMEM((KEY, VAL), F32),
            pltpu.SemaphoreType.DMA((3,)), pltpu.SemaphoreType.DMA((2,)),
        ],
        compiler_params=pltpu.CompilerParams(
            dimension_semantics=("arbitrary",), vmem_limit_bytes=56 * 1024 * 1024,
            collective_id=number, has_side_effects=True,
        ),
        cost_estimate=pl.CostEstimate(
            flops=16 * 10**9, bytes_accessed=80 * 10**6, transcendentals=4 * 10**6
        ),
        name="mixer_forward",
    )(scalars, x, pack, pack, pack, taps, gain, moved)


def unit_back(grad, vector, scale):
    inv = lax.rsqrt(jnp.sum(vector * vector, axis=1, keepdims=True) + 1e-6)
    dot = jnp.sum(grad * vector, axis=1, keepdims=True)
    return (grad - vector * (inv * inv * dot)) * (inv * scale)


def backward_kernel(
    scalars_ref, g_ref, w_in_ref, w_aux_ref, w_out_ref, taps_ref, gain_ref,
    proj_ref, halo_ref, gate_ref, rates_ref, inverse_ref, fresh_ref, o_ref, state_ref,
    part_ref, dproj_ref, drates_ref, dtaps_ref, dgain_ref, dscalars_ref,
    padded, dpadded, dmemory,
):
    at = pl.program_id(0)
    last = pl.num_programs(0) - 1

    @pl.when(at == 0)
    def _():
        dmemory[...] = jnp.zeros_like(dmemory)
        dpadded[CHUNK : CHUNK + 8, :] = jnp.zeros((8, CONV_CH), F32)
        dtaps_ref[...] = jnp.zeros_like(dtaps_ref)
        dgain_ref[...] = jnp.zeros_like(dgain_ref)
        dscalars_ref[...] = jnp.zeros_like(dscalars_ref)

    rows, cols = iotas()
    padded[8 : 8 + CHUNK, :] = proj_ref[...]
    padded[0:8, :] = jnp.where(at == last, 0.0, halo_ref[...])
    conv = conv_rows(padded, taps_ref, 5)
    act, sig = silu_of(conv)
    act_q, act_k, v = act[:, :KEY], act[:, KEY : 2 * KEY], act[:, 2 * KEY :]
    q = act_q * (lax.rsqrt(jnp.sum(act_q * act_q, axis=1, keepdims=True) + 1e-6) * KEY**-0.5)
    k = act_k * lax.rsqrt(jnp.sum(act_k * act_k, axis=1, keepdims=True) + 1e-6)
    rates = rates_ref[...]
    write, step, sig_decay = rates_of(rates, scalars_ref[0], scalars_ref[1])
    decay, growth, rest, final = decay_terms(step, rows, cols)
    growth_v = wide(growth, VAL)
    write_v = wide(write, VAL)
    low_q, low_k = q.astype(BF16), k.astype(BF16)
    below = rows > cols
    strict_decay = jnp.where(below, decay, 0.0)
    keys = mm(low_k, low_k, NT) * strict_decay * wide(write, CHUNK)
    within = mm(low_q, low_k, NT) * decay
    dheads = mm(g_ref[...], w_out_ref[...])
    o = o_ref[...]
    gate_in = gate_ref[...]
    gate, gate_sig = silu_of(gate_in)
    inv = lax.rsqrt(jnp.mean(o * o, axis=1, keepdims=True) + 1e-5)
    normal = o * inv
    gain = gain_ref[...]
    dgate = dheads * normal * gain * (gate_sig * (1.0 + gate_in * (1.0 - gate_sig)))
    dscaled = dheads * gate
    dgain_ref[...] += jnp.sum(dscaled * normal, axis=0, keepdims=True)
    dnormal = dscaled * gain
    do = inv * (dnormal - normal * jnp.mean(dnormal * normal, axis=1, keepdims=True))
    state = state_ref[...]
    low_state = state.astype(BF16)
    fresh = fresh_ref[...]
    low_fresh = fresh.astype(BF16)
    dstate = dmemory[...]
    low_dstate = dstate.astype(BF16)
    low_do = do.astype(BF16)
    k_rest = k * wide(rest, KEY)
    rest_dstate = mm(k_rest, low_dstate)
    dfresh = mm(within, low_do, TN) + rest_dstate
    dsource = mm(inverse_ref[...], dfresh, TN)
    low_dsource = dsource.astype(BF16)
    dv = write_v * dsource
    dread = -(growth_v * dv)
    low_dread = dread.astype(BF16)
    do_growth = growth_v * do
    low_do_growth = do_growth.astype(BF16)
    dwithin = mm(low_do, low_fresh, NT)
    dcoupling = -mm(low_dsource, low_fresh, NT)
    dkeys = dcoupling * strict_decay * wide(write, CHUNK)
    dpairs = dwithin * decay
    dq = mm(low_do_growth, low_state, NT) + mm(dpairs, low_k)
    dk = (
        mm(low_dread, low_state, NT)
        + mm(dpairs, low_q, TN)
        + mm(dkeys + dkeys.T, low_k)
        + wide(rest, KEY) * mm(low_fresh, low_dstate, NT)
    )
    dmemory[...] = (
        wide(final, VAL) * dstate + mm(low_q, low_do_growth, TN) + mm(low_k, low_dread, TN)
    )
    spread = dwithin * within + dcoupling * keys
    straddle = jnp.where(below, mm_exact_left((rows <= cols).astype(BF16), spread), 0.0)
    read_rows = jnp.sum(
        do_growth * mm(low_q, low_state) + dread * mm(low_k, low_state), axis=1, keepdims=True
    )
    rest_rows = jnp.sum(fresh * rest_dstate, axis=1, keepdims=True)
    carried = jnp.sum(dstate * state) * final[0:1, 0:1]
    suffix = mm_exact_left(
        (rows <= cols).astype(BF16), jnp.broadcast_to(read_rows, (CHUNK, LANES))
    ) + mm_exact_left((rows > cols).astype(BF16), jnp.broadcast_to(rest_rows, (CHUNK, LANES)))
    dstep = suffix + jnp.sum(straddle, axis=1, keepdims=True) + carried
    dlogit = dstep * (-scalars_ref[0]) * sig_decay
    dwrite = (1.0 - write) * jnp.sum(dsource * fresh, axis=1, keepdims=True)
    lane = lax.broadcasted_iota(jnp.int32, (CHUNK, LANES), 1)
    drates = jnp.where(lane == 0, dwrite, jnp.where(lane == 1, dlogit, 0.0))
    low_drates = drates.astype(BF16)
    drates_ref[...] = low_drates
    dscalars_ref[0:1, :] += jnp.sum(dstep * step, axis=0, keepdims=True)
    dscalars_ref[1:2, :] += jnp.sum(dlogit, axis=0, keepdims=True)
    dact = jnp.concatenate(
        [unit_back(dq, act_q, KEY**-0.5), unit_back(dk, act_k, 1.0), dv], axis=1
    )
    dconv = dact * (sig * (1.0 + conv * (1.0 - sig)))
    dpadded[0:CHUNK, :] = dconv
    dtaps_ref[...] += jnp.concatenate(
        [
            jnp.sum(dconv * padded[5 + j : 5 + j + CHUNK, :], axis=0, keepdims=True)
            for j in range(4)
        ],
        axis=0,
    )
    dqkv = dconv * taps_ref[3:4, :]
    for j in range(3):
        dqkv = dqkv + dpadded[pl.ds(3 - j, CHUNK), :] * taps_ref[j : j + 1, :]
    dpadded[CHUNK : CHUNK + 8, :] = dconv[0:8, :]
    low_dproj = jnp.concatenate([dqkv, dgate], axis=1).astype(BF16)
    dproj_ref[...] = low_dproj
    part_ref[...] = (
        mm(low_dproj, w_in_ref[...], NT) + mm(low_drates, w_aux_ref[...], NT)
    ).astype(BF16)


def mixer_backward(g, pack, taps, gain, scalars, saved):
    proj, gate_in, rates, inverse, fresh, o, states = saved
    length, width = g.shape
    chunks = length // CHUNK
    back = chunks - 1
    row = lambda cols: pl.BlockSpec((CHUNK, cols), lambda i: (back - i, 0))
    fixed = lambda shape, at: pl.BlockSpec(shape, lambda i: (0, at), pipeline_mode=pl.Buffered(1))
    out = lambda cols, kind: jax.ShapeDtypeStruct((length, cols), kind)
    steps = CHUNK // 8
    return pl.pallas_call(
        backward_kernel,
        grid=(chunks,),
        in_specs=[
            pl.BlockSpec(memory_space=pltpu.SMEM),
            row(width),
            fixed((width, 1536), 0),
            fixed((width, LANES), 16),
            fixed((width, VAL), 3),
            fixed((4, CONV_CH), 0),
            fixed((1, VAL), 0),
            row(CONV_CH),
            pl.BlockSpec((8, CONV_CH), lambda i: (jnp.maximum((back - i) * steps - 1, 0), 0)),
            row(VAL), row(LANES), row(CHUNK), row(VAL), row(VAL),
            pl.BlockSpec((None, KEY, VAL), lambda i: (back - i, 0, 0)),
        ],
        out_specs=[
            row(width), row(1536), row(LANES),
            pl.BlockSpec((4, CONV_CH), lambda i: (0, 0)),
            pl.BlockSpec((1, VAL), lambda i: (0, 0)),
            pl.BlockSpec((8, LANES), lambda i: (0, 0)),
        ],
        out_shape=[
            out(width, BF16), out(1536, BF16), out(LANES, BF16),
            jax.ShapeDtypeStruct((4, CONV_CH), F32),
            jax.ShapeDtypeStruct((1, VAL), F32),
            jax.ShapeDtypeStruct((8, LANES), F32),
        ],
        scratch_shapes=[
            pltpu.VMEM((CHUNK + 8, CONV_CH), F32),
            pltpu.VMEM((CHUNK + 8, CONV_CH), F32),
            pltpu.VMEM((KEY, VAL), F32),
        ],
        compiler_params=pltpu.CompilerParams(
            dimension_semantics=("arbitrary",), vmem_limit_bytes=56 * 1024 * 1024
        ),
        cost_estimate=pl.CostEstimate(
            flops=16 * 10**9, bytes_accessed=80 * 10**6, transcendentals=4 * 10**6
        ),
        name="mixer_backward",
    )(scalars, g, pack, pack, pack, taps, gain, proj, proj, gate_in, rates, inverse, fresh, o, states)


PIECES = 4
AXES = ("chip", "core", "zp", "zl")


def partners():
    core, zl = lax.axis_index("core"), lax.axis_index("zl")
    return core, zl, {"core": 1 - core}, {"zl": 1 - zl}


def greet():
    _, _, beside, across = partners()
    barrier = pltpu.get_barrier_semaphore()
    for device in (beside, across):
        pl.semaphore_signal(
            barrier, inc=1, device_id=device, device_id_type=pl.DeviceIdType.MESH
        )
    pl.semaphore_wait(barrier, 2)


class Block:
    def __init__(self, zl, core, rows):
        self.first = (zl * 2 + core) * rows
        self.size = rows // PIECES

    def piece(self, p):
        return pl.ds(pl.multiple_of(self.first + p * self.size, self.size), self.size)


def remote(src, dst, send, recv, device):
    return pltpu.make_async_remote_copy(
        src_ref=src, dst_ref=dst, send_sem=send, recv_sem=recv,
        device_id=device, device_id_type=pl.DeviceIdType.MESH,
    )


class Scatter:
    def __init__(self, partial, beside_far, beside_own, sums, far, send, recv):
        core, zl, beside, across = partners()
        rows = far.shape[0]
        self.partial, self.beside_far, self.beside_own = partial, beside_far, beside_own
        self.sums, self.far = sums, far
        self.size = rows // PIECES
        self.own = Block(zl, core, rows)
        self.away = Block(1 - zl, core, rows)
        own_beside, away_beside = Block(zl, 1 - core, rows), Block(1 - zl, 1 - core, rows)
        self.to_far = [
            remote(partial.at[away_beside.piece(p)], beside_far.at[self.local(p)],
                   send.at[0, p], recv.at[0, p], beside)
            for p in range(PIECES)
        ]
        self.to_own = [
            remote(partial.at[own_beside.piece(p)], beside_own.at[self.local(p)],
                   send.at[1, p], recv.at[1, p], beside)
            for p in range(PIECES)
        ]
        self.cross = [
            remote(sums.at[self.local(p)], far.at[self.local(p)],
                   send.at[2, p], recv.at[2, p], across)
            for p in range(PIECES)
        ]

    def local(self, p):
        return pl.ds(p * self.size, self.size)

    def start(self):
        for copy in self.to_far:
            copy.start()
        for copy in self.to_own:
            copy.start()
        for p in range(PIECES):
            self.to_far[p].wait_recv()
            at = self.local(p)
            self.sums[at, :] = (
                self.partial[self.away.piece(p), :].astype(F32) + self.beside_far[at, :].astype(F32)
            ).astype(BF16)
            self.cross[p].start()

    def total(self, p):
        self.to_own[p].wait_recv()
        self.cross[p].wait_recv()
        at = self.local(p)
        return (
            self.partial[self.own.piece(p), :].astype(F32)
            + self.beside_own[at, :].astype(F32)
            + self.far[at, :].astype(F32)
        )

    def finish(self):
        for copies in (self.to_far, self.to_own, self.cross):
            for copy in copies:
                copy.wait_send()


class Gather:
    def __init__(self, gathered, send, recv, first):
        core, zl, beside, across = partners()
        rows = gathered.shape[0] // 4
        self.gathered = gathered
        self.own = Block(zl, core, rows)
        other = Block(1 - zl, core, rows)
        make = lambda block, at, device: [
            remote(gathered.at[block.piece(p)], gathered.at[block.piece(p)],
                   send.at[first + at, p], recv.at[first + at, p], device)
            for p in range(PIECES)
        ]
        self.across = make(self.own, 0, across)
        self.beside = make(self.own, 1, beside)
        self.forward = make(other, 2, beside)

    def put(self, p, rows):
        self.gathered[self.own.piece(p), :] = rows
        self.across[p].start()
        self.beside[p].start()

    def finish(self):
        for p in range(PIECES):
            self.across[p].wait_recv()
            self.forward[p].start()
        for p in range(PIECES):
            self.beside[p].wait_recv()
            self.forward[p].wait_recv()
        for copies in (self.across, self.beside, self.forward):
            for copy in copies:
                copy.wait_send()


def normed_of(x, gain):
    return x * lax.rsqrt(jnp.mean(x * x, axis=1, keepdims=True) + 1e-6) * gain


def first_kernel(x_ref, gain_ref, out_ref, send, recv):
    greet()
    gather = Gather(out_ref, send, recv, 0)
    size = x_ref.shape[0] // PIECES
    for p in range(PIECES):
        x = x_ref[p * size : (p + 1) * size, :].astype(F32)
        gather.put(p, normed_of(x, gain_ref[...]).astype(BF16))
    gather.finish()


def forward_bridge_kernel(
    partial, x_ref, gain_ref, new_ref, out_ref, beside_far, beside_own, sums, far, send, recv
):
    greet()
    scatter = Scatter(partial, beside_far, beside_own, sums, far, send, recv)
    gather = Gather(out_ref, send, recv, 3)
    scatter.start()
    for p in range(PIECES):
        at = scatter.local(p)
        x = x_ref[at, :].astype(F32) + scatter.total(p)
        new_ref[at, :] = x
        gather.put(p, normed_of(x, gain_ref[...]).astype(BF16))
    scatter.finish()
    gather.finish()


def norm_back(total, x, gain):
    inv = lax.rsqrt(jnp.mean(x * x, axis=1, keepdims=True) + 1e-6)
    unit = x * inv
    scaled = total * gain
    grad = inv * (scaled - unit * jnp.mean(scaled * unit, axis=1, keepdims=True))
    return grad, jnp.sum(total * unit, axis=0, keepdims=True)


def backward_bridge_kernel(
    partial, x_ref, gain_ref, grad_ref, new_ref, out_ref, dgain_ref,
    beside_far, beside_own, sums, far, send, recv
):
    greet()
    scatter = Scatter(partial, beside_far, beside_own, sums, far, send, recv)
    gather = Gather(out_ref, send, recv, 3)
    scatter.start()
    dgain = jnp.zeros_like(dgain_ref)
    for p in range(PIECES):
        at = scatter.local(p)
        grad, part = norm_back(scatter.total(p), x_ref[at, :].astype(F32), gain_ref[...])
        dgain = dgain + part
        grad = grad + grad_ref[at, :].astype(F32)
        new_ref[at, :] = grad
        gather.put(p, grad.astype(BF16))
    dgain_ref[...] = dgain
    scatter.finish()
    gather.finish()


def forward_last_kernel(partial, x_ref, new_ref, beside_far, beside_own, sums, far, send, recv):
    greet()
    scatter = Scatter(partial, beside_far, beside_own, sums, far, send, recv)
    scatter.start()
    for p in range(PIECES):
        at = scatter.local(p)
        new_ref[at, :] = (x_ref[at, :] + scatter.total(p)).astype(BF16)
    scatter.finish()


def backward_last_kernel(
    partial, x_ref, gain_ref, grad_ref, new_ref, dgain_ref,
    beside_far, beside_own, sums, far, send, recv
):
    greet()
    scatter = Scatter(partial, beside_far, beside_own, sums, far, send, recv)
    scatter.start()
    dgain = jnp.zeros_like(dgain_ref)
    for p in range(PIECES):
        at = scatter.local(p)
        grad, part = norm_back(scatter.total(p), x_ref[at, :].astype(F32), gain_ref[...])
        dgain = dgain + part
        new_ref[at, :] = (grad + grad_ref[at, :]).astype(BF16)
    dgain_ref[...] = dgain
    scatter.finish()


def comm_call(kernel, number, outs, args, scatters, gathers):
    rows = args[1].shape[0] if scatters else args[0].shape[0]
    width = args[0].shape[1]
    vmem = pl.BlockSpec(memory_space=pltpu.VMEM)
    block = lambda: pltpu.VMEM((rows, width), BF16)
    hops = 3 * scatters + 3 * gathers
    kinds = sum(1 << at for at, arg in enumerate(args[1:]) if arg.dtype == BF16)
    return pl.pallas_call(
        kernel,
        in_specs=[vmem] * len(args),
        out_specs=[vmem] * len(outs),
        out_shape=[jax.ShapeDtypeStruct(shape, kind) for shape, kind in outs],
        scratch_shapes=[block() for _ in range(4 * scatters)]
        + [pltpu.SemaphoreType.DMA((hops, PIECES)), pltpu.SemaphoreType.DMA((hops, PIECES))],
        compiler_params=pltpu.CompilerParams(
            collective_id=number + 6 * min(kinds, 2), has_side_effects=True, vmem_limit_bytes=48 * 1024 * 1024
        ),
        cost_estimate=pl.CostEstimate(
            flops=rows * width * 20, bytes_accessed=40 * 1024 * 1024, transcendentals=0
        ),
        name=kernel.__name__.replace("_kernel", ""),
    )(*args)


def first_gather(x, gain):
    rows, width = x.shape
    return comm_call(first_kernel, 0, [((4 * rows, width), BF16)], (x, gain), 0, 1)[0]


def forward_bridge(partial, x, gain):
    rows, width = x.shape
    return comm_call(
        forward_bridge_kernel, 1, [((rows, width), F32), ((4 * rows, width), BF16)],
        (partial, x, gain), 1, 1,
    )


def backward_bridge(partial, x, gain, grad):
    rows, width = x.shape
    return comm_call(
        backward_bridge_kernel, 2,
        [((rows, width), F32), ((4 * rows, width), BF16), ((1, width), F32)],
        (partial, x, gain, grad), 1, 1,
    )


def forward_last(partial, x):
    rows, width = x.shape
    return comm_call(forward_last_kernel, 3, [((rows, width), BF16)], (partial, x), 1, 0)[0]


def backward_last(partial, x, gain, grad):
    rows, width = x.shape
    return comm_call(
        backward_last_kernel, 4, [((rows, width), BF16), ((1, width), F32)],
        (partial, x, gain, grad), 1, 0,
    )


def place(chips):
    chip, core, zp, zl = (lax.axis_index(name) for name in AXES)
    return chip, core, zp, zl, chip * 2 + core


def at_device(chip, core, zp, zl):
    return {"chip": chip, "core": core, "zp": zp, "zl": zl}


def signal(device):
    pl.semaphore_signal(
        pltpu.get_barrier_semaphore(), inc=1, device_id=device,
        device_id_type=pl.DeviceIdType.MESH,
    )


def unless(condition, action):
    pl.when(jnp.logical_not(condition))(action)


class Weights:
    def __init__(self, source, target, send, recv, chips):
        chip, core, zp, zl, _ = place(chips)
        rows = source.shape[0]
        at = pl.ds(pl.multiple_of(core * rows, rows), rows)
        self.fixed = (zp == zl) & (zl == core)
        self.mine = [self.fixed & (zp == to) for to in range(2)]
        self.targets = [at_device(chip, zl, to, zp) for to in range(2)]
        self.sources = [at_device(chip, co, zl, core) for co in range(2)]
        self.source_mine = [self.fixed & (core == co) for co in range(2)]
        self.copies = [
            remote(source, target.at[at], send.at[to], recv.at[core], self.targets[to])
            for to in range(2)
        ]
        self.arrivals = [
            remote(source, target.at[pl.ds(co * rows, rows)], send.at[0], recv.at[co], self.sources[co])
            for co in range(2)
        ]
        self.local = pltpu.make_async_copy(source, target.at[at], send.at[2])

    def greet(self):
        for device, mine in zip(self.sources, self.source_mine):
            unless(mine, functools.partial(signal, device))
        return 2 - self.fixed.astype(jnp.int32)

    def start(self):
        for copy, mine in zip(self.copies, self.mine):
            unless(mine, copy.start)
        pl.when(self.fixed)(self.local.start)

    def finish(self):
        for arrival, mine in zip(self.arrivals, self.source_mine):
            unless(mine, arrival.wait_recv)
        for copy, mine in zip(self.copies, self.mine):
            unless(mine, copy.wait_send)
        pl.when(self.fixed)(self.local.wait)


class Plane:
    def __init__(self, chips):
        self.count = 2 * chips
        _, _, self.zp, self.zl, self.own = place(chips)

    def device(self, index):
        return at_device(index // 2, index % 2, self.zp, self.zl)

    def to(self, j):
        return lax.rem(self.own + j, self.count)

    def source(self, j):
        return lax.rem(self.own + self.count - j, self.count)

    def greet(self):
        for j in range(1, self.count):
            signal(self.device(self.to(j)))
        return self.count - 1


class Trade:
    def __init__(self, chips):
        self.chips, self.count = chips, 2 * chips
        self.chip, self.core, self.zp, self.zl, self.own = place(chips)
        self.fixed = (self.zp == self.zl) & (self.zl == self.core)
        self.slot = self.zp * chips + self.chip

    def role(self, slot):
        return at_device(slot % self.chips, self.zl, slot // self.chips, self.zp)

    def role_mine(self, slot):
        return self.fixed & (self.slot == slot)

    def home(self, index):
        return at_device(index // 2, index % 2, self.zl, self.core)

    def home_mine(self, index):
        return self.fixed & (self.own == index)

    def greet_homes(self):
        for index in range(self.count):
            unless(self.home_mine(index), functools.partial(signal, self.home(index)))
        return self.count - self.fixed.astype(jnp.int32)

    def greet_roles(self):
        for slot in range(self.count):
            unless(self.role_mine(slot), functools.partial(signal, self.role(slot)))
        return self.count - self.fixed.astype(jnp.int32)


def greet_group():
    _, _, beside, across = partners()
    signal(beside)
    signal(across)
    return 2


def wait_greetings(count):
    pl.semaphore_wait(pltpu.get_barrier_semaphore(), count)


def deal_kernel(
    chips, order_ref, x_ref, gain_ref, pack_ref, next_ref, new_ref, out_ref, wide_ref, wide_next_ref,
    spread, picked, send, recv, weight_send, weight_recv, next_send, next_recv, plane_send, plane_recv, role_send, role_recv,
):
    plane, trade = Plane(chips), Trade(chips)
    weights = Weights(pack_ref, wide_ref, weight_send, weight_recv, chips)
    weights_next = Weights(next_ref, wide_next_ref, next_send, next_recv, chips)
    gather = Gather(out_ref, send, recv, 0)
    count = plane.count
    part = x_ref.shape[0] // count
    rows = lambda index: pl.ds(pl.multiple_of(index * part, part), part)
    wait_greetings(plane.greet() + trade.greet_homes() + weights.greet() + greet_group())
    outward, inward = [], []
    for j in range(1, count):
        to, source = plane.to(j), plane.source(j)
        outward.append(
            remote(x_ref.at[rows(to)], spread.at[plane.own], plane_send.at[j], plane_recv.at[j],
                   plane.device(to))
        )
        inward.append(
            remote(x_ref.at[rows(to)], spread.at[source], plane_send.at[j], plane_recv.at[j],
                   plane.device(source))
        )
    for copy in outward:
        copy.start()
    weights.start()
    weights_next.start()
    spread[plane.own] = x_ref[rows(plane.own), :]
    for copy in inward:
        copy.wait_recv()
    to_roles = []
    for slot in range(count):
        picked[slot] = spread[order_ref[slot]]
        copy = remote(picked.at[slot], new_ref.at[rows(plane.own)], role_send.at[slot],
                      role_recv.at[plane.own], trade.role(slot))
        mine = trade.role_mine(slot)
        unless(mine, copy.start)

        @pl.when(mine)
        def _():
            new_ref[rows(plane.own), :] = picked[slot]

        to_roles.append((copy, mine))
    size = x_ref.shape[0] // PIECES
    parts = max(size // part, 1)
    for p in range(PIECES):
        for index in range(p * parts, (p + 1) * parts):
            arrival = remote(picked.at[0], new_ref.at[rows(index)], role_send.at[0],
                             role_recv.at[index], trade.home(index))
            unless(trade.home_mine(index), arrival.wait_recv)
        x = new_ref[p * size : (p + 1) * size, :].astype(F32)
        gather.put(p, normed_of(x, gain_ref[...]).astype(BF16))
    for copy in outward:
        copy.wait_send()
    for copy, mine in to_roles:
        unless(mine, copy.wait_send)
    gather.finish()
    weights.finish()
    weights_next.finish()


def deal_and_gather(order, x, gain, pack, pack_next, chips):
    rows, width = x.shape
    vmem = pl.BlockSpec(memory_space=pltpu.VMEM)
    hbm = pl.BlockSpec(memory_space=pl.ANY)
    count = 2 * chips
    buffer = pltpu.VMEM((count, rows // count, width), BF16)
    sems = lambda *shape: [pltpu.SemaphoreType.DMA(shape), pltpu.SemaphoreType.DMA(shape)]
    return pl.pallas_call(
        functools.partial(deal_kernel, chips),
        in_specs=[pl.BlockSpec(memory_space=pltpu.SMEM), vmem, vmem, hbm, hbm],
        out_specs=[vmem, vmem, hbm, hbm],
        out_shape=[
            jax.ShapeDtypeStruct((rows, width), BF16),
            jax.ShapeDtypeStruct((4 * rows, width), BF16),
            jax.ShapeDtypeStruct((2 * pack.shape[0], pack.shape[1]), BF16),
            jax.ShapeDtypeStruct((2 * pack_next.shape[0], pack_next.shape[1]), BF16),
        ],
        scratch_shapes=[buffer, buffer]
        + sems(3, PIECES) + sems(3) + sems(3) + sems(count) + sems(count),
        compiler_params=pltpu.CompilerParams(
            collective_id=20, has_side_effects=True, vmem_limit_bytes=48 * 1024 * 1024
        ),
        cost_estimate=pl.CostEstimate(
            flops=rows * width * 20, bytes_accessed=100 * 1024 * 1024, transcendentals=0
        ),
        name="deal_and_gather",
    )(order, x, gain, pack, pack_next)


def final_kernel(
    chips, inverse_ref, partial, x_ref, gain_ref, grad_ref, small_ref, home_ref, total_ref,
    beside_far, beside_own, sums, far, last, back, picked, small, by_plane, by_z, plane_sum,
    send, recv, role_send, role_recv, plane_send, plane_recv, small_send, small_recv, z_send, z_recv,
):
    plane, trade = Plane(chips), Trade(chips)
    count = plane.count
    part = x_ref.shape[0] // count
    rows = lambda index: pl.ds(pl.multiple_of(index * part, part), part)
    tier = trade.zp * 2 + trade.zl
    tier_device = lambda at: at_device(trade.chip, trade.core, at // 2, at % 2)
    for k in range(1, 4):
        signal(tier_device(lax.rem(tier + k, 4)))
    wait_greetings(plane.greet() + trade.greet_roles() + greet_group() + 3)
    scatter = Scatter(partial, beside_far, beside_own, sums, far, send, recv)
    scatter.start()
    dgain = jnp.zeros_like(gain_ref)
    to_homes = []
    size = x_ref.shape[0] // PIECES
    parts = max(size // part, 1)
    for p in range(PIECES):
        at = scatter.local(p)
        grad, piece = norm_back(scatter.total(p), x_ref[at, :].astype(F32), gain_ref[...])
        dgain = dgain + piece
        last[at, :] = (grad + grad_ref[at, :]).astype(BF16)
        for index in range(p * parts, (p + 1) * parts):
            copy = remote(last.at[rows(index)], back.at[trade.slot], role_send.at[index],
                          role_recv.at[trade.slot], trade.home(index))
            mine = trade.home_mine(index)
            unless(mine, copy.start)

            @pl.when(mine)
            def _():
                back[trade.slot] = last[rows(index), :]

            to_homes.append((copy, mine))
    small[...] = small_ref[...]
    for r in range(x_ref.shape[1] // LANES):
        small[r : r + 1, :] = dgain[:, r * LANES : (r + 1) * LANES]
    small_out, small_in = [], []
    for j in range(1, count):
        to, source = plane.to(j), plane.source(j)
        small_out.append(
            remote(small, by_plane.at[plane.own], small_send.at[j], small_recv.at[j], plane.device(to))
        )
        small_in.append(
            remote(small, by_plane.at[source], small_send.at[j], small_recv.at[j], plane.device(source))
        )
    for copy in small_out:
        copy.start()
    by_plane[plane.own] = small[...]
    for slot in range(count):
        arrival = remote(last.at[rows(0)], back.at[slot], role_send.at[0], role_recv.at[slot],
                         trade.role(slot))
        unless(trade.role_mine(slot), arrival.wait_recv)
    outward, inward = [], []
    for j in range(count):
        to, source = plane.to(j), plane.source(j)
        picked[j] = back[inverse_ref[to]]
        if j == 0:
            home_ref[rows(plane.own), :] = picked[0]
            continue
        copy = remote(picked.at[j], home_ref.at[rows(plane.own)], plane_send.at[j], plane_recv.at[j],
                      plane.device(to))
        copy.start()
        outward.append(copy)
        inward.append(
            remote(picked.at[j], home_ref.at[rows(source)], plane_send.at[j], plane_recv.at[j],
                   plane.device(source))
        )
    for copy in small_in:
        copy.wait_recv()
    total = by_plane[0]
    for index in range(1, count):
        total = total + by_plane[index]
    plane_sum[...] = total
    z_out, z_in = [], []
    for k in range(1, 4):
        to, source = lax.rem(tier + k, 4), lax.rem(tier + 4 - k, 4)
        z_out.append(remote(plane_sum, by_z.at[tier], z_send.at[k], z_recv.at[k], tier_device(to)))
        z_in.append(remote(plane_sum, by_z.at[source], z_send.at[k], z_recv.at[k], tier_device(source)))
    for copy in z_out:
        copy.start()
    by_z[tier] = total
    for copy in z_in:
        copy.wait_recv()
    total_ref[...] = (by_z[0] + by_z[1]) + (by_z[2] + by_z[3])
    for copy in inward:
        copy.wait_recv()
    scatter.finish()
    for copy, mine in to_homes:
        unless(mine, copy.wait_send)
    for copy in small_out + z_out + outward:
        copy.wait_send()


def final_step(inverse, partial, x, gain, grad, small, chips):
    rows, width = x.shape
    vmem = pl.BlockSpec(memory_space=pltpu.VMEM)
    count = 2 * chips
    block = pltpu.VMEM((rows, width), BF16)
    parted = pltpu.VMEM((count, rows // count, width), BF16)
    sems = lambda *shape: [pltpu.SemaphoreType.DMA(shape), pltpu.SemaphoreType.DMA(shape)]
    return pl.pallas_call(
        functools.partial(final_kernel, chips),
        in_specs=[pl.BlockSpec(memory_space=pltpu.SMEM)] + [vmem] * 5,
        out_specs=[vmem, vmem],
        out_shape=[
            jax.ShapeDtypeStruct((rows, width), BF16),
            jax.ShapeDtypeStruct(small.shape, F32),
        ],
        scratch_shapes=[block] * 5 + [parted] * 2
        + [
            pltpu.VMEM(small.shape, F32), pltpu.VMEM((count,) + small.shape, F32),
            pltpu.VMEM((4,) + small.shape, F32), pltpu.VMEM(small.shape, F32),
        ]
        + sems(3, PIECES) + sems(count) + sems(count) + sems(count) + sems(4),
        compiler_params=pltpu.CompilerParams(
            collective_id=21, has_side_effects=True, vmem_limit_bytes=48 * 1024 * 1024
        ),
        cost_estimate=pl.CostEstimate(
            flops=rows * width * 20, bytes_accessed=100 * 1024 * 1024, transcendentals=0
        ),
        name="final_step",
    )(inverse, partial, x, gain, grad, small)


def weights_back_kernel(chips, grads_ref, out_ref, halves, send, recv):
    chip, core, zp, zl, _ = place(chips)
    rows = out_ref.shape[0]
    fixed = (zp == zl) & (zl == core)
    sources = [at_device(chip, zl, at, zp) for at in range(2)]
    source_mine = [fixed & (zp == at) for at in range(2)]
    for device, mine in zip(sources, source_mine):
        unless(mine, functools.partial(signal, device))
    wait_greetings(2 - fixed.astype(jnp.int32))
    sent = []
    for co in range(2):
        mine = fixed & (core == co)
        src = grads_ref.at[pl.ds(co * rows, rows)]
        copy = remote(src, halves.at[zp], send.at[co], recv.at[zp], at_device(chip, co, zl, core))
        local = pltpu.make_async_copy(src, halves.at[zp], send.at[2])
        unless(mine, copy.start)
        pl.when(mine)(local.start)
        sent.append((copy, local, mine))
    for at in range(2):
        arrival = remote(grads_ref.at[pl.ds(0, rows)], halves.at[at], send.at[0], recv.at[at], sources[at])
        unless(source_mine[at], arrival.wait_recv)
    for copy, local, mine in sent:
        unless(mine, copy.wait_send)
        pl.when(mine)(local.wait)
    out_ref[...] = halves[0].astype(F32) + halves[1].astype(F32)


def weights_back(grads, chips):
    rows, width = grads.shape
    return pl.pallas_call(
        functools.partial(weights_back_kernel, chips),
        in_specs=[pl.BlockSpec(memory_space=pl.ANY)],
        out_specs=pl.BlockSpec(memory_space=pltpu.VMEM),
        out_shape=jax.ShapeDtypeStruct((rows // 2, width), F32),
        scratch_shapes=[
            pltpu.VMEM((2, rows // 2, width), BF16),
            pltpu.SemaphoreType.DMA((3,)), pltpu.SemaphoreType.DMA((2,)),
        ],
        compiler_params=pltpu.CompilerParams(
            collective_id=22, has_side_effects=True, vmem_limit_bytes=48 * 1024 * 1024
        ),
        cost_estimate=pl.CostEstimate(flops=0, bytes_accessed=60 * 1024 * 1024, transcendentals=0),
        name="weights_back",
    )(grads)


def swiglu_rows(paired):
    gate_part, up_part = jnp.split(paired, 2, axis=1)
    return jax.nn.silu(gate_part) * up_part


def dot32(a, b, dims):
    return lax.dot_general(a, b, dims, preferred_element_type=F32)


def row_major(x):
    return with_layout_constraint(x, Layout(major_to_minor=tuple(range(x.ndim))))


def linear(sizes, index):
    place = 0
    for size, at in zip(sizes, index):
        place = place * size + at
    return place


class Roles:
    def __init__(self):
        self.sizes = tuple(lax.axis_size(name) for name in AXES)
        self.chips, self.cores, self.zps, self.zls = self.sizes
        assert self.cores == 2 and self.zps == 2 and self.zls == 2

    def every(self):
        for chip in range(self.chips):
            for core in range(2):
                for zp in range(2):
                    for zl in range(2):
                        yield chip, core, zp, zl

    def rows_pairs(self):
        pairs = []
        for chip, core, zp, zl in self.every():
            slot, part = zp * self.chips + chip, zl * 2 + core
            source = linear(self.sizes, (slot // 2, slot % 2, part // 2, part % 2))
            pairs.append((source, linear(self.sizes, (chip, core, zp, zl))))
        return pairs

    def weight_pairs(self, which):
        pairs = []
        for chip, core, zp, zl in self.every():
            head = zp * 2 + zl
            to = (chip, head % 2, core ^ which, head // 2)
            pairs.append(
                (linear(self.sizes, (chip, core, zp, zl)), linear(self.sizes, to))
            )
        return pairs


def flipped(pairs):
    return [(b, a) for a, b in pairs]


def tie(value, after):
    return lax.optimization_barrier((value, after))[0]


def chip_gather(ordered):
    return row_major(lax.all_gather(row_major(ordered), "chip", axis=0, tiled=True))


def weights_in(pack, roles):
    halves = [lax.ppermute(pack, AXES, roles.weight_pairs(which)) for which in range(2)]
    swap = lax.axis_index("zp") == 1
    ordered = jnp.concatenate(
        [jnp.where(swap, halves[1], halves[0]), jnp.where(swap, halves[0], halves[1])], axis=0
    )
    return chip_gather(ordered)


def chip_scatter(grads):
    return lax.psum_scatter(grads, "chip", scatter_dimension=0, tiled=True)


def weights_home(mine, roles):
    rows = mine.shape[0] // 2
    swap = lax.axis_index("zp") == 1
    low, high = mine[:rows], mine[rows:]
    halves = [jnp.where(swap, high, low), jnp.where(swap, low, high)]
    back = [
        lax.ppermute(half, AXES, flipped(roles.weight_pairs(which)))
        for which, half in enumerate(halves)
    ]
    return back[0].astype(F32) + back[1].astype(F32)


def together(*values):
    return lax.optimization_barrier(values)


def deal(values, order):
    spread = lax.all_to_all(values, ("chip", "core"), split_axis=2, concat_axis=1, tiled=True)
    picked = jnp.take(spread, order, axis=1)
    return lax.all_to_all(picked, ("chip", "core"), split_axis=1, concat_axis=2, tiled=True)


def shards(
    tokens, lengths, order, norm_mix, w_query, w_key, w_value, w_gate, w_decay, conv_filter,
    log_rate, step_bias, norm_heads, w_out, norm_ffn, w_ffn_gate, w_ffn_up, w_ffn_down, cotangent,
):
    roles = Roles()
    layer_count = w_query.shape[0]
    heads_total = log_rate.shape[1]
    chip, core, zp, zl = (lax.axis_index(name) for name in AXES)
    head = zl * 2 + core
    rows_local, slots_local, width = tokens.shape
    assert slots_local == 1 and w_decay.shape[2] == 1
    slot_total = order.shape[0]
    units = w_ffn_gate.shape[2]
    rows_part = w_query.shape[1]
    to_roles = roles.rows_pairs()

    packs = []
    for layer in range(layer_count):
        aux = jnp.concatenate([w_decay[layer, :, 0, :], conv_filter[layer, :, 0, :].T], axis=1)
        aux = jnp.pad(aux, ((0, 0), (0, LANES - aux.shape[1])))
        mix = jnp.concatenate(
            [w_query[layer], w_key[layer], w_value[layer], w_gate[layer], w_out[layer].T, aux], axis=1
        )
        ffn = jnp.concatenate([w_ffn_gate[layer], w_ffn_up[layer], w_ffn_down[layer].T], axis=1)
        packs.append([row_major(mix), row_major(ffn)])
    gains = [
        (norm_mix[layer].astype(F32)[None], norm_ffn[layer].astype(F32)[None])
        for layer in range(layer_count)
    ]
    inverse_order = jnp.sum(
        jnp.where(
            order[None, :] == jnp.arange(slot_total, dtype=jnp.int32)[:, None],
            jnp.arange(slot_total, dtype=jnp.int32)[None, :],
            0,
        ),
        axis=1,
    ).astype(jnp.int32)
    kernel_deal = rows_local % (16 * slot_total) == 0
    if kernel_deal:
        residual, rows_in, ordered, ordered_ffn = deal_and_gather(
            order, tokens[:, 0, :], gains[0][0], packs[0][0], packs[0][1], roles.chips
        )
        packs[0][0] = chip_gather(ordered)
        packs[0][1] = chip_gather(ordered_ffn)
    else:
        dealt = deal(tokens, order)[:, 0, :]
        residual = lax.ppermute(dealt, AXES, to_roles)
        rows_in = first_gather(residual, gains[0][0])
        packs[0][0] = weights_in(packs[0][0], roles)
        packs[0][1] = weights_in(tie(packs[0][1], rows_in), roles)

    positions = (zp * 2 + zl) * rows_local + jnp.arange(rows_local)
    my_slot = jnp.sum(jnp.where(jnp.arange(slot_total) == chip * 2 + core, order, 0))
    my_length = jnp.sum(jnp.where(jnp.arange(slot_total) == my_slot, lengths, 0))
    start = cotangent[:, 0, :] * (positions < my_length).astype(BF16)[:, None]
    gradient = lax.ppermute(tie(start, rows_in), AXES, to_roles)
    grad_rows = lax.all_gather(gradient, ("zl", "core"), axis=0, tiled=True)

    saved = []
    for layer in range(layer_count):
        mix, ffn = packs[layer]
        taps = mix[:, 2050:2054].T.astype(F32)
        gain_heads = norm_heads[layer].astype(F32)[None]
        scalars = jnp.concatenate(
            [
                jnp.exp(lax.dynamic_slice_in_dim(log_rate[layer].astype(F32), head, 1)),
                lax.dynamic_slice_in_dim(step_bias[layer].astype(F32), head, 1),
            ]
        )
        member = layer
        part, heads, *kept, ordered = mixer_forward(
            rows_in, mix, taps, gain_heads, scalars, packs[1][member], roles.chips, 30 + member
        )
        packs[1][member] = chip_gather(ordered)
        ffn = packs[layer][1]
        middle, rows_ffn = forward_bridge(part, residual, gains[layer][1])
        paired = dot32(rows_ffn, ffn[:, : 2 * units], NN)
        hidden, swiglu_back = jax.vjp(swiglu_rows, paired)
        hidden = hidden.astype(BF16)
        part = dot32(hidden, ffn[:, 2 * units :], NT).astype(BF16)
        saved.append(
            (residual, rows_in, taps, gain_heads, scalars, kept, heads, middle, rows_ffn,
             swiglu_back, hidden)
        )
        if layer + 1 < layer_count:
            residual, rows_in = forward_bridge(part, middle, gains[layer + 1][0])
        else:
            total = lax.psum_scatter(part, ("zl", "core"), scatter_dimension=0, tiled=True)
            mixed = (middle + total.astype(F32)).astype(BF16)
    mixed = lax.ppermute(mixed, AXES, flipped(to_roles))

    small_terms = [None] * layer_count
    scattered = [[None] * 3 for _ in range(layer_count)]
    homed = [[None] * 3 for _ in range(layer_count)]
    for layer in reversed(range(layer_count)):
        mix, ffn = packs[layer]
        (residual, rows_in, taps, gain_heads, scalars, kept, heads, middle, rows_ffn,
         swiglu_back, hidden) = saved[layer]
        (grad_paired,) = swiglu_back(dot32(grad_rows, ffn[:, 2 * units :], NN))
        paired_low = grad_paired.astype(BF16)
        part = dot32(paired_low, ffn[:, : 2 * units], NT).astype(BF16)
        ffn_grads = jnp.concatenate(
            [dot32(rows_ffn, paired_low, TN).astype(BF16), dot32(grad_rows, hidden, TN).astype(BF16)],
            axis=1,
        )
        part, ffn_grads = together(part, ffn_grads)
        scattered[layer][2] = chip_scatter(ffn_grads)
        if layer + 1 < layer_count:
            part, scattered[layer + 1][0], scattered[layer + 1][1] = together(
                part, scattered[layer + 1][0], scattered[layer + 1][1]
            )
        gradient, grad_rows, dgain_ffn = backward_bridge(part, middle, gains[layer][1], gradient)
        out_grads = dot32(grad_rows, heads, TN).astype(BF16)
        grad_rows, out_grads = together(grad_rows, out_grads)
        scattered[layer][1] = chip_scatter(out_grads)
        if layer + 1 < layer_count:
            for member in range(3):
                homed[layer + 1][member] = weights_home(scattered[layer + 1][member], roles)
        part, dproj, drates, dtaps, dgain, dscalars = mixer_backward(
            grad_rows, mix, taps, gain_heads, scalars, kept
        )
        aux = dot32(rows_in, drates, TN) + jnp.pad(dtaps.T, ((0, 0), (2, LANES - 6)))
        in_grads = jnp.concatenate(
            [dot32(rows_in, dproj, TN).astype(BF16), aux.astype(BF16)], axis=1
        )
        part, in_grads, scattered[layer][1], scattered[layer][2] = together(
            part, in_grads, scattered[layer][1], scattered[layer][2]
        )
        if layer + 1 < layer_count:
            part, *homed[layer + 1] = together(part, *homed[layer + 1])
        scattered[layer][0] = chip_scatter(in_grads)
        mine = (jnp.arange(heads_total) == head).astype(F32)
        small_terms[layer] = [
            dgain_ffn[0], dgain[0], mine * dscalars[0, 0], mine * dscalars[1, 0]
        ]
        if layer:
            gradient, grad_rows, dgain_mix = backward_bridge(part, residual, gains[layer][0], gradient)
            small_terms[layer].insert(0, dgain_mix[0])
    small_terms[0].insert(0, jnp.zeros((width,), F32))
    flat = jnp.concatenate(
        [small_terms[layer][member] for member in range(5) for layer in range(layer_count)]
    )
    flat = jnp.pad(flat, (0, -flat.shape[0] % (8 * LANES))).reshape(-1, LANES)
    if kernel_deal:
        home, flat = final_step(
            inverse_order, part, residual, gains[0][0], gradient, flat, roles.chips
        )
        grad_home = home[:, None, :].astype(F32)
    else:
        gradient, dgain_mix = backward_last(part, residual, gains[0][0], gradient)
        flat = flat.at[: width // LANES].set(dgain_mix.reshape(-1, LANES))
        flat = lax.psum(flat, AXES)
        dealt_grad = lax.ppermute(gradient, AXES, flipped(to_roles))
        grad_home = deal(dealt_grad[:, None, :], inverse_order).astype(F32)
    flat = flat.reshape(-1)
    if kernel_deal:
        scattered[0][0], _ = together(scattered[0][0], home)
        homed[0][0] = weights_back(scattered[0][0], roles.chips)
    else:
        homed[0][0] = weights_home(scattered[0][0], roles)
    for member in (1, 2):
        homed[0][member] = weights_home(scattered[0][member], roles)
    weight_grads = []
    for in_grads, out_grads, ffn_grads in homed:
        weight_grads.append(
            (
                in_grads[:, :256],
                in_grads[:, 256:512],
                in_grads[:, 512:1024],
                in_grads[:, 1024:1536],
                in_grads[:, 1536:1538].reshape(rows_part, 1, 2),
                in_grads[:, 1538:1542].T.reshape(4, 1, rows_part),
                out_grads.T,
                ffn_grads[:, :units],
                ffn_grads[:, units : 2 * units],
                ffn_grads[:, 2 * units :].T,
            )
        )
    small, at = [], 0
    for size in (width, width, VAL, heads_total, heads_total):
        small.append(flat[at : at + layer_count * size].reshape(layer_count, size))
        at += layer_count * size
    members = [jnp.stack([grads[m] for grads in weight_grads]) for m in range(10)]
    return (
        mixed[:, None, :],
        grad_home,
        small[0],
        members[0], members[1], members[2], members[3], members[4], members[5],
        small[3],
        small[4],
        small[2],
        members[6],
        small[1],
        members[7], members[8], members[9],
    )


def solution(mesh):
    dp, tensor = mesh.devices.shape
    mesh = Mesh(mesh.devices.reshape(dp // 2, 2, tensor // 2, 2), AXES)
    d, t = ("chip", "core"), ("zp", "zl")
    rows = P(t, d, None)
    by_rows, by_columns = P(None, d, t), P(None, t, d)
    heads, filters = P(None, d, t, None), P(None, None, t, d)
    return jax.shard_map(
        shards,
        mesh=mesh,
        in_specs=(
            rows, P(), P(), P(), by_rows, by_rows, by_rows, by_rows, heads, filters,
            P(), P(), P(), by_columns, P(), by_rows, by_rows, by_columns, rows,
        ),
        out_specs=(
            rows, rows, P(), by_rows, by_rows, by_rows, by_rows, heads, filters,
            P(), P(), P(), by_columns, P(), by_rows, by_rows, by_columns,
        ),
        check_vma=False,
    )
```

```python
import functools
import jax
import jax.numpy as jnp
from jax import lax
from jax.experimental import pallas as pl
from jax.experimental.layout import Layout, with_layout_constraint
from jax.experimental.pallas import tpu as pltpu
from jax.sharding import Mesh, PartitionSpec as P

CHUNK = 256
LANES = 128
KEY = 256
VAL = 512
CONV_CH = 2 * KEY + VAL
F32 = jnp.float32
BF16 = jnp.bfloat16
NN = (((1,), (0,)), ((), ()))
NT = (((1,), (1,)), ((), ()))
TN = (((0,), (0,)), ((), ()))


def mm(a, b, dims=NN):
    return lax.dot_general(
        a.astype(BF16), b.astype(BF16), dims, preferred_element_type=F32
    )


def split_low(a):
    high = a.astype(BF16)
    return high, (a - high.astype(F32)).astype(BF16)


def mm3(a, b, dims=NN):
    a_high, a_low = split_low(a)
    b_high, b_low = split_low(b)
    dot = functools.partial(
        lax.dot_general, dimension_numbers=dims, preferred_element_type=F32
    )
    return dot(a_high, b_high) + (dot(a_high, b_low) + dot(a_low, b_high))


def mm_exact_left(a, b, dims=NN):
    a = a.astype(BF16)
    high = b.astype(BF16)
    rest = b - high.astype(F32)
    mid = rest.astype(BF16)
    low = (rest - mid.astype(F32)).astype(BF16)
    dot = functools.partial(
        lax.dot_general, dimension_numbers=dims, preferred_element_type=F32
    )
    return dot(a, high) + (dot(a, mid) + dot(a, low))


def iotas():
    rows = lax.broadcasted_iota(jnp.int32, (CHUNK, CHUNK), 0)
    cols = lax.broadcasted_iota(jnp.int32, (CHUNK, CHUNK), 1)
    return rows, cols


def wide(col_block, width):
    return jnp.concatenate([col_block] * (width // LANES), axis=1)


def rates_of(rates, rate, bias):
    write = jax.nn.sigmoid(jnp.broadcast_to(rates[:, 0:1], (CHUNK, LANES)))
    logit = jnp.broadcast_to(rates[:, 1:2], (CHUNK, LANES)) + bias
    soft = jnp.maximum(logit, 0.0) + jnp.log1p(jnp.exp(-jnp.abs(logit)))
    return write, -rate * soft, jax.nn.sigmoid(logit)


def head_scalars(scalars_ref, layer):
    head = lax.axis_index("zl") * 2 + lax.axis_index("core")
    rate_ref, bias_ref = scalars_ref
    here = lax.broadcasted_iota(jnp.int32, (1, rate_ref.shape[1]), 1) == head
    pick = lambda ref: jnp.sum(
        jnp.where(here, ref[layer : layer + 1, :].astype(F32), 0.0), axis=1, keepdims=True
    )
    return jnp.exp(pick(rate_ref)), pick(bias_ref)


def decay_terms(step, rows, cols):
    inclusive = (rows >= cols).astype(BF16)
    total = mm_exact_left(inclusive, step)
    spread = wide(total, CHUNK) - jnp.concatenate([total.T] * (CHUNK // LANES), axis=0)
    decay = jnp.where(rows >= cols, jnp.exp(jnp.minimum(spread, 0.0)), 0.0)
    last = jnp.broadcast_to(total[CHUNK - 1 : CHUNK, :], (CHUNK, LANES))
    return decay, jnp.exp(total), jnp.exp(last - total), jnp.exp(last)


def solve_unit(coupling, rows, cols, product):
    same = ((rows >> 1) == (cols >> 1)) & (rows != cols)
    inverse = jnp.where(rows == cols, 1.0, 0.0) - jnp.where(same, coupling, 0.0)
    for level in range(1, CHUNK.bit_length() - 1):
        between = ((rows >> (level + 1)) == (cols >> (level + 1))) & (
            (rows >> level) != (cols >> level)
        )
        part = jnp.where(between, coupling, 0.0)
        inverse = inverse - product(product(inverse, part), inverse)
    return inverse


def silu_of(x):
    gate = jax.nn.sigmoid(x)
    return x * gate, gate


def conv_rows(padded_ref, taps_ref, start):
    result = padded_ref[pl.ds(start, CHUNK), :] * taps_ref[0:1, :]
    for j in range(1, 4):
        result = result + padded_ref[pl.ds(start + j, CHUNK), :] * taps_ref[j : j + 1, :]
    return result


def forward_kernel(
    layer, jobs, rate_ref, bias_ref, x_ref, w_qkv_ref, w_gate_ref, w_aux_ref, w_out_ref, gain_ref,
    part_ref, heads_ref, proj_ref, gate_ref, rates_ref, inverse_ref, fresh_ref, o_ref, state_ref,
    padded, memory, taps_ref,
):
    begin_jobs(jobs, pl.program_id(0), pl.num_programs(0))
    @pl.when(pl.program_id(0) == 0)
    def _():
        memory[...] = jnp.zeros_like(memory)
        taps_ref[...] = w_aux_ref[...].astype(F32).T[2:6, :]
        padded[0:8, :] = jnp.zeros((8, CONV_CH), F32)

    x = x_ref[...]
    rates = mm(x, w_aux_ref[...])
    rates_ref[...] = rates
    qkv = mm(x, w_qkv_ref[...])
    proj_ref[...] = qkv
    gate_in = mm(x, w_gate_ref[...])
    gate_ref[...] = gate_in
    padded[8 : 8 + CHUNK, :] = qkv
    conv = conv_rows(padded, taps_ref, 5)
    padded[0:8, :] = qkv[CHUNK - 8 :, :]
    act, _ = silu_of(conv)
    q, k, v = act[:, :KEY], act[:, KEY : 2 * KEY], act[:, 2 * KEY :]
    q = q * (lax.rsqrt(jnp.sum(q * q, axis=1, keepdims=True) + 1e-6) * KEY**-0.5)
    k = k * lax.rsqrt(jnp.sum(k * k, axis=1, keepdims=True) + 1e-6)
    rows, cols = iotas()
    write, step, _ = rates_of(rates, *head_scalars((rate_ref, bias_ref), layer))
    decay, growth, rest, final = decay_terms(step, rows, cols)
    coupling = jnp.where(rows > cols, wide(write, CHUNK) * mm3(k, k, NT) * decay, 0.0)
    inverse = solve_unit(coupling, rows, cols, mm3)
    inverse_ref[...] = inverse.astype(BF16)
    within = mm(q, k, NT) * decay
    state = memory[...]
    state_ref[...] = state
    low_state = state.astype(BF16)
    source = wide(write, VAL) * (v - wide(growth, VAL) * mm(k, low_state))
    fresh = mm3(inverse, source)
    fresh_ref[...] = fresh
    o = wide(growth, VAL) * mm(q, low_state) + mm(within, fresh)
    o_ref[...] = o
    memory[...] = wide(final, VAL) * state + mm(k * wide(rest, KEY), fresh, TN)
    scaled = o * lax.rsqrt(jnp.mean(o * o, axis=1, keepdims=True) + 1e-5) * gain_ref[layer : layer + 1, :].astype(F32)
    heads = (scaled * silu_of(gate_in)[0]).astype(BF16)
    heads_ref[...] = heads
    part_ref[...] = mm(heads, w_out_ref[...], NT).astype(BF16)
    end_jobs(jobs, pl.program_id(0), pl.num_programs(0))


def head_spec(value):
    return pl.BlockSpec(value.shape, lambda i: (0, 0))


def weight_specs(width):
    fixed = lambda shape, at: pl.BlockSpec(shape, lambda i: (0, at), pipeline_mode=pl.Buffered(1))
    return [
        fixed((width, CONV_CH), 0),
        fixed((width, VAL), 0),
        fixed((width, LANES), 2 * VAL // LANES),
        fixed((width, VAL), 1),
        fixed((2, VAL), 0),
    ]


def mixer_forward(layer, x, qkv, pack, gain, scalars, jobs, number):
    length, width = x.shape
    chunks = length // CHUNK
    row = lambda cols: pl.BlockSpec((CHUNK, cols), lambda i: (i, 0))
    out = lambda cols, kind: jax.ShapeDtypeStruct((length, cols), kind)
    return carry_call(
        functools.partial(forward_kernel, layer), jobs, (chunks,),
        [head_spec(scalars[0]), head_spec(scalars[1]), row(width)] + weight_specs(width),
        [
            row(width), row(VAL), row(CONV_CH), row(VAL), row(LANES), row(CHUNK), row(VAL), row(VAL),
            pl.BlockSpec((None, KEY, VAL), lambda i: (i, 0, 0)),
        ],
        [
            out(width, BF16), out(VAL, BF16), out(CONV_CH, F32), out(VAL, F32), out(LANES, F32),
            out(CHUNK, BF16), out(VAL, F32), out(VAL, F32),
            jax.ShapeDtypeStruct((chunks, KEY, VAL), F32),
        ],
        [
            pltpu.VMEM((CHUNK + 8, CONV_CH), F32), pltpu.VMEM((KEY, VAL), F32),
            pltpu.VMEM((4, CONV_CH), F32),
        ],
        (*scalars, x, qkv, pack, pack, pack, gain), number, "mixer_forward", 16 * 10**9,
    )


def unit_back(grad, vector, scale):
    inv = lax.rsqrt(jnp.sum(vector * vector, axis=1, keepdims=True) + 1e-6)
    dot = jnp.sum(grad * vector, axis=1, keepdims=True)
    return (grad - vector * (inv * inv * dot)) * (inv * scale)


def backward_kernel(
    layer, jobs, rate_ref, bias_ref, g_ref, x_ref, w_qkv_ref, w_gate_ref, w_aux_ref, w_out_ref, gain_ref,
    proj_ref, halo_ref, gate_ref, rates_ref, inverse_ref, fresh_ref, o_ref, state_ref,
    part_ref, dqkv_ref, dgate_ref, daux_ref, dgain_ref, dscalars_ref,
    padded, dpadded, dmemory, taps_ref, dtaps_ref, daux_sum,
):
    begin_jobs(jobs, pl.program_id(0), pl.num_programs(0))
    at = pl.program_id(0)
    last = pl.num_programs(0) - 1

    @pl.when(at == 0)
    def _():
        dmemory[...] = jnp.zeros_like(dmemory)
        taps_ref[...] = w_aux_ref[...].astype(F32).T[2:6, :]
        dpadded[CHUNK : CHUNK + 8, :] = jnp.zeros((8, CONV_CH), F32)
        dtaps_ref[...] = jnp.zeros_like(dtaps_ref)
        daux_sum[...] = jnp.zeros_like(daux_sum)
        dgain_ref[...] = jnp.zeros_like(dgain_ref)
        dscalars_ref[...] = jnp.zeros_like(dscalars_ref)

    rows, cols = iotas()
    padded[8 : 8 + CHUNK, :] = proj_ref[...]
    padded[0:8, :] = jnp.where(at == last, 0.0, halo_ref[...])
    conv = conv_rows(padded, taps_ref, 5)
    act, sig = silu_of(conv)
    act_q, act_k, v = act[:, :KEY], act[:, KEY : 2 * KEY], act[:, 2 * KEY :]
    q = act_q * (lax.rsqrt(jnp.sum(act_q * act_q, axis=1, keepdims=True) + 1e-6) * KEY**-0.5)
    k = act_k * lax.rsqrt(jnp.sum(act_k * act_k, axis=1, keepdims=True) + 1e-6)
    rates = rates_ref[...]
    write, step, sig_decay = rates_of(rates, *head_scalars((rate_ref, bias_ref), layer))
    decay, growth, rest, final = decay_terms(step, rows, cols)
    growth_v = wide(growth, VAL)
    write_v = wide(write, VAL)
    low_q, low_k = q.astype(BF16), k.astype(BF16)
    below = rows > cols
    strict_decay = jnp.where(below, decay, 0.0)
    keys = mm(low_k, low_k, NT) * strict_decay * wide(write, CHUNK)
    within = mm(low_q, low_k, NT) * decay
    dheads = mm(g_ref[...], w_out_ref[...])
    o = o_ref[...]
    gate_in = gate_ref[...]
    gate, gate_sig = silu_of(gate_in)
    inv = lax.rsqrt(jnp.mean(o * o, axis=1, keepdims=True) + 1e-5)
    normal = o * inv
    gain = gain_ref[layer : layer + 1, :].astype(F32)
    dgate = dheads * normal * gain * (gate_sig * (1.0 + gate_in * (1.0 - gate_sig)))
    dscaled = dheads * gate
    dgain_ref[...] += jnp.sum(dscaled * normal, axis=0, keepdims=True)
    dnormal = dscaled * gain
    do = inv * (dnormal - normal * jnp.mean(dnormal * normal, axis=1, keepdims=True))
    state = state_ref[...]
    low_state = state.astype(BF16)
    fresh = fresh_ref[...]
    low_fresh = fresh.astype(BF16)
    dstate = dmemory[...]
    low_dstate = dstate.astype(BF16)
    low_do = do.astype(BF16)
    k_rest = k * wide(rest, KEY)
    rest_dstate = mm(k_rest, low_dstate)
    dfresh = mm(within, low_do, TN) + rest_dstate
    dsource = mm(inverse_ref[...], dfresh, TN)
    low_dsource = dsource.astype(BF16)
    dv = write_v * dsource
    dread = -(growth_v * dv)
    low_dread = dread.astype(BF16)
    do_growth = growth_v * do
    low_do_growth = do_growth.astype(BF16)
    dwithin = mm(low_do, low_fresh, NT)
    dcoupling = -mm(low_dsource, low_fresh, NT)
    dkeys = dcoupling * strict_decay * wide(write, CHUNK)
    dpairs = dwithin * decay
    dq = mm(low_do_growth, low_state, NT) + mm(dpairs, low_k)
    dk = (
        mm(low_dread, low_state, NT)
        + mm(dpairs, low_q, TN)
        + mm(dkeys + dkeys.T, low_k)
        + wide(rest, KEY) * mm(low_fresh, low_dstate, NT)
    )
    dmemory[...] = (
        wide(final, VAL) * dstate + mm(low_q, low_do_growth, TN) + mm(low_k, low_dread, TN)
    )
    spread = dwithin * within + dcoupling * keys
    straddle = jnp.where(below, mm_exact_left((rows <= cols).astype(BF16), spread), 0.0)
    read_rows = jnp.sum(
        do_growth * mm(low_q, low_state) + dread * mm(low_k, low_state), axis=1, keepdims=True
    )
    rest_rows = jnp.sum(fresh * rest_dstate, axis=1, keepdims=True)
    carried = jnp.sum(dstate * state) * final[0:1, 0:1]
    suffix = mm_exact_left(
        (rows <= cols).astype(BF16), jnp.broadcast_to(read_rows, (CHUNK, LANES))
    ) + mm_exact_left((rows > cols).astype(BF16), jnp.broadcast_to(rest_rows, (CHUNK, LANES)))
    dstep = suffix + jnp.sum(straddle, axis=1, keepdims=True) + carried
    dlogit = dstep * (-head_scalars((rate_ref, bias_ref), layer)[0]) * sig_decay
    dwrite = (1.0 - write) * jnp.sum(dsource * fresh, axis=1, keepdims=True)
    lane = lax.broadcasted_iota(jnp.int32, (CHUNK, LANES), 1)
    drates = jnp.where(lane == 0, dwrite, jnp.where(lane == 1, dlogit, 0.0))
    low_drates = drates.astype(BF16)
    daux_sum[...] += mm(x_ref[...], low_drates, TN)
    dscalars_ref[0:1, :] += jnp.sum(dstep * step, axis=0, keepdims=True)
    dscalars_ref[1:2, :] += jnp.sum(dlogit, axis=0, keepdims=True)
    dact = jnp.concatenate(
        [unit_back(dq, act_q, KEY**-0.5), unit_back(dk, act_k, 1.0), dv], axis=1
    )
    dconv = dact * (sig * (1.0 + conv * (1.0 - sig)))
    dpadded[0:CHUNK, :] = dconv
    dtaps_ref[2:6, :] += jnp.concatenate(
        [
            jnp.sum(dconv * padded[5 + j : 5 + j + CHUNK, :], axis=0, keepdims=True)
            for j in range(4)
        ],
        axis=0,
    )
    dqkv = dconv * taps_ref[3:4, :]
    for j in range(3):
        dqkv = dqkv + dpadded[pl.ds(3 - j, CHUNK), :] * taps_ref[j : j + 1, :]
    dpadded[CHUNK : CHUNK + 8, :] = dconv[0:8, :]
    low_dqkv, low_dgate = dqkv.astype(BF16), dgate.astype(BF16)
    dqkv_ref[...] = low_dqkv
    dgate_ref[...] = low_dgate
    part_ref[...] = (
        mm(low_dqkv, w_qkv_ref[...], NT)
        + mm(low_dgate, w_gate_ref[...], NT)
        + mm(low_drates, w_aux_ref[...], NT)
    ).astype(BF16)

    @pl.when(at == last)
    def _():
        daux_ref[...] = (daux_sum[...] + dtaps_ref[...].T).astype(BF16)

    end_jobs(jobs, pl.program_id(0), pl.num_programs(0))


def mixer_backward(layer, g, x, qkv, pack, gain, scalars, saved, jobs, number):
    proj, gate_in, rates, inverse, fresh, o, states = saved
    length, width = g.shape
    chunks = length // CHUNK
    back = chunks - 1
    row = lambda cols: pl.BlockSpec((CHUNK, cols), lambda i: (back - i, 0))
    out = lambda cols, kind: jax.ShapeDtypeStruct((length, cols), kind)
    steps = CHUNK // 8
    return carry_call(
        functools.partial(backward_kernel, layer), jobs, (chunks,),
        [head_spec(scalars[0]), head_spec(scalars[1]), row(width), row(width)] + weight_specs(width) + [
            row(CONV_CH),
            pl.BlockSpec((8, CONV_CH), lambda i: (jnp.maximum((back - i) * steps - 1, 0), 0)),
            row(VAL), row(LANES), row(CHUNK), row(VAL), row(VAL),
            pl.BlockSpec((None, KEY, VAL), lambda i: (back - i, 0, 0)),
        ],
        [
            row(width), row(CONV_CH), row(VAL),
            pl.BlockSpec((width, LANES), lambda i: (0, 0)),
            pl.BlockSpec((1, VAL), lambda i: (0, 0)),
            pl.BlockSpec((8, LANES), lambda i: (0, 0)),
        ],
        [
            out(width, BF16), out(CONV_CH, BF16), out(VAL, BF16),
            jax.ShapeDtypeStruct((width, LANES), BF16),
            jax.ShapeDtypeStruct((1, VAL), F32),
            jax.ShapeDtypeStruct((8, LANES), F32),
        ],
        [
            pltpu.VMEM((CHUNK + 8, CONV_CH), F32),
            pltpu.VMEM((CHUNK + 8, CONV_CH), F32),
            pltpu.VMEM((KEY, VAL), F32),
            pltpu.VMEM((4, CONV_CH), F32),
            pltpu.VMEM((LANES, CONV_CH), F32),
            pltpu.VMEM((width, LANES), F32),
        ],
        (*scalars, g, x, qkv, pack, pack, pack, gain, proj, proj, gate_in, rates, inverse, fresh, o,
         states),
        number, "mixer_backward", 16 * 10**9,
    )


PIECES = 4
AXES = ("chip", "core", "zp", "zl")


def partners():
    core, zl = lax.axis_index("core"), lax.axis_index("zl")
    return core, zl, {"core": 1 - core}, {"zl": 1 - zl}


class Block:
    def __init__(self, zl, core, rows):
        self.first = (zl * 2 + core) * rows
        self.size = rows // PIECES

    def piece(self, p):
        return pl.ds(pl.multiple_of(self.first + p * self.size, self.size), self.size)


def remote(src, dst, send, recv, device):
    return pltpu.make_async_remote_copy(
        src_ref=src, dst_ref=dst, send_sem=send, recv_sem=recv,
        device_id=device, device_id_type=pl.DeviceIdType.MESH,
    )


class Scatter:
    def __init__(self, partial, beside_far, beside_own, sums, far, send, recv):
        core, zl, beside, across = partners()
        rows = far.shape[0]
        self.partial, self.beside_far, self.beside_own = partial, beside_far, beside_own
        self.sums, self.far = sums, far
        self.size = rows // PIECES
        self.own = Block(zl, core, rows)
        self.away = Block(1 - zl, core, rows)
        own_beside, away_beside = Block(zl, 1 - core, rows), Block(1 - zl, 1 - core, rows)
        self.to_far = [
            remote(partial.at[away_beside.piece(p)], beside_far.at[self.local(p)],
                   send.at[0, p], recv.at[0, p], beside)
            for p in range(PIECES)
        ]
        self.to_own = [
            remote(partial.at[own_beside.piece(p)], beside_own.at[self.local(p)],
                   send.at[1, p], recv.at[1, p], beside)
            for p in range(PIECES)
        ]
        self.cross = [
            remote(sums.at[self.local(p)], far.at[self.local(p)],
                   send.at[2, p], recv.at[2, p], across)
            for p in range(PIECES)
        ]

    def local(self, p):
        return pl.ds(p * self.size, self.size)

    def start(self):
        for copy in self.to_far:
            copy.start()
        for copy in self.to_own:
            copy.start()
        for p in range(PIECES):
            self.to_far[p].wait_recv()
            at = self.local(p)
            self.sums[at, :] = (
                self.partial[self.away.piece(p), :].astype(F32) + self.beside_far[at, :].astype(F32)
            ).astype(BF16)
            self.cross[p].start()

    def total(self, p):
        self.to_own[p].wait_recv()
        self.cross[p].wait_recv()
        at = self.local(p)
        return (
            self.partial[self.own.piece(p), :].astype(F32)
            + self.beside_own[at, :].astype(F32)
            + self.far[at, :].astype(F32)
        )

    def finish(self):
        for copies in (self.to_far, self.to_own, self.cross):
            for copy in copies:
                copy.wait_send()


class Gather:
    def __init__(self, gathered, send, recv, first):
        core, zl, beside, across = partners()
        rows = gathered.shape[0] // 4
        self.gathered = gathered
        self.own = Block(zl, core, rows)
        other = Block(1 - zl, core, rows)
        make = lambda block, at, device: [
            remote(gathered.at[block.piece(p)], gathered.at[block.piece(p)],
                   send.at[first + at, p], recv.at[first + at, p], device)
            for p in range(PIECES)
        ]
        self.across = make(self.own, 0, across)
        self.beside = make(self.own, 1, beside)
        self.forward = make(other, 2, beside)

    def put(self, p, rows):
        self.gathered[self.own.piece(p), :] = rows
        self.across[p].start()
        self.beside[p].start()

    def finish(self):
        for p in range(PIECES):
            self.across[p].wait_recv()
            self.forward[p].start()
        for p in range(PIECES):
            self.beside[p].wait_recv()
            self.forward[p].wait_recv()
        for copies in (self.across, self.beside, self.forward):
            for copy in copies:
                copy.wait_send()


def normed_of(x, gain):
    return x * lax.rsqrt(jnp.mean(x * x, axis=1, keepdims=True) + 1e-6) * gain


def first_kernel(row, jobs, x_ref, gain_ref, out_ref, send, recv):
    wait_greetings(greet_group() + jobs.greet())
    gather = Gather(out_ref, send, recv, 0)
    jobs.start()
    size = x_ref.shape[0] // PIECES
    for p in range(PIECES):
        x = x_ref[p * size : (p + 1) * size, :].astype(F32)
        gather.put(p, normed_of(x, gain_ref[row : row + 1, :].astype(F32)).astype(BF16))
    jobs.middle()
    gather.finish()
    jobs.finish()


def forward_bridge_kernel(
    row, jobs, partial, x_ref, gain_ref, new_ref, out_ref, beside_far, beside_own, sums, far, send, recv
):
    wait_greetings(greet_group() + jobs.greet())
    scatter = Scatter(partial, beside_far, beside_own, sums, far, send, recv)
    gather = Gather(out_ref, send, recv, 3)
    scatter.start()
    jobs.start()
    for p in range(PIECES):
        at = scatter.local(p)
        x = x_ref[at, :].astype(F32) + scatter.total(p)
        new_ref[at, :] = x
        gather.put(p, normed_of(x, gain_ref[row : row + 1, :].astype(F32)).astype(BF16))
    jobs.middle()
    scatter.finish()
    gather.finish()
    jobs.finish()


def norm_back(total, x, gain):
    inv = lax.rsqrt(jnp.mean(x * x, axis=1, keepdims=True) + 1e-6)
    unit = x * inv
    scaled = total * gain
    grad = inv * (scaled - unit * jnp.mean(scaled * unit, axis=1, keepdims=True))
    return grad, jnp.sum(total * unit, axis=0, keepdims=True)


def backward_bridge_kernel(
    row, jobs, partial, x_ref, gain_ref, grad_ref, new_ref, out_ref, dgain_ref,
    beside_far, beside_own, sums, far, send, recv
):
    wait_greetings(greet_group() + jobs.greet())
    scatter = Scatter(partial, beside_far, beside_own, sums, far, send, recv)
    gather = Gather(out_ref, send, recv, 3)
    scatter.start()
    jobs.start()
    dgain = jnp.zeros(dgain_ref.shape, F32)
    for p in range(PIECES):
        at = scatter.local(p)
        grad, part = norm_back(scatter.total(p), x_ref[at, :].astype(F32), gain_ref[row : row + 1, :].astype(F32))
        dgain = dgain + part
        grad = grad + grad_ref[at, :].astype(F32)
        new_ref[at, :] = grad
        gather.put(p, grad.astype(BF16))
    dgain_ref[...] = dgain
    jobs.middle()
    scatter.finish()
    gather.finish()
    jobs.finish()


def backward_last_kernel(
    row, jobs, partial, x_ref, gain_ref, grad_ref, new_ref, dgain_ref,
    beside_far, beside_own, sums, far, send, recv
):
    wait_greetings(greet_group() + jobs.greet())
    scatter = Scatter(partial, beside_far, beside_own, sums, far, send, recv)
    scatter.start()
    jobs.start()
    dgain = jnp.zeros(dgain_ref.shape, F32)
    for p in range(PIECES):
        at = scatter.local(p)
        grad, part = norm_back(scatter.total(p), x_ref[at, :].astype(F32), gain_ref[row : row + 1, :].astype(F32))
        dgain = dgain + part
        new_ref[at, :] = (grad + grad_ref[at, :]).astype(BF16)
    dgain_ref[...] = dgain
    jobs.middle()
    scatter.finish()
    jobs.finish()


def comm_call(kernel, row, number, outs, args, scatters, gathers, jobs):
    rows = args[1].shape[0] if scatters else args[0].shape[0]
    width = args[0].shape[1]
    vmem = pl.BlockSpec(memory_space=pltpu.VMEM)
    hops = 3 * scatters + 3 * gathers
    return carry_call(
        functools.partial(kernel, row), jobs, (), [vmem] * len(args), [vmem] * len(outs),
        [jax.ShapeDtypeStruct(shape, kind) for shape, kind in outs],
        [pltpu.VMEM((rows, width), BF16) for _ in range(4 * scatters)]
        + [pltpu.SemaphoreType.DMA((hops, PIECES)), pltpu.SemaphoreType.DMA((hops, PIECES))],
        args, number, kernel.__name__.replace("_kernel", ""), rows * width * 20,
    )


def first_gather(x, gain, row, jobs, number):
    rows, width = x.shape
    return comm_call(first_kernel, row, number, [((4 * rows, width), BF16)], (x, gain), 0, 1, jobs)


def forward_bridge(partial, x, gain, row, jobs, number):
    rows, width = x.shape
    return comm_call(
        forward_bridge_kernel, row, number, [((rows, width), F32), ((4 * rows, width), BF16)],
        (partial, x, gain), 1, 1, jobs,
    )


def backward_bridge(partial, x, gain, row, grad, jobs, number):
    rows, width = x.shape
    return comm_call(
        backward_bridge_kernel, row, number,
        [((rows, width), F32), ((4 * rows, width), BF16), ((1, width), F32)],
        (partial, x, gain, grad), 1, 1, jobs,
    )


def backward_last(partial, x, gain, row, grad, jobs, number):
    rows, width = x.shape
    return comm_call(
        backward_last_kernel, row, number, [((rows, width), BF16), ((1, width), F32)],
        (partial, x, gain, grad), 1, 0, jobs,
    )


class Job:
    in_vmem = False

    @staticmethod
    def buffers(shape, chips):
        return []

    def __init__(self, source, target, send, recv, chips, buffers=()):
        self.source, self.target, self.send, self.recv = source, target, send, recv
        self.held = buffers
        self.chips = chips
        self.chip, self.core, self.zp, self.zl, self.own = place(chips)
        self.fixed = (self.zp == self.zl) & (self.zl == self.core)
        self.outward, self.inward, self.locals = [], [], []
        self.plan()

    def copy(self, src, dst, send, recv, device):
        return remote(src, dst, self.send.at[send], self.recv.at[recv], device)

    def local(self, src, dst, at, when=None, through=None):
        if through is None:
            self.locals.append((pltpu.make_async_copy(src, dst, self.send.at[at]), None, when))
        else:
            self.locals.append(
                (pltpu.make_async_copy(src, through, self.send.at[at]),
                 pltpu.make_async_copy(through, dst, self.send.at[at]), when)
            )

    def column(self, chip, core, zp, zl):
        return at_device(chip, core, zp, zl)

    def greet(self):
        count = 0
        for copy, device, mine in self.inward:
            if mine is None:
                signal(device)
            else:
                unless(mine, functools.partial(signal, device))
        for copy, mine in self.outward:
            count = count + (1 if mine is None else 1 - mine.astype(jnp.int32))
        return count

    def start(self):
        for copy, mine in self.outward:
            if mine is None:
                copy.start()
            else:
                unless(mine, copy.start)
        for load, _, when in self.locals:
            if when is None:
                load.start()
            else:
                pl.when(when)(load.start)

    def middle(self):
        for load, store, when in self.locals:
            def turn():
                load.wait()
                store.start()

            if store is not None and when is None:
                turn()
            elif store is not None:
                pl.when(when)(turn)

    def arrivals(self):
        for copy, device, mine in self.inward:
            if mine is None:
                copy.wait_recv()
            else:
                unless(mine, copy.wait_recv)

    def departures(self):
        for copy, mine in self.outward:
            if mine is None:
                copy.wait_send()
            else:
                unless(mine, copy.wait_send)
        for load, store, when in self.locals:
            last = load if store is None else store
            if when is None:
                last.wait()
            else:
                pl.when(when)(last.wait)

    def finish(self):
        self.arrivals()
        self.departures()


def block(index, size):
    return pl.ds(pl.multiple_of(index * size, size), size)


class ToPlane(Job):
    @staticmethod
    def result(shape, chips):
        return (2 * shape[0], shape[1])

    @staticmethod
    def buffers(shape, chips):
        return [pltpu.VMEM(shape, BF16)]

    def plan(self):
        rows = self.source.shape[0]
        at = block(self.core, rows)
        for to in range(2):
            self.outward.append(
                (self.copy(self.source, self.target.at[at], to, self.core,
                           at_device(self.chip, self.zl, to, self.zp)),
                 self.fixed & (self.zp == to))
            )
        for co in range(2):
            device = at_device(self.chip, co, self.zl, self.core)
            self.inward.append(
                (self.copy(self.source, self.target.at[block(co, rows)], 0, co, device), device,
                 self.fixed & (self.core == co))
            )
        self.local(self.source, self.target.at[at], 2, self.fixed, self.held[0] if self.held else None)


class FromPlane(Job):
    @staticmethod
    def result(shape, chips):
        return (2, shape[0] // 2, shape[1])

    @staticmethod
    def buffers(shape, chips):
        return [pltpu.VMEM((shape[0] // 2, shape[1]), BF16)]

    def plan(self):
        rows = self.source.shape[0] // 2
        for co in range(2):
            src, mine = self.source.at[block(co, rows)], self.fixed & (self.core == co)
            self.outward.append(
                (self.copy(src, self.target.at[self.zp], co, self.zp,
                           at_device(self.chip, co, self.zl, self.core)), mine)
            )
            self.local(src, self.target.at[self.zp], 2 + co, mine, self.held[0] if self.held else None)
        for at in range(2):
            device = at_device(self.chip, self.zl, at, self.zp)
            self.inward.append(
                (self.copy(self.source.at[block(0, rows)], self.target.at[at], 0, at, device), device,
                 self.fixed & (self.zp == at))
            )


class Spread(Job):
    @staticmethod
    def result(shape, chips):
        return (chips * shape[0], shape[1])

    @staticmethod
    def buffers(shape, chips):
        return [pltpu.VMEM(shape, BF16)]

    def to(self, chip):
        return at_device(chip, self.core, self.zp, self.zl)

    def plan(self):
        rows = self.source.shape[0]
        own = self.target.at[block(self.chip, rows)]
        self.local(self.source, own, 0, None, self.held[0])
        self.onward, self.later = [], []
        if self.chips != 4:
            for j in range(1, self.chips):
                to = lax.rem(self.chip + j, self.chips)
                source = lax.rem(self.chip + self.chips - j, self.chips)
                self.outward.append((self.copy(self.source, own, j, j, self.to(to)), None))
                self.inward.append(
                    (self.copy(self.source, self.target.at[block(source, rows)], j, j,
                               self.to(source)), self.to(source), None)
                )
            return
        y, x = self.chip // 2, lax.rem(self.chip, 2)
        sides = [y * 2 + (1 - x), (1 - y) * 2 + x]
        across = (1 - y) * 2 + (1 - x)
        half = rows // 2
        for side in range(2):
            device = self.to(sides[side])
            self.outward.append((self.copy(self.source, own, 1 + side, 1 + side, device), None))
            self.inward.append(
                (self.copy(self.source, self.target.at[block(sides[side], rows)], 1 + side, 1 + side,
                           device), device, None)
            )
        for side in range(2):
            part = pl.ds(pl.multiple_of(sides[side] * rows + side * half, half), half)
            self.onward.append(
                self.copy(self.target.at[part], self.target.at[part], 3 + side, 3 + side,
                          self.to(sides[1 - side]))
            )
            part = pl.ds(pl.multiple_of(across * rows + side * half, half), half)
            self.later.append(
                self.copy(self.target.at[part], self.target.at[part], 3 + side, 3 + side,
                          self.to(sides[1 - side]))
            )

    def middle(self):
        super().middle()
        if self.onward:
            self.arrivals()
            for copy in self.onward:
                copy.start()

    def finish(self):
        if not self.onward:
            self.arrivals()
        for copy in self.later:
            copy.wait_recv()
        for copy in self.onward:
            copy.wait_send()
        self.departures()


class Reduce(Job):
    in_vmem = True

    @staticmethod
    def result(shape, chips):
        return (shape[0] // chips, shape[1])

    @staticmethod
    def buffers(shape, chips):
        rows, cols = shape[0] // chips, shape[1]
        if chips != 4:
            return [pltpu.VMEM((chips, rows, cols), BF16)]
        return [pltpu.VMEM((rows // 2, cols), BF16)] * 4 + [pltpu.VMEM((rows, cols), BF16)] * 3

    def plan(self):
        rows = self.source.shape[0] // self.chips
        to = lambda chip: at_device(chip, self.core, self.zp, self.zl)
        if self.chips != 4:
            (parts,) = self.held
            self.local(self.source.at[block(self.chip, rows)], parts.at[self.chip], 0)
            for j in range(1, self.chips):
                target = lax.rem(self.chip + j, self.chips)
                source = lax.rem(self.chip + self.chips - j, self.chips)
                src = self.source.at[block(target, rows)]
                self.outward.append((self.copy(src, parts.at[self.chip], j, j, to(target)), None))
                self.inward.append(
                    (self.copy(src, parts.at[source], j, j, to(source)), to(source), None)
                )
            return
        half = rows // 2
        y, x = self.chip // 2, lax.rem(self.chip, 2)
        sides = [y * 2 + (1 - x), (1 - y) * 2 + x]
        across = (1 - y) * 2 + (1 - x)
        passing, staged, blocks, own = self.held[0:2], self.held[2:4], self.held[4:6], self.held[6]
        piece = lambda chip, at: self.source.at[
            pl.ds(pl.multiple_of(chip * rows + at * half, half), half)
        ]
        self.local(self.source.at[block(self.chip, rows)], own, 0)
        self.loads = []
        self.onward, self.later = [], []
        for side in range(2):
            device = to(sides[side])
            copy = self.copy(piece(across, side), passing[side], 1 + side, 1 + side, device)
            self.outward.append((copy, None))
            self.inward.append((copy, device, None))
        self.direct = []
        for side in range(2):
            device = to(sides[side])
            part = pl.ds(side * half, half)
            self.direct.append(
                self.copy(piece(sides[side], side), blocks[side].at[part], 3 + side, 3 + side, device)
            )
            self.loads.append(
                pltpu.make_async_copy(piece(sides[side], 1 - side), staged[side], self.send.at[5 + side])
            )
            part = pl.ds((1 - side) * half, half)
            self.onward.append(
                self.copy(staged[side], blocks[side].at[part], 7 + side, 5 + side, device)
            )

    def start(self):
        super().start()
        if self.chips == 4:
            for copy in self.direct + self.loads:
                copy.start()

    def middle(self):
        if self.chips == 4:
            for side in range(2):
                self.inward[1 - side][0].wait_recv()
                self.loads[side].wait()
                self.held[2 + side][...] = (
                    self.held[2 + side][...].astype(F32) + self.held[1 - side][...].astype(F32)
                ).astype(BF16)
                self.onward[side].start()

    def finish(self):
        if self.chips == 4:
            for copy in self.direct + self.onward:
                copy.wait_recv()
            self.departures()
            for copy in self.direct + self.onward:
                copy.wait_send()
            total = self.held[6][...].astype(F32) + (
                self.held[4][...].astype(F32) + self.held[5][...].astype(F32)
            )
        else:
            super().finish()
            total = self.held[0][0].astype(F32)
            for chip in range(1, self.chips):
                total = total + self.held[0][chip].astype(F32)
        self.target[...] = total.astype(BF16)


class ToRole(Job):
    @staticmethod
    def result(shape, chips):
        return shape

    @staticmethod
    def buffers(shape, chips):
        return [pltpu.VMEM(shape, BF16)]

    def ends(self):
        role = at_device(self.chip, self.zl, self.core, self.zp)
        home = at_device(self.chip, self.zp, self.zl, self.core)
        return role, home, self.fixed & (self.zp == self.core)

    def plan(self):
        to, source, mine = self.ends()
        self.outward.append((self.copy(self.source, self.target, 0, 0, to), mine))
        self.inward.append((self.copy(self.source, self.target, 0, 0, source), source, mine))
        self.local(self.source, self.target, 1, mine, self.held[0])


class FromRole(ToRole):
    def ends(self):
        role, home, mine = super().ends()
        return home, role, mine


class Share(Job):
    @staticmethod
    def result(shape, chips):
        return (4 * shape[0], shape[1])

    @staticmethod
    def buffers(shape, chips):
        return [pltpu.VMEM(shape, BF16)]

    def plan(self):
        rows = self.source.shape[0]
        own = self.target.at[block(self.zl * 2 + self.core, rows)]
        beside = at_device(self.chip, 1 - self.core, self.zp, self.zl)
        across = at_device(self.chip, self.core, self.zp, 1 - self.zl)
        self.local(self.source, own, 0, None, self.held[0])
        for at, device, zl, core in ((1, beside, self.zl, 1 - self.core), (2, across, 1 - self.zl, self.core)):
            self.outward.append((self.copy(self.source, own, at, at, device), None))
            self.inward.append(
                (self.copy(self.source, self.target.at[block(zl * 2 + core, rows)], at, at, device),
                 device, None)
            )
        other = self.target.at[block((1 - self.zl) * 2 + self.core, rows)]
        self.onward = self.copy(other, other, 3, 3, beside)
        last = self.target.at[block((1 - self.zl) * 2 + 1 - self.core, rows)]
        self.later = self.copy(last, last, 3, 3, beside)

    def middle(self):
        super().middle()
        self.arrivals()
        self.onward.start()

    def finish(self):
        self.later.wait_recv()
        self.onward.wait_send()
        self.departures()


class ShareSum(Job):
    in_vmem = True

    @staticmethod
    def result(shape, chips):
        return (shape[0] // 4, shape[1])

    @staticmethod
    def buffers(shape, chips):
        return [pltpu.VMEM((shape[0] // 4, shape[1]), BF16)] * 5

    def plan(self):
        rows = self.target.shape[0]
        beside = at_device(self.chip, 1 - self.core, self.zp, self.zl)
        across = at_device(self.chip, self.core, self.zp, 1 - self.zl)
        part = lambda zl, core: self.source.at[block(zl * 2 + core, rows)]
        self.far, self.near, self.staged, self.own, self.other = self.held
        for at, src, dst in (
            (0, part(1 - self.zl, 1 - self.core), self.far), (1, part(self.zl, 1 - self.core), self.near)
        ):
            copy = self.copy(src, dst, at, at, beside)
            self.outward.append((copy, None))
            self.inward.append((copy, beside, None))
        self.local(part(1 - self.zl, self.core), self.staged, 2)
        self.local(part(self.zl, self.core), self.own, 3)
        self.onward = self.copy(self.staged, self.other, 4, 2, across)
        self.across = across

    def greet(self):
        signal(self.across)
        return super().greet() + 1

    def middle(self):
        self.arrivals()
        for load, _, _ in self.locals:
            load.wait()
        self.staged[...] = (
            self.staged[...].astype(F32) + self.far[...].astype(F32)
        ).astype(BF16)
        self.onward.start()

    def finish(self):
        for copy, _ in self.outward:
            copy.wait_send()
        self.onward.wait()
        self.target[...] = (
            self.own[...].astype(F32) + self.near[...].astype(F32) + self.other[...].astype(F32)
        ).astype(BF16)


class Jobs:
    def __init__(self, jobs, chips):
        self.kinds = [kind for kind, _ in jobs]
        self.values = [value for _, value in jobs]
        self.chips = chips
        count = max(9, chips + 1)
        any_space = pl.BlockSpec(memory_space=pl.ANY)
        self.in_specs = [any_space] * len(jobs)
        self.out_shape = [
            jax.ShapeDtypeStruct(kind.result(value.shape, chips), BF16) for kind, value in jobs
        ]
        self.buffers = [kind.buffers(value.shape, chips) for kind, value in jobs]
        self.scratch = [pltpu.SemaphoreType.DMA((count,))] * (2 * len(jobs))
        self.scratch += [buffer for buffers in self.buffers for buffer in buffers]

    def out_specs(self, grid):
        specs = []
        for kind, shape in zip(self.kinds, self.out_shape):
            if not kind.in_vmem:
                specs.append(pl.BlockSpec(memory_space=pl.ANY))
            elif grid:
                specs.append(pl.BlockSpec(shape.shape, lambda i: (0, 0)))
            else:
                specs.append(pl.BlockSpec(memory_space=pltpu.VMEM))
        return specs

    def bind(self, sources, targets, scratch):
        sems, scratch = scratch[: 2 * len(self.kinds)], scratch[2 * len(self.kinds) :]
        self.bound = []
        for at, (kind, source, target) in enumerate(zip(self.kinds, sources, targets)):
            held, scratch = scratch[: len(self.buffers[at])], scratch[len(self.buffers[at]) :]
            self.bound.append(
                kind(source, target, sems[2 * at], sems[2 * at + 1], self.chips, held)
            )

    def greet(self):
        count = 0
        for job in self.bound:
            count = count + job.greet()
        return count

    def start(self):
        for job in self.bound:
            job.start()

    def middle(self):
        for job in self.bound:
            job.middle()

    def finish(self):
        for job in self.bound:
            job.finish()


def carrying(body, jobs, ins, outs):
    extra = len(jobs.kinds)

    def kernel(*refs):
        operands, refs = refs[:ins], refs[ins:]
        sources, refs = refs[:extra], refs[extra:]
        results, refs = refs[:outs], refs[outs:]
        targets, refs = refs[:extra], refs[extra:]
        own = len(refs) - len(jobs.scratch)
        scratch = refs[:own]
        jobs.bind(sources, targets, refs[own:])
        body(jobs, *operands, *results, *scratch)

    return kernel


def carry_call(body, jobs, grid, in_specs, out_specs, out_shape, scratch, args, number, name, work):
    outs = len(out_shape)
    results = pl.pallas_call(
        carrying(body, jobs, len(args), outs),
        grid=grid,
        in_specs=list(in_specs) + jobs.in_specs,
        out_specs=list(out_specs) + jobs.out_specs(grid),
        out_shape=list(out_shape) + jobs.out_shape,
        scratch_shapes=list(scratch) + jobs.scratch,
        compiler_params=pltpu.CompilerParams(
            collective_id=number, has_side_effects=True, vmem_limit_bytes=56 * 1024 * 1024
        ),
        cost_estimate=pl.CostEstimate(
            flops=work, bytes_accessed=80 * 1024 * 1024, transcendentals=0
        ),
        name=name,
    )(*args, *jobs.values)
    return list(results[:outs]), list(results[outs:])


def place(chips):
    chip, core, zp, zl = (lax.axis_index(name) for name in AXES)
    return chip, core, zp, zl, chip * 2 + core


def at_device(chip, core, zp, zl):
    return {"chip": chip, "core": core, "zp": zp, "zl": zl}


def signal(device):
    pl.semaphore_signal(
        pltpu.get_barrier_semaphore(), inc=1, device_id=device,
        device_id_type=pl.DeviceIdType.MESH,
    )


def unless(condition, action):
    pl.when(jnp.logical_not(condition))(action)


class Plane:
    def __init__(self, chips):
        self.count = 2 * chips
        _, _, self.zp, self.zl, self.own = place(chips)

    def device(self, index):
        return at_device(index // 2, index % 2, self.zp, self.zl)

    def to(self, j):
        return lax.rem(self.own + j, self.count)

    def source(self, j):
        return lax.rem(self.own + self.count - j, self.count)

    def greet(self):
        for j in range(1, self.count):
            signal(self.device(self.to(j)))
        return self.count - 1


class Trade:
    def __init__(self, chips):
        self.chips, self.count = chips, 2 * chips
        self.chip, self.core, self.zp, self.zl, self.own = place(chips)
        self.fixed = (self.zp == self.zl) & (self.zl == self.core)
        self.slot = self.chip * 2 + self.zp

    def role(self, slot):
        return at_device(slot // 2, self.zl, slot % 2, self.zp)

    def role_mine(self, slot):
        return self.fixed & (self.slot == slot)

    def home(self, index):
        return at_device(index // 2, index % 2, self.zl, self.core)

    def home_mine(self, index):
        return self.fixed & (self.own == index)

    def greet_homes(self):
        for index in range(self.count):
            unless(self.home_mine(index), functools.partial(signal, self.home(index)))
        return self.count - self.fixed.astype(jnp.int32)

    def greet_roles(self):
        for slot in range(self.count):
            unless(self.role_mine(slot), functools.partial(signal, self.role(slot)))
        return self.count - self.fixed.astype(jnp.int32)


def greet_group():
    _, _, beside, across = partners()
    signal(beside)
    signal(across)
    return 2


def wait_greetings(count):
    pl.semaphore_wait(pltpu.get_barrier_semaphore(), count)


class Raw:
    def __init__(self, refs, square):
        (self.query, self.key, self.value, self.gate, self.decay, self.conv, self.out,
         self.ffn_gate, self.ffn_up, self.ffn_down) = refs
        self.square = square

    @staticmethod
    def turned(value):
        return value.astype(F32).T.astype(BF16)

    def qkv(self, layer, ref):
        ref[:, 0:KEY] = self.query[layer]
        ref[:, KEY : 2 * KEY] = self.key[layer]
        ref[:, 2 * KEY :] = self.value[layer]

    def mix(self, layer, ref):
        ref[:, 0:VAL] = self.gate[layer]
        ref[:, VAL : 2 * VAL] = self.turned(self.out[layer])
        self.square[...] = jnp.zeros(self.square.shape, F32)
        self.square[0:2, :] = self.decay[layer].astype(F32)
        self.square[2:6, :] = self.conv[layer].astype(F32)
        ref[:, 2 * VAL :] = self.square[...].T.astype(BF16)

    def pair(self, layer, ref):
        ref[...] = self.turned(
            jnp.concatenate([self.ffn_gate[layer], self.ffn_up[layer]], axis=0)
        )

    def down(self, layer, ref):
        ref[...] = self.turned(self.ffn_down[layer])


def deal_kernel(chips, jobs, order_ref, lengths_ref, x_ref, gain_ref, cotangent_ref, *refs):
    raw, refs = refs[:10], refs[10:]
    (new_ref, out_ref, start_ref, qkv_next, mix_next, pair_ref, pair_next, down_ref, down_next,
     first_full, second_full, first_wide, second_wide), refs = refs[:13], refs[13:]
    (spread, picked, square, first, second, held_first, held_second, send, recv, plane_send,
     plane_recv, role_send, role_recv, *sems) = refs
    raw = Raw(raw, square)
    plane, trade = Plane(chips), Trade(chips)
    first_column = ToPlane(first, first_wide, sems[0], sems[1], chips)
    first_across = Spread(first_wide, first_full, sems[2], sems[3], chips, [held_first])
    second_column = ToPlane(second, second_wide, sems[4], sems[5], chips)
    second_across = Spread(second_wide, second_full, sems[6], sems[7], chips, [held_second])
    gather = Gather(out_ref, send, recv, 0)
    count = plane.count
    part = x_ref.shape[0] // count
    rows = lambda index: pl.ds(pl.multiple_of(index * part, part), part)
    expected = plane.greet() + trade.greet_homes() + greet_group()
    for job in (first_column, first_across, second_column, second_across):
        expected = expected + job.greet()
    raw.qkv(0, first)
    raw.mix(0, second)
    wait_greetings(expected)
    outward, inward = [], []
    for j in range(1, count):
        to, source = plane.to(j), plane.source(j)
        outward.append(
            remote(x_ref.at[rows(to)], spread.at[plane.own], plane_send.at[j], plane_recv.at[j],
                   plane.device(to))
        )
        inward.append(
            remote(x_ref.at[rows(to)], spread.at[source], plane_send.at[j], plane_recv.at[j],
                   plane.device(source))
        )
    for copy in outward:
        copy.start()
    first_column.start()
    spread[plane.own] = x_ref[rows(plane.own), :]
    for copy in inward:
        copy.wait_recv()
    to_roles = []
    for slot in range(count):
        picked[slot] = spread[order_ref[slot]]
        copy = remote(picked.at[slot], new_ref.at[rows(plane.own)], role_send.at[slot],
                      role_recv.at[plane.own], trade.role(slot))
        mine = trade.role_mine(slot)
        unless(mine, copy.start)

        @pl.when(mine)
        def _():
            new_ref[rows(plane.own), :] = picked[slot]

        to_roles.append((copy, mine))
    first_column.finish()
    first_across.start()
    second_column.start()
    size = x_ref.shape[0] // PIECES
    parts = max(size // part, 1)
    for p in range(PIECES):
        for index in range(p * parts, (p + 1) * parts):
            arrival = remote(picked.at[0], new_ref.at[rows(index)], role_send.at[0],
                             role_recv.at[index], trade.home(index))
            unless(trade.home_mine(index), arrival.wait_recv)
        x = new_ref[p * size : (p + 1) * size, :].astype(F32)
        gather.put(p, normed_of(x, gain_ref[0:1, :].astype(F32)).astype(BF16))
    second_column.finish()
    second_across.start()
    first_across.middle()
    length = lengths_ref[order_ref[plane.own]]
    at = (trade.zp * 2 + trade.zl) * x_ref.shape[0]
    positions = lax.broadcasted_iota(jnp.int32, x_ref.shape, 0) + at
    start_ref[...] = jnp.where(positions < length, cotangent_ref[...], jnp.zeros(x_ref.shape, BF16))
    raw.qkv(1, qkv_next)
    raw.mix(1, mix_next)
    raw.pair(0, pair_ref)
    raw.pair(1, pair_next)
    raw.down(0, down_ref)
    raw.down(1, down_next)
    for copy in outward:
        copy.wait_send()
    for copy, mine in to_roles:
        unless(mine, copy.wait_send)
    gather.finish()
    second_across.middle()
    first_across.finish()
    second_across.finish()


def deal_and_gather(order, lengths, x, gain, cotangent, raw, chips, number):
    rows, width = x.shape
    part, units = raw[0].shape[1], raw[7].shape[1]
    vmem = pl.BlockSpec(memory_space=pltpu.VMEM)
    smem = pl.BlockSpec(memory_space=pltpu.SMEM)
    hbm = pl.BlockSpec(memory_space=pl.ANY)
    count = 2 * chips
    buffer = pltpu.VMEM((count, rows // count, width), BF16)
    sems = lambda *shape: [pltpu.SemaphoreType.DMA(shape), pltpu.SemaphoreType.DMA(shape)]
    qkv, mix = CONV_CH, 2 * VAL + LANES
    pair = (part, 2 * units)
    held = [(part, qkv), (part, mix), pair, pair, (part, units), (part, units)]
    spread = [(2 * chips * part, qkv), (2 * chips * part, mix)]
    moved = [(2 * part, qkv), (2 * part, mix)]
    shapes = [(rows, width), (4 * rows, width), (rows, width)] + held + spread + moved
    return carry_call(
        functools.partial(deal_kernel, chips), Jobs([], chips), (),
        [smem, smem] + [vmem] * 13,
        [vmem] * 9 + [hbm] * 4,
        [jax.ShapeDtypeStruct(shape, BF16) for shape in shapes],
        [buffer, buffer, pltpu.VMEM((LANES, LANES), F32)]
        + [pltpu.VMEM(shape, BF16) for shape in (held[0], held[1], moved[0], moved[1])]
        + sems(3, PIECES) + sems(count) + sems(count)
        + [pltpu.SemaphoreType.DMA((max(9, chips + 1),))] * 8,
        (order, lengths, x, gain, cotangent, *raw), number, "deal_and_gather", rows * width * 20,
    )[0]


def small_rows(width):
    rows = (4 * width + 2 * VAL) // LANES + 1
    return rows + -rows % 8


def assemble(small, mix0, mix1, ffn0, ffn1, heads0, heads1, scalars0, scalars1):
    small[...] = jnp.zeros(small.shape, F32)
    at = 0
    for term in (mix0, mix1, ffn0, ffn1, heads0, heads1):
        for r in range(term.shape[1] // LANES):
            small[at : at + 1, :] = term[:, r * LANES : (r + 1) * LANES]
            at += 1
    head = lax.axis_index("zl") * 2 + lax.axis_index("core")
    lane = lax.broadcasted_iota(jnp.int32, (1, LANES), 1)
    row = jnp.zeros((1, LANES), F32)
    values = (scalars0[0:1, :], scalars1[0:1, :], scalars0[1:2, :], scalars1[1:2, :])
    for place, value in enumerate(values):
        row = row + jnp.where(lane == place * 4 + head, value, 0.0)
    small[at : at + 1, :] = row


def final_kernel(
    chips, jobs, order_ref, partial, x_ref, gain_ref, grad_ref, *refs
):
    terms, refs = refs[:7], refs[7:]
    grads, refs = refs[:3], refs[3:]
    home_ref, total_ref, homes, refs = refs[0], refs[1], refs[2:5], refs[5:]
    (beside_far, beside_own, sums, far, last, back, picked, small, by_plane, by_z, plane_sum,
     send, recv, role_send, role_recv, plane_send, plane_recv, small_send, small_recv, z_send,
     z_recv), refs = refs[:21], refs[21:]
    reduces, returns = [], []
    for at in range(3):
        summed, four, refs = refs[0], refs[1:5], refs[5:]
        buffers = len(Reduce.buffers(grads[at].shape, chips))
        reduces.append(Reduce(grads[at], summed, four[0], four[1], chips, refs[:buffers]))
        returns.append(FromPlane(summed, homes[at], four[2], four[3], chips))
        refs = refs[buffers:]
    plane, trade = Plane(chips), Trade(chips)
    count = plane.count
    part = x_ref.shape[0] // count
    rows = lambda index: pl.ds(pl.multiple_of(index * part, part), part)
    tier = trade.zp * 2 + trade.zl
    tier_device = lambda at: at_device(trade.chip, trade.core, at // 2, at % 2)
    for k in range(1, 4):
        signal(tier_device(lax.rem(tier + k, 4)))
    expected = plane.greet() + trade.greet_roles() + greet_group() + jobs.greet() + 3
    for job in reduces + returns:
        expected = expected + job.greet()
    wait_greetings(expected)
    scatter = Scatter(partial, beside_far, beside_own, sums, far, send, recv)
    scatter.start()
    for job in reduces:
        job.start()
    jobs.start()
    dgain = jnp.zeros((1, x_ref.shape[1]), F32)
    to_homes = []
    size = x_ref.shape[0] // PIECES
    parts = max(size // part, 1)
    for p in range(PIECES):
        at = scatter.local(p)
        grad, piece = norm_back(scatter.total(p), x_ref[at, :].astype(F32), gain_ref[0:1, :].astype(F32))
        dgain = dgain + piece
        last[at, :] = (grad + grad_ref[at, :]).astype(BF16)
        for index in range(p * parts, (p + 1) * parts):
            copy = remote(last.at[rows(index)], back.at[trade.slot], role_send.at[index],
                          role_recv.at[trade.slot], trade.home(index))
            mine = trade.home_mine(index)
            unless(mine, copy.start)

            @pl.when(mine)
            def _():
                back[trade.slot] = last[rows(index), :]

            to_homes.append((copy, mine))
    assemble(small, dgain, *terms)
    small_out, small_in = [], []
    for j in range(1, count):
        to, source = plane.to(j), plane.source(j)
        small_out.append(
            remote(small, by_plane.at[plane.own], small_send.at[j], small_recv.at[j], plane.device(to))
        )
        small_in.append(
            remote(small, by_plane.at[source], small_send.at[j], small_recv.at[j], plane.device(source))
        )
    for copy in small_out:
        copy.start()
    by_plane[plane.own] = small[...]
    for job in reduces:
        job.middle()
    for slot in range(count):
        arrival = remote(last.at[rows(0)], back.at[slot], role_send.at[0], role_recv.at[slot],
                         trade.role(slot))
        unless(trade.role_mine(slot), arrival.wait_recv)
    outward, inward = [], []
    for j in range(count):
        to, source = plane.to(j), plane.source(j)
        at = jnp.int32(0)
        for slot in range(count):
            at = jnp.where(order_ref[slot] == to, slot, at)
        picked[j] = back[at]
        if j == 0:
            home_ref[rows(plane.own), :] = picked[0]
            continue
        copy = remote(picked.at[j], home_ref.at[rows(plane.own)], plane_send.at[j], plane_recv.at[j],
                      plane.device(to))
        copy.start()
        outward.append(copy)
        inward.append(
            remote(picked.at[j], home_ref.at[rows(source)], plane_send.at[j], plane_recv.at[j],
                   plane.device(source))
        )
    for reduce, back_home in zip(reduces, returns):
        reduce.finish()
        back_home.start()
    jobs.middle()
    for copy in small_in:
        copy.wait_recv()
    total = by_plane[0]
    for index in range(1, count):
        total = total + by_plane[index]
    plane_sum[...] = total
    z_out, z_in = [], []
    for k in range(1, 4):
        to, source = lax.rem(tier + k, 4), lax.rem(tier + 4 - k, 4)
        z_out.append(remote(plane_sum, by_z.at[tier], z_send.at[k], z_recv.at[k], tier_device(to)))
        z_in.append(remote(plane_sum, by_z.at[source], z_send.at[k], z_recv.at[k], tier_device(source)))
    for copy in z_out:
        copy.start()
    by_z[tier] = total
    for copy in z_in:
        copy.wait_recv()
    total_ref[...] = (by_z[0] + by_z[1]) + (by_z[2] + by_z[3])
    for copy in inward:
        copy.wait_recv()
    scatter.finish()
    for copy, mine in to_homes:
        unless(mine, copy.wait_send)
    for copy in small_out + z_out + outward:
        copy.wait_send()
    jobs.finish()
    for job in returns:
        job.finish()


def final_step(order, partial, x, gain, grad, terms, grads, chips, jobs, number):
    rows, width = x.shape
    small = jax.ShapeDtypeStruct((small_rows(width), LANES), F32)
    vmem = pl.BlockSpec(memory_space=pltpu.VMEM)
    count = 2 * chips
    block = pltpu.VMEM((rows, width), BF16)
    parted = pltpu.VMEM((count, rows // count, width), BF16)
    hbm = pl.BlockSpec(memory_space=pl.ANY)
    chained = []
    for a in grads:
        chained.append(pltpu.VMEM(Reduce.result(a.shape, chips), BF16))
        chained += [pltpu.SemaphoreType.DMA((max(9, chips + 1),))] * 4
        chained += Reduce.buffers(a.shape, chips)
    sems = lambda *shape: [pltpu.SemaphoreType.DMA(shape), pltpu.SemaphoreType.DMA(shape)]
    return carry_call(
        functools.partial(final_kernel, chips), jobs, (),
        [pl.BlockSpec(memory_space=pltpu.SMEM)] + [vmem] * 11 + [hbm] * 3,
        [vmem, vmem] + [hbm] * 3,
        [
            jax.ShapeDtypeStruct((rows, width), BF16),
            jax.ShapeDtypeStruct(small.shape, F32),
        ]
        + [
            jax.ShapeDtypeStruct(FromPlane.result(Reduce.result(a.shape, chips), chips), BF16)
            for a in grads
        ],
        [block] * 5 + [parted] * 2
        + [
            pltpu.VMEM(small.shape, F32), pltpu.VMEM((count,) + small.shape, F32),
            pltpu.VMEM((4,) + small.shape, F32), pltpu.VMEM(small.shape, F32),
        ]
        + sems(3, PIECES) + sems(count) + sems(count) + sems(count) + sems(4) + chained,
        (order, partial, x, gain, grad, *terms, *grads), number, "final_step", rows * width * 20,
    )


def only_jobs_kernel(jobs):
    wait_greetings(jobs.greet())
    jobs.start()
    jobs.middle()
    jobs.finish()


def only_jobs(jobs, number):
    return carry_call(only_jobs_kernel, jobs, (), [], [], [], [], (), number, "weights_back", 0)[1]


def weights_out_kernel(small_ref, home_ref, *refs):
    ins, outs = refs[:12], refs[12:]
    for layer in range(2):
        total = lambda ref: ref[0].astype(F32) + ref[1].astype(F32)
        qkv, gate, aux, out, pair, down = (total(ref) for ref in ins[6 * layer : 6 * layer + 6])
        units = down.shape[1]
        outs[0][layer] = qkv[:, :KEY]
        outs[1][layer] = qkv[:, KEY : 2 * KEY]
        outs[2][layer] = qkv[:, 2 * KEY :]
        outs[3][layer] = gate
        turned = aux.T
        outs[4][layer] = turned[0:2, :]
        outs[14][layer] = turned[2:6, :]
        outs[5][layer] = out.T
        turned = pair.T
        outs[6][layer] = turned[:units, :]
        outs[7][layer] = turned[units:, :]
        outs[8][layer] = down.T
    outs[15][...] = home_ref[...].astype(F32)
    at = 0
    for ref in outs[9:12]:
        for layer in range(2):
            for r in range(ref.shape[1] // LANES):
                ref[layer : layer + 1, r * LANES : (r + 1) * LANES] = small_ref[at : at + 1, :]
                at += 1
    heads = outs[12].shape[1]
    for member in range(2):
        for layer in range(2):
            first = (2 * member + layer) * heads
            outs[12 + member][layer : layer + 1, :] = small_ref[at : at + 1, first : first + heads]


def weights_out(small, home, first, second, heads):
    width = home.shape[1]
    rows, units = first[0].shape[1], first[5].shape[2]
    shapes = [
        (2, rows, KEY), (2, rows, KEY), (2, rows, VAL), (2, rows, VAL), (2, 2, rows), (2, VAL, rows),
        (2, units, rows), (2, units, rows), (2, units, rows),
        (2, width), (2, width), (2, VAL), (2, heads), (2, heads), (2, 4, rows), home.shape,
    ]
    vmem = pl.BlockSpec(memory_space=pltpu.VMEM)
    return pl.pallas_call(
        weights_out_kernel,
        in_specs=[vmem] * 14,
        out_specs=[vmem] * 16,
        out_shape=[jax.ShapeDtypeStruct(shape, F32) for shape in shapes],
        compiler_params=pltpu.CompilerParams(vmem_limit_bytes=56 * 1024 * 1024),
        name="weights_out",
    )(small, home, *first, *second)


def ffn_parts(x, pair):
    paired = mm(x, pair)
    units = paired.shape[1] // 2
    gate, up = paired[:, :units], paired[:, units:]
    act, sig = silu_of(gate)
    return gate, up, act, sig


def begin_jobs(jobs, at, steps):
    if jobs.kinds:
        @pl.when(at == 0)
        def _():
            wait_greetings(jobs.greet())
            jobs.start()

        @pl.when(at == steps // 2)
        def _():
            jobs.middle()


def end_jobs(jobs, at, steps):
    if jobs.kinds:
        @pl.when(at == steps - 1)
        def _():
            jobs.finish()


def ffn_forward_kernel(jobs, x_ref, pair_ref, down_ref, part_ref):
    at, steps = pl.program_id(0), pl.num_programs(0)
    begin_jobs(jobs, at, steps)
    _, up, act, _ = ffn_parts(x_ref[...], pair_ref[...])
    part_ref[...] = mm((act * up).astype(BF16), down_ref[...], NT).astype(BF16)
    end_jobs(jobs, at, steps)


def whole(shape):
    return pl.BlockSpec(shape, lambda i: (0, 0), pipeline_mode=pl.Buffered(1))


def ffn_forward(x, pair, down, jobs, number):
    length, width = x.shape
    rows = pl.BlockSpec((CHUNK, width), lambda i: (i, 0))
    return carry_call(
        ffn_forward_kernel, jobs, (length // CHUNK,),
        [rows, whole(pair.shape), whole(down.shape)], [rows],
        [jax.ShapeDtypeStruct((length, width), BF16)], [], (x, pair, down), number, "ffn_forward",
        4 * 10**9,
    )


def ffn_backward_kernel(both, jobs, x_ref, g_ref, pair_ref, down_ref, *refs):
    outs, (low_ref, hidden_ref) = refs[:-2], refs[-2:]
    part_ref, dpair_ref, ddown_ref = outs[:3]
    at, steps = pl.program_id(0), pl.num_programs(0)
    chunks = steps // 2
    begin_jobs(jobs, at, steps)

    @pl.when(at < chunks)
    def _():
        rows = pl.ds(pl.multiple_of(at * CHUNK, CHUNK), CHUNK)
        gate, up, act, sig = ffn_parts(x_ref[rows, :], pair_ref[...])
        hidden = (act * up).astype(BF16)
        hidden_ref[rows, :] = hidden
        if both:
            outs[3][...] = mm(hidden, down_ref[...], NT).astype(BF16)
        dhidden = mm(g_ref[rows, :], down_ref[...])
        dgate = dhidden * up * (sig * (1.0 + gate * (1.0 - sig)))
        low = jnp.concatenate([dgate, dhidden * act], axis=1).astype(BF16)
        low_ref[rows, :] = low
        part_ref[...] = mm(low, pair_ref[...], NT).astype(BF16)

    @pl.when(at >= chunks)
    def _():
        columns = pl.ds(pl.multiple_of((at - chunks) * CHUNK, CHUNK), CHUNK)
        dpair_ref[...] = mm(x_ref[:, columns], low_ref[...], TN).astype(BF16)
        ddown_ref[...] = mm(g_ref[:, columns], hidden_ref[...], TN).astype(BF16)

    end_jobs(jobs, at, steps)


def ffn_backward(x, g, pair, down, jobs, number, both=False):
    length, width = x.shape
    chunks = length // CHUNK
    assert length == width
    rows = pl.BlockSpec((CHUNK, width), lambda i: (jnp.minimum(i, chunks - 1), 0))
    late = lambda cols: pl.BlockSpec((CHUNK, cols), lambda i: (jnp.maximum(i - chunks, 0), 0))
    out = lambda cols: jax.ShapeDtypeStruct((length, cols), BF16)
    return carry_call(
        functools.partial(ffn_backward_kernel, both), jobs, (2 * chunks,),
        [whole(x.shape), whole(g.shape), whole(pair.shape), whole(down.shape)],
        [rows, late(pair.shape[1]), late(down.shape[1])] + [rows] * both,
        [out(width), out(pair.shape[1]), out(down.shape[1])] + [out(width)] * both,
        [pltpu.VMEM((length, pair.shape[1]), BF16), pltpu.VMEM((length, down.shape[1]), BF16)],
        (x, g, pair, down), number, "ffn_backward", 12 * 10**9,
    )


def dot32(a, b, dims):
    return lax.dot_general(a, b, dims, preferred_element_type=F32)


def row_major(x):
    return with_layout_constraint(x, Layout(major_to_minor=tuple(range(x.ndim))))


def linear(sizes, index):
    place = 0
    for size, at in zip(sizes, index):
        place = place * size + at
    return place


class Roles:
    def __init__(self):
        self.sizes = tuple(lax.axis_size(name) for name in AXES)
        self.chips, self.cores, self.zps, self.zls = self.sizes
        assert self.cores == 2 and self.zps == 2 and self.zls == 2

    def every(self):
        for chip in range(self.chips):
            for core in range(2):
                for zp in range(2):
                    for zl in range(2):
                        yield chip, core, zp, zl

    def rows_pairs(self):
        pairs = []
        for chip, core, zp, zl in self.every():
            slot, part = chip * 2 + zp, zl * 2 + core
            source = linear(self.sizes, (slot // 2, slot % 2, part // 2, part % 2))
            pairs.append((source, linear(self.sizes, (chip, core, zp, zl))))
        return pairs

    def weight_pairs(self, which):
        pairs = []
        for chip, core, zp, zl in self.every():
            head = zp * 2 + zl
            to = (chip, head % 2, core ^ which, head // 2)
            pairs.append(
                (linear(self.sizes, (chip, core, zp, zl)), linear(self.sizes, to))
            )
        return pairs


def flipped(pairs):
    return [(b, a) for a, b in pairs]


def chip_gather(ordered):
    return lax.all_gather(ordered, "chip", axis=0, tiled=True)


def to_plane(pack, roles):
    halves = [lax.ppermute(pack, AXES, roles.weight_pairs(which)) for which in range(2)]
    swap = lax.axis_index("zp") == 1
    return jnp.concatenate(
        [jnp.where(swap, halves[1], halves[0]), jnp.where(swap, halves[0], halves[1])], axis=0
    )


def summed(parts, kind):
    return jnp.sum(parts.astype(F32), axis=0).astype(kind)


def deal(values, order):
    spread = lax.all_to_all(values, ("chip", "core"), split_axis=2, concat_axis=1, tiled=True)
    picked = jnp.take(spread, order, axis=1)
    return lax.all_to_all(picked, ("chip", "core"), split_axis=1, concat_axis=2, tiled=True)


def shards(
    tokens, lengths, order, norm_mix, w_query, w_key, w_value, w_gate, w_decay, conv_filter,
    log_rate, step_bias, norm_heads, w_out, norm_ffn, w_ffn_gate, w_ffn_up, w_ffn_down, cotangent,
):
    roles = Roles()
    layer_count = w_query.shape[0]
    assert layer_count == 2
    heads_total = log_rate.shape[1]
    chip, core, zp, zl = (lax.axis_index(name) for name in AXES)
    head = zl * 2 + core
    rows_local, slots_local, width = tokens.shape
    assert slots_local == 1 and w_decay.shape[2] == 1
    slot_total = order.shape[0]
    units = w_ffn_gate.shape[2]
    rows_part = w_query.shape[1]
    to_roles = roles.rows_pairs()

    def carry(*jobs):
        return Jobs(list(jobs), roles.chips)

    scalars = (log_rate, step_bias)
    kernel_deal = rows_local % (16 * slot_total) == 0
    if kernel_deal:
        turned = lambda w: w.transpose(0, 2, 1)
        raw = (
            w_query, w_key, w_value, w_gate, turned(w_decay[:, :, 0, :]), conv_filter[:, :, 0, :],
            w_out, turned(w_ffn_gate), turned(w_ffn_up), w_ffn_down,
        )
        (residual, rows_in, start, qkv_next, mix_next, pair_first, pair_next, down_first, down_next,
         qkv, mix, _, _) = deal_and_gather(
            order, lengths, tokens[:, 0, :], norm_mix, cotangent[:, 0, :], raw, roles.chips, 1
        )
    else:
        qkv_packs, mix_packs, pair_packs, down_packs = [], [], [], []
        for layer in range(layer_count):
            aux = jnp.concatenate([w_decay[layer, :, 0, :], conv_filter[layer, :, 0, :].T], axis=1)
            aux = jnp.pad(aux, ((0, 0), (0, LANES - aux.shape[1])))
            qkv_packs.append(
                row_major(jnp.concatenate([w_query[layer], w_key[layer], w_value[layer]], axis=1))
            )
            mix_packs.append(
                row_major(jnp.concatenate([w_gate[layer], w_out[layer].T, aux], axis=1))
            )
            pair_packs.append(
                row_major(jnp.concatenate([w_ffn_gate[layer], w_ffn_up[layer]], axis=1))
            )
            down_packs.append(row_major(w_ffn_down[layer].T))
        qkv_next, mix_next = qkv_packs[1], mix_packs[1]
        (pair_first, pair_next), (down_first, down_next) = pair_packs, down_packs
        positions = (zp * 2 + zl) * rows_local + jnp.arange(rows_local)
        start = cotangent[:, 0, :] * (positions < lengths[order[chip * 2 + core]]).astype(BF16)[:, None]
        residual = lax.ppermute(deal(tokens, order)[:, 0, :], AXES, to_roles)
        (rows_in,), _ = first_gather(residual, norm_mix, 0, carry(), 1)
        qkv = chip_gather(to_plane(qkv_packs[0], roles))
        mix = chip_gather(to_plane(mix_packs[0], roles))

    def in_gradients(rows_in, dqkv, dgate):
        return dot32(rows_in, dqkv, TN).astype(BF16), dot32(rows_in, dgate, TN).astype(BF16)

    (part, heads0, *kept0), (pair_wide, down_wide) = mixer_forward(
        0, rows_in, qkv, mix, norm_heads, scalars,
        carry((ToPlane, pair_first), (ToPlane, down_first)), 2,
    )
    rows_in0, qkv0, mix0, residual0 = rows_in, qkv, mix, residual
    (middle0, rows_ffn0), (pair0, down0, qkv_wide, mix_wide) = forward_bridge(
        part, residual0, norm_ffn, 0,
        carry((Spread, pair_wide), (Spread, down_wide), (ToPlane, qkv_next), (ToPlane, mix_next)), 3,
    )
    (part,), _ = ffn_forward(rows_ffn0, pair0, down0, carry(), None)
    (residual1, rows_in1), (qkv1, mix1, down_wide) = forward_bridge(
        part, middle0, norm_mix, 1,
        carry((Spread, qkv_wide), (Spread, mix_wide), (ToPlane, down_next)), 4,
    )
    (part, heads1, *kept1), (down1, pair_wide, gradient) = mixer_forward(
        1, rows_in1, qkv1, mix1, norm_heads, scalars,
        carry((Spread, down_wide), (ToPlane, pair_next), (ToRole, start)), 5,
    )
    (middle1, rows_ffn1), (pair1, grad_rows) = forward_bridge(
        part, residual1, norm_ffn, 1, carry((Spread, pair_wide), (Share, gradient)), 6
    )
    (part, dpair1, ddown1, part_out), _ = ffn_backward(
        rows_ffn1, grad_rows, pair1, down1, carry(), None, both=True
    )

    (gradient, grad_rows, dgain_ffn1), (dpair1,) = backward_bridge(
        part, middle1, norm_ffn, 1, gradient, carry((Reduce, dpair1)), 7
    )
    dout1 = dot32(grad_rows, heads1, TN).astype(BF16)
    (part, dqkv, dgate, daux1, dgain1, dscalars1), jobs_results = mixer_backward(
        1, grad_rows, rows_in1, qkv1, mix1, norm_heads, scalars, kept1,
        carry((Reduce, ddown1), (Reduce, dout1), (FromPlane, dpair1), (ShareSum, part_out)), 8,
    )
    ddown1, dout1, pair_home1, total = jobs_results
    mixed = (middle1 + total.astype(F32)).astype(BF16)
    dqkv1, dgate1 = in_gradients(rows_in1, dqkv, dgate)
    results, jobs_results = backward_bridge(
        part, residual1, norm_mix, 1, gradient,
        carry((Reduce, dqkv1), (Reduce, dgate1), (Reduce, daux1), (FromRole, mixed)), 9,
    )
    gradient, grad_rows, dgain_mix1 = results
    dqkv1, dgate1, daux1, mixed = jobs_results
    (part, dpair0, ddown0), (qkv_home1, gate_home1, aux_home1) = ffn_backward(
        rows_ffn0, grad_rows, pair0, down0,
        carry((FromPlane, dqkv1), (FromPlane, dgate1), (FromPlane, daux1)), 14,
    )
    results, jobs_results = backward_bridge(
        part, middle0, norm_ffn, 0, gradient,
        carry((Reduce, dpair0)), 10,
    )
    gradient, grad_rows, dgain_ffn0 = results
    (dpair0,) = jobs_results
    dout0 = dot32(grad_rows, heads0, TN).astype(BF16)
    results, jobs_results = mixer_backward(
        0, grad_rows, rows_in0, qkv0, mix0, norm_heads, scalars, kept0,
        carry((Reduce, ddown0), (Reduce, dout0), (FromPlane, dpair0), (FromPlane, ddown1),
              (FromPlane, dout1)),
        11,
    )
    part, dqkv, dgate, daux0, dgain0, dscalars0 = results
    ddown0, dout0, pair_home0, down_home1, out_home1 = jobs_results
    dqkv0, dgate0 = in_gradients(rows_in0, dqkv, dgate)
    terms = (dgain_mix1, dgain_ffn0, dgain_ffn1, dgain0, dgain1, dscalars0, dscalars1)
    last = (dqkv0, dgate0, daux0)
    last_jobs = carry((FromPlane, ddown0), (FromPlane, dout0))
    if kernel_deal:
        (home, flat, *last), results = final_step(
            order, part, residual0, norm_mix, gradient, terms, last, roles.chips, last_jobs, 12
        )
    else:
        (gradient, dgain_mix), results = backward_last(
            part, residual0, norm_mix, 0, gradient, last_jobs, 12
        )
        mine = (jnp.arange(heads_total) == head).astype(F32)
        flat = jnp.concatenate(
            [dgain_mix[0], *(term[0] for term in terms[:5])]
            + [mine * term[row, 0] for row in range(2) for term in terms[5:]]
        )
        flat = jnp.pad(flat, (0, small_rows(width) * LANES - flat.shape[0])).reshape(-1, LANES)
        flat = lax.psum(flat, AXES)
        dealt_grad = lax.ppermute(gradient, AXES, flipped(to_roles))
        places = jnp.arange(slot_total, dtype=jnp.int32)
        inverse = jnp.sum(jnp.where(order[None, :] == places[:, None], places[None, :], 0), axis=1)
        home = deal(dealt_grad[:, None, :], inverse)[:, 0, :]
        last = only_jobs(carry(*[(Reduce, a) for a in last]), 13)
        last = only_jobs(carry(*[(FromPlane, a) for a in last]), 15)
    down_home0, out_home0 = results
    qkv_home0, gate_home0, aux_home0 = last
    first = (qkv_home0, gate_home0, aux_home0, out_home0, pair_home0, down_home0)
    second = (qkv_home1, gate_home1, aux_home1, out_home1, pair_home1, down_home1)
    if rows_part % LANES == 0:
        outs = weights_out(flat, home, first, second, heads_total)
    else:
        flat = flat.reshape(-1)
        small, at = [], 0
        for size in (width, width, VAL, heads_total, heads_total):
            small.append(flat[at : at + layer_count * size].reshape(layer_count, size))
            at += layer_count * size
        qkv, gate, aux, out, pair, down = (
            jnp.stack([summed(a, F32), summed(b, F32)]) for a, b in zip(first, second)
        )
        turned = lambda a: a.transpose(0, 2, 1)
        outs = [
            qkv[:, :, :KEY], qkv[:, :, KEY : 2 * KEY], qkv[:, :, 2 * KEY :], gate, turned(aux)[:, :2],
            turned(out), turned(pair)[:, :units], turned(pair)[:, units:], turned(down), *small,
            turned(aux)[:, 2:6], home.astype(F32),
        ]
    return (
        mixed[:, None, :],
        outs[15][:, None, :],
        outs[9],
        outs[0], outs[1], outs[2], outs[3],
        outs[4].transpose(0, 2, 1)[:, :, None, :],
        outs[14][:, :, None, :],
        outs[12],
        outs[13],
        outs[11],
        outs[5],
        outs[10],
        outs[6].transpose(0, 2, 1), outs[7].transpose(0, 2, 1), outs[8],
    )


def solution(mesh):
    dp, tensor = mesh.devices.shape
    mesh = Mesh(mesh.devices.reshape(dp // 2, 2, tensor // 2, 2), AXES)
    d, t = ("chip", "core"), ("zp", "zl")
    rows = P(t, d, None)
    by_rows, by_columns = P(None, d, t), P(None, t, d)
    heads, filters = P(None, d, t, None), P(None, None, t, d)
    return jax.shard_map(
        shards,
        mesh=mesh,
        in_specs=(
            rows, P(), P(), P(), by_rows, by_rows, by_rows, by_rows, heads, filters,
            P(), P(), P(), by_columns, P(), by_rows, by_rows, by_columns, rows,
        ),
        out_specs=(
            rows, rows, P(), by_rows, by_rows, by_rows, by_rows, heads, filters,
            P(), P(), P(), by_columns, P(), by_rows, by_rows, by_columns,
        ),
        check_vma=False,
    )
```

```python
import functools
import jax
import jax.numpy as jnp
from jax import lax
from jax.experimental import pallas as pl
from jax.experimental.layout import Layout, with_layout_constraint
from jax.experimental.pallas import tpu as pltpu
from jax.sharding import Mesh, PartitionSpec as P

CHUNK = 256
LANES = 128
KEY = 256
VAL = 512
CONV_CH = 2 * KEY + VAL
F32 = jnp.float32
BF16 = jnp.bfloat16
NN = (((1,), (0,)), ((), ()))
NT = (((1,), (1,)), ((), ()))
TN = (((0,), (0,)), ((), ()))


def mm(a, b, dims=NN):
    return lax.dot_general(
        a.astype(BF16), b.astype(BF16), dims, preferred_element_type=F32
    )


def split_low(a):
    high = a.astype(BF16)
    return high, (a - high.astype(F32)).astype(BF16)


def mm3(a, b, dims=NN):
    a_high, a_low = split_low(a)
    b_high, b_low = split_low(b)
    dot = functools.partial(
        lax.dot_general, dimension_numbers=dims, preferred_element_type=F32
    )
    return dot(a_high, b_high) + (dot(a_high, b_low) + dot(a_low, b_high))


def mm_exact_left(a, b, dims=NN):
    a = a.astype(BF16)
    high = b.astype(BF16)
    rest = b - high.astype(F32)
    mid = rest.astype(BF16)
    low = (rest - mid.astype(F32)).astype(BF16)
    dot = functools.partial(
        lax.dot_general, dimension_numbers=dims, preferred_element_type=F32
    )
    return dot(a, high) + (dot(a, mid) + dot(a, low))


def iotas():
    rows = lax.broadcasted_iota(jnp.int32, (CHUNK, CHUNK), 0)
    cols = lax.broadcasted_iota(jnp.int32, (CHUNK, CHUNK), 1)
    return rows, cols


def wide(col_block, width):
    return jnp.concatenate([col_block] * (width // LANES), axis=1)


def rates_of(rates, rate, bias):
    write = jax.nn.sigmoid(jnp.broadcast_to(rates[:, 0:1], (CHUNK, LANES)))
    logit = jnp.broadcast_to(rates[:, 1:2], (CHUNK, LANES)) + bias
    soft = jnp.maximum(logit, 0.0) + jnp.log1p(jnp.exp(-jnp.abs(logit)))
    return write, -rate * soft, jax.nn.sigmoid(logit)


def head_scalars(scalars_ref, layer):
    head = lax.axis_index("zl") * 2 + lax.axis_index("core")
    rate_ref, bias_ref = scalars_ref
    here = lax.broadcasted_iota(jnp.int32, (1, rate_ref.shape[1]), 1) == head
    pick = lambda ref: jnp.sum(
        jnp.where(here, ref[layer : layer + 1, :].astype(F32), 0.0), axis=1, keepdims=True
    )
    return jnp.exp(pick(rate_ref)), pick(bias_ref)


def decay_terms(step, rows, cols):
    inclusive = (rows >= cols).astype(BF16)
    total = mm_exact_left(inclusive, step)
    spread = wide(total, CHUNK) - jnp.concatenate([total.T] * (CHUNK // LANES), axis=0)
    decay = jnp.where(rows >= cols, jnp.exp(jnp.minimum(spread, 0.0)), 0.0)
    last = jnp.broadcast_to(total[CHUNK - 1 : CHUNK, :], (CHUNK, LANES))
    return decay, jnp.exp(total), jnp.exp(last - total), jnp.exp(last)


def solve_unit(coupling, rows, cols):
    unit = jnp.where(rows == cols, 1.0, 0.0)
    same = ((rows >> 1) == (cols >> 1)) & (rows != cols)
    inverse = unit - jnp.where(same, coupling, 0.0)
    for level in range(1, CHUNK.bit_length() - 1):
        between = ((rows >> (level + 1)) == (cols >> (level + 1))) & (
            (rows >> level) != (cols >> level)
        )
        part = jnp.where(between, coupling, 0.0)
        inverse = inverse - mm(mm(inverse, part), inverse)
    return inverse + mm(inverse, unit - inverse - mm3(coupling, inverse))


def silu_of(x):
    gate = jax.nn.sigmoid(x)
    return x * gate, gate


def conv_rows(padded_ref, taps_ref, start):
    result = padded_ref[pl.ds(start, CHUNK), :] * taps_ref[0:1, :]
    for j in range(1, 4):
        result = result + padded_ref[pl.ds(start + j, CHUNK), :] * taps_ref[j : j + 1, :]
    return result


def forward_kernel(
    layer, jobs, rate_ref, bias_ref, x_ref, w_qkv_ref, w_gate_ref, w_aux_ref, gain_ref,
    heads_ref, proj_ref, conv_ref, gate_ref, rates_ref, inverse_ref, fresh_ref, o_ref, state_ref,
    padded, memory, taps_ref,
):
    begin_jobs(jobs, pl.program_id(0), pl.num_programs(0))
    @pl.when(pl.program_id(0) == 0)
    def _():
        memory[...] = jnp.zeros_like(memory)
        taps_ref[...] = w_aux_ref[...].astype(F32).T[2:6, :]
        padded[0:8, :] = jnp.zeros((8, CONV_CH), F32)

    x = x_ref[...]
    rates = mm(x, w_aux_ref[...])
    rates_ref[...] = rates
    qkv = mm(x, w_qkv_ref[...])
    proj_ref[...] = qkv
    gate_in = mm(x, w_gate_ref[...])
    gate_ref[...] = gate_in
    padded[8 : 8 + CHUNK, :] = qkv
    conv = conv_rows(padded, taps_ref, 5)
    padded[0:8, :] = qkv[CHUNK - 8 :, :]
    conv_ref[...] = conv
    act, _ = silu_of(conv)
    q, k, v = act[:, :KEY], act[:, KEY : 2 * KEY], act[:, 2 * KEY :]
    q = q * (lax.rsqrt(jnp.sum(q * q, axis=1, keepdims=True) + 1e-6) * KEY**-0.5)
    k = k * lax.rsqrt(jnp.sum(k * k, axis=1, keepdims=True) + 1e-6)
    rows, cols = iotas()
    write, step, _ = rates_of(rates, *head_scalars((rate_ref, bias_ref), layer))
    decay, growth, rest, final = decay_terms(step, rows, cols)
    coupling = jnp.where(rows > cols, wide(write, CHUNK) * mm3(k, k, NT) * decay, 0.0)
    inverse = solve_unit(coupling, rows, cols)
    inverse_ref[...] = inverse.astype(BF16)
    within = mm(q, k, NT) * decay
    state = memory[...]
    state_ref[...] = state
    low_state = state.astype(BF16)
    source = wide(write, VAL) * (v - wide(growth, VAL) * mm(k, low_state))
    fresh = mm3(inverse, source)
    fresh_ref[...] = fresh
    o = wide(growth, VAL) * mm(q, low_state) + mm(within, fresh)
    o_ref[...] = o
    memory[...] = wide(final, VAL) * state + mm(k * wide(rest, KEY), fresh, TN)
    scaled = o * lax.rsqrt(jnp.mean(o * o, axis=1, keepdims=True) + 1e-5) * gain_ref[layer : layer + 1, :].astype(F32)
    heads = (scaled * silu_of(gate_in)[0]).astype(BF16)
    heads_ref[...] = heads
    end_jobs(jobs, pl.program_id(0), pl.num_programs(0))


def head_spec(value):
    return pl.BlockSpec(value.shape, lambda i: (0, 0))


def weight_specs(width):
    fixed = lambda shape, at: pl.BlockSpec(shape, lambda i: (0, at), pipeline_mode=pl.Buffered(1))
    return [
        fixed((width, CONV_CH), 0),
        fixed((width, VAL), 0),
        fixed((width, LANES), VAL // LANES),
        fixed((2, VAL), 0),
    ]


def mixer_forward(layer, x, qkv, pack, gain, scalars, jobs, number):
    length, width = x.shape
    chunks = length // CHUNK
    row = lambda cols: pl.BlockSpec((CHUNK, cols), lambda i: (i, 0))
    out = lambda cols, kind: jax.ShapeDtypeStruct((length, cols), kind)
    return carry_call(
        functools.partial(forward_kernel, layer), jobs, (chunks,),
        [head_spec(scalars[0]), head_spec(scalars[1]), row(width)] + weight_specs(width),
        [
            row(VAL), row(CONV_CH), row(CONV_CH), row(VAL), row(LANES), row(CHUNK), row(VAL), row(VAL),
            pl.BlockSpec((None, KEY, VAL), lambda i: (i, 0, 0)),
        ],
        [
            out(VAL, BF16), out(CONV_CH, F32), out(CONV_CH, F32), out(VAL, F32), out(LANES, F32),
            out(CHUNK, BF16), out(VAL, F32), out(VAL, F32),
            jax.ShapeDtypeStruct((chunks, KEY, VAL), F32),
        ],
        [
            pltpu.VMEM((CHUNK + 8, CONV_CH), F32), pltpu.VMEM((KEY, VAL), F32),
            pltpu.VMEM((4, CONV_CH), F32),
        ],
        (*scalars, x, qkv, pack, pack, gain), number, "mixer_forward", 16 * 10**9,
    )


def unit_back(grad, vector, scale):
    inv = lax.rsqrt(jnp.sum(vector * vector, axis=1, keepdims=True) + 1e-6)
    dot = jnp.sum(grad * vector, axis=1, keepdims=True)
    return (grad - vector * (inv * inv * dot)) * (inv * scale)


def backward_kernel(
    layer, jobs, rate_ref, bias_ref, g_ref, x_ref, w_out_ref, w_qkv_ref, w_gate_ref, w_aux_ref, gain_ref,
    proj_ref, halo_ref, conv_ref, gate_ref, rates_ref, inverse_ref, fresh_ref, o_ref, state_ref,
    part_ref, din_ref, daux_ref, dgain_ref, dscalars_ref,
    padded, dpadded, dmemory, taps_ref, dtaps_ref, daux_sum, x_held, dproj_ref,
):
    at, steps = pl.program_id(0), pl.num_programs(0)
    chunks = steps // 2
    last = chunks - 1
    begin_jobs(jobs, at, steps, (chunks // 2, chunks - 1))

    @pl.when(at == 0)
    def _():
        dmemory[...] = jnp.zeros_like(dmemory)
        taps_ref[...] = w_aux_ref[...].astype(F32).T[2:6, :]
        dpadded[CHUNK : CHUNK + 8, :] = jnp.zeros((8, CONV_CH), F32)
        dtaps_ref[...] = jnp.zeros_like(dtaps_ref)
        daux_sum[...] = jnp.zeros_like(daux_sum)
        dgain_ref[...] = jnp.zeros_like(dgain_ref)
        dscalars_ref[...] = jnp.zeros_like(dscalars_ref)

    @pl.when(at < chunks)
    def _():
        rows, cols = iotas()
        padded[8 : 8 + CHUNK, :] = proj_ref[...]
        padded[0:8, :] = jnp.where(at == last, 0.0, halo_ref[...])
        conv = conv_ref[...]
        act, sig = silu_of(conv)
        act_q, act_k, v = act[:, :KEY], act[:, KEY : 2 * KEY], act[:, 2 * KEY :]
        q = act_q * (lax.rsqrt(jnp.sum(act_q * act_q, axis=1, keepdims=True) + 1e-6) * KEY**-0.5)
        k = act_k * lax.rsqrt(jnp.sum(act_k * act_k, axis=1, keepdims=True) + 1e-6)
        rates = rates_ref[...]
        write, step, sig_decay = rates_of(rates, *head_scalars((rate_ref, bias_ref), layer))
        decay, growth, rest, final = decay_terms(step, rows, cols)
        growth_v = wide(growth, VAL)
        write_v = wide(write, VAL)
        low_q, low_k = q.astype(BF16), k.astype(BF16)
        below = rows > cols
        strict_decay = jnp.where(below, decay, 0.0)
        keys = mm(low_k, low_k, NT) * strict_decay * wide(write, CHUNK)
        within = mm(low_q, low_k, NT) * decay
        dheads = mm(g_ref[...], w_out_ref[...])
        o = o_ref[...]
        gate_in = gate_ref[...]
        gate, gate_sig = silu_of(gate_in)
        inv = lax.rsqrt(jnp.mean(o * o, axis=1, keepdims=True) + 1e-5)
        normal = o * inv
        gain = gain_ref[layer : layer + 1, :].astype(F32)
        dgate = dheads * normal * gain * (gate_sig * (1.0 + gate_in * (1.0 - gate_sig)))
        dscaled = dheads * gate
        dgain_ref[...] += jnp.sum(dscaled * normal, axis=0, keepdims=True)
        dnormal = dscaled * gain
        do = inv * (dnormal - normal * jnp.mean(dnormal * normal, axis=1, keepdims=True))
        state = state_ref[...]
        low_state = state.astype(BF16)
        fresh = fresh_ref[...]
        low_fresh = fresh.astype(BF16)
        dstate = dmemory[...]
        low_dstate = dstate.astype(BF16)
        low_do = do.astype(BF16)
        k_rest = k * wide(rest, KEY)
        rest_dstate = mm(k_rest, low_dstate)
        dfresh = mm(within, low_do, TN) + rest_dstate
        dsource = mm(inverse_ref[...], dfresh, TN)
        low_dsource = dsource.astype(BF16)
        dv = write_v * dsource
        dread = -(growth_v * dv)
        low_dread = dread.astype(BF16)
        do_growth = growth_v * do
        low_do_growth = do_growth.astype(BF16)
        dwithin = mm(low_do, low_fresh, NT)
        dcoupling = -mm(low_dsource, low_fresh, NT)
        dkeys = dcoupling * strict_decay * wide(write, CHUNK)
        dpairs = dwithin * decay
        dq = mm(low_do_growth, low_state, NT) + mm(dpairs, low_k)
        dk = (
            mm(low_dread, low_state, NT)
            + mm(dpairs, low_q, TN)
            + mm(dkeys + dkeys.T, low_k)
            + wide(rest, KEY) * mm(low_fresh, low_dstate, NT)
        )
        dmemory[...] = (
            wide(final, VAL) * dstate + mm(low_q, low_do_growth, TN) + mm(low_k, low_dread, TN)
        )
        spread = dwithin * within + dcoupling * keys
        straddle = jnp.where(below, mm_exact_left((rows <= cols).astype(BF16), spread), 0.0)
        read_rows = jnp.sum(
            do_growth * mm(low_q, low_state) + dread * mm(low_k, low_state), axis=1, keepdims=True
        )
        rest_rows = jnp.sum(fresh * rest_dstate, axis=1, keepdims=True)
        carried = jnp.sum(dstate * state) * final[0:1, 0:1]
        suffix = mm_exact_left(
            (rows <= cols).astype(BF16), jnp.broadcast_to(read_rows, (CHUNK, LANES))
        ) + mm_exact_left((rows > cols).astype(BF16), jnp.broadcast_to(rest_rows, (CHUNK, LANES)))
        dstep = suffix + jnp.sum(straddle, axis=1, keepdims=True) + carried
        dlogit = dstep * (-head_scalars((rate_ref, bias_ref), layer)[0]) * sig_decay
        dwrite = (1.0 - write) * jnp.sum(dsource * fresh, axis=1, keepdims=True)
        lane = lax.broadcasted_iota(jnp.int32, (CHUNK, LANES), 1)
        drates = jnp.where(lane == 0, dwrite, jnp.where(lane == 1, dlogit, 0.0))
        low_drates = drates.astype(BF16)
        daux_sum[...] += mm(low_drates, x_ref[...], TN)
        dscalars_ref[0:1, :] += jnp.sum(dstep * step, axis=0, keepdims=True)
        dscalars_ref[1:2, :] += jnp.sum(dlogit, axis=0, keepdims=True)
        dact = jnp.concatenate(
            [unit_back(dq, act_q, KEY**-0.5), unit_back(dk, act_k, 1.0), dv], axis=1
        )
        dconv = dact * (sig * (1.0 + conv * (1.0 - sig)))
        dpadded[0:CHUNK, :] = dconv
        dtaps_ref[2:6, :] += jnp.concatenate(
            [
                jnp.sum(dconv * padded[5 + j : 5 + j + CHUNK, :], axis=0, keepdims=True)
                for j in range(4)
            ],
            axis=0,
        )
        dqkv = dconv * taps_ref[3:4, :]
        for j in range(3):
            dqkv = dqkv + dpadded[pl.ds(3 - j, CHUNK), :] * taps_ref[j : j + 1, :]
        dpadded[CHUNK : CHUNK + 8, :] = dconv[0:8, :]
        low_dqkv, low_dgate = dqkv.astype(BF16), dgate.astype(BF16)
        place = block(last - at, CHUNK)
        dproj_ref[place, :CONV_CH] = low_dqkv
        dproj_ref[place, CONV_CH:] = low_dgate
        x_held[place, :] = x_ref[...]
        part_ref[...] = (
            mm(low_dqkv, w_qkv_ref[...], NT)
            + mm(low_dgate, w_gate_ref[...], NT)
            + mm(low_drates, w_aux_ref[...], NT)
        ).astype(BF16)

    @pl.when(at == last)
    def _():
        daux_ref[...] = (daux_sum[...] + dtaps_ref[...]).T.astype(BF16)

    @pl.when(at >= chunks)
    def _():
        columns = block(at - chunks, CHUNK)
        din_ref[...] = mm(x_held[:, columns], dproj_ref[...], TN).astype(BF16)

    end_jobs(jobs, at, steps)


def mixer_backward(layer, g, x, qkv, pack, w_out, gain, scalars, saved, jobs, number):
    proj, conv, gate_in, rates, inverse, fresh, o, states = saved
    length, width = g.shape
    chunks = length // CHUNK
    back = chunks - 1
    at = lambda i: jnp.maximum(back - i, 0)
    row = lambda cols: pl.BlockSpec((CHUNK, cols), lambda i: (at(i), 0))
    out = lambda cols, kind: jax.ShapeDtypeStruct((length, cols), kind)
    steps = CHUNK // 8
    return carry_call(
        functools.partial(backward_kernel, layer), jobs, (2 * chunks,),
        [head_spec(scalars[0]), head_spec(scalars[1]), row(width), row(width), whole(w_out.shape)]
        + weight_specs(width) + [
            row(CONV_CH),
            pl.BlockSpec((8, CONV_CH), lambda i: (jnp.maximum(at(i) * steps - 1, 0), 0)),
            row(CONV_CH), row(VAL), row(LANES), row(CHUNK), row(VAL), row(VAL),
            pl.BlockSpec((None, KEY, VAL), lambda i: (at(i), 0, 0)),
        ],
        [
            row(width),
            pl.BlockSpec((CHUNK, CONV_CH + VAL), lambda i: (jnp.maximum(i - chunks, 0), 0)),
            pl.BlockSpec((width, LANES), lambda i: (0, 0)),
            pl.BlockSpec((1, VAL), lambda i: (0, 0)),
            pl.BlockSpec((8, LANES), lambda i: (0, 0)),
        ],
        [
            out(width, BF16), jax.ShapeDtypeStruct((width, CONV_CH + VAL), BF16),
            jax.ShapeDtypeStruct((width, LANES), BF16),
            jax.ShapeDtypeStruct((1, VAL), F32),
            jax.ShapeDtypeStruct((8, LANES), F32),
        ],
        [
            pltpu.VMEM((CHUNK + 8, CONV_CH), F32),
            pltpu.VMEM((CHUNK + 8, CONV_CH), F32),
            pltpu.VMEM((KEY, VAL), F32),
            pltpu.VMEM((4, CONV_CH), F32),
            pltpu.VMEM((LANES, CONV_CH), F32),
            pltpu.VMEM((LANES, width), F32),
            pltpu.VMEM((length, width), BF16),
            pltpu.VMEM((length, CONV_CH + VAL), BF16),
        ],
        (*scalars, g, x, w_out, qkv, pack, pack, gain, proj, proj, conv, gate_in, rates, inverse, fresh, o,
         states),
        number, "mixer_backward", 16 * 10**9,
    )


PIECES = 4
AXES = ("chip", "core", "zp", "zl")


def partners():
    core, zl = lax.axis_index("core"), lax.axis_index("zl")
    return core, zl, {"core": 1 - core}, {"zl": 1 - zl}


class Block:
    def __init__(self, zl, core, rows):
        self.first = (zl * 2 + core) * rows
        self.size = rows // PIECES

    def piece(self, p):
        return pl.ds(pl.multiple_of(self.first + p * self.size, self.size), self.size)

    def rows(self):
        rows = self.size * PIECES
        return pl.ds(pl.multiple_of(self.first, rows), rows)


def remote(src, dst, send, recv, device):
    return pltpu.make_async_remote_copy(
        src_ref=src, dst_ref=dst, send_sem=send, recv_sem=recv,
        device_id=device, device_id_type=pl.DeviceIdType.MESH,
    )


class Scatter:
    def __init__(self, partial, beside_far, beside_own, sums, far, send, recv):
        core, zl, beside, across = partners()
        rows = far.shape[0]
        self.partial, self.beside_far, self.beside_own = partial, beside_far, beside_own
        self.sums, self.far = sums, far
        self.size = rows // PIECES
        self.own = Block(zl, core, rows)
        self.away = Block(1 - zl, core, rows)
        own_beside, away_beside = Block(zl, 1 - core, rows), Block(1 - zl, 1 - core, rows)
        self.blocks = (away_beside, own_beside, self.away, self.own)
        self.to_far = [
            remote(partial.at[away_beside.piece(p)], beside_far.at[self.local(p)],
                   send.at[0, p], recv.at[0, p], beside)
            for p in range(PIECES)
        ]
        self.to_own = [
            remote(partial.at[own_beside.piece(p)], beside_own.at[self.local(p)],
                   send.at[1, p], recv.at[1, p], beside)
            for p in range(PIECES)
        ]
        self.cross = [
            remote(sums.at[self.local(p)], far.at[self.local(p)],
                   send.at[2, p], recv.at[2, p], across)
            for p in range(PIECES)
        ]

    def local(self, p):
        return pl.ds(p * self.size, self.size)

    def start(self, make=None):
        if make is not None:
            make(self.blocks[0].rows())
        for copy in self.to_far:
            copy.start()
        if make is not None:
            make(self.blocks[1].rows())
        for copy in self.to_own:
            copy.start()
        if make is not None:
            make(self.blocks[2].rows())
            make(self.blocks[3].rows())
        for p in range(PIECES):
            self.to_far[p].wait_recv()
            at = self.local(p)
            self.sums[at, :] = (
                self.partial[self.away.piece(p), :].astype(F32) + self.beside_far[at, :].astype(F32)
            ).astype(BF16)
            self.cross[p].start()

    def total(self, p):
        self.to_own[p].wait_recv()
        self.cross[p].wait_recv()
        at = self.local(p)
        return (
            self.partial[self.own.piece(p), :].astype(F32)
            + self.beside_own[at, :].astype(F32)
            + self.far[at, :].astype(F32)
        )

    def finish(self):
        for copies in (self.to_far, self.to_own, self.cross):
            for copy in copies:
                copy.wait_send()


class Gather:
    def __init__(self, gathered, send, recv, first):
        core, zl, beside, across = partners()
        rows = gathered.shape[0] // 4
        self.gathered = gathered
        self.own = Block(zl, core, rows)
        other = Block(1 - zl, core, rows)
        make = lambda block, at, device: [
            remote(gathered.at[block.piece(p)], gathered.at[block.piece(p)],
                   send.at[first + at, p], recv.at[first + at, p], device)
            for p in range(PIECES)
        ]
        self.across = make(self.own, 0, across)
        self.beside = make(self.own, 1, beside)
        self.forward = make(other, 2, beside)

    def put(self, p, rows):
        self.gathered[self.own.piece(p), :] = rows
        self.across[p].start()
        self.beside[p].start()

    def finish(self):
        for p in range(PIECES):
            self.across[p].wait_recv()
            self.forward[p].start()
        for p in range(PIECES):
            self.beside[p].wait_recv()
            self.forward[p].wait_recv()
        for copies in (self.across, self.beside, self.forward):
            for copy in copies:
                copy.wait_send()


def normed_of(x, gain):
    return x * lax.rsqrt(jnp.mean(x * x, axis=1, keepdims=True) + 1e-6) * gain


def first_kernel(row, jobs, x_ref, gain_ref, out_ref, send, recv):
    wait_greetings(greet_group() + jobs.greet())
    gather = Gather(out_ref, send, recv, 0)
    jobs.start()
    size = x_ref.shape[0] // PIECES
    for p in range(PIECES):
        x = x_ref[p * size : (p + 1) * size, :].astype(F32)
        gather.put(p, normed_of(x, gain_ref[row : row + 1, :].astype(F32)).astype(BF16))
    jobs.middle()
    gather.finish()
    jobs.finish()


def forward_bridge_kernel(
    row, jobs, partial, x_ref, gain_ref, new_ref, out_ref, beside_far, beside_own, sums, far, send, recv
):
    wait_greetings(greet_group() + jobs.greet())
    scatter = Scatter(partial, beside_far, beside_own, sums, far, send, recv)
    gather = Gather(out_ref, send, recv, 3)
    scatter.start()
    jobs.start()
    for p in range(PIECES):
        at = scatter.local(p)
        x = x_ref[at, :].astype(F32) + scatter.total(p)
        new_ref[at, :] = x
        gather.put(p, normed_of(x, gain_ref[row : row + 1, :].astype(F32)).astype(BF16))
    jobs.middle()
    scatter.finish()
    gather.finish()
    jobs.finish()


def mixer_bridge_kernel(
    row, jobs, heads_ref, w_out_ref, x_ref, gain_ref, new_ref, out_ref, partial, beside_far, beside_own,
    sums, far, send, recv
):
    wait_greetings(greet_group() + jobs.greet())
    scatter = Scatter(partial, beside_far, beside_own, sums, far, send, recv)
    gather = Gather(out_ref, send, recv, 3)

    def make(rows):
        partial[rows, :] = mm(heads_ref[rows, :], w_out_ref[...], NT).astype(BF16)

    scatter.start(make)
    jobs.start()
    for p in range(PIECES):
        at = scatter.local(p)
        x = x_ref[at, :].astype(F32) + scatter.total(p)
        new_ref[at, :] = x
        gather.put(p, normed_of(x, gain_ref[row : row + 1, :].astype(F32)).astype(BF16))
    jobs.middle()
    scatter.finish()
    gather.finish()
    jobs.finish()


def norm_back(total, x, gain):
    inv = lax.rsqrt(jnp.mean(x * x, axis=1, keepdims=True) + 1e-6)
    unit = x * inv
    scaled = total * gain
    grad = inv * (scaled - unit * jnp.mean(scaled * unit, axis=1, keepdims=True))
    return grad, jnp.sum(total * unit, axis=0, keepdims=True)


def backward_bridge_kernel(row, last, jobs, partial, x_ref, gain_ref, grad_ref, *refs):
    if last:
        heads_ref, new_ref, out_ref, dgain_ref, dout_ref, *refs = refs
    else:
        new_ref, out_ref, dgain_ref, *refs = refs
    beside_far, beside_own, sums, far, send, recv = refs
    wait_greetings(greet_group() + jobs.greet())
    scatter = Scatter(partial, beside_far, beside_own, sums, far, send, recv)
    gather = Gather(out_ref, send, recv, 3)
    scatter.start()
    jobs.start()
    dgain = jnp.zeros(dgain_ref.shape, F32)
    for p in range(PIECES):
        at = scatter.local(p)
        grad, part = norm_back(scatter.total(p), x_ref[at, :].astype(F32), gain_ref[row : row + 1, :].astype(F32))
        dgain = dgain + part
        grad = grad + grad_ref[at, :].astype(F32)
        new_ref[at, :] = grad
        gather.put(p, grad.astype(BF16))
    dgain_ref[...] = dgain
    jobs.middle()
    scatter.finish()
    gather.finish()
    if last:
        for first in range(0, out_ref.shape[1], 256):
            columns = slice(first, first + 256)
            dout_ref[columns, :] = mm(out_ref[:, columns], heads_ref[...], TN).astype(BF16)
    jobs.finish()


def backward_last_kernel(
    row, jobs, partial, x_ref, gain_ref, grad_ref, new_ref, dgain_ref,
    beside_far, beside_own, sums, far, send, recv
):
    wait_greetings(greet_group() + jobs.greet())
    scatter = Scatter(partial, beside_far, beside_own, sums, far, send, recv)
    scatter.start()
    jobs.start()
    dgain = jnp.zeros(dgain_ref.shape, F32)
    for p in range(PIECES):
        at = scatter.local(p)
        grad, part = norm_back(scatter.total(p), x_ref[at, :].astype(F32), gain_ref[row : row + 1, :].astype(F32))
        dgain = dgain + part
        new_ref[at, :] = (grad + grad_ref[at, :]).astype(BF16)
    dgain_ref[...] = dgain
    jobs.middle()
    scatter.finish()
    jobs.finish()


def comm_call(kernel, row, number, outs, args, scatters, gathers, jobs, name=None):
    rows = args[1].shape[0] if scatters else args[0].shape[0]
    width = args[0].shape[1]
    vmem = pl.BlockSpec(memory_space=pltpu.VMEM)
    hops = 3 * scatters + 3 * gathers
    return carry_call(
        kernel if row is None else functools.partial(kernel, row), jobs, (), [vmem] * len(args), [vmem] * len(outs),
        [jax.ShapeDtypeStruct(shape, kind) for shape, kind in outs],
        [pltpu.VMEM((rows, width), BF16) for _ in range(4 * scatters)]
        + [pltpu.SemaphoreType.DMA((hops, PIECES)), pltpu.SemaphoreType.DMA((hops, PIECES))],
        args, number, name or kernel.__name__.replace("_kernel", ""), rows * width * 20,
    )


def first_gather(x, gain, row, jobs, number):
    rows, width = x.shape
    return comm_call(first_kernel, row, number, [((4 * rows, width), BF16)], (x, gain), 0, 1, jobs)


def forward_bridge(partial, x, gain, row, jobs, number):
    rows, width = x.shape
    return comm_call(
        forward_bridge_kernel, row, number, [((rows, width), F32), ((4 * rows, width), BF16)],
        (partial, x, gain), 1, 1, jobs,
    )


def mixer_bridge(heads, w_out, x, gain, row, jobs, number):
    rows, width = x.shape
    vmem = pl.BlockSpec(memory_space=pltpu.VMEM)
    sems = pltpu.SemaphoreType.DMA((6, PIECES))
    return carry_call(
        functools.partial(mixer_bridge_kernel, row), jobs, (), [vmem] * 4, [vmem] * 2,
        [
            jax.ShapeDtypeStruct((rows, width), F32),
            jax.ShapeDtypeStruct((4 * rows, width), BF16),
        ],
        [pltpu.VMEM((4 * rows, width), BF16)]
        + [pltpu.VMEM((rows, width), BF16) for _ in range(4)] + [sems, sems],
        (heads, w_out, x, gain), number, "mixer_bridge", 10**9,
    )


def backward_bridge(partial, x, gain, row, grad, jobs, number, heads=None):
    rows, width = x.shape
    last = heads is not None
    outs = [((rows, width), F32), ((4 * rows, width), BF16), ((1, width), F32)]
    if last:
        outs.append(((width, heads.shape[1]), BF16))
    return comm_call(
        functools.partial(backward_bridge_kernel, row, last), None, number, outs,
        (partial, x, gain, grad) + ((heads,) if last else ()), 1, 1, jobs, "backward_bridge",
    )


def backward_last(partial, x, gain, row, grad, jobs, number):
    rows, width = x.shape
    return comm_call(
        backward_last_kernel, row, number, [((rows, width), BF16), ((1, width), F32)],
        (partial, x, gain, grad), 1, 0, jobs,
    )


class Job:
    in_vmem = False
    late = False

    @staticmethod
    def buffers(shape, chips):
        return []

    def __init__(self, source, target, send, recv, chips, buffers=()):
        self.source, self.target, self.send, self.recv = source, target, send, recv
        self.held = buffers
        self.chips = chips
        self.chip, self.core, self.zp, self.zl, self.own = place(chips)
        self.fixed = (self.zp == self.zl) & (self.zl == self.core)
        self.outward, self.inward, self.locals = [], [], []
        self.plan()

    def copy(self, src, dst, send, recv, device):
        return remote(src, dst, self.send.at[send], self.recv.at[recv], device)

    def local(self, src, dst, at, when=None, through=None):
        if through is None:
            self.locals.append((pltpu.make_async_copy(src, dst, self.send.at[at]), None, when))
        else:
            self.locals.append(
                (pltpu.make_async_copy(src, through, self.send.at[at]),
                 pltpu.make_async_copy(through, dst, self.send.at[at]), when)
            )

    def column(self, chip, core, zp, zl):
        return at_device(chip, core, zp, zl)

    def greet(self):
        count = 0
        for copy, device, mine in self.inward:
            if mine is None:
                signal(device)
            else:
                unless(mine, functools.partial(signal, device))
        for copy, mine in self.outward:
            count = count + (1 if mine is None else 1 - mine.astype(jnp.int32))
        return count

    def start(self):
        for copy, mine in self.outward:
            if mine is None:
                copy.start()
            else:
                unless(mine, copy.start)
        for load, _, when in self.locals:
            if when is None:
                load.start()
            else:
                pl.when(when)(load.start)

    def middle(self):
        for load, store, when in self.locals:
            def turn():
                load.wait()
                store.start()

            if store is not None and when is None:
                turn()
            elif store is not None:
                pl.when(when)(turn)

    def arrivals(self):
        for copy, device, mine in self.inward:
            if mine is None:
                copy.wait_recv()
            else:
                unless(mine, copy.wait_recv)

    def departures(self):
        for copy, mine in self.outward:
            if mine is None:
                copy.wait_send()
            else:
                unless(mine, copy.wait_send)
        for load, store, when in self.locals:
            last = load if store is None else store
            if when is None:
                last.wait()
            else:
                pl.when(when)(last.wait)

    def finish(self):
        self.arrivals()
        self.departures()


def block(index, size):
    return pl.ds(pl.multiple_of(index * size, size), size)


class ToPlane(Job):
    @staticmethod
    def result(shape, chips):
        return (2 * shape[0], shape[1])

    @staticmethod
    def buffers(shape, chips):
        return [pltpu.VMEM(shape, BF16)]

    def plan(self):
        rows = self.source.shape[0]
        at = block(self.core, rows)
        for to in range(2):
            self.outward.append(
                (self.copy(self.source, self.target.at[at], to, self.core,
                           at_device(self.chip, self.zl, to, self.zp)),
                 self.fixed & (self.zp == to))
            )
        for co in range(2):
            device = at_device(self.chip, co, self.zl, self.core)
            self.inward.append(
                (self.copy(self.source, self.target.at[block(co, rows)], 0, co, device), device,
                 self.fixed & (self.core == co))
            )
        self.local(self.source, self.target.at[at], 2, self.fixed, self.held[0] if self.held else None)


class FromPlane(Job):
    @staticmethod
    def result(shape, chips):
        return (2, shape[0] // 2, shape[1])

    @staticmethod
    def buffers(shape, chips):
        return [pltpu.VMEM((shape[0] // 2, shape[1]), BF16)]

    def plan(self):
        rows = self.source.shape[0] // 2
        for co in range(2):
            src, mine = self.source.at[block(co, rows)], self.fixed & (self.core == co)
            self.outward.append(
                (self.copy(src, self.target.at[self.zp], co, self.zp,
                           at_device(self.chip, co, self.zl, self.core)), mine)
            )
            self.local(src, self.target.at[self.zp], 2 + co, mine, self.held[0] if self.held else None)
        for at in range(2):
            device = at_device(self.chip, self.zl, at, self.zp)
            self.inward.append(
                (self.copy(self.source.at[block(0, rows)], self.target.at[at], 0, at, device), device,
                 self.fixed & (self.zp == at))
            )


class Spread(Job):
    @staticmethod
    def result(shape, chips):
        return (chips * shape[0], shape[1])

    @staticmethod
    def buffers(shape, chips):
        return [pltpu.VMEM(shape, BF16)]

    def to(self, chip):
        return at_device(chip, self.core, self.zp, self.zl)

    def plan(self):
        rows = self.source.shape[0]
        own = self.target.at[block(self.chip, rows)]
        self.local(self.source, own, 0, None, self.held[0])
        self.onward, self.later = [], []
        if self.chips != 4:
            for j in range(1, self.chips):
                to = lax.rem(self.chip + j, self.chips)
                source = lax.rem(self.chip + self.chips - j, self.chips)
                self.outward.append((self.copy(self.source, own, j, j, self.to(to)), None))
                self.inward.append(
                    (self.copy(self.source, self.target.at[block(source, rows)], j, j,
                               self.to(source)), self.to(source), None)
                )
            return
        y, x = self.chip // 2, lax.rem(self.chip, 2)
        sides = [y * 2 + (1 - x), (1 - y) * 2 + x]
        across = (1 - y) * 2 + (1 - x)
        half = rows // 2
        for side in range(2):
            device = self.to(sides[side])
            self.outward.append((self.copy(self.source, own, 1 + side, 1 + side, device), None))
            self.inward.append(
                (self.copy(self.source, self.target.at[block(sides[side], rows)], 1 + side, 1 + side,
                           device), device, None)
            )
        for side in range(2):
            part = pl.ds(pl.multiple_of(sides[side] * rows + side * half, half), half)
            self.onward.append(
                self.copy(self.target.at[part], self.target.at[part], 3 + side, 3 + side,
                          self.to(sides[1 - side]))
            )
            part = pl.ds(pl.multiple_of(across * rows + side * half, half), half)
            self.later.append(
                self.copy(self.target.at[part], self.target.at[part], 3 + side, 3 + side,
                          self.to(sides[1 - side]))
            )

    def middle(self):
        super().middle()
        if self.onward:
            self.arrivals()
            for copy in self.onward:
                copy.start()

    def finish(self):
        if not self.onward:
            self.arrivals()
        for copy in self.later:
            copy.wait_recv()
        for copy in self.onward:
            copy.wait_send()
        self.departures()


class Reduce(Job):
    in_vmem = True

    @staticmethod
    def result(shape, chips):
        return (shape[0] // chips, shape[1])

    @staticmethod
    def buffers(shape, chips):
        rows, cols = shape[0] // chips, shape[1]
        if chips != 4:
            return [pltpu.VMEM((chips, rows, cols), BF16)]
        return [pltpu.VMEM((rows // 2, cols), BF16)] * 4 + [pltpu.VMEM((rows, cols), BF16)] * 3

    def plan(self):
        rows = self.source.shape[0] // self.chips
        to = lambda chip: at_device(chip, self.core, self.zp, self.zl)
        if self.chips != 4:
            (parts,) = self.held
            self.local(self.source.at[block(self.chip, rows)], parts.at[self.chip], 0)
            for j in range(1, self.chips):
                target = lax.rem(self.chip + j, self.chips)
                source = lax.rem(self.chip + self.chips - j, self.chips)
                src = self.source.at[block(target, rows)]
                self.outward.append((self.copy(src, parts.at[self.chip], j, j, to(target)), None))
                self.inward.append(
                    (self.copy(src, parts.at[source], j, j, to(source)), to(source), None)
                )
            return
        half = rows // 2
        y, x = self.chip // 2, lax.rem(self.chip, 2)
        sides = [y * 2 + (1 - x), (1 - y) * 2 + x]
        across = (1 - y) * 2 + (1 - x)
        passing, staged, blocks, own = self.held[0:2], self.held[2:4], self.held[4:6], self.held[6]
        piece = lambda chip, at: self.source.at[
            pl.ds(pl.multiple_of(chip * rows + at * half, half), half)
        ]
        self.local(self.source.at[block(self.chip, rows)], own, 0)
        self.loads = []
        self.onward, self.later = [], []
        for side in range(2):
            device = to(sides[side])
            copy = self.copy(piece(across, side), passing[side], 1 + side, 1 + side, device)
            self.outward.append((copy, None))
            self.inward.append((copy, device, None))
        self.direct = []
        for side in range(2):
            device = to(sides[side])
            part = pl.ds(side * half, half)
            self.direct.append(
                self.copy(piece(sides[side], side), blocks[side].at[part], 3 + side, 3 + side, device)
            )
            self.loads.append(
                pltpu.make_async_copy(piece(sides[side], 1 - side), staged[side], self.send.at[5 + side])
            )
            part = pl.ds((1 - side) * half, half)
            self.onward.append(
                self.copy(staged[side], blocks[side].at[part], 7 + side, 5 + side, device)
            )

    def start(self):
        super().start()
        if self.chips == 4:
            for copy in self.direct + self.loads:
                copy.start()

    def middle(self):
        if self.chips == 4:
            for side in range(2):
                self.inward[1 - side][0].wait_recv()
                self.loads[side].wait()
                self.held[2 + side][...] = (
                    self.held[2 + side][...].astype(F32) + self.held[1 - side][...].astype(F32)
                ).astype(BF16)
                self.onward[side].start()

    def finish(self):
        if self.chips == 4:
            for copy in self.direct + self.onward:
                copy.wait_recv()
            self.departures()
            for copy in self.direct + self.onward:
                copy.wait_send()
            total = self.held[6][...].astype(F32) + (
                self.held[4][...].astype(F32) + self.held[5][...].astype(F32)
            )
        else:
            super().finish()
            total = self.held[0][0].astype(F32)
            for chip in range(1, self.chips):
                total = total + self.held[0][chip].astype(F32)
        self.target[...] = total.astype(BF16)


class ToRole(Job):
    @staticmethod
    def result(shape, chips):
        return shape

    @staticmethod
    def buffers(shape, chips):
        return [pltpu.VMEM(shape, BF16)]

    def ends(self):
        role = at_device(self.chip, self.zl, self.core, self.zp)
        home = at_device(self.chip, self.zp, self.zl, self.core)
        return role, home, self.fixed & (self.zp == self.core)

    def plan(self):
        to, source, mine = self.ends()
        self.outward.append((self.copy(self.source, self.target, 0, 0, to), mine))
        self.inward.append((self.copy(self.source, self.target, 0, 0, source), source, mine))
        self.local(self.source, self.target, 1, mine, self.held[0])


class FromRole(ToRole):
    def ends(self):
        role, home, mine = super().ends()
        return home, role, mine


class Share(Job):
    late = True
    @staticmethod
    def result(shape, chips):
        return (4 * shape[0], shape[1])

    @staticmethod
    def buffers(shape, chips):
        return [pltpu.VMEM(shape, BF16)]

    def plan(self):
        rows = self.source.shape[0]
        own = self.target.at[block(self.zl * 2 + self.core, rows)]
        beside = at_device(self.chip, 1 - self.core, self.zp, self.zl)
        across = at_device(self.chip, self.core, self.zp, 1 - self.zl)
        self.local(self.source, own, 0, None, self.held[0])
        for at, device, zl, core in ((1, beside, self.zl, 1 - self.core), (2, across, 1 - self.zl, self.core)):
            self.outward.append((self.copy(self.source, own, at, at, device), None))
            self.inward.append(
                (self.copy(self.source, self.target.at[block(zl * 2 + core, rows)], at, at, device),
                 device, None)
            )
        other = self.target.at[block((1 - self.zl) * 2 + self.core, rows)]
        self.onward = self.copy(other, other, 3, 3, beside)
        last = self.target.at[block((1 - self.zl) * 2 + 1 - self.core, rows)]
        self.later = self.copy(last, last, 3, 3, beside)

    def middle(self):
        super().middle()
        self.arrivals()
        self.onward.start()

    def finish(self):
        self.later.wait_recv()
        self.onward.wait_send()
        self.departures()


class ShareSum(Job):
    late = True
    in_vmem = True

    @staticmethod
    def result(shape, chips):
        return (shape[0] // 4, shape[1])

    @staticmethod
    def buffers(shape, chips):
        return [pltpu.VMEM((shape[0] // 4, shape[1]), BF16)] * 5

    def plan(self):
        rows = self.target.shape[0]
        beside = at_device(self.chip, 1 - self.core, self.zp, self.zl)
        across = at_device(self.chip, self.core, self.zp, 1 - self.zl)
        part = lambda zl, core: self.source.at[block(zl * 2 + core, rows)]
        self.far, self.near, self.staged, self.own, self.other = self.held
        for at, src, dst in (
            (0, part(1 - self.zl, 1 - self.core), self.far), (1, part(self.zl, 1 - self.core), self.near)
        ):
            copy = self.copy(src, dst, at, at, beside)
            self.outward.append((copy, None))
            self.inward.append((copy, beside, None))
        self.local(part(1 - self.zl, self.core), self.staged, 2)
        self.local(part(self.zl, self.core), self.own, 3)
        self.onward = self.copy(self.staged, self.other, 4, 2, across)
        self.across = across

    def greet(self):
        signal(self.across)
        return super().greet() + 1

    def middle(self):
        self.arrivals()
        for load, _, _ in self.locals:
            load.wait()
        self.staged[...] = (
            self.staged[...].astype(F32) + self.far[...].astype(F32)
        ).astype(BF16)
        self.onward.start()

    def finish(self):
        for copy, _ in self.outward:
            copy.wait_send()
        self.onward.wait()
        self.target[...] = (
            self.own[...].astype(F32) + self.near[...].astype(F32) + self.other[...].astype(F32)
        ).astype(BF16)


class Jobs:
    def __init__(self, jobs, chips):
        self.kinds = [kind for kind, _ in jobs]
        self.values = [value for _, value in jobs]
        self.chips = chips
        count = max(9, chips + 1)
        any_space = pl.BlockSpec(memory_space=pl.ANY)
        self.in_specs = [any_space] * len(jobs)
        self.out_shape = [
            jax.ShapeDtypeStruct(kind.result(value.shape, chips), BF16) for kind, value in jobs
        ]
        self.buffers = [kind.buffers(value.shape, chips) for kind, value in jobs]
        self.scratch = [pltpu.SemaphoreType.DMA((count,))] * (2 * len(jobs))
        self.scratch += [buffer for buffers in self.buffers for buffer in buffers]

    def out_specs(self, grid):
        specs = []
        for kind, shape in zip(self.kinds, self.out_shape):
            if not kind.in_vmem:
                specs.append(pl.BlockSpec(memory_space=pl.ANY))
            elif grid:
                specs.append(pl.BlockSpec(shape.shape, lambda i: (0, 0)))
            else:
                specs.append(pl.BlockSpec(memory_space=pltpu.VMEM))
        return specs

    def bind(self, sources, targets, scratch):
        sems, scratch = scratch[: 2 * len(self.kinds)], scratch[2 * len(self.kinds) :]
        self.bound = []
        for at, (kind, source, target) in enumerate(zip(self.kinds, sources, targets)):
            held, scratch = scratch[: len(self.buffers[at])], scratch[len(self.buffers[at]) :]
            self.bound.append(
                kind(source, target, sems[2 * at], sems[2 * at + 1], self.chips, held)
            )

    def greet(self):
        count = 0
        for job in self.bound:
            count = count + job.greet()
        return count

    def start(self):
        for job in self.bound:
            job.start()

    def middle(self, late=None):
        for job in self.bound:
            if late is None or job.late == late:
                job.middle()

    def finish(self):
        for job in self.bound:
            job.finish()


def carrying(body, jobs, ins, outs):
    extra = len(jobs.kinds)

    def kernel(*refs):
        operands, refs = refs[:ins], refs[ins:]
        sources, refs = refs[:extra], refs[extra:]
        results, refs = refs[:outs], refs[outs:]
        targets, refs = refs[:extra], refs[extra:]
        own = len(refs) - len(jobs.scratch)
        scratch = refs[:own]
        jobs.bind(sources, targets, refs[own:])
        body(jobs, *operands, *results, *scratch)

    return kernel


def carry_call(body, jobs, grid, in_specs, out_specs, out_shape, scratch, args, number, name, work):
    outs = len(out_shape)
    results = pl.pallas_call(
        carrying(body, jobs, len(args), outs),
        grid=grid,
        in_specs=list(in_specs) + jobs.in_specs,
        out_specs=list(out_specs) + jobs.out_specs(grid),
        out_shape=list(out_shape) + jobs.out_shape,
        scratch_shapes=list(scratch) + jobs.scratch,
        compiler_params=pltpu.CompilerParams(
            collective_id=number, has_side_effects=True, vmem_limit_bytes=56 * 1024 * 1024
        ),
        cost_estimate=pl.CostEstimate(
            flops=work, bytes_accessed=80 * 1024 * 1024, transcendentals=0
        ),
        name=name,
    )(*args, *jobs.values)
    return list(results[:outs]), list(results[outs:])


def place(chips):
    chip, core, zp, zl = (lax.axis_index(name) for name in AXES)
    return chip, core, zp, zl, chip * 2 + core


def at_device(chip, core, zp, zl):
    return {"chip": chip, "core": core, "zp": zp, "zl": zl}


def signal(device):
    pl.semaphore_signal(
        pltpu.get_barrier_semaphore(), inc=1, device_id=device,
        device_id_type=pl.DeviceIdType.MESH,
    )


def unless(condition, action):
    pl.when(jnp.logical_not(condition))(action)


class Plane:
    def __init__(self, chips):
        self.count = 2 * chips
        _, _, self.zp, self.zl, self.own = place(chips)

    def device(self, index):
        return at_device(index // 2, index % 2, self.zp, self.zl)

    def to(self, j):
        return lax.rem(self.own + j, self.count)

    def source(self, j):
        return lax.rem(self.own + self.count - j, self.count)

    def greet(self):
        for j in range(1, self.count):
            signal(self.device(self.to(j)))
        return self.count - 1


class Trade:
    def __init__(self, chips):
        self.chips, self.count = chips, 2 * chips
        self.chip, self.core, self.zp, self.zl, self.own = place(chips)
        self.fixed = (self.zp == self.zl) & (self.zl == self.core)
        self.slot = self.chip * 2 + self.zp

    def role(self, slot):
        return at_device(slot // 2, self.zl, slot % 2, self.zp)

    def role_mine(self, slot):
        return self.fixed & (self.slot == slot)

    def home(self, index):
        return at_device(index // 2, index % 2, self.zl, self.core)

    def home_mine(self, index):
        return self.fixed & (self.own == index)

    def greet_homes(self):
        for index in range(self.count):
            unless(self.home_mine(index), functools.partial(signal, self.home(index)))
        return self.count - self.fixed.astype(jnp.int32)

    def greet_roles(self):
        for slot in range(self.count):
            unless(self.role_mine(slot), functools.partial(signal, self.role(slot)))
        return self.count - self.fixed.astype(jnp.int32)


def greet_group():
    _, _, beside, across = partners()
    signal(beside)
    signal(across)
    return 2


def wait_greetings(count):
    pl.semaphore_wait(pltpu.get_barrier_semaphore(), count)


class Raw:
    def __init__(self, refs, square):
        (self.query, self.key, self.value, self.gate, self.decay, self.conv, self.out,
         self.ffn_gate, self.ffn_up, self.ffn_down) = refs
        self.square = square

    def qkv(self, layer, ref):
        ref[:, 0:KEY] = self.query[layer]
        ref[:, KEY : 2 * KEY] = self.key[layer]
        ref[:, 2 * KEY :] = self.value[layer]

    def side(self, layer, ref):
        ref[:, 0:VAL] = self.gate[layer]
        self.square[...] = jnp.zeros(self.square.shape, F32)
        self.square[0:2, :] = self.decay[layer].astype(F32)
        self.square[2:6, :] = self.conv[layer].astype(F32)
        ref[:, VAL:] = self.square[...].T.astype(BF16)

    def turn(self, value, ref):
        ref[...] = value.astype(F32).T.astype(BF16)


def deal_kernel(chips, jobs, order_ref, lengths_ref, x_ref, gain_ref, cotangent_ref, *refs):
    raw, refs = refs[:10], refs[10:]
    (new_ref, out_ref, start_ref, qkv_next, side_next, out_next, gate_next, up_ref, up_next, down_ref,
     down_next, first_full, second_full, first_wide, second_wide, third_wide, fourth_wide) = refs[:17]
    (spread, picked, square, first, second, third, fourth, held_first, held_second, send, recv,
     plane_send, plane_recv, role_send, role_recv, *sems) = refs[17:]
    raw = Raw(raw, square)
    plane, trade = Plane(chips), Trade(chips)
    first_column = ToPlane(first, first_wide, sems[0], sems[1], chips)
    first_across = Spread(first_wide, first_full, sems[2], sems[3], chips, [held_first])
    second_column = ToPlane(second, second_wide, sems[4], sems[5], chips)
    second_across = Spread(second_wide, second_full, sems[6], sems[7], chips, [held_second])
    third_column = ToPlane(third, third_wide, sems[8], sems[9], chips)
    fourth_column = ToPlane(fourth, fourth_wide, sems[10], sems[11], chips)
    gather = Gather(out_ref, send, recv, 0)
    count = plane.count
    part = x_ref.shape[0] // count
    rows = lambda index: pl.ds(pl.multiple_of(index * part, part), part)
    expected = plane.greet() + trade.greet_homes() + greet_group()
    for job in (first_column, first_across, second_column, second_across, third_column, fourth_column):
        expected = expected + job.greet()
    raw.qkv(0, first)
    raw.side(0, second)
    wait_greetings(expected)
    outward, inward = [], []
    for j in range(1, count):
        to, source = plane.to(j), plane.source(j)
        outward.append(
            remote(x_ref.at[rows(to)], spread.at[plane.own], plane_send.at[j], plane_recv.at[j],
                   plane.device(to))
        )
        inward.append(
            remote(x_ref.at[rows(to)], spread.at[source], plane_send.at[j], plane_recv.at[j],
                   plane.device(source))
        )
    for copy in outward:
        copy.start()
    first_column.start()
    spread[plane.own] = x_ref[rows(plane.own), :]
    for copy in inward:
        copy.wait_recv()
    to_roles = []
    for slot in range(count):
        picked[slot] = spread[order_ref[slot]]
        copy = remote(picked.at[slot], new_ref.at[rows(plane.own)], role_send.at[slot],
                      role_recv.at[plane.own], trade.role(slot))
        mine = trade.role_mine(slot)
        unless(mine, copy.start)

        @pl.when(mine)
        def _():
            new_ref[rows(plane.own), :] = picked[slot]

        to_roles.append((copy, mine))
    second_column.start()
    raw.turn(raw.out[0], third)
    raw.turn(raw.ffn_gate[0], fourth)
    first_column.finish()
    first_across.start()
    size = x_ref.shape[0] // PIECES
    parts = max(size // part, 1)
    for p in range(PIECES):
        for index in range(p * parts, (p + 1) * parts):
            arrival = remote(picked.at[0], new_ref.at[rows(index)], role_send.at[0],
                             role_recv.at[index], trade.home(index))
            unless(trade.home_mine(index), arrival.wait_recv)
        x = new_ref[p * size : (p + 1) * size, :].astype(F32)
        gather.put(p, normed_of(x, gain_ref[0:1, :].astype(F32)).astype(BF16))
    second_column.finish()
    second_across.start()
    third_column.start()
    fourth_column.start()
    first_across.middle()
    length = lengths_ref[order_ref[plane.own]]
    at = (trade.zp * 2 + trade.zl) * x_ref.shape[0]
    positions = lax.broadcasted_iota(jnp.int32, x_ref.shape, 0) + at
    start_ref[...] = jnp.where(positions < length, cotangent_ref[...], jnp.zeros(x_ref.shape, BF16))
    raw.qkv(1, qkv_next)
    raw.side(1, side_next)
    raw.turn(raw.out[1], out_next)
    raw.turn(raw.ffn_gate[1], gate_next)
    raw.turn(raw.ffn_up[0], up_ref)
    raw.turn(raw.ffn_up[1], up_next)
    raw.turn(raw.ffn_down[0], down_ref)
    raw.turn(raw.ffn_down[1], down_next)
    for copy in outward:
        copy.wait_send()
    for copy, mine in to_roles:
        unless(mine, copy.wait_send)
    gather.finish()
    second_across.middle()
    first_across.finish()
    second_across.finish()
    third_column.finish()
    fourth_column.finish()


def deal_and_gather(order, lengths, x, gain, cotangent, raw, chips, number):
    rows, width = x.shape
    part, units = raw[0].shape[1], raw[7].shape[1]
    vmem = pl.BlockSpec(memory_space=pltpu.VMEM)
    smem = pl.BlockSpec(memory_space=pltpu.SMEM)
    hbm = pl.BlockSpec(memory_space=pl.ANY)
    count = 2 * chips
    buffer = pltpu.VMEM((count, rows // count, width), BF16)
    sems = lambda *shape: [pltpu.SemaphoreType.DMA(shape), pltpu.SemaphoreType.DMA(shape)]
    qkv, side = CONV_CH, VAL + LANES
    held = [(part, cols) for cols in (qkv, side, VAL, units, units, units, units, units)]
    spread = [(2 * chips * part, qkv), (2 * chips * part, side)]
    moved = [(2 * part, cols) for cols in (qkv, side, VAL, units)]
    shapes = [(rows, width), (4 * rows, width), (rows, width)] + held + spread + moved
    own = [(part, qkv), (part, side), (part, VAL), (part, units), moved[0], moved[1]]
    return carry_call(
        functools.partial(deal_kernel, chips), Jobs([], chips), (),
        [smem, smem] + [vmem] * 13,
        [vmem] * 11 + [hbm] * 6,
        [jax.ShapeDtypeStruct(shape, BF16) for shape in shapes],
        [buffer, buffer, pltpu.VMEM((LANES, LANES), F32)]
        + [pltpu.VMEM(shape, BF16) for shape in own]
        + sems(3, PIECES) + sems(count) + sems(count)
        + [pltpu.SemaphoreType.DMA((max(9, chips + 1),))] * 12,
        (order, lengths, x, gain, cotangent, *raw), number, "deal_and_gather", rows * width * 20,
    )[0]


def small_rows(width):
    rows = (4 * width + 2 * VAL) // LANES + 1
    return rows + -rows % 8


def assemble(small, mix0, mix1, ffn0, ffn1, heads0, heads1, scalars0, scalars1):
    small[...] = jnp.zeros(small.shape, F32)
    at = 0
    for term in (mix0, mix1, ffn0, ffn1, heads0, heads1):
        for r in range(term.shape[1] // LANES):
            small[at : at + 1, :] = term[:, r * LANES : (r + 1) * LANES]
            at += 1
    head = lax.axis_index("zl") * 2 + lax.axis_index("core")
    lane = lax.broadcasted_iota(jnp.int32, (1, LANES), 1)
    row = jnp.zeros((1, LANES), F32)
    values = (scalars0[0:1, :], scalars1[0:1, :], scalars0[1:2, :], scalars1[1:2, :])
    for place, value in enumerate(values):
        row = row + jnp.where(lane == place * 4 + head, value, 0.0)
    small[at : at + 1, :] = row


def final_kernel(
    chips, jobs, order_ref, partial, x_ref, gain_ref, grad_ref, *refs
):
    terms, refs = refs[:7], refs[7:]
    (in_ref, aux_ref), refs = refs[:2], refs[2:]
    home_ref, total_ref, in_home, aux_home, refs = *refs[:4], refs[4:]
    cut = [pl.ds(0, CONV_CH), pl.ds(CONV_CH, VAL)]
    grads = [in_ref.at[:, cut[0]], in_ref.at[:, cut[1]], aux_ref]
    homes = [in_home.at[:, :, cut[0]], in_home.at[:, :, cut[1]], aux_home]
    (beside_far, beside_own, sums, far, last, back, picked, small, by_plane, by_z, plane_sum,
     send, recv, role_send, role_recv, plane_send, plane_recv, small_send, small_recv, z_send,
     z_recv), refs = refs[:21], refs[21:]
    reduces, returns = [], []
    for at in range(3):
        summed, four, refs = refs[0], refs[1:5], refs[5:]
        buffers = len(Reduce.buffers(grads[at].shape, chips))
        reduces.append(Reduce(grads[at], summed, four[0], four[1], chips, refs[:buffers]))
        returns.append(FromPlane(summed, homes[at], four[2], four[3], chips))
        refs = refs[buffers:]
    plane, trade = Plane(chips), Trade(chips)
    count = plane.count
    part = x_ref.shape[0] // count
    rows = lambda index: pl.ds(pl.multiple_of(index * part, part), part)
    tier = trade.zp * 2 + trade.zl
    tier_device = lambda at: at_device(trade.chip, trade.core, at // 2, at % 2)
    for k in range(1, 4):
        signal(tier_device(lax.rem(tier + k, 4)))
    expected = plane.greet() + trade.greet_roles() + greet_group() + jobs.greet() + 3
    for job in reduces + returns:
        expected = expected + job.greet()
    wait_greetings(expected)
    scatter = Scatter(partial, beside_far, beside_own, sums, far, send, recv)
    scatter.start()
    reduces[0].start()
    jobs.start()
    dgain = jnp.zeros((1, x_ref.shape[1]), F32)
    to_homes = []
    size = x_ref.shape[0] // PIECES
    parts = max(size // part, 1)
    for p in range(PIECES):
        at = scatter.local(p)
        grad, piece = norm_back(scatter.total(p), x_ref[at, :].astype(F32), gain_ref[0:1, :].astype(F32))
        dgain = dgain + piece
        last[at, :] = (grad + grad_ref[at, :]).astype(BF16)
        for index in range(p * parts, (p + 1) * parts):
            copy = remote(last.at[rows(index)], back.at[trade.slot], role_send.at[index],
                          role_recv.at[trade.slot], trade.home(index))
            mine = trade.home_mine(index)
            unless(mine, copy.start)

            @pl.when(mine)
            def _():
                back[trade.slot] = last[rows(index), :]

            to_homes.append((copy, mine))
    assemble(small, dgain, *terms)
    small_out, small_in = [], []
    for j in range(1, count):
        to, source = plane.to(j), plane.source(j)
        small_out.append(
            remote(small, by_plane.at[plane.own], small_send.at[j], small_recv.at[j], plane.device(to))
        )
        small_in.append(
            remote(small, by_plane.at[source], small_send.at[j], small_recv.at[j], plane.device(source))
        )
    for copy in small_out:
        copy.start()
    by_plane[plane.own] = small[...]
    reduces[0].middle()
    reduces[1].start()
    reduces[2].start()
    for slot in range(count):
        arrival = remote(last.at[rows(0)], back.at[slot], role_send.at[0], role_recv.at[slot],
                         trade.role(slot))
        unless(trade.role_mine(slot), arrival.wait_recv)
    reduces[0].finish()
    returns[0].start()
    outward, inward = [], []
    for j in range(count):
        to, source = plane.to(j), plane.source(j)
        at = jnp.int32(0)
        for slot in range(count):
            at = jnp.where(order_ref[slot] == to, slot, at)
        picked[j] = back[at]
        if j == 0:
            home_ref[rows(plane.own), :] = picked[0]
            continue
        copy = remote(picked.at[j], home_ref.at[rows(plane.own)], plane_send.at[j], plane_recv.at[j],
                      plane.device(to))
        copy.start()
        outward.append(copy)
        inward.append(
            remote(picked.at[j], home_ref.at[rows(source)], plane_send.at[j], plane_recv.at[j],
                   plane.device(source))
        )
    for job in reduces[1:]:
        job.middle()
    jobs.middle()
    for reduce, back_home in zip(reduces[1:], returns[1:]):
        reduce.finish()
        back_home.start()
    for copy in small_in:
        copy.wait_recv()
    total = by_plane[0]
    for index in range(1, count):
        total = total + by_plane[index]
    plane_sum[...] = total
    z_out, z_in = [], []
    for k in range(1, 4):
        to, source = lax.rem(tier + k, 4), lax.rem(tier + 4 - k, 4)
        z_out.append(remote(plane_sum, by_z.at[tier], z_send.at[k], z_recv.at[k], tier_device(to)))
        z_in.append(remote(plane_sum, by_z.at[source], z_send.at[k], z_recv.at[k], tier_device(source)))
    for copy in z_out:
        copy.start()
    by_z[tier] = total
    for copy in z_in:
        copy.wait_recv()
    total_ref[...] = (by_z[0] + by_z[1]) + (by_z[2] + by_z[3])
    for copy in inward:
        copy.wait_recv()
    scatter.finish()
    for copy, mine in to_homes:
        unless(mine, copy.wait_send)
    for copy in small_out + z_out + outward:
        copy.wait_send()
    jobs.finish()
    for job in returns:
        job.finish()


def final_step(order, partial, x, gain, grad, terms, grads, chips, jobs, number):
    rows, width = x.shape
    small = jax.ShapeDtypeStruct((small_rows(width), LANES), F32)
    vmem = pl.BlockSpec(memory_space=pltpu.VMEM)
    count = 2 * chips
    block = pltpu.VMEM((rows, width), BF16)
    parted = pltpu.VMEM((count, rows // count, width), BF16)
    hbm = pl.BlockSpec(memory_space=pl.ANY)
    chained = []
    for a in [(grads[0].shape[0], cols) for cols in (CONV_CH, VAL, LANES)]:
        chained.append(pltpu.VMEM(Reduce.result(a, chips), BF16))
        chained += [pltpu.SemaphoreType.DMA((max(9, chips + 1),))] * 4
        chained += Reduce.buffers(a, chips)
    sems = lambda *shape: [pltpu.SemaphoreType.DMA(shape), pltpu.SemaphoreType.DMA(shape)]
    return carry_call(
        functools.partial(final_kernel, chips), jobs, (),
        [pl.BlockSpec(memory_space=pltpu.SMEM)] + [vmem] * 11 + [hbm] * 2,
        [vmem, vmem] + [hbm] * 2,
        [
            jax.ShapeDtypeStruct((rows, width), BF16),
            jax.ShapeDtypeStruct(small.shape, F32),
        ]
        + [
            jax.ShapeDtypeStruct(FromPlane.result(Reduce.result(a.shape, chips), chips), BF16)
            for a in grads
        ],
        [block] * 5 + [parted] * 2
        + [
            pltpu.VMEM(small.shape, F32), pltpu.VMEM((count,) + small.shape, F32),
            pltpu.VMEM((4,) + small.shape, F32), pltpu.VMEM(small.shape, F32),
        ]
        + sems(3, PIECES) + sems(count) + sems(count) + sems(count) + sems(4) + chained,
        (order, partial, x, gain, grad, *terms, *grads), number, "final_step", rows * width * 20,
    )


def only_jobs_kernel(jobs):
    wait_greetings(jobs.greet())
    jobs.start()
    jobs.middle()
    jobs.finish()


def only_jobs(jobs, number):
    return carry_call(only_jobs_kernel, jobs, (), [], [], [], [], (), number, "weights_back", 0)[1]


def weights_out_kernel(small_ref, home_ref, *refs):
    ins, outs = refs[:12], refs[12:]
    for layer in range(2):
        total = lambda ref: ref[0].astype(F32) + ref[1].astype(F32)
        proj, aux, out, gate, up, down = (total(ref) for ref in ins[6 * layer : 6 * layer + 6])
        outs[0][layer] = proj[:, :KEY]
        outs[1][layer] = proj[:, KEY : 2 * KEY]
        outs[2][layer] = proj[:, 2 * KEY : CONV_CH]
        outs[3][layer] = proj[:, CONV_CH:]
        turned = aux.T
        outs[4][layer] = turned[0:2, :]
        outs[14][layer] = turned[2:6, :]
        outs[5][layer] = out.T
        outs[6][layer] = gate.T
        outs[7][layer] = up.T
        outs[8][layer] = down.T
    outs[15][...] = home_ref[...].astype(F32)[:, None, :]
    at = 0
    for ref in outs[9:12]:
        for layer in range(2):
            for r in range(ref.shape[1] // LANES):
                ref[layer : layer + 1, r * LANES : (r + 1) * LANES] = small_ref[at : at + 1, :]
                at += 1
    heads = outs[12].shape[1]
    for member in range(2):
        for layer in range(2):
            first = (2 * member + layer) * heads
            outs[12 + member][layer : layer + 1, :] = small_ref[at : at + 1, first : first + heads]


def weights_out(small, home, first, second, heads):
    width = home.shape[1]
    rows, units = first[0].shape[1], first[5].shape[2]
    shapes = [
        (2, rows, KEY), (2, rows, KEY), (2, rows, VAL), (2, rows, VAL), (2, 2, rows), (2, VAL, rows),
        (2, units, rows), (2, units, rows), (2, units, rows),
        (2, width), (2, width), (2, VAL), (2, heads), (2, heads), (2, 4, rows),
        (home.shape[0], 1, width),
    ]
    vmem = pl.BlockSpec(memory_space=pltpu.VMEM)
    return pl.pallas_call(
        weights_out_kernel,
        in_specs=[vmem] * 14,
        out_specs=[vmem] * 16,
        out_shape=[jax.ShapeDtypeStruct(shape, F32) for shape in shapes],
        compiler_params=pltpu.CompilerParams(vmem_limit_bytes=56 * 1024 * 1024),
        name="weights_out",
    )(small, home, *first, *second)


def ffn_parts(x, gate_ref, up_ref):
    gate, up = mm(x, gate_ref[...]), mm(x, up_ref[...])
    act, sig = silu_of(gate)
    return gate, up, act, sig


def begin_jobs(jobs, at, steps, turns=None):
    if jobs.kinds:
        @pl.when(at == 0)
        def _():
            wait_greetings(jobs.greet())
            jobs.start()

        early, late = turns or (steps // 2, steps - 1)

        @pl.when(at == early)
        def _():
            jobs.middle(late=False)

        @pl.when(at == late)
        def _():
            jobs.middle(late=True)


def end_jobs(jobs, at, steps):
    if jobs.kinds:
        @pl.when(at == steps - 1)
        def _():
            jobs.finish()


def ffn_forward_kernel(jobs, x_ref, gate_ref, up_ref, down_ref, part_ref):
    at, steps = pl.program_id(0), pl.num_programs(0)
    begin_jobs(jobs, at, steps)
    _, up, act, _ = ffn_parts(x_ref[...], gate_ref, up_ref)
    part_ref[...] = mm((act * up).astype(BF16), down_ref[...], NT).astype(BF16)
    end_jobs(jobs, at, steps)


def whole(shape):
    return pl.BlockSpec(shape, lambda i: (0, 0), pipeline_mode=pl.Buffered(1))


def ffn_forward(x, weights, jobs, number):
    length, width = x.shape
    rows = pl.BlockSpec((CHUNK, width), lambda i: (i, 0))
    return carry_call(
        ffn_forward_kernel, jobs, (length // CHUNK,),
        [rows] + [whole(weight.shape) for weight in weights], [rows],
        [jax.ShapeDtypeStruct((length, width), BF16)], [], (x, *weights), number, "ffn_forward",
        4 * 10**9,
    )


def ffn_backward_kernel(both, jobs, x_ref, g_ref, gate_ref, up_ref, down_ref, *refs):
    outs, (low_gate, low_up, hidden_ref, x_held, g_held) = refs[:-5], refs[-5:]
    if both:
        residual_ref, outs = outs[0], outs[1:]
    part_ref, dgate_ref, dup_ref, ddown_ref = outs[:4]
    at, steps = pl.program_id(0), pl.num_programs(0)
    chunks = steps // 2
    begin_jobs(jobs, at, steps)

    @pl.when(at < chunks)
    def _():
        rows = pl.ds(pl.multiple_of(at * CHUNK, CHUNK), CHUNK)
        x, g = x_ref[...], g_ref[...]
        x_held[rows, :] = x
        g_held[rows, :] = g
        gate, up, act, sig = ffn_parts(x, gate_ref, up_ref)
        hidden = (act * up).astype(BF16)
        hidden_ref[rows, :] = hidden
        if both:
            own = lax.axis_index("zl") * 2 + lax.axis_index("core")
            outs[4][...] = (
                mm(hidden, down_ref[...], NT) + jnp.where(at == own, residual_ref[...], 0.0)
            ).astype(BF16)
        dhidden = mm(g, down_ref[...])
        dgate = (dhidden * up * (sig * (1.0 + gate * (1.0 - sig)))).astype(BF16)
        dup = (dhidden * act).astype(BF16)
        low_gate[rows, :] = dgate
        low_up[rows, :] = dup
        part_ref[...] = (mm(dgate, gate_ref[...], NT) + mm(dup, up_ref[...], NT)).astype(BF16)

    @pl.when(at >= chunks)
    def _():
        columns = pl.ds(pl.multiple_of((at - chunks) * CHUNK, CHUNK), CHUNK)
        dgate_ref[...] = mm(x_held[:, columns], low_gate[...], TN).astype(BF16)
        dup_ref[...] = mm(x_held[:, columns], low_up[...], TN).astype(BF16)
        ddown_ref[...] = mm(g_held[:, columns], hidden_ref[...], TN).astype(BF16)

    end_jobs(jobs, at, steps)


def ffn_backward(x, g, weights, jobs, number, residual=None):
    both = residual is not None
    length, width = x.shape
    chunks = length // CHUNK
    units = weights[0].shape[1]
    assert length == width and (not both or residual.shape[0] == CHUNK)
    rows = pl.BlockSpec((CHUNK, width), lambda i: (jnp.minimum(i, chunks - 1), 0))
    late = pl.BlockSpec((CHUNK, units), lambda i: (jnp.maximum(i - chunks, 0), 0))
    out = lambda cols: jax.ShapeDtypeStruct((length, cols), BF16)
    return carry_call(
        functools.partial(ffn_backward_kernel, both), jobs, (2 * chunks,),
        [rows, rows] + [whole(weight.shape) for weight in weights] + [whole((CHUNK, width))] * both,
        [rows] + [late] * 3 + [rows] * both,
        [out(width)] + [out(units)] * 3 + [out(width)] * both,
        [pltpu.VMEM((length, units), BF16)] * 3 + [pltpu.VMEM((length, width), BF16)] * 2,
        (x, g, *weights) + ((residual,) if both else ()), number, "ffn_backward", 12 * 10**9,
    )


def row_major(x):
    return with_layout_constraint(x, Layout(major_to_minor=tuple(range(x.ndim))))


def linear(sizes, index):
    place = 0
    for size, at in zip(sizes, index):
        place = place * size + at
    return place


class Roles:
    def __init__(self):
        self.sizes = tuple(lax.axis_size(name) for name in AXES)
        self.chips, self.cores, self.zps, self.zls = self.sizes
        assert self.cores == 2 and self.zps == 2 and self.zls == 2

    def every(self):
        for chip in range(self.chips):
            for core in range(2):
                for zp in range(2):
                    for zl in range(2):
                        yield chip, core, zp, zl

    def rows_pairs(self):
        pairs = []
        for chip, core, zp, zl in self.every():
            slot, part = chip * 2 + zp, zl * 2 + core
            source = linear(self.sizes, (slot // 2, slot % 2, part // 2, part % 2))
            pairs.append((source, linear(self.sizes, (chip, core, zp, zl))))
        return pairs

    def weight_pairs(self, which):
        pairs = []
        for chip, core, zp, zl in self.every():
            head = zp * 2 + zl
            to = (chip, head % 2, core ^ which, head // 2)
            pairs.append(
                (linear(self.sizes, (chip, core, zp, zl)), linear(self.sizes, to))
            )
        return pairs


def flipped(pairs):
    return [(b, a) for a, b in pairs]


def chip_gather(ordered):
    return lax.all_gather(ordered, "chip", axis=0, tiled=True)


def to_plane(pack, roles):
    halves = [lax.ppermute(pack, AXES, roles.weight_pairs(which)) for which in range(2)]
    swap = lax.axis_index("zp") == 1
    return jnp.concatenate(
        [jnp.where(swap, halves[1], halves[0]), jnp.where(swap, halves[0], halves[1])], axis=0
    )


def summed(parts, kind):
    return jnp.sum(parts.astype(F32), axis=0).astype(kind)


def deal(values, order):
    spread = lax.all_to_all(values, ("chip", "core"), split_axis=2, concat_axis=1, tiled=True)
    picked = jnp.take(spread, order, axis=1)
    return lax.all_to_all(picked, ("chip", "core"), split_axis=1, concat_axis=2, tiled=True)


def shards(
    tokens, lengths, order, norm_mix, w_query, w_key, w_value, w_gate, w_decay, conv_filter,
    log_rate, step_bias, norm_heads, w_out, norm_ffn, w_ffn_gate, w_ffn_up, w_ffn_down, cotangent,
):
    roles = Roles()
    layer_count = w_query.shape[0]
    assert layer_count == 2
    heads_total = log_rate.shape[1]
    chip, core, zp, zl = (lax.axis_index(name) for name in AXES)
    head = zl * 2 + core
    rows_local, slots_local, width = tokens.shape
    assert slots_local == 1 and w_decay.shape[2] == 1
    slot_total = order.shape[0]
    units = w_ffn_gate.shape[2]
    rows_part = w_query.shape[1]
    to_roles = roles.rows_pairs()

    def carry(*jobs):
        return Jobs(list(jobs), roles.chips)

    scalars = (log_rate, step_bias)
    kernel_deal = rows_local % (16 * slot_total) == 0
    if kernel_deal:
        turned = lambda w: w.transpose(0, 2, 1)
        raw = (
            w_query, w_key, w_value, w_gate, turned(w_decay[:, :, 0, :]), conv_filter[:, :, 0, :],
            w_out, turned(w_ffn_gate), turned(w_ffn_up), w_ffn_down,
        )
        (residual, rows_in, start, qkv_next, side_next, out_next, gate_next, up_first, up_next,
         down_first, down_next, qkv0, side0, _, _, out_wide, gate_wide) = deal_and_gather(
            order, lengths, tokens[:, 0, :], norm_mix, cotangent[:, 0, :], raw, roles.chips, 1
        )
    else:
        packs = []
        for layer in range(layer_count):
            aux = jnp.concatenate([w_decay[layer, :, 0, :], conv_filter[layer, :, 0, :].T], axis=1)
            aux = jnp.pad(aux, ((0, 0), (0, LANES - aux.shape[1])))
            packs.append(
                [
                    row_major(pack) for pack in (
                        jnp.concatenate([w_query[layer], w_key[layer], w_value[layer]], axis=1),
                        jnp.concatenate([w_gate[layer], aux], axis=1),
                        w_out[layer].T, w_ffn_gate[layer], w_ffn_up[layer], w_ffn_down[layer].T,
                    )
                ]
            )
        (qkv0, side0, out_wide, gate_wide, up_first, down_first) = packs[0]
        (qkv_next, side_next, out_next, gate_next, up_next, down_next) = packs[1]
        positions = (zp * 2 + zl) * rows_local + jnp.arange(rows_local)
        start = cotangent[:, 0, :] * (positions < lengths[order[chip * 2 + core]]).astype(BF16)[:, None]
        residual = lax.ppermute(deal(tokens, order)[:, 0, :], AXES, to_roles)
        (rows_in,), _ = first_gather(residual, norm_mix, 0, carry(), 1)
        qkv0, side0 = (chip_gather(to_plane(pack, roles)) for pack in (qkv0, side0))
        out_wide, gate_wide = (to_plane(pack, roles) for pack in (out_wide, gate_wide))

    (heads0, *kept0), (out0, gate0, up_wide, down_wide, qkv_wide) = mixer_forward(
        0, rows_in, qkv0, side0, norm_heads, scalars,
        carry((Spread, out_wide), (Spread, gate_wide), (ToPlane, up_first), (ToPlane, down_first),
              (ToPlane, qkv_next)),
        2,
    )
    rows_in0, residual0 = rows_in, residual
    (middle0, rows_ffn0), (up0, down0, side_wide, gradient) = mixer_bridge(
        heads0, out0, residual0, norm_ffn, 0,
        carry((Spread, up_wide), (Spread, down_wide), (ToPlane, side_next), (ToRole, start)), 3,
    )
    ffn0 = (gate0, up0, down0)
    (part,), _ = ffn_forward(rows_ffn0, ffn0, carry(), None)
    (residual1, rows_in1), (qkv1, side1, out_wide, down_wide) = forward_bridge(
        part, middle0, norm_mix, 1,
        carry((Spread, qkv_wide), (Spread, side_wide), (ToPlane, out_next), (ToPlane, down_next)), 4,
    )
    (heads1, *kept1), (out1, down1, gate_wide, up_wide, grad_rows) = mixer_forward(
        1, rows_in1, qkv1, side1, norm_heads, scalars,
        carry((Spread, out_wide), (Spread, down_wide), (ToPlane, gate_next), (ToPlane, up_next),
              (Share, gradient)),
        5,
    )
    (middle1, rows_ffn1), (gate1, up1) = mixer_bridge(
        heads1, out1, residual1, norm_ffn, 1, carry((Spread, gate_wide), (Spread, up_wide)), 6
    )
    ffn1 = (gate1, up1, down1)
    (part, dgate1, dup1, ddown1, part_out), _ = ffn_backward(
        rows_ffn1, grad_rows, ffn1, carry(), None, residual=middle1
    )

    (gradient, grad_rows, dgain_ffn1, dout1), (dgate1, dup1) = backward_bridge(
        part, middle1, norm_ffn, 1, gradient, carry((Reduce, dgate1), (Reduce, dup1)), 7, heads1
    )
    (part, din1, daux1, dgain1, dscalars1), jobs_results = mixer_backward(
        1, grad_rows, rows_in1, qkv1, side1, out1, norm_heads, scalars, kept1,
        carry((Reduce, ddown1), (Reduce, dout1), (FromPlane, dgate1), (FromPlane, dup1),
              (ShareSum, part_out)),
        8,
    )
    ddown1, dout1, gate_home1, up_home1, mixed = jobs_results
    (gradient, grad_rows, dgain_mix1), (din1, daux1, mixed) = backward_bridge(
        part, residual1, norm_mix, 1, gradient,
        carry((Reduce, din1), (Reduce, daux1), (FromRole, mixed)), 9,
    )
    (part, dgate0, dup0, ddown0), (in_home1, aux_home1) = ffn_backward(
        rows_ffn0, grad_rows, ffn0, carry((FromPlane, din1), (FromPlane, daux1)), 14,
    )
    (gradient, grad_rows, dgain_ffn0, dout0), (dgate0, dup0) = backward_bridge(
        part, middle0, norm_ffn, 0, gradient, carry((Reduce, dgate0), (Reduce, dup0)), 10, heads0
    )
    (part, din0, daux0, dgain0, dscalars0), jobs_results = mixer_backward(
        0, grad_rows, rows_in0, qkv0, side0, out0, norm_heads, scalars, kept0,
        carry((Reduce, ddown0), (Reduce, dout0), (FromPlane, dgate0), (FromPlane, dup0),
              (FromPlane, ddown1), (FromPlane, dout1)),
        11,
    )
    ddown0, dout0, gate_home0, up_home0, down_home1, out_home1 = jobs_results
    terms = (dgain_mix1, dgain_ffn0, dgain_ffn1, dgain0, dgain1, dscalars0, dscalars1)
    last = (din0, daux0)
    last_jobs = carry((FromPlane, ddown0), (FromPlane, dout0))
    if kernel_deal:
        (home, flat, *last), results = final_step(
            order, part, residual0, norm_mix, gradient, terms, last, roles.chips, last_jobs, 12
        )
    else:
        (gradient, dgain_mix), results = backward_last(
            part, residual0, norm_mix, 0, gradient, last_jobs, 12
        )
        mine = (jnp.arange(heads_total) == head).astype(F32)
        flat = jnp.concatenate(
            [dgain_mix[0], *(term[0] for term in terms[:5])]
            + [mine * term[row, 0] for row in range(2) for term in terms[5:]]
        )
        flat = jnp.pad(flat, (0, small_rows(width) * LANES - flat.shape[0])).reshape(-1, LANES)
        flat = lax.psum(flat, AXES)
        dealt_grad = lax.ppermute(gradient, AXES, flipped(to_roles))
        places = jnp.arange(slot_total, dtype=jnp.int32)
        inverse = jnp.sum(jnp.where(order[None, :] == places[:, None], places[None, :], 0), axis=1)
        home = deal(dealt_grad[:, None, :], inverse)[:, 0, :]
        last = only_jobs(carry(*[(Reduce, a) for a in last]), 13)
        last = only_jobs(carry(*[(FromPlane, a) for a in last]), 15)
    down_home0, out_home0 = results
    in_home0, aux_home0 = last
    first = (in_home0, aux_home0, out_home0, gate_home0, up_home0, down_home0)
    second = (in_home1, aux_home1, out_home1, gate_home1, up_home1, down_home1)
    if rows_part % LANES == 0:
        outs = weights_out(flat, home, first, second, heads_total)
    else:
        flat = flat.reshape(-1)
        small, at = [], 0
        for size in (width, width, VAL, heads_total, heads_total):
            small.append(flat[at : at + layer_count * size].reshape(layer_count, size))
            at += layer_count * size
        proj, aux, out, gate, up, down = (
            jnp.stack([summed(a, F32), summed(b, F32)]) for a, b in zip(first, second)
        )
        turned = lambda a: a.transpose(0, 2, 1)
        outs = [
            proj[:, :, :KEY], proj[:, :, KEY : 2 * KEY], proj[:, :, 2 * KEY : CONV_CH],
            proj[:, :, CONV_CH:], turned(aux)[:, :2], turned(out), turned(gate), turned(up),
            turned(down), *small, turned(aux)[:, 2:6], home.astype(F32)[:, None, :],
        ]
    return (
        mixed[:, None, :],
        outs[15],
        outs[9],
        outs[0], outs[1], outs[2], outs[3],
        outs[4].transpose(0, 2, 1)[:, :, None, :],
        outs[14][:, :, None, :],
        outs[12],
        outs[13],
        outs[11],
        outs[5],
        outs[10],
        outs[6].transpose(0, 2, 1), outs[7].transpose(0, 2, 1), outs[8],
    )


def solution(mesh):
    dp, tensor = mesh.devices.shape
    mesh = Mesh(mesh.devices.reshape(dp // 2, 2, tensor // 2, 2), AXES)
    d, t = ("chip", "core"), ("zp", "zl")
    rows = P(t, d, None)
    by_rows, by_columns = P(None, d, t), P(None, t, d)
    heads, filters = P(None, d, t, None), P(None, None, t, d)
    return jax.shard_map(
        shards,
        mesh=mesh,
        in_specs=(
            rows, P(), P(), P(), by_rows, by_rows, by_rows, by_rows, heads, filters,
            P(), P(), P(), by_columns, P(), by_rows, by_rows, by_columns, rows,
        ),
        out_specs=(
            rows, rows, P(), by_rows, by_rows, by_rows, by_rows, heads, filters,
            P(), P(), P(), by_columns, P(), by_rows, by_rows, by_columns,
        ),
        check_vma=False,
    )
```

```python
import functools
import jax
import jax.numpy as jnp
from jax import lax
from jax.experimental import pallas as pl
from jax.experimental.layout import Layout, with_layout_constraint
from jax.experimental.pallas import tpu as pltpu
from jax.sharding import Mesh, PartitionSpec as P

CHUNK = 256
LANES = 128
KEY = 256
VAL = 512
CONV_CH = 2 * KEY + VAL
F32 = jnp.float32
BF16 = jnp.bfloat16
NN = (((1,), (0,)), ((), ()))
NT = (((1,), (1,)), ((), ()))
TN = (((0,), (0,)), ((), ()))


def mm(a, b, dims=NN):
    return lax.dot_general(
        a.astype(BF16), b.astype(BF16), dims, preferred_element_type=F32
    )


def split_low(a):
    high = a.astype(BF16)
    return high, (a - high.astype(F32)).astype(BF16)


def mm3(a, b, dims=NN):
    a_high, a_low = split_low(a)
    b_high, b_low = split_low(b)
    dot = functools.partial(
        lax.dot_general, dimension_numbers=dims, preferred_element_type=F32
    )
    return dot(a_high, b_high) + (dot(a_high, b_low) + dot(a_low, b_high))


def mm_exact_left(a, b, dims=NN):
    a = a.astype(BF16)
    high = b.astype(BF16)
    rest = b - high.astype(F32)
    mid = rest.astype(BF16)
    low = (rest - mid.astype(F32)).astype(BF16)
    dot = functools.partial(
        lax.dot_general, dimension_numbers=dims, preferred_element_type=F32
    )
    return dot(a, high) + (dot(a, mid) + dot(a, low))


def iotas():
    rows = lax.broadcasted_iota(jnp.int32, (CHUNK, CHUNK), 0)
    cols = lax.broadcasted_iota(jnp.int32, (CHUNK, CHUNK), 1)
    return rows, cols


def wide(col_block, width):
    return jnp.concatenate([col_block] * (width // LANES), axis=1)


def rates_of(rates, rate, bias):
    write = jax.nn.sigmoid(jnp.broadcast_to(rates[:, 0:1], (CHUNK, LANES)))
    logit = jnp.broadcast_to(rates[:, 1:2], (CHUNK, LANES)) + bias
    soft = jnp.maximum(logit, 0.0) + jnp.log1p(jnp.exp(-jnp.abs(logit)))
    return write, -rate * soft, jax.nn.sigmoid(logit)


def head_scalars(scalars_ref, layer):
    head = lax.axis_index("zl") * 2 + lax.axis_index("core")
    rate_ref, bias_ref = scalars_ref
    here = lax.broadcasted_iota(jnp.int32, (1, rate_ref.shape[1]), 1) == head
    pick = lambda ref: jnp.sum(
        jnp.where(here, ref[layer : layer + 1, :].astype(F32), 0.0), axis=1, keepdims=True
    )
    return jnp.exp(pick(rate_ref)), pick(bias_ref)


def decay_terms(step, rows, cols):
    inclusive = (rows >= cols).astype(BF16)
    total = mm_exact_left(inclusive, step)
    spread = wide(total, CHUNK) - jnp.concatenate([total.T] * (CHUNK // LANES), axis=0)
    decay = jnp.where(rows >= cols, jnp.exp(jnp.minimum(spread, 0.0)), 0.0)
    last = jnp.broadcast_to(total[CHUNK - 1 : CHUNK, :], (CHUNK, LANES))
    return decay, jnp.exp(total), jnp.exp(last - total), jnp.exp(last)


def solve_unit(coupling, rows, cols):
    unit = jnp.where(rows == cols, 1.0, 0.0)
    same = ((rows >> 1) == (cols >> 1)) & (rows != cols)
    inverse = unit - jnp.where(same, coupling, 0.0)
    for level in range(1, CHUNK.bit_length() - 1):
        between = ((rows >> (level + 1)) == (cols >> (level + 1))) & (
            (rows >> level) != (cols >> level)
        )
        part = jnp.where(between, coupling, 0.0)
        inverse = inverse - mm(mm(inverse, part), inverse)
    return inverse + mm(inverse, unit - inverse - mm3(coupling, inverse))


def silu_of(x):
    gate = jax.nn.sigmoid(x)
    return x * gate, gate


def conv_rows(padded_ref, taps_ref, start):
    result = padded_ref[pl.ds(start, CHUNK), :] * taps_ref[0:1, :]
    for j in range(1, 4):
        result = result + padded_ref[pl.ds(start + j, CHUNK), :] * taps_ref[j : j + 1, :]
    return result


def forward_kernel(
    layer, jobs, rate_ref, bias_ref, x_ref, w_qkv_ref, w_gate_ref, w_aux_ref, gain_ref,
    heads_ref, proj_ref, conv_ref, gate_ref, rates_ref, inverse_ref, fresh_ref, o_ref, state_ref,
    padded, memory, taps_ref,
):
    begin_jobs(jobs, pl.program_id(0), pl.num_programs(0))
    @pl.when(pl.program_id(0) == 0)
    def _():
        memory[...] = jnp.zeros_like(memory)
        taps_ref[...] = w_aux_ref[...].astype(F32).T[2:6, :]
        padded[0:8, :] = jnp.zeros((8, CONV_CH), F32)

    x = x_ref[...]
    rates = mm(x, w_aux_ref[...])
    rates_ref[...] = rates
    qkv = mm(x, w_qkv_ref[...])
    proj_ref[...] = qkv
    gate_in = mm(x, w_gate_ref[...])
    gate_ref[...] = gate_in
    padded[8 : 8 + CHUNK, :] = qkv
    conv = conv_rows(padded, taps_ref, 5)
    padded[0:8, :] = qkv[CHUNK - 8 :, :]
    conv_ref[...] = conv
    act, _ = silu_of(conv)
    q, k, v = act[:, :KEY], act[:, KEY : 2 * KEY], act[:, 2 * KEY :]
    q = q * (lax.rsqrt(jnp.sum(q * q, axis=1, keepdims=True) + 1e-6) * KEY**-0.5)
    k = k * lax.rsqrt(jnp.sum(k * k, axis=1, keepdims=True) + 1e-6)
    rows, cols = iotas()
    write, step, _ = rates_of(rates, *head_scalars((rate_ref, bias_ref), layer))
    decay, growth, rest, final = decay_terms(step, rows, cols)
    coupling = jnp.where(rows > cols, wide(write, CHUNK) * mm3(k, k, NT) * decay, 0.0)
    inverse = solve_unit(coupling, rows, cols)
    inverse_ref[...] = inverse.astype(BF16)
    within = mm(q, k, NT) * decay
    state = memory[...]
    state_ref[...] = state
    low_state = state.astype(BF16)
    source = wide(write, VAL) * (v - wide(growth, VAL) * mm(k, low_state))
    fresh = mm3(inverse, source)
    fresh_ref[...] = fresh
    o = wide(growth, VAL) * mm(q, low_state) + mm(within, fresh)
    o_ref[...] = o
    memory[...] = wide(final, VAL) * state + mm(k * wide(rest, KEY), fresh, TN)
    scaled = o * lax.rsqrt(jnp.mean(o * o, axis=1, keepdims=True) + 1e-5) * gain_ref[layer : layer + 1, :].astype(F32)
    heads = (scaled * silu_of(gate_in)[0]).astype(BF16)
    heads_ref[...] = heads
    end_jobs(jobs, pl.program_id(0), pl.num_programs(0))


def head_spec(value):
    return pl.BlockSpec(value.shape, lambda i: (0, 0))


def weight_specs(width):
    fixed = lambda shape, at: pl.BlockSpec(shape, lambda i: (0, at), pipeline_mode=pl.Buffered(1))
    return [
        fixed((width, CONV_CH), 0),
        fixed((width, VAL), 0),
        fixed((width, LANES), VAL // LANES),
        fixed((2, VAL), 0),
    ]


def mixer_forward(layer, x, qkv, pack, gain, scalars, jobs, number):
    length, width = x.shape
    chunks = length // CHUNK
    row = lambda cols: pl.BlockSpec((CHUNK, cols), lambda i: (i, 0))
    out = lambda cols, kind: jax.ShapeDtypeStruct((length, cols), kind)
    return carry_call(
        functools.partial(forward_kernel, layer), jobs, (chunks,),
        [head_spec(scalars[0]), head_spec(scalars[1]), row(width)] + weight_specs(width),
        [
            row(VAL), row(CONV_CH), row(CONV_CH), row(VAL), row(LANES), row(CHUNK), row(VAL), row(VAL),
            pl.BlockSpec((None, KEY, VAL), lambda i: (i, 0, 0)),
        ],
        [
            out(VAL, BF16), out(CONV_CH, F32), out(CONV_CH, F32), out(VAL, F32), out(LANES, F32),
            out(CHUNK, BF16), out(VAL, F32), out(VAL, F32),
            jax.ShapeDtypeStruct((chunks, KEY, VAL), F32),
        ],
        [
            pltpu.VMEM((CHUNK + 8, CONV_CH), F32), pltpu.VMEM((KEY, VAL), F32),
            pltpu.VMEM((4, CONV_CH), F32),
        ],
        (*scalars, x, qkv, pack, pack, gain), number, "mixer_forward", 16 * 10**9,
    )


def unit_back(grad, vector, scale):
    inv = lax.rsqrt(jnp.sum(vector * vector, axis=1, keepdims=True) + 1e-6)
    dot = jnp.sum(grad * vector, axis=1, keepdims=True)
    return (grad - vector * (inv * inv * dot)) * (inv * scale)


def backward_kernel(
    layer, jobs, rate_ref, bias_ref, g_ref, x_ref, w_out_ref, w_qkv_ref, w_gate_ref, w_aux_ref, gain_ref,
    proj_ref, halo_ref, conv_ref, gate_ref, rates_ref, inverse_ref, fresh_ref, o_ref, state_ref,
    part_ref, din_ref, daux_ref, dgain_ref, dscalars_ref,
    padded, dpadded, dmemory, taps_ref, dtaps_ref, daux_sum, x_held, dproj_ref,
):
    at, steps = pl.program_id(0), pl.num_programs(0)
    chunks = steps // 2
    last = chunks - 1
    begin_jobs(jobs, at, steps, (chunks // 2, chunks - 1))

    @pl.when(at == 0)
    def _():
        dmemory[...] = jnp.zeros_like(dmemory)
        taps_ref[...] = w_aux_ref[...].astype(F32).T[2:6, :]
        dpadded[CHUNK : CHUNK + 8, :] = jnp.zeros((8, CONV_CH), F32)
        dtaps_ref[...] = jnp.zeros_like(dtaps_ref)
        daux_sum[...] = jnp.zeros_like(daux_sum)
        dgain_ref[...] = jnp.zeros_like(dgain_ref)
        dscalars_ref[...] = jnp.zeros_like(dscalars_ref)

    @pl.when(at < chunks)
    def _():
        rows, cols = iotas()
        padded[8 : 8 + CHUNK, :] = proj_ref[...]
        padded[0:8, :] = jnp.where(at == last, 0.0, halo_ref[...])
        conv = conv_ref[...]
        act, sig = silu_of(conv)
        act_q, act_k, v = act[:, :KEY], act[:, KEY : 2 * KEY], act[:, 2 * KEY :]
        q = act_q * (lax.rsqrt(jnp.sum(act_q * act_q, axis=1, keepdims=True) + 1e-6) * KEY**-0.5)
        k = act_k * lax.rsqrt(jnp.sum(act_k * act_k, axis=1, keepdims=True) + 1e-6)
        rates = rates_ref[...]
        write, step, sig_decay = rates_of(rates, *head_scalars((rate_ref, bias_ref), layer))
        decay, growth, rest, final = decay_terms(step, rows, cols)
        growth_v = wide(growth, VAL)
        write_v = wide(write, VAL)
        low_q, low_k = q.astype(BF16), k.astype(BF16)
        below = rows > cols
        strict_decay = jnp.where(below, decay, 0.0)
        keys = mm(low_k, low_k, NT) * strict_decay * wide(write, CHUNK)
        within = mm(low_q, low_k, NT) * decay
        dheads = mm(g_ref[...], w_out_ref[...])
        o = o_ref[...]
        gate_in = gate_ref[...]
        gate, gate_sig = silu_of(gate_in)
        inv = lax.rsqrt(jnp.mean(o * o, axis=1, keepdims=True) + 1e-5)
        normal = o * inv
        gain = gain_ref[layer : layer + 1, :].astype(F32)
        dgate = dheads * normal * gain * (gate_sig * (1.0 + gate_in * (1.0 - gate_sig)))
        dscaled = dheads * gate
        dgain_ref[...] += jnp.sum(dscaled * normal, axis=0, keepdims=True)
        dnormal = dscaled * gain
        do = inv * (dnormal - normal * jnp.mean(dnormal * normal, axis=1, keepdims=True))
        state = state_ref[...]
        low_state = state.astype(BF16)
        fresh = fresh_ref[...]
        low_fresh = fresh.astype(BF16)
        dstate = dmemory[...]
        low_dstate = dstate.astype(BF16)
        low_do = do.astype(BF16)
        k_rest = k * wide(rest, KEY)
        rest_dstate = mm(k_rest, low_dstate)
        dfresh = mm(within, low_do, TN) + rest_dstate
        dsource = mm(inverse_ref[...], dfresh, TN)
        low_dsource = dsource.astype(BF16)
        dv = write_v * dsource
        dread = -(growth_v * dv)
        low_dread = dread.astype(BF16)
        do_growth = growth_v * do
        low_do_growth = do_growth.astype(BF16)
        dwithin = mm(low_do, low_fresh, NT)
        dcoupling = -mm(low_dsource, low_fresh, NT)
        dkeys = dcoupling * strict_decay * wide(write, CHUNK)
        dpairs = dwithin * decay
        dq = mm(low_do_growth, low_state, NT) + mm(dpairs, low_k)
        dk = (
            mm(low_dread, low_state, NT)
            + mm(dpairs, low_q, TN)
            + mm(dkeys + dkeys.T, low_k)
            + wide(rest, KEY) * mm(low_fresh, low_dstate, NT)
        )
        dmemory[...] = (
            wide(final, VAL) * dstate + mm(low_q, low_do_growth, TN) + mm(low_k, low_dread, TN)
        )
        spread = dwithin * within + dcoupling * keys
        straddle = jnp.where(below, mm_exact_left((rows <= cols).astype(BF16), spread), 0.0)
        read_rows = jnp.sum(
            do_growth * mm(low_q, low_state) + dread * mm(low_k, low_state), axis=1, keepdims=True
        )
        rest_rows = jnp.sum(fresh * rest_dstate, axis=1, keepdims=True)
        carried = jnp.sum(dstate * state) * final[0:1, 0:1]
        suffix = mm_exact_left(
            (rows <= cols).astype(BF16), jnp.broadcast_to(read_rows, (CHUNK, LANES))
        ) + mm_exact_left((rows > cols).astype(BF16), jnp.broadcast_to(rest_rows, (CHUNK, LANES)))
        dstep = suffix + jnp.sum(straddle, axis=1, keepdims=True) + carried
        dlogit = dstep * (-head_scalars((rate_ref, bias_ref), layer)[0]) * sig_decay
        dwrite = (1.0 - write) * jnp.sum(dsource * fresh, axis=1, keepdims=True)
        lane = lax.broadcasted_iota(jnp.int32, (CHUNK, LANES), 1)
        drates = jnp.where(lane == 0, dwrite, jnp.where(lane == 1, dlogit, 0.0))
        low_drates = drates.astype(BF16)
        daux_sum[...] += mm(low_drates, x_ref[...], TN)
        dscalars_ref[0:1, :] += jnp.sum(dstep * step, axis=0, keepdims=True)
        dscalars_ref[1:2, :] += jnp.sum(dlogit, axis=0, keepdims=True)
        dact = jnp.concatenate(
            [unit_back(dq, act_q, KEY**-0.5), unit_back(dk, act_k, 1.0), dv], axis=1
        )
        dconv = dact * (sig * (1.0 + conv * (1.0 - sig)))
        dpadded[0:CHUNK, :] = dconv
        dtaps_ref[2:6, :] += jnp.concatenate(
            [
                jnp.sum(dconv * padded[5 + j : 5 + j + CHUNK, :], axis=0, keepdims=True)
                for j in range(4)
            ],
            axis=0,
        )
        dqkv = dconv * taps_ref[3:4, :]
        for j in range(3):
            dqkv = dqkv + dpadded[pl.ds(3 - j, CHUNK), :] * taps_ref[j : j + 1, :]
        dpadded[CHUNK : CHUNK + 8, :] = dconv[0:8, :]
        low_dqkv, low_dgate = dqkv.astype(BF16), dgate.astype(BF16)
        place = block(last - at, CHUNK)
        dproj_ref[place, :CONV_CH] = low_dqkv
        dproj_ref[place, CONV_CH:] = low_dgate
        x_held[place, :] = x_ref[...]
        part_ref[...] = (
            mm(low_dqkv, w_qkv_ref[...], NT)
            + mm(low_dgate, w_gate_ref[...], NT)
            + mm(low_drates, w_aux_ref[...], NT)
        ).astype(BF16)

    @pl.when(at == last)
    def _():
        daux_ref[...] = (daux_sum[...] + dtaps_ref[...]).T.astype(BF16)

    @pl.when(at >= chunks)
    def _():
        columns = block(at - chunks, CHUNK)
        din_ref[...] = mm(x_held[:, columns], dproj_ref[...], TN).astype(BF16)

    end_jobs(jobs, at, steps)


def mixer_backward(layer, g, x, qkv, pack, w_out, gain, scalars, saved, jobs, number):
    proj, conv, gate_in, rates, inverse, fresh, o, states = saved
    length, width = g.shape
    chunks = length // CHUNK
    back = chunks - 1
    at = lambda i: jnp.maximum(back - i, 0)
    row = lambda cols: pl.BlockSpec((CHUNK, cols), lambda i: (at(i), 0))
    out = lambda cols, kind: jax.ShapeDtypeStruct((length, cols), kind)
    steps = CHUNK // 8
    return carry_call(
        functools.partial(backward_kernel, layer), jobs, (2 * chunks,),
        [head_spec(scalars[0]), head_spec(scalars[1]), row(width), row(width), whole(w_out.shape)]
        + weight_specs(width) + [
            row(CONV_CH),
            pl.BlockSpec((8, CONV_CH), lambda i: (jnp.maximum(at(i) * steps - 1, 0), 0)),
            row(CONV_CH), row(VAL), row(LANES), row(CHUNK), row(VAL), row(VAL),
            pl.BlockSpec((None, KEY, VAL), lambda i: (at(i), 0, 0)),
        ],
        [
            row(width),
            pl.BlockSpec((CHUNK, CONV_CH + VAL), lambda i: (jnp.maximum(i - chunks, 0), 0)),
            pl.BlockSpec((width, LANES), lambda i: (0, 0)),
            pl.BlockSpec((1, VAL), lambda i: (0, 0)),
            pl.BlockSpec((8, LANES), lambda i: (0, 0)),
        ],
        [
            out(width, BF16), jax.ShapeDtypeStruct((width, CONV_CH + VAL), BF16),
            jax.ShapeDtypeStruct((width, LANES), BF16),
            jax.ShapeDtypeStruct((1, VAL), F32),
            jax.ShapeDtypeStruct((8, LANES), F32),
        ],
        [
            pltpu.VMEM((CHUNK + 8, CONV_CH), F32),
            pltpu.VMEM((CHUNK + 8, CONV_CH), F32),
            pltpu.VMEM((KEY, VAL), F32),
            pltpu.VMEM((4, CONV_CH), F32),
            pltpu.VMEM((LANES, CONV_CH), F32),
            pltpu.VMEM((LANES, width), F32),
            pltpu.VMEM((length, width), BF16),
            pltpu.VMEM((length, CONV_CH + VAL), BF16),
        ],
        (*scalars, g, x, w_out, qkv, pack, pack, gain, proj, proj, conv, gate_in, rates, inverse, fresh, o,
         states),
        number, "mixer_backward", 16 * 10**9,
    )


PIECES = 4
TURN = (1, 2)
AXES = ("chip", "core", "zp", "zl")


def partners():
    core, zl = lax.axis_index("core"), lax.axis_index("zl")
    return core, zl, {"core": 1 - core}, {"zl": 1 - zl}


def remote(src, dst, send, recv, device):
    return pltpu.make_async_remote_copy(
        src_ref=src, dst_ref=dst, send_sem=send, recv_sem=recv,
        device_id=device, device_id_type=pl.DeviceIdType.MESH,
    )


class Block:
    def __init__(self, zl, core, rows):
        self.first = (zl * 2 + core) * rows
        self.size = rows // PIECES

    def piece(self, p):
        return pl.ds(pl.multiple_of(self.first + p * self.size, self.size), self.size)

    def rows(self):
        rows = self.size * PIECES
        return pl.ds(pl.multiple_of(self.first, rows), rows)


class Scatter:
    def __init__(self, partial, beside_far, beside_own, sums, far, send, recv):
        core, zl, beside, across = partners()
        rows = far.shape[0]
        self.partial, self.beside_far, self.beside_own = partial, beside_far, beside_own
        self.sums, self.far = sums, far
        self.size = rows // PIECES
        self.own = Block(zl, core, rows)
        self.away = Block(1 - zl, core, rows)
        own_beside, away_beside = Block(zl, 1 - core, rows), Block(1 - zl, 1 - core, rows)
        self.to_far = [
            remote(partial.at[away_beside.piece(p)], beside_far.at[self.local(p)],
                   send.at[0, p], recv.at[0, p], beside)
            for p in range(PIECES)
        ]
        self.to_own = [
            remote(partial.at[own_beside.piece(p)], beside_own.at[self.local(p)],
                   send.at[1, p], recv.at[1, p], beside)
            for p in range(PIECES)
        ]
        self.cross = [
            remote(sums.at[self.local(p)], far.at[self.local(p)],
                   send.at[2, p], recv.at[2, p], across)
            for p in range(PIECES)
        ]

    def local(self, p):
        return pl.ds(p * self.size, self.size)

    def start(self):
        for copy in self.to_far:
            copy.start()
        for copy in self.to_own:
            copy.start()
        for p in range(PIECES):
            self.to_far[p].wait_recv()
            at = self.local(p)
            self.sums[at, :] = (
                self.partial[self.away.piece(p), :].astype(F32) + self.beside_far[at, :].astype(F32)
            ).astype(BF16)
            self.cross[p].start()

    def total(self, p):
        self.to_own[p].wait_recv()
        self.cross[p].wait_recv()
        at = self.local(p)
        return (
            self.partial[self.own.piece(p), :].astype(F32)
            + self.beside_own[at, :].astype(F32)
            + self.far[at, :].astype(F32)
        )

    def finish(self):
        for copies in (self.to_far, self.to_own, self.cross):
            for copy in copies:
                copy.wait_send()


class Exchange:
    def __init__(self, partial, near, sums, far, send, recv):
        core, zl, beside, across = partners()
        rows = far.shape[1]
        self.near, self.sums, self.far = near, sums, far
        self.size = rows // PIECES
        self.blocks = [Block(l, core, rows) for l in range(2)]
        self.others = [Block(l, 1 - core, rows) for l in range(2)]
        self.order = [(l, p) for l in range(2) for p in range(PIECES)]
        self.beside = [
            [
                remote(partial.at[self.others[l].piece(p)], near.at[l, self.local(p)],
                       send.at[l, p], recv.at[l, p], beside)
                for p in range(PIECES)
            ]
            for l in range(2)
        ]
        self.across = [
            [
                remote(sums.at[l, self.local(p)], far.at[l, self.local(p)],
                       send.at[2 + l, p], recv.at[2 + l, p], across)
                for p in range(PIECES)
            ]
            for l in range(2)
        ]

    def local(self, p):
        return pl.ds(p * self.size, self.size)

    def send(self, l):
        for copy in self.beside[l]:
            copy.start()

    def pass_on(self, l, mine):
        for p in range(PIECES):
            self.beside[l][p].wait_recv()
            at = self.local(p)
            self.sums[l, at, :] = (
                mine(l, p).astype(F32) + self.near[l, at, :].astype(F32)
            ).astype(BF16)
            self.across[l][p].start()

    def total(self, l, p):
        self.across[l][p].wait_recv()
        at = self.local(p)
        return self.sums[l, at, :].astype(F32) + self.far[l, at, :].astype(F32)

    def finish(self):
        for l, p in self.order:
            self.beside[l][p].wait_send()
            self.across[l][p].wait_send()


class Sharing:
    def __init__(self, held, out, send, recv, stores):
        core, _, beside, _ = partners()
        rows = held.shape[0] // 4
        self.held = held
        self.blocks = [Block(l, core, rows) for l in range(2)]
        self.copies = [
            [
                remote(held.at[block.piece(p)], held.at[block.piece(p)], send.at[l, p], recv.at[l, p],
                       beside)
                for p in range(PIECES)
            ]
            for l, block in enumerate(self.blocks)
        ]
        others = [Block(l, 1 - core, rows) for l in range(2)]
        self.stores = [
            pltpu.make_async_copy(held.at[block.rows()], out.at[block.rows()], stores.at[at])
            for at, block in enumerate(self.blocks + others)
        ]

    def put(self, l, p, rows):
        self.held[self.blocks[l].piece(p), :] = rows
        self.copies[l][p].start()
        if p == PIECES - 1:
            self.stores[l].start()

    def arrive(self):
        for l in range(2):
            for copy in self.copies[l]:
                copy.wait_recv()
            self.stores[2 + l].start()

    def finish(self):
        for l in range(2):
            for copy in self.copies[l]:
                copy.wait_send()
        for store in self.stores:
            store.wait()


def normed_of(x, gain):
    return x * lax.rsqrt(jnp.mean(x * x, axis=1, keepdims=True) + 1e-6) * gain


def load_all(copies):
    for copy in copies:
        copy.start()


def first_kernel(row, jobs, x_ref, gain_ref, new_ref, out_ref, raw, held, cross_send, cross_recv, send,
                 recv, stores):
    _, zl, _, across = partners()
    wait_greetings(greet_group() + jobs.greet())
    swap = remote(raw.at[zl], raw.at[zl], cross_send.at[0], cross_recv.at[0], across)
    raw[zl] = x_ref[...]
    swap.start()
    jobs.start()
    sharing = Sharing(held, out_ref, send, recv, stores)
    swap.wait()
    size = raw.shape[1] // PIECES
    for l in range(2):
        for p in range(PIECES):
            x = raw[l, p * size : (p + 1) * size, :].astype(F32)
            sharing.put(l, p, normed_of(x, gain_ref[row : row + 1, :].astype(F32)).astype(BF16))
    new_ref[...] = raw[...]
    jobs.middle()
    sharing.arrive()
    sharing.finish()
    jobs.finish()


def forward_bridge_kernel(
    row, jobs, partial, x_ref, gain_ref, new_ref, out_ref, mine, near, sums, far, x, held, send, recv,
    share_send, share_recv, loads, stores
):
    exchange = Exchange(partial, near, sums, far, send, recv)
    sharing = Sharing(held, out_ref, share_send, share_recv, stores)
    own = [
        pltpu.make_async_copy(partial.at[exchange.blocks[l].rows()], mine.at[l], loads.at[l])
        for l in range(2)
    ]
    old = [pltpu.make_async_copy(x_ref.at[l], x.at[l], loads.at[2 + l]) for l in range(2)]
    new = [pltpu.make_async_copy(x.at[l], new_ref.at[l], stores.at[4 + l]) for l in range(2)]
    load_all(own + old)
    wait_greetings(greet_group() + jobs.greet())
    for l in range(2):
        exchange.send(l)
    jobs.start()
    for l in range(2):
        own[l].wait()
        exchange.pass_on(l, lambda l, p: mine[l, exchange.local(p), :])
    forward_rows(row, jobs, exchange, sharing, old, new, x, gain_ref)


def forward_rows(row, jobs, exchange, sharing, old, new, x, gain_ref):
    gain = gain_ref[row : row + 1, :].astype(F32)
    for l in range(2):
        old[l].wait()
        for p in range(PIECES):
            if (l, p) == TURN:
                jobs.middle()
            at = exchange.local(p)
            rows = x[l, at, :] + exchange.total(l, p)
            x[l, at, :] = rows
            sharing.put(l, p, normed_of(rows, gain).astype(BF16))
        new[l].start()
    sharing.arrive()
    exchange.finish()
    sharing.finish()
    for store in new:
        store.wait()
    jobs.finish()


def mixer_bridge_kernel(
    row, jobs, heads_ref, w_out_ref, x_ref, gain_ref, new_ref, out_ref, partial, raw, near, sums, far, x,
    held, send, recv, share_send, share_recv, loads, stores
):
    exchange = Exchange(partial, near, sums, far, send, recv)
    sharing = Sharing(held, out_ref, share_send, share_recv, stores)
    old = [pltpu.make_async_copy(x_ref.at[l], raw.at[l], loads.at[2 + l]) for l in range(2)]
    new = [pltpu.make_async_copy(x.at[l], new_ref.at[l], stores.at[4 + l]) for l in range(2)]
    load_all(old)
    wait_greetings(greet_group() + jobs.greet())

    def make(block):
        rows = block.rows()
        partial[rows, :] = mm(heads_ref[rows, :], w_out_ref[...], NT).astype(BF16)

    for l in range(2):
        make(exchange.others[l])
        exchange.send(l)
    jobs.start()
    for l in range(2):
        make(exchange.blocks[l])
        exchange.pass_on(l, lambda l, p: partial[exchange.blocks[l].piece(p), :])
    for l in range(2):
        old[l].wait()
        if x_ref.dtype != F32:
            x[l] = raw[l].astype(F32)
        old[l] = Done()
    forward_rows(row, jobs, exchange, sharing, old, new, x, gain_ref)


class Done:
    def wait(self):
        pass


def norm_back(total, x, gain):
    inv = lax.rsqrt(jnp.mean(x * x, axis=1, keepdims=True) + 1e-6)
    unit = x * inv
    scaled = total * gain
    grad = inv * (scaled - unit * jnp.mean(scaled * unit, axis=1, keepdims=True))
    return grad, jnp.sum(total * unit, axis=0, keepdims=True)


def backward_bridge_kernel(row, last, jobs, partial, x_ref, gain_ref, grad_ref, *refs):
    if last:
        heads_ref, new_ref, out_ref, dgain_ref, dout_ref, *refs = refs
    else:
        new_ref, out_ref, dgain_ref, *refs = refs
    (mine, near, sums, far, x, grad, new_rows, held, send, recv, share_send, share_recv, loads,
     stores) = refs
    exchange = Exchange(partial, near, sums, far, send, recv)
    sharing = Sharing(held, out_ref, share_send, share_recv, stores)
    zl = lax.axis_index("zl")
    place = lambda ref, l: ref.at[exchange.blocks[l].rows()] if len(ref.shape) == 2 else ref.at[l]
    own, old = [], []
    for l in range(2):
        own.append(
            pltpu.make_async_copy(partial.at[exchange.blocks[l].rows()], mine.at[l], loads.at[l])
        )
        old.append(
            (pltpu.make_async_copy(x_ref.at[l], x.at[l], loads.at[2 + l]),
             pltpu.make_async_copy(place(grad_ref, l), grad.at[l], loads.at[4 + l]))
        )
    new = [pltpu.make_async_copy(new_rows.at[l], new_ref.at[l], stores.at[4 + l]) for l in range(2)]
    load_all(own + [copy for pair in old for copy in pair])
    wait_greetings(greet_group() + jobs.greet())
    for l in range(2):
        exchange.send(l)
    jobs.start()
    for l in range(2):
        own[l].wait()
        exchange.pass_on(l, lambda l, p: mine[l, exchange.local(p), :])
    gain = gain_ref[row : row + 1, :].astype(F32)
    dgain = jnp.zeros(dgain_ref.shape, F32)
    for l in range(2):
        for copy in old[l]:
            copy.wait()
        for p in range(PIECES):
            if (l, p) == TURN:
                jobs.middle()
            at = exchange.local(p)
            rows, part = norm_back(exchange.total(l, p), x[l, at, :].astype(F32), gain)
            dgain = dgain + jnp.where(zl == l, part, 0.0)
            rows = rows + grad[l, at, :].astype(F32)
            new_rows[l, at, :] = rows
            sharing.put(l, p, rows.astype(BF16))
        new[l].start()
    dgain_ref[...] = dgain
    sharing.arrive()
    if last:
        for first in range(0, held.shape[1], 256):
            columns = slice(first, first + 256)
            dout_ref[columns, :] = mm(held[:, columns], heads_ref[...], TN).astype(BF16)
    exchange.finish()
    sharing.finish()
    for store in new:
        store.wait()
    jobs.finish()


def backward_last_kernel(
    row, jobs, partial, x_ref, gain_ref, grad_ref, new_ref, dgain_ref,
    beside_far, beside_own, sums, far, send, recv
):
    wait_greetings(greet_group() + jobs.greet())
    scatter = Scatter(partial, beside_far, beside_own, sums, far, send, recv)
    scatter.start()
    jobs.start()
    zl = lax.axis_index("zl")
    dgain = jnp.zeros(dgain_ref.shape, F32)
    for p in range(PIECES):
        at = scatter.local(p)
        grad, part = norm_back(
            scatter.total(p), x_ref[zl, at, :].astype(F32), gain_ref[row : row + 1, :].astype(F32)
        )
        dgain = dgain + part
        new_ref[at, :] = (grad + grad_ref[zl, at, :]).astype(BF16)
    dgain_ref[...] = dgain
    jobs.middle()
    scatter.finish()
    jobs.finish()


VMEM_SPEC = pl.BlockSpec(memory_space=pltpu.VMEM)
ANY_SPEC = pl.BlockSpec(memory_space=pl.ANY)


def pair_scratch(rows, width, kinds):
    return [pltpu.VMEM((2, rows, width), kind) for kind in kinds]


def bridge_sems():
    many = pltpu.SemaphoreType.DMA((4, PIECES))
    few = pltpu.SemaphoreType.DMA((2, PIECES))
    return [many, many, few, few, pltpu.SemaphoreType.DMA((6,)), pltpu.SemaphoreType.DMA((6,))]


def bridge_shapes(rows, width):
    return [
        jax.ShapeDtypeStruct((2, rows, width), F32),
        jax.ShapeDtypeStruct((4 * rows, width), BF16),
    ]


def first_gather(x, gain, row, jobs, number):
    rows, width = x.shape
    few = pltpu.SemaphoreType.DMA((2, PIECES))
    one = pltpu.SemaphoreType.DMA((1,))
    return carry_call(
        functools.partial(first_kernel, row), jobs, (), [VMEM_SPEC] * 2, [VMEM_SPEC, ANY_SPEC],
        [
            jax.ShapeDtypeStruct((2, rows, width), BF16),
            jax.ShapeDtypeStruct((4 * rows, width), BF16),
        ],
        [pltpu.VMEM((2, rows, width), BF16), pltpu.VMEM((4 * rows, width), BF16), one, one, few, few,
         pltpu.SemaphoreType.DMA((4,))],
        (x, gain), number, "first", rows * width * 20,
    )


def forward_bridge(partial, x, gain, row, jobs, number):
    _, rows, width = x.shape
    return carry_call(
        functools.partial(forward_bridge_kernel, row), jobs, (),
        [ANY_SPEC, ANY_SPEC, VMEM_SPEC], [ANY_SPEC] * 2, bridge_shapes(rows, width),
        pair_scratch(rows, width, [BF16] * 4 + [F32]) + [pltpu.VMEM((4 * rows, width), BF16)]
        + bridge_sems(),
        (partial, x, gain), number, "forward_bridge", rows * width * 20,
    )


def mixer_bridge(heads, w_out, x, gain, row, jobs, number):
    _, rows, width = x.shape
    kernel = functools.partial(
        mixer_bridge_kernel if x.dtype != F32 else mixer_bridge_kernel_f32, row
    )
    raw = pair_scratch(rows, width, [BF16]) if x.dtype != F32 else []
    return carry_call(
        kernel, jobs, (), [VMEM_SPEC, VMEM_SPEC, ANY_SPEC, VMEM_SPEC], [ANY_SPEC] * 2,
        bridge_shapes(rows, width),
        [pltpu.VMEM((4 * rows, width), BF16)] + raw + pair_scratch(rows, width, [BF16] * 3 + [F32])
        + [pltpu.VMEM((4 * rows, width), BF16)] + bridge_sems(),
        (heads, w_out, x, gain), number, "mixer_bridge", 10**9,
    )


def mixer_bridge_kernel_f32(row, jobs, heads_ref, w_out_ref, x_ref, gain_ref, new_ref, out_ref, partial,
                            near, sums, far, x, *refs):
    mixer_bridge_kernel(row, jobs, heads_ref, w_out_ref, x_ref, gain_ref, new_ref, out_ref, partial, x,
                        near, sums, far, x, *refs)


def backward_bridge(partial, x, gain, row, grad, jobs, number, heads=None):
    _, rows, width = x.shape
    last = heads is not None
    outs = bridge_shapes(rows, width) + [jax.ShapeDtypeStruct((1, width), F32)]
    if last:
        outs.append(jax.ShapeDtypeStruct((width, heads.shape[1]), BF16))
    return carry_call(
        functools.partial(backward_bridge_kernel, row, last), jobs, (),
        [ANY_SPEC, ANY_SPEC, VMEM_SPEC, ANY_SPEC] + [VMEM_SPEC] * last,
        [ANY_SPEC, ANY_SPEC, VMEM_SPEC] + [VMEM_SPEC] * last, outs,
        pair_scratch(rows, width, [BF16] * 4 + [x.dtype, grad.dtype, F32])
        + [pltpu.VMEM((4 * rows, width), BF16)] + bridge_sems(),
        (partial, x, gain, grad) + ((heads,) if last else ()), number, "backward_bridge",
        rows * width * 20,
    )


def backward_last(partial, x, gain, row, grad, jobs, number):
    _, rows, width = x.shape
    hops = pltpu.SemaphoreType.DMA((3, PIECES))
    return carry_call(
        functools.partial(backward_last_kernel, row), jobs, (), [VMEM_SPEC] * 4, [VMEM_SPEC] * 2,
        [jax.ShapeDtypeStruct((rows, width), BF16), jax.ShapeDtypeStruct((1, width), F32)],
        [pltpu.VMEM((rows, width), BF16) for _ in range(4)] + [hops, hops],
        (partial, x, gain, grad), number, "backward_last", rows * width * 20,
    )


class Job:
    in_vmem = False
    late = False

    @staticmethod
    def buffers(shape, chips):
        return []

    def __init__(self, source, target, send, recv, chips, buffers=()):
        self.source, self.target, self.send, self.recv = source, target, send, recv
        self.held = buffers
        self.chips = chips
        self.chip, self.core, self.zp, self.zl, self.own = place(chips)
        self.fixed = (self.zp == self.zl) & (self.zl == self.core)
        self.outward, self.inward, self.locals = [], [], []
        self.plan()

    def copy(self, src, dst, send, recv, device):
        return remote(src, dst, self.send.at[send], self.recv.at[recv], device)

    def local(self, src, dst, at, when=None, through=None):
        if through is None:
            self.locals.append((pltpu.make_async_copy(src, dst, self.send.at[at]), None, when))
        else:
            self.locals.append(
                (pltpu.make_async_copy(src, through, self.send.at[at]),
                 pltpu.make_async_copy(through, dst, self.send.at[at]), when)
            )

    def column(self, chip, core, zp, zl):
        return at_device(chip, core, zp, zl)

    def greet(self):
        count = 0
        for copy, device, mine in self.inward:
            if mine is None:
                signal(device)
            else:
                unless(mine, functools.partial(signal, device))
        for copy, mine in self.outward:
            count = count + (1 if mine is None else 1 - mine.astype(jnp.int32))
        return count

    def start(self):
        for copy, mine in self.outward:
            if mine is None:
                copy.start()
            else:
                unless(mine, copy.start)
        for load, _, when in self.locals:
            if when is None:
                load.start()
            else:
                pl.when(when)(load.start)

    def middle(self):
        for load, store, when in self.locals:
            def turn():
                load.wait()
                store.start()

            if store is not None and when is None:
                turn()
            elif store is not None:
                pl.when(when)(turn)

    def arrivals(self):
        for copy, device, mine in self.inward:
            if mine is None:
                copy.wait_recv()
            else:
                unless(mine, copy.wait_recv)

    def departures(self):
        for copy, mine in self.outward:
            if mine is None:
                copy.wait_send()
            else:
                unless(mine, copy.wait_send)
        for load, store, when in self.locals:
            last = load if store is None else store
            if when is None:
                last.wait()
            else:
                pl.when(when)(last.wait)

    def finish(self):
        self.arrivals()
        self.departures()


def block(index, size):
    return pl.ds(pl.multiple_of(index * size, size), size)


class ToPlane(Job):
    @staticmethod
    def result(shape, chips):
        return (2 * shape[0], shape[1])

    @staticmethod
    def buffers(shape, chips):
        return [pltpu.VMEM(shape, BF16)]

    def plan(self):
        rows = self.source.shape[0]
        at = block(self.core, rows)
        for to in range(2):
            self.outward.append(
                (self.copy(self.source, self.target.at[at], to, self.core,
                           at_device(self.chip, self.zl, to, self.zp)),
                 self.fixed & (self.zp == to))
            )
        for co in range(2):
            device = at_device(self.chip, co, self.zl, self.core)
            self.inward.append(
                (self.copy(self.source, self.target.at[block(co, rows)], 0, co, device), device,
                 self.fixed & (self.core == co))
            )
        self.local(self.source, self.target.at[at], 2, self.fixed, self.held[0] if self.held else None)


class FromPlane(Job):
    @staticmethod
    def result(shape, chips):
        return (2, shape[0] // 2, shape[1])

    @staticmethod
    def buffers(shape, chips):
        return [pltpu.VMEM((shape[0] // 2, shape[1]), BF16)]

    def plan(self):
        rows = self.source.shape[0] // 2
        for co in range(2):
            src, mine = self.source.at[block(co, rows)], self.fixed & (self.core == co)
            self.outward.append(
                (self.copy(src, self.target.at[self.zp], co, self.zp,
                           at_device(self.chip, co, self.zl, self.core)), mine)
            )
            self.local(src, self.target.at[self.zp], 2 + co, mine, self.held[0] if self.held else None)
        for at in range(2):
            device = at_device(self.chip, self.zl, at, self.zp)
            self.inward.append(
                (self.copy(self.source.at[block(0, rows)], self.target.at[at], 0, at, device), device,
                 self.fixed & (self.zp == at))
            )


class Spread(Job):
    @staticmethod
    def result(shape, chips):
        return (chips * shape[0], shape[1])

    @staticmethod
    def buffers(shape, chips):
        return [pltpu.VMEM(shape, BF16)]

    def to(self, chip):
        return at_device(chip, self.core, self.zp, self.zl)

    def plan(self):
        rows = self.source.shape[0]
        own = self.target.at[block(self.chip, rows)]
        self.local(self.source, own, 0, None, self.held[0])
        self.onward, self.later = [], []
        if self.chips != 4:
            for j in range(1, self.chips):
                to = lax.rem(self.chip + j, self.chips)
                source = lax.rem(self.chip + self.chips - j, self.chips)
                self.outward.append((self.copy(self.source, own, j, j, self.to(to)), None))
                self.inward.append(
                    (self.copy(self.source, self.target.at[block(source, rows)], j, j,
                               self.to(source)), self.to(source), None)
                )
            return
        y, x = self.chip // 2, lax.rem(self.chip, 2)
        sides = [y * 2 + (1 - x), (1 - y) * 2 + x]
        across = (1 - y) * 2 + (1 - x)
        half = rows // 2
        for side in range(2):
            device = self.to(sides[side])
            self.outward.append((self.copy(self.source, own, 1 + side, 1 + side, device), None))
            self.inward.append(
                (self.copy(self.source, self.target.at[block(sides[side], rows)], 1 + side, 1 + side,
                           device), device, None)
            )
        for side in range(2):
            part = pl.ds(pl.multiple_of(sides[side] * rows + side * half, half), half)
            self.onward.append(
                self.copy(self.target.at[part], self.target.at[part], 3 + side, 3 + side,
                          self.to(sides[1 - side]))
            )
            part = pl.ds(pl.multiple_of(across * rows + side * half, half), half)
            self.later.append(
                self.copy(self.target.at[part], self.target.at[part], 3 + side, 3 + side,
                          self.to(sides[1 - side]))
            )

    def middle(self):
        super().middle()
        if self.onward:
            self.arrivals()
            for copy in self.onward:
                copy.start()

    def finish(self):
        if not self.onward:
            self.arrivals()
        for copy in self.later:
            copy.wait_recv()
        for copy in self.onward:
            copy.wait_send()
        self.departures()


class Reduce(Job):
    in_vmem = True

    @staticmethod
    def result(shape, chips):
        return (shape[0] // chips, shape[1])

    @staticmethod
    def buffers(shape, chips):
        rows, cols = shape[0] // chips, shape[1]
        if chips != 4:
            return [pltpu.VMEM((chips, rows, cols), BF16)]
        return [pltpu.VMEM((rows // 2, cols), BF16)] * 4 + [pltpu.VMEM((rows, cols), BF16)] * 3

    def plan(self):
        rows = self.source.shape[0] // self.chips
        to = lambda chip: at_device(chip, self.core, self.zp, self.zl)
        if self.chips != 4:
            (parts,) = self.held
            self.local(self.source.at[block(self.chip, rows)], parts.at[self.chip], 0)
            for j in range(1, self.chips):
                target = lax.rem(self.chip + j, self.chips)
                source = lax.rem(self.chip + self.chips - j, self.chips)
                src = self.source.at[block(target, rows)]
                self.outward.append((self.copy(src, parts.at[self.chip], j, j, to(target)), None))
                self.inward.append(
                    (self.copy(src, parts.at[source], j, j, to(source)), to(source), None)
                )
            return
        half = rows // 2
        y, x = self.chip // 2, lax.rem(self.chip, 2)
        sides = [y * 2 + (1 - x), (1 - y) * 2 + x]
        across = (1 - y) * 2 + (1 - x)
        passing, staged, blocks, own = self.held[0:2], self.held[2:4], self.held[4:6], self.held[6]
        piece = lambda chip, at: self.source.at[
            pl.ds(pl.multiple_of(chip * rows + at * half, half), half)
        ]
        self.local(self.source.at[block(self.chip, rows)], own, 0)
        self.loads = []
        self.onward, self.later = [], []
        for side in range(2):
            device = to(sides[side])
            copy = self.copy(piece(across, side), passing[side], 1 + side, 1 + side, device)
            self.outward.append((copy, None))
            self.inward.append((copy, device, None))
        self.direct = []
        for side in range(2):
            device = to(sides[side])
            part = pl.ds(side * half, half)
            self.direct.append(
                self.copy(piece(sides[side], side), blocks[side].at[part], 3 + side, 3 + side, device)
            )
            self.loads.append(
                pltpu.make_async_copy(piece(sides[side], 1 - side), staged[side], self.send.at[5 + side])
            )
            part = pl.ds((1 - side) * half, half)
            self.onward.append(
                self.copy(staged[side], blocks[side].at[part], 7 + side, 5 + side, device)
            )

    def start(self):
        super().start()
        if self.chips == 4:
            for copy in self.direct + self.loads:
                copy.start()

    def middle(self):
        if self.chips == 4:
            for side in range(2):
                self.inward[1 - side][0].wait_recv()
                self.loads[side].wait()
                self.held[2 + side][...] = (
                    self.held[2 + side][...].astype(F32) + self.held[1 - side][...].astype(F32)
                ).astype(BF16)
                self.onward[side].start()

    def finish(self):
        if self.chips == 4:
            for copy in self.direct + self.onward:
                copy.wait_recv()
            self.departures()
            for copy in self.direct + self.onward:
                copy.wait_send()
            total = self.held[6][...].astype(F32) + (
                self.held[4][...].astype(F32) + self.held[5][...].astype(F32)
            )
        else:
            super().finish()
            total = self.held[0][0].astype(F32)
            for chip in range(1, self.chips):
                total = total + self.held[0][chip].astype(F32)
        self.target[...] = total.astype(BF16)


class ToRole(Job):
    @staticmethod
    def result(shape, chips):
        return shape

    @staticmethod
    def buffers(shape, chips):
        return [pltpu.VMEM(shape, BF16)]

    def ends(self):
        role = at_device(self.chip, self.zl, self.core, self.zp)
        home = at_device(self.chip, self.zp, self.zl, self.core)
        return role, home, self.fixed & (self.zp == self.core)

    def plan(self):
        to, source, mine = self.ends()
        self.outward.append((self.copy(self.source, self.target, 0, 0, to), mine))
        self.inward.append((self.copy(self.source, self.target, 0, 0, source), source, mine))
        self.local(self.source, self.target, 1, mine, self.held[0])


class FromRole(ToRole):
    def ends(self):
        role, home, mine = super().ends()
        return home, role, mine


class Share(Job):
    late = True
    @staticmethod
    def result(shape, chips):
        return (4 * shape[0], shape[1])

    @staticmethod
    def buffers(shape, chips):
        return [pltpu.VMEM(shape, BF16)]

    def plan(self):
        rows = self.source.shape[0]
        own = self.target.at[block(self.zl * 2 + self.core, rows)]
        beside = at_device(self.chip, 1 - self.core, self.zp, self.zl)
        across = at_device(self.chip, self.core, self.zp, 1 - self.zl)
        self.local(self.source, own, 0, None, self.held[0])
        for at, device, zl, core in ((1, beside, self.zl, 1 - self.core), (2, across, 1 - self.zl, self.core)):
            self.outward.append((self.copy(self.source, own, at, at, device), None))
            self.inward.append(
                (self.copy(self.source, self.target.at[block(zl * 2 + core, rows)], at, at, device),
                 device, None)
            )
        other = self.target.at[block((1 - self.zl) * 2 + self.core, rows)]
        self.onward = self.copy(other, other, 3, 3, beside)
        last = self.target.at[block((1 - self.zl) * 2 + 1 - self.core, rows)]
        self.later = self.copy(last, last, 3, 3, beside)

    def middle(self):
        super().middle()
        self.arrivals()
        self.onward.start()

    def finish(self):
        self.later.wait_recv()
        self.onward.wait_send()
        self.departures()


class ShareSum(Job):
    late = True
    in_vmem = True

    @staticmethod
    def result(shape, chips):
        return (shape[0] // 4, shape[1])

    @staticmethod
    def buffers(shape, chips):
        return [pltpu.VMEM((shape[0] // 4, shape[1]), BF16)] * 5

    def plan(self):
        rows = self.target.shape[0]
        beside = at_device(self.chip, 1 - self.core, self.zp, self.zl)
        across = at_device(self.chip, self.core, self.zp, 1 - self.zl)
        part = lambda zl, core: self.source.at[block(zl * 2 + core, rows)]
        self.far, self.near, self.staged, self.own, self.other = self.held
        for at, src, dst in (
            (0, part(1 - self.zl, 1 - self.core), self.far), (1, part(self.zl, 1 - self.core), self.near)
        ):
            copy = self.copy(src, dst, at, at, beside)
            self.outward.append((copy, None))
            self.inward.append((copy, beside, None))
        self.local(part(1 - self.zl, self.core), self.staged, 2)
        self.local(part(self.zl, self.core), self.own, 3)
        self.onward = self.copy(self.staged, self.other, 4, 2, across)
        self.across = across

    def greet(self):
        signal(self.across)
        return super().greet() + 1

    def middle(self):
        self.arrivals()
        for load, _, _ in self.locals:
            load.wait()
        self.staged[...] = (
            self.staged[...].astype(F32) + self.far[...].astype(F32)
        ).astype(BF16)
        self.onward.start()

    def finish(self):
        for copy, _ in self.outward:
            copy.wait_send()
        self.onward.wait()
        self.target[...] = (
            self.own[...].astype(F32) + self.near[...].astype(F32) + self.other[...].astype(F32)
        ).astype(BF16)


class Jobs:
    def __init__(self, jobs, chips):
        self.kinds = [job[0] for job in jobs]
        self.values = [job[1] for job in jobs]
        self.columns = [job[2] if len(job) > 2 else None for job in jobs]
        shapes = [
            value.shape if columns is None else (value.shape[0], columns[1])
            for value, columns in zip(self.values, self.columns)
        ]
        self.chips = chips
        count = max(9, chips + 1)
        any_space = pl.BlockSpec(memory_space=pl.ANY)
        self.in_specs = [any_space] * len(jobs)
        self.out_shape = [
            jax.ShapeDtypeStruct(kind.result(shape, chips), BF16)
            for kind, shape in zip(self.kinds, shapes)
        ]
        self.buffers = [kind.buffers(shape, chips) for kind, shape in zip(self.kinds, shapes)]
        self.scratch = [pltpu.SemaphoreType.DMA((count,))] * (2 * len(jobs))
        self.scratch += [buffer for buffers in self.buffers for buffer in buffers]

    def out_specs(self, grid):
        specs = []
        for kind, shape in zip(self.kinds, self.out_shape):
            if not kind.in_vmem:
                specs.append(pl.BlockSpec(memory_space=pl.ANY))
            elif grid:
                specs.append(pl.BlockSpec(shape.shape, lambda i: (0, 0)))
            else:
                specs.append(pl.BlockSpec(memory_space=pltpu.VMEM))
        return specs

    def bind(self, sources, targets, scratch):
        sems, scratch = scratch[: 2 * len(self.kinds)], scratch[2 * len(self.kinds) :]
        self.bound = []
        for at, (kind, source, target) in enumerate(zip(self.kinds, sources, targets)):
            if self.columns[at] is not None:
                source = source.at[:, pl.ds(*self.columns[at])]
            held, scratch = scratch[: len(self.buffers[at])], scratch[len(self.buffers[at]) :]
            self.bound.append(
                kind(source, target, sems[2 * at], sems[2 * at + 1], self.chips, held)
            )

    def greet(self):
        count = 0
        for job in self.bound:
            count = count + job.greet()
        return count

    def start(self):
        for job in self.bound:
            job.start()

    def middle(self, late=None):
        for job in self.bound:
            if late is None or job.late == late:
                job.middle()

    def finish(self):
        for job in self.bound:
            job.finish()


def carrying(body, jobs, ins, outs):
    extra = len(jobs.kinds)

    def kernel(*refs):
        operands, refs = refs[:ins], refs[ins:]
        sources, refs = refs[:extra], refs[extra:]
        results, refs = refs[:outs], refs[outs:]
        targets, refs = refs[:extra], refs[extra:]
        own = len(refs) - len(jobs.scratch)
        scratch = refs[:own]
        jobs.bind(sources, targets, refs[own:])
        body(jobs, *operands, *results, *scratch)

    return kernel


def carry_call(body, jobs, grid, in_specs, out_specs, out_shape, scratch, args, number, name, work):
    outs = len(out_shape)
    results = pl.pallas_call(
        carrying(body, jobs, len(args), outs),
        grid=grid,
        in_specs=list(in_specs) + jobs.in_specs,
        out_specs=list(out_specs) + jobs.out_specs(grid),
        out_shape=list(out_shape) + jobs.out_shape,
        scratch_shapes=list(scratch) + jobs.scratch,
        compiler_params=pltpu.CompilerParams(
            collective_id=number, has_side_effects=True, vmem_limit_bytes=56 * 1024 * 1024
        ),
        cost_estimate=pl.CostEstimate(
            flops=work, bytes_accessed=80 * 1024 * 1024, transcendentals=0
        ),
        name=name,
    )(*args, *jobs.values)
    return list(results[:outs]), list(results[outs:])


def place(chips):
    chip, core, zp, zl = (lax.axis_index(name) for name in AXES)
    return chip, core, zp, zl, chip * 2 + core


def at_device(chip, core, zp, zl):
    return {"chip": chip, "core": core, "zp": zp, "zl": zl}


def signal(device):
    pl.semaphore_signal(
        pltpu.get_barrier_semaphore(), inc=1, device_id=device,
        device_id_type=pl.DeviceIdType.MESH,
    )


def unless(condition, action):
    pl.when(jnp.logical_not(condition))(action)


class Plane:
    def __init__(self, chips):
        self.count = 2 * chips
        _, _, self.zp, self.zl, self.own = place(chips)

    def device(self, index):
        return at_device(index // 2, index % 2, self.zp, self.zl)

    def to(self, j):
        return lax.rem(self.own + j, self.count)

    def source(self, j):
        return lax.rem(self.own + self.count - j, self.count)

    def greet(self):
        for j in range(1, self.count):
            signal(self.device(self.to(j)))
        return self.count - 1


class Trade:
    def __init__(self, chips):
        self.chips, self.count = chips, 2 * chips
        self.chip, self.core, self.zp, self.zl, self.own = place(chips)
        self.fixed = (self.zp == self.zl) & (self.zl == self.core)
        self.slot = self.chip * 2 + self.zp

    def role(self, slot):
        return at_device(slot // 2, self.zl, slot % 2, self.zp)

    def role_mine(self, slot):
        return self.fixed & (self.slot == slot)

    def home(self, index):
        return at_device(index // 2, index % 2, self.zl, self.core)

    def home_mine(self, index):
        return self.fixed & (self.own == index)

    def greet_homes(self):
        for index in range(self.count):
            unless(self.home_mine(index), functools.partial(signal, self.home(index)))
        return self.count - self.fixed.astype(jnp.int32)

    def greet_roles(self):
        for slot in range(self.count):
            unless(self.role_mine(slot), functools.partial(signal, self.role(slot)))
        return self.count - self.fixed.astype(jnp.int32)


def greet_group():
    _, _, beside, across = partners()
    signal(beside)
    signal(across)
    return 2


def wait_greetings(count):
    pl.semaphore_wait(pltpu.get_barrier_semaphore(), count)


class Raw:
    def __init__(self, refs, square):
        (self.query, self.key, self.value, self.gate, self.decay, self.conv, self.out,
         self.ffn_gate, self.ffn_up, self.ffn_down) = refs
        self.square = square

    def qkv(self, layer, ref):
        ref[:, 0:KEY] = self.query[layer]
        ref[:, KEY : 2 * KEY] = self.key[layer]
        ref[:, 2 * KEY :] = self.value[layer]

    def side(self, layer, ref):
        ref[:, 0:VAL] = self.gate[layer]
        self.square[...] = jnp.zeros(self.square.shape, F32)
        self.square[0:2, :] = self.decay[layer].astype(F32)
        self.square[2:6, :] = self.conv[layer].astype(F32)
        ref[:, VAL:] = self.square[...].T.astype(BF16)

    def turn(self, value, ref):
        ref[...] = value.astype(F32).T.astype(BF16)


def deal_kernel(chips, jobs, order_ref, lengths_ref, x_ref, gain_ref, cotangent_ref, *refs):
    raw, refs = refs[:10], refs[10:]
    (new_ref, out_ref, start_ref, qkv_next, side_next, out_next, gate_next, up_ref, up_next, down_ref,
     down_next, first_full, second_full, first_wide, second_wide, third_wide, fourth_wide) = refs[:17]
    (spread, picked, square, first, second, third, fourth, held_first, held_second, held, send, recv, stores,
     cross_send, cross_recv,
     plane_send, plane_recv, role_send, role_recv, *sems) = refs[17:]
    raw = Raw(raw, square)
    plane, trade = Plane(chips), Trade(chips)
    first_column = ToPlane(first, first_wide, sems[0], sems[1], chips)
    first_across = Spread(first_wide, first_full, sems[2], sems[3], chips, [held_first])
    second_column = ToPlane(second, second_wide, sems[4], sems[5], chips)
    second_across = Spread(second_wide, second_full, sems[6], sems[7], chips, [held_second])
    third_column = ToPlane(third, third_wide, sems[8], sems[9], chips)
    fourth_column = ToPlane(fourth, fourth_wide, sems[10], sems[11], chips)
    sharing = Sharing(held, out_ref, send, recv, stores)
    across = {"zl": 1 - trade.zl}
    count = plane.count
    part = x_ref.shape[0] // count
    rows = lambda index: pl.ds(pl.multiple_of(index * part, part), part)
    expected = plane.greet() + trade.greet_homes() + greet_group()
    for job in (first_column, first_across, second_column, second_across, third_column, fourth_column):
        expected = expected + job.greet()
    raw.qkv(0, first)
    raw.side(0, second)
    wait_greetings(expected)
    outward, inward = [], []
    for j in range(1, count):
        to, source = plane.to(j), plane.source(j)
        outward.append(
            remote(x_ref.at[rows(to)], spread.at[plane.own], plane_send.at[j], plane_recv.at[j],
                   plane.device(to))
        )
        inward.append(
            remote(x_ref.at[rows(to)], spread.at[source], plane_send.at[j], plane_recv.at[j],
                   plane.device(source))
        )
    for copy in outward:
        copy.start()
    first_column.start()
    spread[plane.own] = x_ref[rows(plane.own), :]
    for copy in inward:
        copy.wait_recv()
    to_roles = []
    for slot in range(count):
        picked[slot] = spread[order_ref[slot]]
        copy = remote(picked.at[slot], new_ref.at[trade.zp, rows(plane.own)], role_send.at[slot],
                      role_recv.at[plane.own], trade.role(slot))
        mine = trade.role_mine(slot)
        unless(mine, copy.start)

        @pl.when(mine)
        def _():
            new_ref[trade.zl, rows(plane.own), :] = picked[slot]

        to_roles.append((copy, mine))
    second_column.start()
    raw.turn(raw.out[0], third)
    raw.turn(raw.ffn_gate[0], fourth)
    first_column.finish()
    first_across.start()
    size = x_ref.shape[0] // PIECES
    parts = max(size // part, 1)
    swaps = []
    for p in range(PIECES):
        piece = new_ref.at[trade.zl, pl.ds(p * size, size)]
        swaps.append(remote(piece, piece, cross_send.at[p], cross_recv.at[p], across))
    for p in range(PIECES):
        for index in range(p * parts, (p + 1) * parts):
            arrival = remote(picked.at[0], new_ref.at[trade.zl, rows(index)], role_send.at[0],
                             role_recv.at[index], trade.home(index))
            unless(trade.home_mine(index), arrival.wait_recv)
        swaps[p].start()
    gain = gain_ref[0:1, :].astype(F32)

    def share(l):
        for p in range(PIECES):
            x = new_ref[l, p * size : (p + 1) * size, :].astype(F32)
            sharing.put(l, p, normed_of(x, gain).astype(BF16))

    for l in range(2):
        pl.when(trade.zl == l)(functools.partial(share, l))
    second_column.finish()
    second_across.start()
    third_column.start()
    fourth_column.start()
    first_across.middle()
    for swap in swaps:
        swap.wait_recv()
    for l in range(2):
        pl.when(trade.zl != l)(functools.partial(share, l))
    length = lengths_ref[order_ref[plane.own]]
    at = (trade.zp * 2 + trade.zl) * x_ref.shape[0]
    positions = lax.broadcasted_iota(jnp.int32, x_ref.shape, 0) + at
    start_ref[...] = jnp.where(positions < length, cotangent_ref[...], jnp.zeros(x_ref.shape, BF16))
    raw.qkv(1, qkv_next)
    raw.side(1, side_next)
    raw.turn(raw.out[1], out_next)
    raw.turn(raw.ffn_gate[1], gate_next)
    raw.turn(raw.ffn_up[0], up_ref)
    raw.turn(raw.ffn_up[1], up_next)
    raw.turn(raw.ffn_down[0], down_ref)
    raw.turn(raw.ffn_down[1], down_next)
    for copy in outward:
        copy.wait_send()
    for copy, mine in to_roles:
        unless(mine, copy.wait_send)
    for swap in swaps:
        swap.wait_send()
    sharing.arrive()
    sharing.finish()
    second_across.middle()
    first_across.finish()
    second_across.finish()
    third_column.finish()
    fourth_column.finish()


def deal_and_gather(order, lengths, x, gain, cotangent, raw, chips, number):
    rows, width = x.shape
    part, units = raw[0].shape[1], raw[7].shape[1]
    vmem = pl.BlockSpec(memory_space=pltpu.VMEM)
    smem = pl.BlockSpec(memory_space=pltpu.SMEM)
    hbm = pl.BlockSpec(memory_space=pl.ANY)
    count = 2 * chips
    buffer = pltpu.VMEM((count, rows // count, width), BF16)
    sems = lambda *shape: [pltpu.SemaphoreType.DMA(shape), pltpu.SemaphoreType.DMA(shape)]
    qkv, side = CONV_CH, VAL + LANES
    held = [(part, cols) for cols in (qkv, side, VAL, units, units, units, units, units)]
    spread = [(2 * chips * part, qkv), (2 * chips * part, side)]
    moved = [(2 * part, cols) for cols in (qkv, side, VAL, units)]
    shapes = [(2, rows, width), (4 * rows, width), (rows, width)] + held + spread + moved
    own = [(part, qkv), (part, side), (part, VAL), (part, units), moved[0], moved[1]]
    return carry_call(
        functools.partial(deal_kernel, chips), Jobs([], chips), (),
        [smem, smem] + [vmem] * 13,
        [vmem, hbm] + [vmem] * 9 + [hbm] * 6,
        [jax.ShapeDtypeStruct(shape, BF16) for shape in shapes],
        [buffer, buffer, pltpu.VMEM((LANES, LANES), F32)]
        + [pltpu.VMEM(shape, BF16) for shape in own]
        + [pltpu.VMEM((4 * rows, width), BF16)] + sems(2, PIECES) + [pltpu.SemaphoreType.DMA((4,))]
        + sems(PIECES) + sems(count) + sems(count)
        + [pltpu.SemaphoreType.DMA((max(9, chips + 1),))] * 12,
        (order, lengths, x, gain, cotangent, *raw), number, "deal_and_gather", rows * width * 20,
    )[0]


def small_rows(width):
    rows = (4 * width + 2 * VAL) // LANES + 1
    return rows + -rows % 8


def assemble(small, mix0, mix1, ffn0, ffn1, heads0, heads1, scalars0, scalars1):
    small[...] = jnp.zeros(small.shape, F32)
    at = 0
    for term in (mix0, mix1, ffn0, ffn1, heads0, heads1):
        for r in range(term.shape[1] // LANES):
            small[at : at + 1, :] = term[:, r * LANES : (r + 1) * LANES]
            at += 1
    head = lax.axis_index("zl") * 2 + lax.axis_index("core")
    lane = lax.broadcasted_iota(jnp.int32, (1, LANES), 1)
    row = jnp.zeros((1, LANES), F32)
    values = (scalars0[0:1, :], scalars1[0:1, :], scalars0[1:2, :], scalars1[1:2, :])
    for place, value in enumerate(values):
        row = row + jnp.where(lane == place * 4 + head, value, 0.0)
    small[at : at + 1, :] = row


def final_kernel(
    chips, jobs, order_ref, partial, x_ref, gain_ref, grad_ref, *refs
):
    terms, refs = refs[:7], refs[7:]
    (in_ref, aux_ref), refs = refs[:2], refs[2:]
    home_ref, total_ref, *homes = refs[:5]
    refs = refs[5:]
    cut = [pl.ds(0, CONV_CH), pl.ds(CONV_CH, VAL)]
    grads = [in_ref.at[:, cut[0]], in_ref.at[:, cut[1]], aux_ref]
    (beside_far, beside_own, sums, far, last, back, picked, small, by_plane, by_z, plane_sum,
     send, recv, role_send, role_recv, plane_send, plane_recv, small_send, small_recv, z_send,
     z_recv), refs = refs[:21], refs[21:]
    reduces, returns = [], []
    for at in range(3):
        summed, four, refs = refs[0], refs[1:5], refs[5:]
        buffers = len(Reduce.buffers(grads[at].shape, chips))
        reduces.append(Reduce(grads[at], summed, four[0], four[1], chips, refs[:buffers]))
        returns.append(FromPlane(summed, homes[at], four[2], four[3], chips))
        refs = refs[buffers:]
    plane, trade = Plane(chips), Trade(chips)
    count = plane.count
    part = x_ref.shape[1] // count
    rows = lambda index: pl.ds(pl.multiple_of(index * part, part), part)
    tier = trade.zp * 2 + trade.zl
    tier_device = lambda at: at_device(trade.chip, trade.core, at // 2, at % 2)
    for k in range(1, 4):
        signal(tier_device(lax.rem(tier + k, 4)))
    expected = plane.greet() + trade.greet_roles() + greet_group() + jobs.greet() + 3
    for job in reduces + returns:
        expected = expected + job.greet()
    wait_greetings(expected)
    scatter = Scatter(partial, beside_far, beside_own, sums, far, send, recv)
    scatter.start()
    reduces[0].start()
    jobs.start()
    dgain = jnp.zeros((1, x_ref.shape[2]), F32)
    to_homes = []
    size = x_ref.shape[1] // PIECES
    parts = max(size // part, 1)
    for p in range(PIECES):
        at = scatter.local(p)
        grad, piece = norm_back(scatter.total(p), x_ref[trade.zl, at, :].astype(F32), gain_ref[0:1, :].astype(F32))
        dgain = dgain + piece
        last[at, :] = (grad + grad_ref[trade.zl, at, :]).astype(BF16)
        for index in range(p * parts, (p + 1) * parts):
            copy = remote(last.at[rows(index)], back.at[trade.slot], role_send.at[index],
                          role_recv.at[trade.slot], trade.home(index))
            mine = trade.home_mine(index)
            unless(mine, copy.start)

            @pl.when(mine)
            def _():
                back[trade.slot] = last[rows(index), :]

            to_homes.append((copy, mine))
    assemble(small, dgain, *terms)
    small_out, small_in = [], []
    for j in range(1, count):
        to, source = plane.to(j), plane.source(j)
        small_out.append(
            remote(small, by_plane.at[plane.own], small_send.at[j], small_recv.at[j], plane.device(to))
        )
        small_in.append(
            remote(small, by_plane.at[source], small_send.at[j], small_recv.at[j], plane.device(source))
        )
    for copy in small_out:
        copy.start()
    by_plane[plane.own] = small[...]
    reduces[0].middle()
    reduces[1].start()
    reduces[2].start()
    for slot in range(count):
        arrival = remote(last.at[rows(0)], back.at[slot], role_send.at[0], role_recv.at[slot],
                         trade.role(slot))
        unless(trade.role_mine(slot), arrival.wait_recv)
    reduces[0].finish()
    returns[0].start()
    outward, inward = [], []
    for j in range(count):
        to, source = plane.to(j), plane.source(j)
        at = jnp.int32(0)
        for slot in range(count):
            at = jnp.where(order_ref[slot] == to, slot, at)
        picked[j] = back[at]
        if j == 0:
            home_ref[rows(plane.own), :] = picked[0]
            continue
        copy = remote(picked.at[j], home_ref.at[rows(plane.own)], plane_send.at[j], plane_recv.at[j],
                      plane.device(to))
        copy.start()
        outward.append(copy)
        inward.append(
            remote(picked.at[j], home_ref.at[rows(source)], plane_send.at[j], plane_recv.at[j],
                   plane.device(source))
        )
    for job in reduces[1:]:
        job.middle()
    jobs.middle()
    for reduce, back_home in zip(reduces[1:], returns[1:]):
        reduce.finish()
        back_home.start()
    for copy in small_in:
        copy.wait_recv()
    total = by_plane[0]
    for index in range(1, count):
        total = total + by_plane[index]
    plane_sum[...] = total
    z_out, z_in = [], []
    for k in range(1, 4):
        to, source = lax.rem(tier + k, 4), lax.rem(tier + 4 - k, 4)
        z_out.append(remote(plane_sum, by_z.at[tier], z_send.at[k], z_recv.at[k], tier_device(to)))
        z_in.append(remote(plane_sum, by_z.at[source], z_send.at[k], z_recv.at[k], tier_device(source)))
    for copy in z_out:
        copy.start()
    by_z[tier] = total
    for copy in z_in:
        copy.wait_recv()
    total_ref[...] = (by_z[0] + by_z[1]) + (by_z[2] + by_z[3])
    for copy in inward:
        copy.wait_recv()
    scatter.finish()
    for copy, mine in to_homes:
        unless(mine, copy.wait_send)
    for copy in small_out + z_out + outward:
        copy.wait_send()
    jobs.finish()
    for job in returns:
        job.finish()


def final_step(order, partial, x, gain, grad, terms, grads, chips, jobs, number):
    _, rows, width = x.shape
    small = jax.ShapeDtypeStruct((small_rows(width), LANES), F32)
    vmem = pl.BlockSpec(memory_space=pltpu.VMEM)
    count = 2 * chips
    block = pltpu.VMEM((rows, width), BF16)
    parted = pltpu.VMEM((count, rows // count, width), BF16)
    hbm = pl.BlockSpec(memory_space=pl.ANY)
    chained = []
    pieces = [(grads[0].shape[0], cols) for cols in (CONV_CH, VAL, LANES)]
    for a in pieces:
        chained.append(pltpu.VMEM(Reduce.result(a, chips), BF16))
        chained += [pltpu.SemaphoreType.DMA((max(9, chips + 1),))] * 4
        chained += Reduce.buffers(a, chips)
    sems = lambda *shape: [pltpu.SemaphoreType.DMA(shape), pltpu.SemaphoreType.DMA(shape)]
    return carry_call(
        functools.partial(final_kernel, chips), jobs, (),
        [pl.BlockSpec(memory_space=pltpu.SMEM)] + [vmem] * 11 + [hbm] * 2,
        [vmem, vmem] + [hbm] * 3,
        [
            jax.ShapeDtypeStruct((rows, width), BF16),
            jax.ShapeDtypeStruct(small.shape, F32),
        ]
        + [
            jax.ShapeDtypeStruct(FromPlane.result(Reduce.result(a, chips), chips), BF16)
            for a in pieces
        ],
        [block] * 5 + [parted] * 2
        + [
            pltpu.VMEM(small.shape, F32), pltpu.VMEM((count,) + small.shape, F32),
            pltpu.VMEM((4,) + small.shape, F32), pltpu.VMEM(small.shape, F32),
        ]
        + sems(3, PIECES) + sems(count) + sems(count) + sems(count) + sems(4) + chained,
        (order, partial, x, gain, grad, *terms, *grads), number, "final_step", rows * width * 20,
    )


def only_jobs_kernel(jobs):
    wait_greetings(jobs.greet())
    jobs.start()
    jobs.middle()
    jobs.finish()


def only_jobs(jobs, number):
    return carry_call(only_jobs_kernel, jobs, (), [], [], [], [], (), number, "weights_back", 0)[1]


def weights_out_kernel(small_ref, home_ref, *refs):
    ins, outs = refs[:14], refs[14:]
    for layer in range(2):
        total = lambda ref: ref[0].astype(F32) + ref[1].astype(F32)
        qkv, head_gate, aux, out, gate, up, down = (
            total(ref) for ref in ins[7 * layer : 7 * layer + 7]
        )
        outs[0][layer] = qkv[:, :KEY]
        outs[1][layer] = qkv[:, KEY : 2 * KEY]
        outs[2][layer] = qkv[:, 2 * KEY :]
        outs[3][layer] = head_gate
        turned = aux.T
        outs[4][layer] = turned[0:2, :]
        outs[14][layer] = turned[2:6, :]
        outs[5][layer] = out.T
        outs[6][layer] = gate.T
        outs[7][layer] = up.T
        outs[8][layer] = down.T
    outs[15][...] = home_ref[...].astype(F32)[:, None, :]
    at = 0
    for ref in outs[9:12]:
        for layer in range(2):
            for r in range(ref.shape[1] // LANES):
                ref[layer : layer + 1, r * LANES : (r + 1) * LANES] = small_ref[at : at + 1, :]
                at += 1
    heads = outs[12].shape[1]
    for member in range(2):
        for layer in range(2):
            first = (2 * member + layer) * heads
            outs[12 + member][layer : layer + 1, :] = small_ref[at : at + 1, first : first + heads]


def weights_out(small, home, first, second, heads):
    width = home.shape[1]
    rows, units = first[0].shape[1], first[6].shape[2]
    shapes = [
        (2, rows, KEY), (2, rows, KEY), (2, rows, VAL), (2, rows, VAL), (2, 2, rows), (2, VAL, rows),
        (2, units, rows), (2, units, rows), (2, units, rows),
        (2, width), (2, width), (2, VAL), (2, heads), (2, heads), (2, 4, rows),
        (home.shape[0], 1, width),
    ]
    vmem = pl.BlockSpec(memory_space=pltpu.VMEM)
    return pl.pallas_call(
        weights_out_kernel,
        in_specs=[vmem] * 16,
        out_specs=[vmem] * 16,
        out_shape=[jax.ShapeDtypeStruct(shape, F32) for shape in shapes],
        compiler_params=pltpu.CompilerParams(vmem_limit_bytes=56 * 1024 * 1024),
        name="weights_out",
    )(small, home, *first, *second)


def ffn_parts(x, gate_ref, up_ref):
    gate, up = mm(x, gate_ref[...]), mm(x, up_ref[...])
    act, sig = silu_of(gate)
    return gate, up, act, sig


def begin_jobs(jobs, at, steps, turns=None):
    if jobs.kinds:
        @pl.when(at == 0)
        def _():
            wait_greetings(jobs.greet())
            jobs.start()

        early, late = turns or (steps // 2, steps - 1)

        @pl.when(at == early)
        def _():
            jobs.middle(late=False)

        @pl.when(at == late)
        def _():
            jobs.middle(late=True)


def end_jobs(jobs, at, steps):
    if jobs.kinds:
        @pl.when(at == steps - 1)
        def _():
            jobs.finish()


def ffn_forward_kernel(jobs, x_ref, gate_ref, up_ref, down_ref, part_ref):
    at, steps = pl.program_id(0), pl.num_programs(0)
    begin_jobs(jobs, at, steps)
    _, up, act, _ = ffn_parts(x_ref[...], gate_ref, up_ref)
    part_ref[...] = mm((act * up).astype(BF16), down_ref[...], NT).astype(BF16)
    end_jobs(jobs, at, steps)


def whole(shape):
    return pl.BlockSpec(shape, lambda i: (0, 0), pipeline_mode=pl.Buffered(1))


def ffn_forward(x, weights, jobs, number):
    length, width = x.shape
    rows = pl.BlockSpec((CHUNK, width), lambda i: (i, 0))
    return carry_call(
        ffn_forward_kernel, jobs, (length // CHUNK,),
        [rows] + [whole(weight.shape) for weight in weights], [rows],
        [jax.ShapeDtypeStruct((length, width), BF16)], [], (x, *weights), number, "ffn_forward",
        4 * 10**9,
    )


def ffn_backward_kernel(both, jobs, x_ref, g_ref, gate_ref, up_ref, down_ref, *refs):
    outs, (low_gate, low_up, hidden_ref, x_held, g_held) = refs[:-5], refs[-5:]
    if both:
        residual_ref, outs = outs[0], outs[1:]
    part_ref, dgate_ref, dup_ref, ddown_ref = outs[:4]
    at, steps = pl.program_id(0), pl.num_programs(0)
    chunks = steps // 2
    begin_jobs(jobs, at, steps)

    @pl.when(at < chunks)
    def _():
        rows = pl.ds(pl.multiple_of(at * CHUNK, CHUNK), CHUNK)
        x, g = x_ref[...], g_ref[...]
        x_held[rows, :] = x
        g_held[rows, :] = g
        gate, up, act, sig = ffn_parts(x, gate_ref, up_ref)
        hidden = (act * up).astype(BF16)
        hidden_ref[rows, :] = hidden
        if both:
            own = lax.axis_index("zl") * 2 + lax.axis_index("core")
            outs[4][...] = (
                mm(hidden, down_ref[...], NT) + jnp.where(at == own, residual_ref[lax.axis_index("zl")], 0.0)
            ).astype(BF16)
        dhidden = mm(g, down_ref[...])
        dgate = (dhidden * up * (sig * (1.0 + gate * (1.0 - sig)))).astype(BF16)
        dup = (dhidden * act).astype(BF16)
        low_gate[rows, :] = dgate
        low_up[rows, :] = dup
        part_ref[...] = (mm(dgate, gate_ref[...], NT) + mm(dup, up_ref[...], NT)).astype(BF16)

    @pl.when(at >= chunks)
    def _():
        columns = pl.ds(pl.multiple_of((at - chunks) * CHUNK, CHUNK), CHUNK)
        dgate_ref[...] = mm(x_held[:, columns], low_gate[...], TN).astype(BF16)
        dup_ref[...] = mm(x_held[:, columns], low_up[...], TN).astype(BF16)
        ddown_ref[...] = mm(g_held[:, columns], hidden_ref[...], TN).astype(BF16)

    end_jobs(jobs, at, steps)


def ffn_backward(x, g, weights, jobs, number, residual=None):
    both = residual is not None
    length, width = x.shape
    chunks = length // CHUNK
    units = weights[0].shape[1]
    assert length == width and (not both or residual.shape[1] == CHUNK)
    rows = pl.BlockSpec((CHUNK, width), lambda i: (jnp.minimum(i, chunks - 1), 0))
    late = pl.BlockSpec((CHUNK, units), lambda i: (jnp.maximum(i - chunks, 0), 0))
    out = lambda cols: jax.ShapeDtypeStruct((length, cols), BF16)
    return carry_call(
        functools.partial(ffn_backward_kernel, both), jobs, (2 * chunks,),
        [rows, rows] + [whole(weight.shape) for weight in weights] + [
            pl.BlockSpec((2, CHUNK, width), lambda i: (0, 0, 0), pipeline_mode=pl.Buffered(1))
        ] * both,
        [rows] + [late] * 3 + [rows] * both,
        [out(width)] + [out(units)] * 3 + [out(width)] * both,
        [pltpu.VMEM((length, units), BF16)] * 3 + [pltpu.VMEM((length, width), BF16)] * 2,
        (x, g, *weights) + ((residual,) if both else ()), number, "ffn_backward", 12 * 10**9,
    )


def row_major(x):
    return with_layout_constraint(x, Layout(major_to_minor=tuple(range(x.ndim))))


def linear(sizes, index):
    place = 0
    for size, at in zip(sizes, index):
        place = place * size + at
    return place


class Roles:
    def __init__(self):
        self.sizes = tuple(lax.axis_size(name) for name in AXES)
        self.chips, self.cores, self.zps, self.zls = self.sizes
        assert self.cores == 2 and self.zps == 2 and self.zls == 2

    def every(self):
        for chip in range(self.chips):
            for core in range(2):
                for zp in range(2):
                    for zl in range(2):
                        yield chip, core, zp, zl

    def rows_pairs(self):
        pairs = []
        for chip, core, zp, zl in self.every():
            slot, part = chip * 2 + zp, zl * 2 + core
            source = linear(self.sizes, (slot // 2, slot % 2, part // 2, part % 2))
            pairs.append((source, linear(self.sizes, (chip, core, zp, zl))))
        return pairs

    def weight_pairs(self, which):
        pairs = []
        for chip, core, zp, zl in self.every():
            head = zp * 2 + zl
            to = (chip, head % 2, core ^ which, head // 2)
            pairs.append(
                (linear(self.sizes, (chip, core, zp, zl)), linear(self.sizes, to))
            )
        return pairs


def flipped(pairs):
    return [(b, a) for a, b in pairs]


def chip_gather(ordered):
    return lax.all_gather(ordered, "chip", axis=0, tiled=True)


def to_plane(pack, roles):
    halves = [lax.ppermute(pack, AXES, roles.weight_pairs(which)) for which in range(2)]
    swap = lax.axis_index("zp") == 1
    return jnp.concatenate(
        [jnp.where(swap, halves[1], halves[0]), jnp.where(swap, halves[0], halves[1])], axis=0
    )


def summed(parts, kind):
    return jnp.sum(parts.astype(F32), axis=0).astype(kind)


def deal(values, order):
    spread = lax.all_to_all(values, ("chip", "core"), split_axis=2, concat_axis=1, tiled=True)
    picked = jnp.take(spread, order, axis=1)
    return lax.all_to_all(picked, ("chip", "core"), split_axis=1, concat_axis=2, tiled=True)


def shards(
    tokens, lengths, order, norm_mix, w_query, w_key, w_value, w_gate, w_decay, conv_filter,
    log_rate, step_bias, norm_heads, w_out, norm_ffn, w_ffn_gate, w_ffn_up, w_ffn_down, cotangent,
):
    roles = Roles()
    layer_count = w_query.shape[0]
    assert layer_count == 2
    heads_total = log_rate.shape[1]
    chip, core, zp, zl = (lax.axis_index(name) for name in AXES)
    head = zl * 2 + core
    rows_local, slots_local, width = tokens.shape
    assert slots_local == 1 and w_decay.shape[2] == 1
    slot_total = order.shape[0]
    units = w_ffn_gate.shape[2]
    rows_part = w_query.shape[1]
    to_roles = roles.rows_pairs()

    def carry(*jobs):
        return Jobs(list(jobs), roles.chips)

    scalars = (log_rate, step_bias)
    kernel_deal = rows_local % (16 * slot_total) == 0
    if kernel_deal:
        turned = lambda w: w.transpose(0, 2, 1)
        raw = (
            w_query, w_key, w_value, w_gate, turned(w_decay[:, :, 0, :]), conv_filter[:, :, 0, :],
            w_out, turned(w_ffn_gate), turned(w_ffn_up), w_ffn_down,
        )
        (residual, rows_in, start, qkv_next, side_next, out_next, gate_next, up_first, up_next,
         down_first, down_next, qkv0, side0, _, _, out_wide, gate_wide) = deal_and_gather(
            order, lengths, tokens[:, 0, :], norm_mix, cotangent[:, 0, :], raw, roles.chips, 1
        )
    else:
        packs = []
        for layer in range(layer_count):
            aux = jnp.concatenate([w_decay[layer, :, 0, :], conv_filter[layer, :, 0, :].T], axis=1)
            aux = jnp.pad(aux, ((0, 0), (0, LANES - aux.shape[1])))
            packs.append(
                [
                    row_major(pack) for pack in (
                        jnp.concatenate([w_query[layer], w_key[layer], w_value[layer]], axis=1),
                        jnp.concatenate([w_gate[layer], aux], axis=1),
                        w_out[layer].T, w_ffn_gate[layer], w_ffn_up[layer], w_ffn_down[layer].T,
                    )
                ]
            )
        (qkv0, side0, out_wide, gate_wide, up_first, down_first) = packs[0]
        (qkv_next, side_next, out_next, gate_next, up_next, down_next) = packs[1]
        positions = (zp * 2 + zl) * rows_local + jnp.arange(rows_local)
        start = cotangent[:, 0, :] * (positions < lengths[order[chip * 2 + core]]).astype(BF16)[:, None]
        residual = lax.ppermute(deal(tokens, order)[:, 0, :], AXES, to_roles)
        (residual, rows_in), _ = first_gather(residual, norm_mix, 0, carry(), 1)
        qkv0, side0 = (chip_gather(to_plane(pack, roles)) for pack in (qkv0, side0))
        out_wide, gate_wide = (to_plane(pack, roles) for pack in (out_wide, gate_wide))

    (heads0, *kept0), (out0, gate0, up_wide, down_wide, qkv_wide) = mixer_forward(
        0, rows_in, qkv0, side0, norm_heads, scalars,
        carry((Spread, out_wide), (Spread, gate_wide), (ToPlane, up_first), (ToPlane, down_first),
              (ToPlane, qkv_next)),
        2,
    )
    rows_in0, residual0 = rows_in, residual
    (middle0, rows_ffn0), (up0, down0, side_wide, gradient) = mixer_bridge(
        heads0, out0, residual0, norm_ffn, 0,
        carry((Spread, up_wide), (Spread, down_wide), (ToPlane, side_next), (ToRole, start)), 3,
    )
    ffn0 = (gate0, up0, down0)
    (part,), _ = ffn_forward(rows_ffn0, ffn0, carry(), None)
    (residual1, rows_in1), (qkv1, side1, out_wide, down_wide) = forward_bridge(
        part, middle0, norm_mix, 1,
        carry((Spread, qkv_wide), (Spread, side_wide), (ToPlane, out_next), (ToPlane, down_next)), 4,
    )
    (heads1, *kept1), (out1, down1, gate_wide, up_wide, grad_rows) = mixer_forward(
        1, rows_in1, qkv1, side1, norm_heads, scalars,
        carry((Spread, out_wide), (Spread, down_wide), (ToPlane, gate_next), (ToPlane, up_next),
              (Share, gradient)),
        5,
    )
    (middle1, rows_ffn1), (gate1, up1) = mixer_bridge(
        heads1, out1, residual1, norm_ffn, 1, carry((Spread, gate_wide), (Spread, up_wide)), 6
    )
    ffn1 = (gate1, up1, down1)
    (part, dgate1, dup1, ddown1, part_out), _ = ffn_backward(
        rows_ffn1, grad_rows, ffn1, carry(), None, residual=middle1
    )

    (gradient, grad_rows, dgain_ffn1, dout1), (dgate1, dup1) = backward_bridge(
        part, middle1, norm_ffn, 1, grad_rows, carry((Reduce, dgate1), (Reduce, dup1)), 7, heads1
    )
    (part, din1, daux1, dgain1, dscalars1), jobs_results = mixer_backward(
        1, grad_rows, rows_in1, qkv1, side1, out1, norm_heads, scalars, kept1,
        carry((Reduce, ddown1), (Reduce, dout1), (FromPlane, dgate1), (FromPlane, dup1),
              (ShareSum, part_out)),
        8,
    )
    ddown1, dout1, gate_home1, up_home1, mixed = jobs_results
    (gradient, grad_rows, dgain_mix1), (dqkv1, daux1, mixed) = backward_bridge(
        part, residual1, norm_mix, 1, gradient,
        carry((Reduce, din1, (0, CONV_CH)), (Reduce, daux1), (FromRole, mixed)), 9,
    )
    (part, dgate0, dup0, ddown0), (side1, qkv_home1, aux_home1, down_home1) = ffn_backward(
        rows_ffn0, grad_rows, ffn0,
        carry((Reduce, din1, (CONV_CH, VAL)), (FromPlane, dqkv1), (FromPlane, daux1),
              (FromPlane, ddown1)),
        14,
    )
    (gradient, grad_rows, dgain_ffn0, dout0), (dgate0, dup0) = backward_bridge(
        part, middle0, norm_ffn, 0, gradient, carry((Reduce, dgate0), (Reduce, dup0)), 10, heads0
    )
    (part, din0, daux0, dgain0, dscalars0), jobs_results = mixer_backward(
        0, grad_rows, rows_in0, qkv0, side0, out0, norm_heads, scalars, kept0,
        carry((Reduce, ddown0), (Reduce, dout0), (FromPlane, dgate0), (FromPlane, dup0),
              (FromPlane, side1), (FromPlane, dout1)),
        11,
    )
    ddown0, dout0, gate_home0, up_home0, side_home1, out_home1 = jobs_results
    terms = (dgain_mix1, dgain_ffn0, dgain_ffn1, dgain0, dgain1, dscalars0, dscalars1)
    last = (din0, daux0)
    last_jobs = carry((FromPlane, ddown0), (FromPlane, dout0))
    if kernel_deal:
        (home, flat, *last), results = final_step(
            order, part, residual0, norm_mix, gradient, terms, last, roles.chips, last_jobs, 12
        )
    else:
        (gradient, dgain_mix), results = backward_last(
            part, residual0, norm_mix, 0, gradient, last_jobs, 12
        )
        mine = (jnp.arange(heads_total) == head).astype(F32)
        flat = jnp.concatenate(
            [dgain_mix[0], *(term[0] for term in terms[:5])]
            + [mine * term[row, 0] for row in range(2) for term in terms[5:]]
        )
        flat = jnp.pad(flat, (0, small_rows(width) * LANES - flat.shape[0])).reshape(-1, LANES)
        flat = lax.psum(flat, AXES)
        dealt_grad = lax.ppermute(gradient, AXES, flipped(to_roles))
        places = jnp.arange(slot_total, dtype=jnp.int32)
        inverse = jnp.sum(jnp.where(order[None, :] == places[:, None], places[None, :], 0), axis=1)
        home = deal(dealt_grad[:, None, :], inverse)[:, 0, :]
        last = only_jobs(
            carry((Reduce, din0, (0, CONV_CH)), (Reduce, din0, (CONV_CH, VAL)), (Reduce, daux0)), 13
        )
        last = only_jobs(carry(*[(FromPlane, a) for a in last]), 15)
    down_home0, out_home0 = results
    qkv_home0, side_home0, aux_home0 = last
    first = (qkv_home0, side_home0, aux_home0, out_home0, gate_home0, up_home0, down_home0)
    second = (qkv_home1, side_home1, aux_home1, out_home1, gate_home1, up_home1, down_home1)
    if rows_part % LANES == 0:
        outs = weights_out(flat, home, first, second, heads_total)
    else:
        flat = flat.reshape(-1)
        small, at = [], 0
        for size in (width, width, VAL, heads_total, heads_total):
            small.append(flat[at : at + layer_count * size].reshape(layer_count, size))
            at += layer_count * size
        qkv, side, aux, out, gate, up, down = (
            jnp.stack([summed(a, F32), summed(b, F32)]) for a, b in zip(first, second)
        )
        turned = lambda a: a.transpose(0, 2, 1)
        outs = [
            qkv[:, :, :KEY], qkv[:, :, KEY : 2 * KEY], qkv[:, :, 2 * KEY :], side, turned(aux)[:, :2], turned(out), turned(gate), turned(up),
            turned(down), *small, turned(aux)[:, 2:6], home.astype(F32)[:, None, :],
        ]
    return (
        mixed[:, None, :],
        outs[15],
        outs[9],
        outs[0], outs[1], outs[2], outs[3],
        outs[4].transpose(0, 2, 1)[:, :, None, :],
        outs[14][:, :, None, :],
        outs[12],
        outs[13],
        outs[11],
        outs[5],
        outs[10],
        outs[6].transpose(0, 2, 1), outs[7].transpose(0, 2, 1), outs[8],
    )


def solution(mesh):
    dp, tensor = mesh.devices.shape
    mesh = Mesh(mesh.devices.reshape(dp // 2, 2, tensor // 2, 2), AXES)
    d, t = ("chip", "core"), ("zp", "zl")
    rows = P(t, d, None)
    by_rows, by_columns = P(None, d, t), P(None, t, d)
    heads, filters = P(None, d, t, None), P(None, None, t, d)
    return jax.shard_map(
        shards,
        mesh=mesh,
        in_specs=(
            rows, P(), P(), P(), by_rows, by_rows, by_rows, by_rows, heads, filters,
            P(), P(), P(), by_columns, P(), by_rows, by_rows, by_columns, rows,
        ),
        out_specs=(
            rows, rows, P(), by_rows, by_rows, by_rows, by_rows, heads, filters,
            P(), P(), P(), by_columns, P(), by_rows, by_rows, by_columns,
        ),
        check_vma=False,
    )
```

```python
import functools
import jax
import jax.numpy as jnp
from jax import lax
from jax.experimental import pallas as pl
from jax.experimental.layout import Layout, with_layout_constraint
from jax.experimental.pallas import tpu as pltpu
from jax.sharding import Mesh, PartitionSpec as P

CHUNK = 256
LANES = 128
KEY = 256
VAL = 512
CONV_CH = 2 * KEY + VAL
F32 = jnp.float32
BF16 = jnp.bfloat16
NN = (((1,), (0,)), ((), ()))
NT = (((1,), (1,)), ((), ()))
TN = (((0,), (0,)), ((), ()))


def mm(a, b, dims=NN):
    return lax.dot_general(
        a.astype(BF16), b.astype(BF16), dims, preferred_element_type=F32
    )


def split_low(a):
    high = a.astype(BF16)
    return high, (a - high.astype(F32)).astype(BF16)


def mm3(a, b, dims=NN):
    a_high, a_low = split_low(a)
    b_high, b_low = split_low(b)
    dot = functools.partial(
        lax.dot_general, dimension_numbers=dims, preferred_element_type=F32
    )
    return dot(a_high, b_high) + (dot(a_high, b_low) + dot(a_low, b_high))


def mm_exact_left(a, b, dims=NN):
    a = a.astype(BF16)
    high = b.astype(BF16)
    rest = b - high.astype(F32)
    mid = rest.astype(BF16)
    low = (rest - mid.astype(F32)).astype(BF16)
    dot = functools.partial(
        lax.dot_general, dimension_numbers=dims, preferred_element_type=F32
    )
    return dot(a, high) + (dot(a, mid) + dot(a, low))


def iotas():
    rows = lax.broadcasted_iota(jnp.int32, (CHUNK, CHUNK), 0)
    cols = lax.broadcasted_iota(jnp.int32, (CHUNK, CHUNK), 1)
    return rows, cols


def wide(col_block, width):
    return jnp.concatenate([col_block] * (width // LANES), axis=1)


def rates_of(rates, rate, bias):
    write = jax.nn.sigmoid(jnp.broadcast_to(rates[:, 0:1], (CHUNK, LANES)))
    logit = jnp.broadcast_to(rates[:, 1:2], (CHUNK, LANES)) + bias
    soft = jnp.maximum(logit, 0.0) + jnp.log1p(jnp.exp(-jnp.abs(logit)))
    return write, -rate * soft, jax.nn.sigmoid(logit)


def head_scalars(scalars_ref, layer):
    head = lax.axis_index("zl") * 2 + lax.axis_index("core")
    rate_ref, bias_ref = scalars_ref
    here = lax.broadcasted_iota(jnp.int32, (1, rate_ref.shape[1]), 1) == head
    pick = lambda ref: jnp.sum(
        jnp.where(here, ref[layer : layer + 1, :].astype(F32), 0.0), axis=1, keepdims=True
    )
    return jnp.exp(pick(rate_ref)), pick(bias_ref)


def decay_terms(step, rows, cols):
    inclusive = (rows >= cols).astype(BF16)
    total = mm_exact_left(inclusive, step)
    spread = wide(total, CHUNK) - jnp.concatenate([total.T] * (CHUNK // LANES), axis=0)
    decay = jnp.where(rows >= cols, jnp.exp(jnp.minimum(spread, 0.0)), 0.0)
    last = jnp.broadcast_to(total[CHUNK - 1 : CHUNK, :], (CHUNK, LANES))
    return decay, jnp.exp(total), jnp.exp(last - total), jnp.exp(last)


def solve_unit(coupling, rows, cols):
    unit = jnp.where(rows == cols, 1.0, 0.0)
    same = ((rows >> 1) == (cols >> 1)) & (rows != cols)
    inverse = unit - jnp.where(same, coupling, 0.0)
    for level in range(1, CHUNK.bit_length() - 1):
        between = ((rows >> (level + 1)) == (cols >> (level + 1))) & (
            (rows >> level) != (cols >> level)
        )
        part = jnp.where(between, coupling, 0.0)
        inverse = inverse - mm(mm(inverse, part), inverse)
    return inverse + mm(inverse, unit - inverse - mm3(coupling, inverse))


def silu_of(x):
    gate = jax.nn.sigmoid(x)
    return x * gate, gate


def conv_rows(padded_ref, taps_ref, start):
    result = padded_ref[pl.ds(start, CHUNK), :] * taps_ref[0:1, :]
    for j in range(1, 4):
        result = result + padded_ref[pl.ds(start + j, CHUNK), :] * taps_ref[j : j + 1, :]
    return result


def forward_kernel(
    layer, jobs, rate_ref, bias_ref, x_ref, qkv_hbm, side_hbm, gain_ref,
    heads_ref, proj_ref, conv_ref, gate_ref, rates_ref, inverse_ref, fresh_ref, o_ref, state_ref,
    padded, memory, taps_ref, w_qkv_ref, w_side_ref, sems,
):
    at = pl.program_id(0)
    held = Held(at, (qkv_hbm, side_hbm), (w_qkv_ref, w_side_ref), sems)
    held.start()
    begin_jobs(jobs, pl.program_id(0), pl.num_programs(0))
    @pl.when(pl.program_id(0) == 0)
    def _():
        memory[...] = jnp.zeros_like(memory)
        padded[0:8, :] = jnp.zeros((8, CONV_CH), F32)

    x = x_ref[...]
    held.ready(0)
    qkv = mm(x, w_qkv_ref[...])
    held.ready(1)

    @pl.when(at == 0)
    def _():
        taps_ref[...] = w_side_ref[:, VAL:].astype(F32).T[2:6, :]

    rates = mm(x, w_side_ref[:, VAL:])
    rates_ref[...] = rates
    proj_ref[...] = qkv
    gate_in = mm(x, w_side_ref[:, :VAL])
    gate_ref[...] = gate_in
    padded[8 : 8 + CHUNK, :] = qkv
    conv = conv_rows(padded, taps_ref, 5)
    padded[0:8, :] = qkv[CHUNK - 8 :, :]
    conv_ref[...] = conv
    act, _ = silu_of(conv)
    q, k, v = act[:, :KEY], act[:, KEY : 2 * KEY], act[:, 2 * KEY :]
    q = q * (lax.rsqrt(jnp.sum(q * q, axis=1, keepdims=True) + 1e-6) * KEY**-0.5)
    k = k * lax.rsqrt(jnp.sum(k * k, axis=1, keepdims=True) + 1e-6)
    rows, cols = iotas()
    write, step, _ = rates_of(rates, *head_scalars((rate_ref, bias_ref), layer))
    decay, growth, rest, final = decay_terms(step, rows, cols)
    coupling = jnp.where(rows > cols, wide(write, CHUNK) * mm3(k, k, NT) * decay, 0.0)
    inverse = solve_unit(coupling, rows, cols)
    inverse_ref[...] = inverse.astype(BF16)
    within = mm(q, k, NT) * decay
    state = memory[...]
    state_ref[...] = state
    low_state = state.astype(BF16)
    source = wide(write, VAL) * (v - wide(growth, VAL) * mm(k, low_state))
    fresh = mm3(inverse, source)
    fresh_ref[...] = fresh
    o = wide(growth, VAL) * mm(q, low_state) + mm(within, fresh)
    o_ref[...] = o
    memory[...] = wide(final, VAL) * state + mm(k * wide(rest, KEY), fresh, TN)
    scaled = o * lax.rsqrt(jnp.mean(o * o, axis=1, keepdims=True) + 1e-5) * gain_ref[layer : layer + 1, :].astype(F32)
    heads = (scaled * silu_of(gate_in)[0]).astype(BF16)
    heads_ref[...] = heads
    end_jobs(jobs, pl.program_id(0), pl.num_programs(0))


def head_spec(value):
    return pl.BlockSpec(value.shape, lambda i: (0, 0))


def mixer_forward(layer, x, qkv, pack, gain, scalars, jobs, number):
    length, width = x.shape
    chunks = length // CHUNK
    row = lambda cols: pl.BlockSpec((CHUNK, cols), lambda i: (i, 0))
    out = lambda cols, kind: jax.ShapeDtypeStruct((length, cols), kind)
    return carry_call(
        functools.partial(forward_kernel, layer), jobs, (chunks,),
        [head_spec(scalars[0]), head_spec(scalars[1]), row(width), ANY_SPEC, ANY_SPEC, head_spec(gain)],
        [
            row(VAL), row(CONV_CH), row(CONV_CH), row(VAL), row(LANES), row(CHUNK), row(VAL), row(VAL),
            pl.BlockSpec((None, KEY, VAL), lambda i: (i, 0, 0)),
        ],
        [
            out(VAL, BF16), out(CONV_CH, F32), out(CONV_CH, F32), out(VAL, F32), out(LANES, F32),
            out(CHUNK, BF16), out(VAL, F32), out(VAL, F32),
            jax.ShapeDtypeStruct((chunks, KEY, VAL), F32),
        ],
        [
            pltpu.VMEM((CHUNK + 8, CONV_CH), F32), pltpu.VMEM((KEY, VAL), F32),
            pltpu.VMEM((4, CONV_CH), F32),
        ] + held_scratch((qkv, pack)),
        (*scalars, x, qkv, pack, gain), number, "mixer_forward", 16 * 10**9,
    )


def unit_back(grad, vector, scale):
    inv = lax.rsqrt(jnp.sum(vector * vector, axis=1, keepdims=True) + 1e-6)
    dot = jnp.sum(grad * vector, axis=1, keepdims=True)
    return (grad - vector * (inv * inv * dot)) * (inv * scale)


def backward_kernel(
    layer, jobs, rate_ref, bias_ref, g_ref, x_ref, out_hbm, qkv_hbm, side_hbm, gain_ref,
    proj_ref, halo_ref, conv_ref, gate_ref, rates_ref, inverse_ref, fresh_ref, o_ref, state_ref,
    part_ref, din_ref, daux_ref, dgain_ref, dscalars_ref,
    padded, dpadded, dmemory, taps_ref, dtaps_ref, daux_sum, x_held, dproj_ref,
    w_out_ref, w_qkv_ref, w_side_ref, sems,
):
    at, steps = pl.program_id(0), pl.num_programs(0)
    chunks = steps // 2
    last = chunks - 1
    held = Held(at, (out_hbm, qkv_hbm, side_hbm), (w_out_ref, w_qkv_ref, w_side_ref), sems)
    held.start()
    begin_jobs(jobs, at, steps, (chunks // 2, chunks - 1))

    @pl.when(at == 0)
    def _():
        dmemory[...] = jnp.zeros_like(dmemory)
        dpadded[CHUNK : CHUNK + 8, :] = jnp.zeros((8, CONV_CH), F32)
        dtaps_ref[...] = jnp.zeros_like(dtaps_ref)
        daux_sum[...] = jnp.zeros_like(daux_sum)
        dgain_ref[...] = jnp.zeros_like(dgain_ref)
        dscalars_ref[...] = jnp.zeros_like(dscalars_ref)

    @pl.when(at < chunks)
    def _():
        rows, cols = iotas()
        padded[8 : 8 + CHUNK, :] = proj_ref[...]
        padded[0:8, :] = jnp.where(at == last, 0.0, halo_ref[...])
        conv = conv_ref[...]
        act, sig = silu_of(conv)
        act_q, act_k, v = act[:, :KEY], act[:, KEY : 2 * KEY], act[:, 2 * KEY :]
        q = act_q * (lax.rsqrt(jnp.sum(act_q * act_q, axis=1, keepdims=True) + 1e-6) * KEY**-0.5)
        k = act_k * lax.rsqrt(jnp.sum(act_k * act_k, axis=1, keepdims=True) + 1e-6)
        rates = rates_ref[...]
        write, step, sig_decay = rates_of(rates, *head_scalars((rate_ref, bias_ref), layer))
        decay, growth, rest, final = decay_terms(step, rows, cols)
        growth_v = wide(growth, VAL)
        write_v = wide(write, VAL)
        low_q, low_k = q.astype(BF16), k.astype(BF16)
        below = rows > cols
        strict_decay = jnp.where(below, decay, 0.0)
        keys = mm(low_k, low_k, NT) * strict_decay * wide(write, CHUNK)
        within = mm(low_q, low_k, NT) * decay
        held.ready(0)
        dheads = mm(g_ref[...], w_out_ref[...])
        o = o_ref[...]
        gate_in = gate_ref[...]
        gate, gate_sig = silu_of(gate_in)
        inv = lax.rsqrt(jnp.mean(o * o, axis=1, keepdims=True) + 1e-5)
        normal = o * inv
        gain = gain_ref[layer : layer + 1, :].astype(F32)
        dgate = dheads * normal * gain * (gate_sig * (1.0 + gate_in * (1.0 - gate_sig)))
        dscaled = dheads * gate
        dgain_ref[...] += jnp.sum(dscaled * normal, axis=0, keepdims=True)
        dnormal = dscaled * gain
        do = inv * (dnormal - normal * jnp.mean(dnormal * normal, axis=1, keepdims=True))
        state = state_ref[...]
        low_state = state.astype(BF16)
        fresh = fresh_ref[...]
        low_fresh = fresh.astype(BF16)
        dstate = dmemory[...]
        low_dstate = dstate.astype(BF16)
        low_do = do.astype(BF16)
        k_rest = k * wide(rest, KEY)
        rest_dstate = mm(k_rest, low_dstate)
        dfresh = mm(within, low_do, TN) + rest_dstate
        dsource = mm(inverse_ref[...], dfresh, TN)
        low_dsource = dsource.astype(BF16)
        dv = write_v * dsource
        dread = -(growth_v * dv)
        low_dread = dread.astype(BF16)
        do_growth = growth_v * do
        low_do_growth = do_growth.astype(BF16)
        dwithin = mm(low_do, low_fresh, NT)
        dcoupling = -mm(low_dsource, low_fresh, NT)
        dkeys = dcoupling * strict_decay * wide(write, CHUNK)
        dpairs = dwithin * decay
        dq = mm(low_do_growth, low_state, NT) + mm(dpairs, low_k)
        dk = (
            mm(low_dread, low_state, NT)
            + mm(dpairs, low_q, TN)
            + mm(dkeys + dkeys.T, low_k)
            + wide(rest, KEY) * mm(low_fresh, low_dstate, NT)
        )
        dmemory[...] = (
            wide(final, VAL) * dstate + mm(low_q, low_do_growth, TN) + mm(low_k, low_dread, TN)
        )
        spread = dwithin * within + dcoupling * keys
        straddle = jnp.where(below, mm_exact_left((rows <= cols).astype(BF16), spread), 0.0)
        read_rows = jnp.sum(
            do_growth * mm(low_q, low_state) + dread * mm(low_k, low_state), axis=1, keepdims=True
        )
        rest_rows = jnp.sum(fresh * rest_dstate, axis=1, keepdims=True)
        carried = jnp.sum(dstate * state) * final[0:1, 0:1]
        suffix = mm_exact_left(
            (rows <= cols).astype(BF16), jnp.broadcast_to(read_rows, (CHUNK, LANES))
        ) + mm_exact_left((rows > cols).astype(BF16), jnp.broadcast_to(rest_rows, (CHUNK, LANES)))
        dstep = suffix + jnp.sum(straddle, axis=1, keepdims=True) + carried
        dlogit = dstep * (-head_scalars((rate_ref, bias_ref), layer)[0]) * sig_decay
        dwrite = (1.0 - write) * jnp.sum(dsource * fresh, axis=1, keepdims=True)
        lane = lax.broadcasted_iota(jnp.int32, (CHUNK, LANES), 1)
        drates = jnp.where(lane == 0, dwrite, jnp.where(lane == 1, dlogit, 0.0))
        low_drates = drates.astype(BF16)
        daux_sum[...] += mm(low_drates, x_ref[...], TN)
        dscalars_ref[0:1, :] += jnp.sum(dstep * step, axis=0, keepdims=True)
        dscalars_ref[1:2, :] += jnp.sum(dlogit, axis=0, keepdims=True)
        dact = jnp.concatenate(
            [unit_back(dq, act_q, KEY**-0.5), unit_back(dk, act_k, 1.0), dv], axis=1
        )
        dconv = dact * (sig * (1.0 + conv * (1.0 - sig)))
        dpadded[0:CHUNK, :] = dconv
        dtaps_ref[2:6, :] += jnp.concatenate(
            [
                jnp.sum(dconv * padded[5 + j : 5 + j + CHUNK, :], axis=0, keepdims=True)
                for j in range(4)
            ],
            axis=0,
        )
        held.ready(1)
        held.ready(2)

        @pl.when(at == 0)
        def _():
            taps_ref[...] = w_side_ref[:, VAL:].astype(F32).T[2:6, :]

        dqkv = dconv * taps_ref[3:4, :]
        for j in range(3):
            dqkv = dqkv + dpadded[pl.ds(3 - j, CHUNK), :] * taps_ref[j : j + 1, :]
        dpadded[CHUNK : CHUNK + 8, :] = dconv[0:8, :]
        low_dqkv, low_dgate = dqkv.astype(BF16), dgate.astype(BF16)
        place = block(last - at, CHUNK)
        dproj_ref[place, :CONV_CH] = low_dqkv
        dproj_ref[place, CONV_CH:] = low_dgate
        x_held[place, :] = x_ref[...]
        part_ref[...] = (
            mm(low_dqkv, w_qkv_ref[...], NT)
            + mm(low_dgate, w_side_ref[:, :VAL], NT)
            + mm(low_drates, w_side_ref[:, VAL:], NT)
        ).astype(BF16)

    @pl.when(at == last)
    def _():
        daux_ref[...] = (daux_sum[...] + dtaps_ref[...]).T.astype(BF16)

    @pl.when(at >= chunks)
    def _():
        columns = block(at - chunks, CHUNK)
        din_ref[...] = mm(x_held[:, columns], dproj_ref[...], TN).astype(BF16)

    end_jobs(jobs, at, steps)


def mixer_backward(layer, g, x, qkv, pack, w_out, gain, scalars, saved, jobs, number):
    proj, conv, gate_in, rates, inverse, fresh, o, states = saved
    length, width = g.shape
    chunks = length // CHUNK
    back = chunks - 1
    at = lambda i: jnp.maximum(back - i, 0)
    row = lambda cols: pl.BlockSpec((CHUNK, cols), lambda i: (at(i), 0))
    out = lambda cols, kind: jax.ShapeDtypeStruct((length, cols), kind)
    steps = CHUNK // 8
    return carry_call(
        functools.partial(backward_kernel, layer), jobs, (2 * chunks,),
        [head_spec(scalars[0]), head_spec(scalars[1]), row(width), row(width)]
        + [ANY_SPEC] * 3 + [head_spec(gain),
            row(CONV_CH),
            pl.BlockSpec((8, CONV_CH), lambda i: (jnp.maximum(at(i) * steps - 1, 0), 0)),
            row(CONV_CH), row(VAL), row(LANES), row(CHUNK), row(VAL), row(VAL),
            pl.BlockSpec((None, KEY, VAL), lambda i: (at(i), 0, 0)),
        ],
        [
            row(width),
            pl.BlockSpec((CHUNK, CONV_CH + VAL), lambda i: (jnp.maximum(i - chunks, 0), 0)),
            pl.BlockSpec((width, LANES), lambda i: (0, 0)),
            pl.BlockSpec((1, VAL), lambda i: (0, 0)),
            pl.BlockSpec((8, LANES), lambda i: (0, 0)),
        ],
        [
            out(width, BF16), jax.ShapeDtypeStruct((width, CONV_CH + VAL), BF16),
            jax.ShapeDtypeStruct((width, LANES), BF16),
            jax.ShapeDtypeStruct((1, VAL), F32),
            jax.ShapeDtypeStruct((8, LANES), F32),
        ],
        [
            pltpu.VMEM((CHUNK + 8, CONV_CH), F32),
            pltpu.VMEM((CHUNK + 8, CONV_CH), F32),
            pltpu.VMEM((KEY, VAL), F32),
            pltpu.VMEM((4, CONV_CH), F32),
            pltpu.VMEM((LANES, CONV_CH), F32),
            pltpu.VMEM((LANES, width), F32),
            pltpu.VMEM((length, width), BF16),
            pltpu.VMEM((length, CONV_CH + VAL), BF16),
        ] + held_scratch((w_out, qkv, pack)),
        (*scalars, g, x, w_out, qkv, pack, gain, proj, proj, conv, gate_in, rates, inverse, fresh, o,
         states),
        number, "mixer_backward", 16 * 10**9,
    )


PIECES = 4
TURN = (1, 2)
AXES = ("chip", "core", "zp", "zl")


def partners():
    core, zl = lax.axis_index("core"), lax.axis_index("zl")
    return core, zl, {"core": 1 - core}, {"zl": 1 - zl}


def remote(src, dst, send, recv, device):
    return pltpu.make_async_remote_copy(
        src_ref=src, dst_ref=dst, send_sem=send, recv_sem=recv,
        device_id=device, device_id_type=pl.DeviceIdType.MESH,
    )


class Block:
    def __init__(self, zl, core, rows):
        self.first = (zl * 2 + core) * rows
        self.size = rows // PIECES

    def piece(self, p):
        return pl.ds(pl.multiple_of(self.first + p * self.size, self.size), self.size)

    def rows(self):
        rows = self.size * PIECES
        return pl.ds(pl.multiple_of(self.first, rows), rows)


class Scatter:
    def __init__(self, partial, beside_far, beside_own, sums, far, send, recv, held=None):
        core, zl, beside, across = partners()
        self.held = held
        rows = far.shape[0]
        self.partial, self.beside_far, self.beside_own = partial, beside_far, beside_own
        self.sums, self.far = sums, far
        self.size = rows // PIECES
        self.own = Block(zl, core, rows)
        self.away = Block(1 - zl, core, rows)
        own_beside, away_beside = Block(zl, 1 - core, rows), Block(1 - zl, 1 - core, rows)
        self.to_far = [
            remote(partial.at[away_beside.piece(p)], beside_far.at[self.local(p)],
                   send.at[0, p], recv.at[0, p], beside)
            for p in range(PIECES)
        ]
        self.to_own = [
            remote(partial.at[own_beside.piece(p)], beside_own.at[self.local(p)],
                   send.at[1, p], recv.at[1, p], beside)
            for p in range(PIECES)
        ]
        self.cross = [
            remote(sums.at[self.local(p)], far.at[self.local(p)],
                   send.at[2, p], recv.at[2, p], across)
            for p in range(PIECES)
        ]

    def local(self, p):
        return pl.ds(p * self.size, self.size)

    def load(self):
        away, own, sems = self.held
        self.loads = [
            pltpu.make_async_copy(self.partial.at[block.rows()], ref, sems.at[at])
            for at, (block, ref) in enumerate(((self.away, away), (self.own, own)))
        ]
        for copy in self.loads:
            copy.start()

    def mine(self, which, p):
        if self.held is None:
            return self.partial[(self.away, self.own)[which].piece(p), :]
        if p == 0:
            self.loads[which].wait()
        return self.held[which][self.local(p), :]

    def start(self):
        for copy in self.to_far:
            copy.start()
        for copy in self.to_own:
            copy.start()
        for p in range(PIECES):
            self.to_far[p].wait_recv()
            at = self.local(p)
            self.sums[at, :] = (
                self.mine(0, p).astype(F32) + self.beside_far[at, :].astype(F32)
            ).astype(BF16)
            self.cross[p].start()

    def total(self, p):
        self.to_own[p].wait_recv()
        self.cross[p].wait_recv()
        at = self.local(p)
        return (
            self.mine(1, p).astype(F32)
            + self.beside_own[at, :].astype(F32)
            + self.far[at, :].astype(F32)
        )

    def finish(self):
        for copies in (self.to_far, self.to_own, self.cross):
            for copy in copies:
                copy.wait_send()


class Exchange:
    def __init__(self, partial, near, sums, far, send, recv):
        core, zl, beside, across = partners()
        rows = far.shape[1]
        self.near, self.sums, self.far = near, sums, far
        self.size = rows // PIECES
        self.blocks = [Block(l, core, rows) for l in range(2)]
        self.others = [Block(l, 1 - core, rows) for l in range(2)]
        self.order = [(l, p) for l in range(2) for p in range(PIECES)]
        self.beside = [
            [
                remote(partial.at[self.others[l].piece(p)], near.at[l, self.local(p)],
                       send.at[l, p], recv.at[l, p], beside)
                for p in range(PIECES)
            ]
            for l in range(2)
        ]
        self.across = [
            [
                remote(sums.at[l, self.local(p)], far.at[l, self.local(p)],
                       send.at[2 + l, p], recv.at[2 + l, p], across)
                for p in range(PIECES)
            ]
            for l in range(2)
        ]

    def local(self, p):
        return pl.ds(p * self.size, self.size)

    def send(self, l):
        for copy in self.beside[l]:
            copy.start()

    def pass_on(self, l, mine):
        for p in range(PIECES):
            self.beside[l][p].wait_recv()
            at = self.local(p)
            self.sums[l, at, :] = (
                mine(l, p).astype(F32) + self.near[l, at, :].astype(F32)
            ).astype(BF16)
            self.across[l][p].start()

    def total(self, l, p):
        self.across[l][p].wait_recv()
        at = self.local(p)
        return self.sums[l, at, :].astype(F32) + self.far[l, at, :].astype(F32)

    def finish(self):
        for l, p in self.order:
            self.beside[l][p].wait_send()
            self.across[l][p].wait_send()


class Sharing:
    def __init__(self, held, out, send, recv, stores):
        core, _, beside, _ = partners()
        rows = held.shape[0] // 4
        self.held = held
        self.blocks = [Block(l, core, rows) for l in range(2)]
        self.copies = [
            [
                remote(held.at[block.piece(p)], held.at[block.piece(p)], send.at[l, p], recv.at[l, p],
                       beside)
                for p in range(PIECES)
            ]
            for l, block in enumerate(self.blocks)
        ]
        others = [Block(l, 1 - core, rows) for l in range(2)]
        self.stores = [
            pltpu.make_async_copy(held.at[block.rows()], out.at[block.rows()], stores.at[at])
            for at, block in enumerate(self.blocks + others)
        ]

    def put(self, l, p, rows):
        self.held[self.blocks[l].piece(p), :] = rows
        self.copies[l][p].start()
        if p == PIECES - 1:
            self.stores[l].start()

    def arrive(self):
        for l in range(2):
            for copy in self.copies[l]:
                copy.wait_recv()
            self.stores[2 + l].start()

    def finish(self):
        for l in range(2):
            for copy in self.copies[l]:
                copy.wait_send()
        for store in self.stores:
            store.wait()


def normed_of(x, gain):
    return x * lax.rsqrt(jnp.mean(x * x, axis=1, keepdims=True) + 1e-6) * gain


def load_all(copies):
    for copy in copies:
        copy.start()


def first_kernel(row, jobs, x_ref, gain_ref, new_ref, out_ref, raw, held, cross_send, cross_recv, send,
                 recv, stores):
    _, zl, _, across = partners()
    wait_greetings(greet_group() + jobs.greet())
    swap = remote(raw.at[zl], raw.at[zl], cross_send.at[0], cross_recv.at[0], across)
    raw[zl] = x_ref[...]
    swap.start()
    jobs.start()
    sharing = Sharing(held, out_ref, send, recv, stores)
    swap.wait()
    size = raw.shape[1] // PIECES
    for l in range(2):
        for p in range(PIECES):
            x = raw[l, p * size : (p + 1) * size, :].astype(F32)
            sharing.put(l, p, normed_of(x, gain_ref[row : row + 1, :].astype(F32)).astype(BF16))
    new_ref[...] = raw[...]
    jobs.middle()
    sharing.arrive()
    sharing.finish()
    jobs.finish()


def forward_bridge_kernel(
    row, jobs, partial, x_ref, gain_ref, new_ref, out_ref, mine, near, sums, far, x, held, send, recv,
    share_send, share_recv, loads, stores
):
    exchange = Exchange(partial, near, sums, far, send, recv)
    sharing = Sharing(held, out_ref, share_send, share_recv, stores)
    own = [
        pltpu.make_async_copy(partial.at[exchange.blocks[l].rows()], mine.at[l], loads.at[l])
        for l in range(2)
    ]
    old = [pltpu.make_async_copy(x_ref.at[l], x.at[l], loads.at[2 + l]) for l in range(2)]
    new = [pltpu.make_async_copy(x.at[l], new_ref.at[l], stores.at[4 + l]) for l in range(2)]
    load_all(own + old)
    wait_greetings(greet_group() + jobs.greet())
    for l in range(2):
        exchange.send(l)
    jobs.start()
    for l in range(2):
        own[l].wait()
        exchange.pass_on(l, lambda l, p: mine[l, exchange.local(p), :])
    forward_rows(row, jobs, exchange, sharing, old, new, x, gain_ref)


def forward_rows(row, jobs, exchange, sharing, old, new, x, gain_ref):
    gain = gain_ref[row : row + 1, :].astype(F32)
    for l in range(2):
        old[l].wait()
        for p in range(PIECES):
            if (l, p) == TURN:
                jobs.middle()
            at = exchange.local(p)
            rows = x[l, at, :] + exchange.total(l, p)
            x[l, at, :] = rows
            sharing.put(l, p, normed_of(rows, gain).astype(BF16))
        new[l].start()
    sharing.arrive()
    exchange.finish()
    sharing.finish()
    for store in new:
        store.wait()
    jobs.finish()


def mixer_bridge_kernel(
    row, jobs, heads_ref, w_out_ref, x_ref, gain_ref, new_ref, out_ref, partial, raw, near, sums, far, x,
    held, send, recv, share_send, share_recv, loads, stores
):
    exchange = Exchange(partial, near, sums, far, send, recv)
    sharing = Sharing(held, out_ref, share_send, share_recv, stores)
    old = [pltpu.make_async_copy(x_ref.at[l], raw.at[l], loads.at[2 + l]) for l in range(2)]
    new = [pltpu.make_async_copy(x.at[l], new_ref.at[l], stores.at[4 + l]) for l in range(2)]
    load_all(old)
    wait_greetings(greet_group() + jobs.greet())

    def make(block):
        rows = block.rows()
        partial[rows, :] = mm(heads_ref[rows, :], w_out_ref[...], NT).astype(BF16)

    for l in range(2):
        make(exchange.others[l])
        exchange.send(l)
    jobs.start()
    for l in range(2):
        make(exchange.blocks[l])
        exchange.pass_on(l, lambda l, p: partial[exchange.blocks[l].piece(p), :])
    for l in range(2):
        old[l].wait()
        if x_ref.dtype != F32:
            x[l] = raw[l].astype(F32)
        old[l] = Done()
    forward_rows(row, jobs, exchange, sharing, old, new, x, gain_ref)


class Done:
    def wait(self):
        pass


def norm_back(total, x, gain):
    inv = lax.rsqrt(jnp.mean(x * x, axis=1, keepdims=True) + 1e-6)
    unit = x * inv
    scaled = total * gain
    grad = inv * (scaled - unit * jnp.mean(scaled * unit, axis=1, keepdims=True))
    return grad, jnp.sum(total * unit, axis=0, keepdims=True)


def backward_bridge_kernel(row, last, jobs, partial, x_ref, gain_ref, grad_ref, *refs):
    if last:
        heads_ref, new_ref, out_ref, dgain_ref, dout_ref, *refs = refs
    else:
        new_ref, out_ref, dgain_ref, *refs = refs
    (mine, near, sums, far, x, grad, new_rows, held, send, recv, share_send, share_recv, loads,
     stores) = refs
    exchange = Exchange(partial, near, sums, far, send, recv)
    sharing = Sharing(held, out_ref, share_send, share_recv, stores)
    zl = lax.axis_index("zl")
    place = lambda ref, l: ref.at[exchange.blocks[l].rows()] if len(ref.shape) == 2 else ref.at[l]
    own, old = [], []
    for l in range(2):
        own.append(
            pltpu.make_async_copy(partial.at[exchange.blocks[l].rows()], mine.at[l], loads.at[l])
        )
        old.append(
            (pltpu.make_async_copy(x_ref.at[l], x.at[l], loads.at[2 + l]),
             pltpu.make_async_copy(place(grad_ref, l), grad.at[l], loads.at[4 + l]))
        )
    new = [pltpu.make_async_copy(new_rows.at[l], new_ref.at[l], stores.at[4 + l]) for l in range(2)]
    load_all(own + [copy for pair in old for copy in pair])
    wait_greetings(greet_group() + jobs.greet())
    for l in range(2):
        exchange.send(l)
    jobs.start()
    for l in range(2):
        own[l].wait()
        exchange.pass_on(l, lambda l, p: mine[l, exchange.local(p), :])
    gain = gain_ref[row : row + 1, :].astype(F32)
    dgain = jnp.zeros(dgain_ref.shape, F32)
    for l in range(2):
        for copy in old[l]:
            copy.wait()
        for p in range(PIECES):
            if (l, p) == TURN:
                jobs.middle()
            at = exchange.local(p)
            rows, part = norm_back(exchange.total(l, p), x[l, at, :].astype(F32), gain)
            dgain = dgain + jnp.where(zl == l, part, 0.0)
            rows = rows + grad[l, at, :].astype(F32)
            new_rows[l, at, :] = rows
            sharing.put(l, p, rows.astype(BF16))
        new[l].start()
    dgain_ref[...] = dgain
    sharing.arrive()
    if last:
        for first in range(0, held.shape[1], 256):
            columns = slice(first, first + 256)
            dout_ref[columns, :] = mm(held[:, columns], heads_ref[...], TN).astype(BF16)
    exchange.finish()
    sharing.finish()
    for store in new:
        store.wait()
    jobs.finish()


def backward_last_kernel(
    row, jobs, partial, x_ref, gain_ref, grad_ref, new_ref, dgain_ref,
    beside_far, beside_own, sums, far, send, recv
):
    wait_greetings(greet_group() + jobs.greet())
    scatter = Scatter(partial, beside_far, beside_own, sums, far, send, recv)
    scatter.start()
    jobs.start()
    zl = lax.axis_index("zl")
    dgain = jnp.zeros(dgain_ref.shape, F32)
    for p in range(PIECES):
        at = scatter.local(p)
        grad, part = norm_back(
            scatter.total(p), x_ref[zl, at, :].astype(F32), gain_ref[row : row + 1, :].astype(F32)
        )
        dgain = dgain + part
        new_ref[at, :] = (grad + grad_ref[zl, at, :]).astype(BF16)
    dgain_ref[...] = dgain
    jobs.middle()
    scatter.finish()
    jobs.finish()


VMEM_SPEC = pl.BlockSpec(memory_space=pltpu.VMEM)
ANY_SPEC = pl.BlockSpec(memory_space=pl.ANY)


def pair_scratch(rows, width, kinds):
    return [pltpu.VMEM((2, rows, width), kind) for kind in kinds]


def bridge_sems():
    many = pltpu.SemaphoreType.DMA((4, PIECES))
    few = pltpu.SemaphoreType.DMA((2, PIECES))
    return [many, many, few, few, pltpu.SemaphoreType.DMA((6,)), pltpu.SemaphoreType.DMA((6,))]


def bridge_shapes(rows, width):
    return [
        jax.ShapeDtypeStruct((2, rows, width), F32),
        jax.ShapeDtypeStruct((4 * rows, width), BF16),
    ]


def first_gather(x, gain, row, jobs, number):
    rows, width = x.shape
    few = pltpu.SemaphoreType.DMA((2, PIECES))
    one = pltpu.SemaphoreType.DMA((1,))
    return carry_call(
        functools.partial(first_kernel, row), jobs, (), [VMEM_SPEC] * 2, [VMEM_SPEC, ANY_SPEC],
        [
            jax.ShapeDtypeStruct((2, rows, width), BF16),
            jax.ShapeDtypeStruct((4 * rows, width), BF16),
        ],
        [pltpu.VMEM((2, rows, width), BF16), pltpu.VMEM((4 * rows, width), BF16), one, one, few, few,
         pltpu.SemaphoreType.DMA((4,))],
        (x, gain), number, "first", rows * width * 20,
    )


def forward_bridge(partial, x, gain, row, jobs, number):
    _, rows, width = x.shape
    return carry_call(
        functools.partial(forward_bridge_kernel, row), jobs, (),
        [ANY_SPEC, ANY_SPEC, VMEM_SPEC], [ANY_SPEC] * 2, bridge_shapes(rows, width),
        pair_scratch(rows, width, [BF16] * 4 + [F32]) + [pltpu.VMEM((4 * rows, width), BF16)]
        + bridge_sems(),
        (partial, x, gain), number, "forward_bridge", rows * width * 20,
    )


def mixer_bridge(heads, w_out, x, gain, row, jobs, number):
    _, rows, width = x.shape
    kernel = functools.partial(
        mixer_bridge_kernel if x.dtype != F32 else mixer_bridge_kernel_f32, row
    )
    raw = pair_scratch(rows, width, [BF16]) if x.dtype != F32 else []
    return carry_call(
        kernel, jobs, (), [VMEM_SPEC, VMEM_SPEC, ANY_SPEC, VMEM_SPEC], [ANY_SPEC] * 2,
        bridge_shapes(rows, width),
        [pltpu.VMEM((4 * rows, width), BF16)] + raw + pair_scratch(rows, width, [BF16] * 3 + [F32])
        + [pltpu.VMEM((4 * rows, width), BF16)] + bridge_sems(),
        (heads, w_out, x, gain), number, "mixer_bridge", 10**9,
    )


def mixer_bridge_kernel_f32(row, jobs, heads_ref, w_out_ref, x_ref, gain_ref, new_ref, out_ref, partial,
                            near, sums, far, x, *refs):
    mixer_bridge_kernel(row, jobs, heads_ref, w_out_ref, x_ref, gain_ref, new_ref, out_ref, partial, x,
                        near, sums, far, x, *refs)


def backward_bridge(partial, x, gain, row, grad, jobs, number, heads=None):
    _, rows, width = x.shape
    last = heads is not None
    outs = bridge_shapes(rows, width) + [jax.ShapeDtypeStruct((1, width), F32)]
    if last:
        outs.append(jax.ShapeDtypeStruct((width, heads.shape[1]), BF16))
    return carry_call(
        functools.partial(backward_bridge_kernel, row, last), jobs, (),
        [ANY_SPEC, ANY_SPEC, VMEM_SPEC, ANY_SPEC] + [VMEM_SPEC] * last,
        [ANY_SPEC, ANY_SPEC, VMEM_SPEC] + [VMEM_SPEC] * last, outs,
        pair_scratch(rows, width, [BF16] * 4 + [x.dtype, grad.dtype, F32])
        + [pltpu.VMEM((4 * rows, width), BF16)] + bridge_sems(),
        (partial, x, gain, grad) + ((heads,) if last else ()), number, "backward_bridge",
        rows * width * 20,
    )


def backward_last(partial, x, gain, row, grad, jobs, number):
    _, rows, width = x.shape
    hops = pltpu.SemaphoreType.DMA((3, PIECES))
    return carry_call(
        functools.partial(backward_last_kernel, row), jobs, (), [VMEM_SPEC] * 4, [VMEM_SPEC] * 2,
        [jax.ShapeDtypeStruct((rows, width), BF16), jax.ShapeDtypeStruct((1, width), F32)],
        [pltpu.VMEM((rows, width), BF16) for _ in range(4)] + [hops, hops],
        (partial, x, gain, grad), number, "backward_last", rows * width * 20,
    )


class Job:
    in_vmem = False
    late = False

    @staticmethod
    def buffers(shape, chips):
        return []

    def __init__(self, source, target, send, recv, chips, buffers=()):
        self.source, self.target, self.send, self.recv = source, target, send, recv
        self.held = buffers
        self.chips = chips
        self.chip, self.core, self.zp, self.zl, self.own = place(chips)
        self.fixed = (self.zp == self.zl) & (self.zl == self.core)
        self.outward, self.inward, self.locals = [], [], []
        self.plan()

    def copy(self, src, dst, send, recv, device):
        return remote(src, dst, self.send.at[send], self.recv.at[recv], device)

    def local(self, src, dst, at, when=None, through=None):
        if through is None:
            self.locals.append((pltpu.make_async_copy(src, dst, self.send.at[at]), None, when))
        else:
            self.locals.append(
                (pltpu.make_async_copy(src, through, self.send.at[at]),
                 pltpu.make_async_copy(through, dst, self.send.at[at]), when)
            )

    def column(self, chip, core, zp, zl):
        return at_device(chip, core, zp, zl)

    def greet(self):
        count = 0
        for copy, device, mine in self.inward:
            if mine is None:
                signal(device)
            else:
                unless(mine, functools.partial(signal, device))
        for copy, mine in self.outward:
            count = count + (1 if mine is None else 1 - mine.astype(jnp.int32))
        return count

    def start(self):
        for copy, mine in self.outward:
            if mine is None:
                copy.start()
            else:
                unless(mine, copy.start)
        for load, _, when in self.locals:
            if when is None:
                load.start()
            else:
                pl.when(when)(load.start)

    def middle(self):
        for load, store, when in self.locals:
            def turn():
                load.wait()
                store.start()

            if store is not None and when is None:
                turn()
            elif store is not None:
                pl.when(when)(turn)

    def arrivals(self):
        for copy, device, mine in self.inward:
            if mine is None:
                copy.wait_recv()
            else:
                unless(mine, copy.wait_recv)

    def departures(self):
        for copy, mine in self.outward:
            if mine is None:
                copy.wait_send()
            else:
                unless(mine, copy.wait_send)
        for load, store, when in self.locals:
            last = load if store is None else store
            if when is None:
                last.wait()
            else:
                pl.when(when)(last.wait)

    def finish(self):
        self.arrivals()
        self.departures()


def block(index, size):
    return pl.ds(pl.multiple_of(index * size, size), size)


class ToPlane(Job):
    @staticmethod
    def result(shape, chips):
        return (2 * shape[0], shape[1])

    @staticmethod
    def buffers(shape, chips):
        return [pltpu.VMEM(shape, BF16)]

    def plan(self):
        rows = self.source.shape[0]
        at = block(self.core, rows)
        for to in range(2):
            self.outward.append(
                (self.copy(self.source, self.target.at[at], to, self.core,
                           at_device(self.chip, self.zl, to, self.zp)),
                 self.fixed & (self.zp == to))
            )
        for co in range(2):
            device = at_device(self.chip, co, self.zl, self.core)
            self.inward.append(
                (self.copy(self.source, self.target.at[block(co, rows)], 0, co, device), device,
                 self.fixed & (self.core == co))
            )
        self.local(self.source, self.target.at[at], 2, self.fixed, self.held[0] if self.held else None)


class FromPlane(Job):
    @staticmethod
    def result(shape, chips):
        return (2, shape[0] // 2, shape[1])

    @staticmethod
    def buffers(shape, chips):
        return [pltpu.VMEM((shape[0] // 2, shape[1]), BF16)]

    def plan(self):
        rows = self.source.shape[0] // 2
        for co in range(2):
            src, mine = self.source.at[block(co, rows)], self.fixed & (self.core == co)
            self.outward.append(
                (self.copy(src, self.target.at[self.zp], co, self.zp,
                           at_device(self.chip, co, self.zl, self.core)), mine)
            )
            self.local(src, self.target.at[self.zp], 2 + co, mine, self.held[0] if self.held else None)
        for at in range(2):
            device = at_device(self.chip, self.zl, at, self.zp)
            self.inward.append(
                (self.copy(self.source.at[block(0, rows)], self.target.at[at], 0, at, device), device,
                 self.fixed & (self.zp == at))
            )


class Spread(Job):
    @staticmethod
    def result(shape, chips):
        return (chips * shape[0], shape[1])

    @staticmethod
    def buffers(shape, chips):
        return [pltpu.VMEM(shape, BF16)]

    def to(self, chip):
        return at_device(chip, self.core, self.zp, self.zl)

    def plan(self):
        rows = self.source.shape[0]
        own = self.target.at[block(self.chip, rows)]
        self.local(self.source, own, 0, None, self.held[0])
        self.onward, self.later = [], []
        if self.chips != 4:
            for j in range(1, self.chips):
                to = lax.rem(self.chip + j, self.chips)
                source = lax.rem(self.chip + self.chips - j, self.chips)
                self.outward.append((self.copy(self.source, own, j, j, self.to(to)), None))
                self.inward.append(
                    (self.copy(self.source, self.target.at[block(source, rows)], j, j,
                               self.to(source)), self.to(source), None)
                )
            return
        y, x = self.chip // 2, lax.rem(self.chip, 2)
        sides = [y * 2 + (1 - x), (1 - y) * 2 + x]
        across = (1 - y) * 2 + (1 - x)
        half = rows // 2
        for side in range(2):
            device = self.to(sides[side])
            self.outward.append((self.copy(self.source, own, 1 + side, 1 + side, device), None))
            self.inward.append(
                (self.copy(self.source, self.target.at[block(sides[side], rows)], 1 + side, 1 + side,
                           device), device, None)
            )
        for side in range(2):
            part = pl.ds(pl.multiple_of(sides[side] * rows + side * half, half), half)
            self.onward.append(
                self.copy(self.target.at[part], self.target.at[part], 3 + side, 3 + side,
                          self.to(sides[1 - side]))
            )
            part = pl.ds(pl.multiple_of(across * rows + side * half, half), half)
            self.later.append(
                self.copy(self.target.at[part], self.target.at[part], 3 + side, 3 + side,
                          self.to(sides[1 - side]))
            )

    def middle(self):
        super().middle()
        if self.onward:
            self.arrivals()
            for copy in self.onward:
                copy.start()

    def finish(self):
        if not self.onward:
            self.arrivals()
        for copy in self.later:
            copy.wait_recv()
        for copy in self.onward:
            copy.wait_send()
        self.departures()


class Reduce(Job):
    in_vmem = True

    @staticmethod
    def result(shape, chips):
        return (shape[0] // chips, shape[1])

    @staticmethod
    def buffers(shape, chips):
        rows, cols = shape[0] // chips, shape[1]
        if chips != 4:
            return [pltpu.VMEM((chips, rows, cols), BF16)]
        return [pltpu.VMEM((rows // 2, cols), BF16)] * 4 + [pltpu.VMEM((rows, cols), BF16)] * 3

    def plan(self):
        rows = self.source.shape[0] // self.chips
        to = lambda chip: at_device(chip, self.core, self.zp, self.zl)
        if self.chips != 4:
            (parts,) = self.held
            self.local(self.source.at[block(self.chip, rows)], parts.at[self.chip], 0)
            for j in range(1, self.chips):
                target = lax.rem(self.chip + j, self.chips)
                source = lax.rem(self.chip + self.chips - j, self.chips)
                src = self.source.at[block(target, rows)]
                self.outward.append((self.copy(src, parts.at[self.chip], j, j, to(target)), None))
                self.inward.append(
                    (self.copy(src, parts.at[source], j, j, to(source)), to(source), None)
                )
            return
        half = rows // 2
        y, x = self.chip // 2, lax.rem(self.chip, 2)
        sides = [y * 2 + (1 - x), (1 - y) * 2 + x]
        across = (1 - y) * 2 + (1 - x)
        passing, staged, blocks, own = self.held[0:2], self.held[2:4], self.held[4:6], self.held[6]
        piece = lambda chip, at: self.source.at[
            pl.ds(pl.multiple_of(chip * rows + at * half, half), half)
        ]
        self.local(self.source.at[block(self.chip, rows)], own, 0)
        self.loads = []
        self.onward, self.later = [], []
        for side in range(2):
            device = to(sides[side])
            copy = self.copy(piece(across, side), passing[side], 1 + side, 1 + side, device)
            self.outward.append((copy, None))
            self.inward.append((copy, device, None))
        self.direct = []
        for side in range(2):
            device = to(sides[side])
            part = pl.ds(side * half, half)
            self.direct.append(
                self.copy(piece(sides[side], side), blocks[side].at[part], 3 + side, 3 + side, device)
            )
            self.loads.append(
                pltpu.make_async_copy(piece(sides[side], 1 - side), staged[side], self.send.at[5 + side])
            )
            part = pl.ds((1 - side) * half, half)
            self.onward.append(
                self.copy(staged[side], blocks[side].at[part], 7 + side, 5 + side, device)
            )

    def start(self):
        super().start()
        if self.chips == 4:
            for copy in self.direct + self.loads:
                copy.start()

    def middle(self):
        if self.chips == 4:
            for side in range(2):
                self.inward[1 - side][0].wait_recv()
                self.loads[side].wait()
                self.held[2 + side][...] = (
                    self.held[2 + side][...].astype(F32) + self.held[1 - side][...].astype(F32)
                ).astype(BF16)
                self.onward[side].start()

    def finish(self):
        if self.chips == 4:
            for copy in self.direct + self.onward:
                copy.wait_recv()
            self.departures()
            for copy in self.direct + self.onward:
                copy.wait_send()
            total = self.held[6][...].astype(F32) + (
                self.held[4][...].astype(F32) + self.held[5][...].astype(F32)
            )
        else:
            super().finish()
            total = self.held[0][0].astype(F32)
            for chip in range(1, self.chips):
                total = total + self.held[0][chip].astype(F32)
        self.target[...] = total.astype(BF16)


class ToRole(Job):
    @staticmethod
    def result(shape, chips):
        return shape

    @staticmethod
    def buffers(shape, chips):
        return [pltpu.VMEM(shape, BF16)]

    def ends(self):
        role = at_device(self.chip, self.zl, self.core, self.zp)
        home = at_device(self.chip, self.zp, self.zl, self.core)
        return role, home, self.fixed & (self.zp == self.core)

    def plan(self):
        to, source, mine = self.ends()
        self.outward.append((self.copy(self.source, self.target, 0, 0, to), mine))
        self.inward.append((self.copy(self.source, self.target, 0, 0, source), source, mine))
        self.local(self.source, self.target, 1, mine, self.held[0])


class FromRole(ToRole):
    def ends(self):
        role, home, mine = super().ends()
        return home, role, mine


class Share(Job):
    late = True
    @staticmethod
    def result(shape, chips):
        return (4 * shape[0], shape[1])

    @staticmethod
    def buffers(shape, chips):
        return [pltpu.VMEM(shape, BF16)]

    def plan(self):
        rows = self.source.shape[0]
        own = self.target.at[block(self.zl * 2 + self.core, rows)]
        beside = at_device(self.chip, 1 - self.core, self.zp, self.zl)
        across = at_device(self.chip, self.core, self.zp, 1 - self.zl)
        self.local(self.source, own, 0, None, self.held[0])
        for at, device, zl, core in ((1, beside, self.zl, 1 - self.core), (2, across, 1 - self.zl, self.core)):
            self.outward.append((self.copy(self.source, own, at, at, device), None))
            self.inward.append(
                (self.copy(self.source, self.target.at[block(zl * 2 + core, rows)], at, at, device),
                 device, None)
            )
        other = self.target.at[block((1 - self.zl) * 2 + self.core, rows)]
        self.onward = self.copy(other, other, 3, 3, beside)
        last = self.target.at[block((1 - self.zl) * 2 + 1 - self.core, rows)]
        self.later = self.copy(last, last, 3, 3, beside)

    def middle(self):
        super().middle()
        self.arrivals()
        self.onward.start()

    def finish(self):
        self.later.wait_recv()
        self.onward.wait_send()
        self.departures()


class ShareSum(Job):
    late = True
    in_vmem = True

    @staticmethod
    def result(shape, chips):
        return (shape[0] // 4, shape[1])

    @staticmethod
    def buffers(shape, chips):
        return [pltpu.VMEM((shape[0] // 4, shape[1]), BF16)] * 5

    def plan(self):
        rows = self.target.shape[0]
        beside = at_device(self.chip, 1 - self.core, self.zp, self.zl)
        across = at_device(self.chip, self.core, self.zp, 1 - self.zl)
        part = lambda zl, core: self.source.at[block(zl * 2 + core, rows)]
        self.far, self.near, self.staged, self.own, self.other = self.held
        for at, src, dst in (
            (0, part(1 - self.zl, 1 - self.core), self.far), (1, part(self.zl, 1 - self.core), self.near)
        ):
            copy = self.copy(src, dst, at, at, beside)
            self.outward.append((copy, None))
            self.inward.append((copy, beside, None))
        self.local(part(1 - self.zl, self.core), self.staged, 2)
        self.local(part(self.zl, self.core), self.own, 3)
        self.onward = self.copy(self.staged, self.other, 4, 2, across)
        self.across = across

    def greet(self):
        signal(self.across)
        return super().greet() + 1

    def middle(self):
        self.arrivals()
        for load, _, _ in self.locals:
            load.wait()
        self.staged[...] = (
            self.staged[...].astype(F32) + self.far[...].astype(F32)
        ).astype(BF16)
        self.onward.start()

    def finish(self):
        for copy, _ in self.outward:
            copy.wait_send()
        self.onward.wait()
        self.target[...] = (
            self.own[...].astype(F32) + self.near[...].astype(F32) + self.other[...].astype(F32)
        ).astype(BF16)


class Jobs:
    def __init__(self, jobs, chips):
        self.kinds = [job[0] for job in jobs]
        self.values = [job[1] for job in jobs]
        self.columns = [job[2] if len(job) > 2 else None for job in jobs]
        shapes = [
            value.shape if columns is None else (value.shape[0], columns[1])
            for value, columns in zip(self.values, self.columns)
        ]
        self.chips = chips
        count = max(9, chips + 1)
        any_space = pl.BlockSpec(memory_space=pl.ANY)
        self.in_specs = [any_space] * len(jobs)
        self.out_shape = [
            jax.ShapeDtypeStruct(kind.result(shape, chips), BF16)
            for kind, shape in zip(self.kinds, shapes)
        ]
        self.buffers = [kind.buffers(shape, chips) for kind, shape in zip(self.kinds, shapes)]
        self.scratch = [pltpu.SemaphoreType.DMA((count,))] * (2 * len(jobs))
        self.scratch += [buffer for buffers in self.buffers for buffer in buffers]

    def out_specs(self, grid):
        specs = []
        for kind, shape in zip(self.kinds, self.out_shape):
            if not kind.in_vmem:
                specs.append(pl.BlockSpec(memory_space=pl.ANY))
            elif grid:
                specs.append(pl.BlockSpec(shape.shape, lambda i: (0, 0)))
            else:
                specs.append(pl.BlockSpec(memory_space=pltpu.VMEM))
        return specs

    def bind(self, sources, targets, scratch):
        sems, scratch = scratch[: 2 * len(self.kinds)], scratch[2 * len(self.kinds) :]
        self.bound = []
        for at, (kind, source, target) in enumerate(zip(self.kinds, sources, targets)):
            if self.columns[at] is not None:
                source = source.at[:, pl.ds(*self.columns[at])]
            held, scratch = scratch[: len(self.buffers[at])], scratch[len(self.buffers[at]) :]
            self.bound.append(
                kind(source, target, sems[2 * at], sems[2 * at + 1], self.chips, held)
            )

    def greet(self):
        count = 0
        for job in self.bound:
            count = count + job.greet()
        return count

    def start(self):
        for job in self.bound:
            job.start()

    def middle(self, late=None):
        for job in self.bound:
            if late is None or job.late == late:
                job.middle()

    def finish(self):
        for job in self.bound:
            job.finish()


def carrying(body, jobs, ins, outs):
    extra = len(jobs.kinds)

    def kernel(*refs):
        operands, refs = refs[:ins], refs[ins:]
        sources, refs = refs[:extra], refs[extra:]
        results, refs = refs[:outs], refs[outs:]
        targets, refs = refs[:extra], refs[extra:]
        own = len(refs) - len(jobs.scratch)
        scratch = refs[:own]
        jobs.bind(sources, targets, refs[own:])
        body(jobs, *operands, *results, *scratch)

    return kernel


def carry_call(body, jobs, grid, in_specs, out_specs, out_shape, scratch, args, number, name, work):
    outs = len(out_shape)
    results = pl.pallas_call(
        carrying(body, jobs, len(args), outs),
        grid=grid,
        in_specs=list(in_specs) + jobs.in_specs,
        out_specs=list(out_specs) + jobs.out_specs(grid),
        out_shape=list(out_shape) + jobs.out_shape,
        scratch_shapes=list(scratch) + jobs.scratch,
        compiler_params=pltpu.CompilerParams(
            collective_id=number, has_side_effects=True, vmem_limit_bytes=56 * 1024 * 1024
        ),
        cost_estimate=pl.CostEstimate(
            flops=work, bytes_accessed=80 * 1024 * 1024, transcendentals=0
        ),
        name=name,
    )(*args, *jobs.values)
    return list(results[:outs]), list(results[outs:])


def place(chips):
    chip, core, zp, zl = (lax.axis_index(name) for name in AXES)
    return chip, core, zp, zl, chip * 2 + core


def at_device(chip, core, zp, zl):
    return {"chip": chip, "core": core, "zp": zp, "zl": zl}


def signal(device):
    pl.semaphore_signal(
        pltpu.get_barrier_semaphore(), inc=1, device_id=device,
        device_id_type=pl.DeviceIdType.MESH,
    )


def unless(condition, action):
    pl.when(jnp.logical_not(condition))(action)


class Plane:
    def __init__(self, chips):
        self.count = 2 * chips
        _, _, self.zp, self.zl, self.own = place(chips)

    def device(self, index):
        return at_device(index // 2, index % 2, self.zp, self.zl)

    def to(self, j):
        return lax.rem(self.own + j, self.count)

    def source(self, j):
        return lax.rem(self.own + self.count - j, self.count)

    def greet(self):
        for j in range(1, self.count):
            signal(self.device(self.to(j)))
        return self.count - 1


class Trade:
    def __init__(self, chips):
        self.chips, self.count = chips, 2 * chips
        self.chip, self.core, self.zp, self.zl, self.own = place(chips)
        self.fixed = (self.zp == self.zl) & (self.zl == self.core)
        self.slot = self.chip * 2 + self.zp

    def role(self, slot):
        return at_device(slot // 2, self.zl, slot % 2, self.zp)

    def role_mine(self, slot):
        return self.fixed & (self.slot == slot)

    def home(self, index):
        return at_device(index // 2, index % 2, self.zl, self.core)

    def home_mine(self, index):
        return self.fixed & (self.own == index)

    def greet_homes(self):
        for index in range(self.count):
            unless(self.home_mine(index), functools.partial(signal, self.home(index)))
        return self.count - self.fixed.astype(jnp.int32)

    def greet_roles(self):
        for slot in range(self.count):
            unless(self.role_mine(slot), functools.partial(signal, self.role(slot)))
        return self.count - self.fixed.astype(jnp.int32)


def greet_group():
    _, _, beside, across = partners()
    signal(beside)
    signal(across)
    return 2


def wait_greetings(count):
    pl.semaphore_wait(pltpu.get_barrier_semaphore(), count)


class Raw:
    def __init__(self, refs, square):
        (self.query, self.key, self.value, self.gate, self.decay, self.conv, self.out,
         self.ffn_gate, self.ffn_up, self.ffn_down) = refs
        self.square = square

    def qkv(self, layer, ref):
        ref[:, 0:KEY] = self.query[layer]
        ref[:, KEY : 2 * KEY] = self.key[layer]
        ref[:, 2 * KEY :] = self.value[layer]

    def side(self, layer, ref):
        ref[:, 0:VAL] = self.gate[layer]
        self.square[...] = jnp.zeros(self.square.shape, F32)
        self.square[0:2, :] = self.decay[layer].astype(F32)
        self.square[2:6, :] = self.conv[layer].astype(F32)
        ref[:, VAL:] = self.square[...].T.astype(BF16)

    def turn(self, value, ref):
        ref[...] = value.astype(F32).T.astype(BF16)


def deal_kernel(chips, jobs, order_ref, lengths_ref, x_ref, gain_ref, cotangent_ref, *refs):
    raw, refs = refs[:10], refs[10:]
    (new_ref, out_ref, start_ref, qkv_next, side_next, out_next, gate_next, up_ref, up_next, down_ref,
     down_next, first_full, second_full, first_wide, second_wide, third_wide, fourth_wide) = refs[:17]
    (spread, picked, square, first, second, third, fourth, held_first, held_other, held_second, held, send, recv,
     stores,     cross_send, cross_recv,
     plane_send, plane_recv, role_send, role_recv, *sems) = refs[17:]
    raw = Raw(raw, square)
    plane, trade = Plane(chips), Trade(chips)
    half = CONV_CH // 2
    halves = []
    for at, (own, four) in enumerate(((held_first, sems[0:4]), (held_other, sems[12:16]))):
        cut = pl.ds(at * half, half)
        wide = first_wide.at[:, cut]
        halves.append(
            (ToPlane(first.at[:, cut], wide, four[0], four[1], chips),
             Spread(wide, first_full.at[:, cut], four[2], four[3], chips, [own]))
        )
    second_column = ToPlane(second, second_wide, sems[4], sems[5], chips)
    second_across = Spread(second_wide, second_full, sems[6], sems[7], chips, [held_second])
    third_column = ToPlane(third, third_wide, sems[8], sems[9], chips)
    fourth_column = ToPlane(fourth, fourth_wide, sems[10], sems[11], chips)
    sharing = Sharing(held, out_ref, send, recv, stores)
    across = {"zl": 1 - trade.zl}
    count = plane.count
    part = x_ref.shape[0] // count
    rows = lambda index: pl.ds(pl.multiple_of(index * part, part), part)
    expected = plane.greet() + trade.greet_homes() + greet_group()
    for job in (*halves[0], *halves[1], second_column, second_across, third_column, fourth_column):
        expected = expected + job.greet()
    raw.qkv(0, first)
    raw.side(0, second)
    wait_greetings(expected)
    outward, inward = [], []
    for j in range(1, count):
        to, source = plane.to(j), plane.source(j)
        outward.append(
            remote(x_ref.at[rows(to)], spread.at[plane.own], plane_send.at[j], plane_recv.at[j],
                   plane.device(to))
        )
        inward.append(
            remote(x_ref.at[rows(to)], spread.at[source], plane_send.at[j], plane_recv.at[j],
                   plane.device(source))
        )
    for copy in outward:
        copy.start()
    for column, _ in halves:
        column.start()
    spread[plane.own] = x_ref[rows(plane.own), :]
    for copy in inward:
        copy.wait_recv()
    halves[0][0].finish()
    halves[0][1].start()
    to_roles = []
    for slot in range(count):
        picked[slot] = spread[order_ref[slot]]
        copy = remote(picked.at[slot], new_ref.at[trade.zp, rows(plane.own)], role_send.at[slot],
                      role_recv.at[plane.own], trade.role(slot))
        mine = trade.role_mine(slot)
        unless(mine, copy.start)

        @pl.when(mine)
        def _():
            new_ref[trade.zl, rows(plane.own), :] = picked[slot]

        to_roles.append((copy, mine))
    second_column.start()
    raw.turn(raw.out[0], third)
    raw.turn(raw.ffn_gate[0], fourth)
    halves[1][0].finish()
    halves[1][1].start()
    size = x_ref.shape[0] // PIECES
    parts = max(size // part, 1)
    swaps = []
    for p in range(PIECES):
        piece = new_ref.at[trade.zl, pl.ds(p * size, size)]
        swaps.append(remote(piece, piece, cross_send.at[p], cross_recv.at[p], across))
    for p in range(PIECES):
        for index in range(p * parts, (p + 1) * parts):
            arrival = remote(picked.at[0], new_ref.at[trade.zl, rows(index)], role_send.at[0],
                             role_recv.at[index], trade.home(index))
            unless(trade.home_mine(index), arrival.wait_recv)
        swaps[p].start()
    gain = gain_ref[0:1, :].astype(F32)

    def share(l):
        for p in range(PIECES):
            x = new_ref[l, p * size : (p + 1) * size, :].astype(F32)
            sharing.put(l, p, normed_of(x, gain).astype(BF16))

    for l in range(2):
        pl.when(trade.zl == l)(functools.partial(share, l))
    second_column.finish()
    second_across.start()
    third_column.start()
    fourth_column.start()
    for _, across_chips in halves:
        across_chips.middle()
    for swap in swaps:
        swap.wait_recv()
    for l in range(2):
        pl.when(trade.zl != l)(functools.partial(share, l))
    length = lengths_ref[order_ref[plane.own]]
    at = (trade.zp * 2 + trade.zl) * x_ref.shape[0]
    positions = lax.broadcasted_iota(jnp.int32, x_ref.shape, 0) + at
    start_ref[...] = jnp.where(positions < length, cotangent_ref[...], jnp.zeros(x_ref.shape, BF16))
    raw.qkv(1, qkv_next)
    raw.side(1, side_next)
    raw.turn(raw.out[1], out_next)
    raw.turn(raw.ffn_gate[1], gate_next)
    raw.turn(raw.ffn_up[0], up_ref)
    raw.turn(raw.ffn_up[1], up_next)
    raw.turn(raw.ffn_down[0], down_ref)
    raw.turn(raw.ffn_down[1], down_next)
    for copy in outward:
        copy.wait_send()
    for copy, mine in to_roles:
        unless(mine, copy.wait_send)
    for swap in swaps:
        swap.wait_send()
    sharing.arrive()
    sharing.finish()
    second_across.middle()
    for _, across_chips in halves:
        across_chips.finish()
    second_across.finish()
    third_column.finish()
    fourth_column.finish()


def deal_and_gather(order, lengths, x, gain, cotangent, raw, chips, number):
    rows, width = x.shape
    part, units = raw[0].shape[1], raw[7].shape[1]
    vmem = pl.BlockSpec(memory_space=pltpu.VMEM)
    smem = pl.BlockSpec(memory_space=pltpu.SMEM)
    hbm = pl.BlockSpec(memory_space=pl.ANY)
    count = 2 * chips
    buffer = pltpu.VMEM((count, rows // count, width), BF16)
    sems = lambda *shape: [pltpu.SemaphoreType.DMA(shape), pltpu.SemaphoreType.DMA(shape)]
    qkv, side = CONV_CH, VAL + LANES
    held = [(part, cols) for cols in (qkv, side, VAL, units, units, units, units, units)]
    spread = [(2 * chips * part, qkv), (2 * chips * part, side)]
    moved = [(2 * part, cols) for cols in (qkv, side, VAL, units)]
    shapes = [(2, rows, width), (4 * rows, width), (rows, width)] + held + spread + moved
    halved = (2 * part, qkv // 2)
    own = [(part, qkv), (part, side), (part, VAL), (part, units), halved, halved, moved[1]]
    return carry_call(
        functools.partial(deal_kernel, chips), Jobs([], chips), (),
        [smem, smem] + [vmem] * 13,
        [vmem, hbm] + [vmem] * 9 + [hbm] * 6,
        [jax.ShapeDtypeStruct(shape, BF16) for shape in shapes],
        [buffer, buffer, pltpu.VMEM((LANES, LANES), F32)]
        + [pltpu.VMEM(shape, BF16) for shape in own]
        + [pltpu.VMEM((4 * rows, width), BF16)] + sems(2, PIECES) + [pltpu.SemaphoreType.DMA((4,))]
        + sems(PIECES) + sems(count) + sems(count)
        + [pltpu.SemaphoreType.DMA((max(9, chips + 1),))] * 16,
        (order, lengths, x, gain, cotangent, *raw), number, "deal_and_gather", rows * width * 20,
    )[0]


def small_rows(width):
    rows = (4 * width + 2 * VAL) // LANES + 1
    return rows + -rows % 8


def assemble(small, mix0, mix1, ffn0, ffn1, heads0, heads1, scalars0, scalars1):
    small[...] = jnp.zeros(small.shape, F32)
    at = 0
    for term in (mix0, mix1, ffn0, ffn1, heads0, heads1):
        for r in range(term.shape[1] // LANES):
            small[at : at + 1, :] = term[:, r * LANES : (r + 1) * LANES]
            at += 1
    head = lax.axis_index("zl") * 2 + lax.axis_index("core")
    lane = lax.broadcasted_iota(jnp.int32, (1, LANES), 1)
    row = jnp.zeros((1, LANES), F32)
    values = (scalars0[0:1, :], scalars1[0:1, :], scalars0[1:2, :], scalars1[1:2, :])
    for place, value in enumerate(values):
        row = row + jnp.where(lane == place * 4 + head, value, 0.0)
    small[at : at + 1, :] = row


def final_kernel(
    chips, jobs, order_ref, partial, x_hbm, gain_ref, grad_hbm, *refs
):
    terms, refs = refs[:7], refs[7:]
    (in_ref, aux_ref), refs = refs[:2], refs[2:]
    home_ref, total_ref, *homes = refs[:5]
    refs = refs[5:]
    cut = [pl.ds(0, CONV_CH), pl.ds(CONV_CH, VAL)]
    grads = [in_ref.at[:, cut[0]], in_ref.at[:, cut[1]], aux_ref]
    (away_held, own_held, x_ref, grad_ref, loads, beside_far, beside_own, sums, far, last, back,
     picked, small, by_plane, by_z, plane_sum,
     send, recv, role_send, role_recv, plane_send, plane_recv, small_send, small_recv, z_send,
     z_recv), refs = refs[:26], refs[26:]
    reduces, returns = [], []
    for at in range(3):
        summed, four, refs = refs[0], refs[1:5], refs[5:]
        buffers = len(Reduce.buffers(grads[at].shape, chips))
        reduces.append(Reduce(grads[at], summed, four[0], four[1], chips, refs[:buffers]))
        returns.append(FromPlane(summed, homes[at], four[2], four[3], chips))
        refs = refs[buffers:]
    plane, trade = Plane(chips), Trade(chips)
    scatter = Scatter(
        partial, beside_far, beside_own, sums, far, send, recv, (away_held, own_held, loads)
    )
    scatter.load()
    rows_in = [
        pltpu.make_async_copy(x_hbm.at[trade.zl], x_ref, loads.at[2]),
        pltpu.make_async_copy(grad_hbm.at[trade.zl], grad_ref, loads.at[3]),
    ]
    load_all(rows_in)
    count = plane.count
    part = x_ref.shape[0] // count
    rows = lambda index: pl.ds(pl.multiple_of(index * part, part), part)
    tier = trade.zp * 2 + trade.zl
    tier_device = lambda at: at_device(trade.chip, trade.core, at // 2, at % 2)
    for k in range(1, 4):
        signal(tier_device(lax.rem(tier + k, 4)))
    expected = plane.greet() + trade.greet_roles() + greet_group() + jobs.greet() + 3
    for job in reduces + returns:
        expected = expected + job.greet()
    wait_greetings(expected)
    scatter.start()
    reduces[0].start()
    jobs.start()
    dgain = jnp.zeros((1, x_ref.shape[1]), F32)
    for copy in rows_in:
        copy.wait()
    to_homes = []
    size = x_ref.shape[0] // PIECES
    parts = max(size // part, 1)
    for p in range(PIECES):
        at = scatter.local(p)
        grad, piece = norm_back(scatter.total(p), x_ref[at, :].astype(F32), gain_ref[0:1, :].astype(F32))
        dgain = dgain + piece
        last[at, :] = (grad + grad_ref[at, :]).astype(BF16)
        for index in range(p * parts, (p + 1) * parts):
            copy = remote(last.at[rows(index)], back.at[trade.slot], role_send.at[index],
                          role_recv.at[trade.slot], trade.home(index))
            mine = trade.home_mine(index)
            unless(mine, copy.start)

            @pl.when(mine)
            def _():
                back[trade.slot] = last[rows(index), :]

            to_homes.append((copy, mine))
    assemble(small, dgain, *terms)
    small_out, small_in = [], []
    for j in range(1, count):
        to, source = plane.to(j), plane.source(j)
        small_out.append(
            remote(small, by_plane.at[plane.own], small_send.at[j], small_recv.at[j], plane.device(to))
        )
        small_in.append(
            remote(small, by_plane.at[source], small_send.at[j], small_recv.at[j], plane.device(source))
        )
    for copy in small_out:
        copy.start()
    by_plane[plane.own] = small[...]
    reduces[0].middle()
    reduces[1].start()
    reduces[2].start()
    for slot in range(count):
        arrival = remote(last.at[rows(0)], back.at[slot], role_send.at[0], role_recv.at[slot],
                         trade.role(slot))
        unless(trade.role_mine(slot), arrival.wait_recv)
    reduces[0].finish()
    returns[0].start()
    outward, inward = [], []
    for j in range(count):
        to, source = plane.to(j), plane.source(j)
        at = jnp.int32(0)
        for slot in range(count):
            at = jnp.where(order_ref[slot] == to, slot, at)
        picked[j] = back[at]
        if j == 0:
            home_ref[rows(plane.own), :] = picked[0]
            continue
        copy = remote(picked.at[j], home_ref.at[rows(plane.own)], plane_send.at[j], plane_recv.at[j],
                      plane.device(to))
        copy.start()
        outward.append(copy)
        inward.append(
            remote(picked.at[j], home_ref.at[rows(source)], plane_send.at[j], plane_recv.at[j],
                   plane.device(source))
        )
    for job in reduces[1:]:
        job.middle()
    jobs.middle()
    for reduce, back_home in zip(reduces[1:], returns[1:]):
        reduce.finish()
        back_home.start()
    for copy in small_in:
        copy.wait_recv()
    total = by_plane[0]
    for index in range(1, count):
        total = total + by_plane[index]
    plane_sum[...] = total
    z_out, z_in = [], []
    for k in range(1, 4):
        to, source = lax.rem(tier + k, 4), lax.rem(tier + 4 - k, 4)
        z_out.append(remote(plane_sum, by_z.at[tier], z_send.at[k], z_recv.at[k], tier_device(to)))
        z_in.append(remote(plane_sum, by_z.at[source], z_send.at[k], z_recv.at[k], tier_device(source)))
    for copy in z_out:
        copy.start()
    by_z[tier] = total
    for copy in z_in:
        copy.wait_recv()
    total_ref[...] = (by_z[0] + by_z[1]) + (by_z[2] + by_z[3])
    for copy in inward:
        copy.wait_recv()
    scatter.finish()
    for copy, mine in to_homes:
        unless(mine, copy.wait_send)
    for copy in small_out + z_out + outward:
        copy.wait_send()
    jobs.finish()
    for job in returns:
        job.finish()


def final_step(order, partial, x, gain, grad, terms, grads, chips, jobs, number):
    _, rows, width = x.shape
    small = jax.ShapeDtypeStruct((small_rows(width), LANES), F32)
    vmem = pl.BlockSpec(memory_space=pltpu.VMEM)
    count = 2 * chips
    block = pltpu.VMEM((rows, width), BF16)
    parted = pltpu.VMEM((count, rows // count, width), BF16)
    hbm = pl.BlockSpec(memory_space=pl.ANY)
    chained = []
    pieces = [(grads[0].shape[0], cols) for cols in (CONV_CH, VAL, LANES)]
    for a in pieces:
        chained.append(pltpu.VMEM(Reduce.result(a, chips), BF16))
        chained += [pltpu.SemaphoreType.DMA((max(9, chips + 1),))] * 4
        chained += Reduce.buffers(a, chips)
    sems = lambda *shape: [pltpu.SemaphoreType.DMA(shape), pltpu.SemaphoreType.DMA(shape)]
    return carry_call(
        functools.partial(final_kernel, chips), jobs, (),
        [pl.BlockSpec(memory_space=pltpu.SMEM), hbm, hbm, vmem, hbm] + [vmem] * 7 + [hbm] * 2,
        [vmem, vmem] + [hbm] * 3,
        [
            jax.ShapeDtypeStruct((rows, width), BF16),
            jax.ShapeDtypeStruct(small.shape, F32),
        ]
        + [
            jax.ShapeDtypeStruct(FromPlane.result(Reduce.result(a, chips), chips), BF16)
            for a in pieces
        ],
        [block] * 2 + [pltpu.VMEM((rows, width), x.dtype), pltpu.VMEM((rows, width), F32)]
        + [pltpu.SemaphoreType.DMA((4,))] + [block] * 5 + [parted] * 2
        + [
            pltpu.VMEM(small.shape, F32), pltpu.VMEM((count,) + small.shape, F32),
            pltpu.VMEM((4,) + small.shape, F32), pltpu.VMEM(small.shape, F32),
        ]
        + sems(3, PIECES) + sems(count) + sems(count) + sems(count) + sems(4) + chained,
        (order, partial, x, gain, grad, *terms, *grads), number, "final_step", rows * width * 20,
    )


def only_jobs_kernel(jobs):
    wait_greetings(jobs.greet())
    jobs.start()
    jobs.middle()
    jobs.finish()


def only_jobs(jobs, number):
    return carry_call(only_jobs_kernel, jobs, (), [], [], [], [], (), number, "weights_back", 0)[1]


def weights_out_kernel(small_ref, home_ref, *refs):
    ins, outs = refs[:14], refs[14:]
    for layer in range(2):
        total = lambda ref: ref[0].astype(F32) + ref[1].astype(F32)
        qkv, head_gate, aux, out, gate, up, down = (
            total(ref) for ref in ins[7 * layer : 7 * layer + 7]
        )
        outs[0][layer] = qkv[:, :KEY]
        outs[1][layer] = qkv[:, KEY : 2 * KEY]
        outs[2][layer] = qkv[:, 2 * KEY :]
        outs[3][layer] = head_gate
        turned = aux.T
        outs[4][layer] = turned[0:2, :]
        outs[14][layer] = turned[2:6, :]
        outs[5][layer] = out.T
        outs[6][layer] = gate.T
        outs[7][layer] = up.T
        outs[8][layer] = down.T
    outs[15][...] = home_ref[...].astype(F32)[:, None, :]
    at = 0
    for ref in outs[9:12]:
        for layer in range(2):
            for r in range(ref.shape[1] // LANES):
                ref[layer : layer + 1, r * LANES : (r + 1) * LANES] = small_ref[at : at + 1, :]
                at += 1
    heads = outs[12].shape[1]
    for member in range(2):
        for layer in range(2):
            first = (2 * member + layer) * heads
            outs[12 + member][layer : layer + 1, :] = small_ref[at : at + 1, first : first + heads]


def weights_out(small, home, first, second, heads):
    width = home.shape[1]
    rows, units = first[0].shape[1], first[6].shape[2]
    shapes = [
        (2, rows, KEY), (2, rows, KEY), (2, rows, VAL), (2, rows, VAL), (2, 2, rows), (2, VAL, rows),
        (2, units, rows), (2, units, rows), (2, units, rows),
        (2, width), (2, width), (2, VAL), (2, heads), (2, heads), (2, 4, rows),
        (home.shape[0], 1, width),
    ]
    vmem = pl.BlockSpec(memory_space=pltpu.VMEM)
    return pl.pallas_call(
        weights_out_kernel,
        in_specs=[vmem] * 16,
        out_specs=[vmem] * 16,
        out_shape=[jax.ShapeDtypeStruct(shape, F32) for shape in shapes],
        compiler_params=pltpu.CompilerParams(vmem_limit_bytes=56 * 1024 * 1024),
        name="weights_out",
    )(small, home, *first, *second)


def ffn_parts(x, gate_ref, up_ref):
    gate, up = mm(x, gate_ref[...]), mm(x, up_ref[...])
    act, sig = silu_of(gate)
    return gate, up, act, sig


def begin_jobs(jobs, at, steps, turns=None):
    if jobs.kinds:
        @pl.when(at == 0)
        def _():
            wait_greetings(jobs.greet())
            jobs.start()

        early, late = turns or (steps // 2, steps - 1)

        @pl.when(at == early)
        def _():
            jobs.middle(late=False)

        @pl.when(at == late)
        def _():
            jobs.middle(late=True)


def end_jobs(jobs, at, steps):
    if jobs.kinds:
        @pl.when(at == steps - 1)
        def _():
            jobs.finish()


def ffn_forward_kernel(jobs, x_ref, gate_ref, up_ref, down_ref, part_ref):
    at, steps = pl.program_id(0), pl.num_programs(0)
    begin_jobs(jobs, at, steps)
    _, up, act, _ = ffn_parts(x_ref[...], gate_ref, up_ref)
    part_ref[...] = mm((act * up).astype(BF16), down_ref[...], NT).astype(BF16)
    end_jobs(jobs, at, steps)


def whole(shape):
    return pl.BlockSpec(shape, lambda i: (0, 0), pipeline_mode=pl.Buffered(1))


def ffn_forward(x, weights, jobs, number):
    length, width = x.shape
    rows = pl.BlockSpec((CHUNK, width), lambda i: (i, 0))
    return carry_call(
        ffn_forward_kernel, jobs, (length // CHUNK,),
        [rows] + [whole(weight.shape) for weight in weights], [rows],
        [jax.ShapeDtypeStruct((length, width), BF16)], [], (x, *weights), number, "ffn_forward",
        4 * 10**9,
    )


def ffn_backward_kernel(both, jobs, x_ref, g_ref, gate_ref, up_ref, down_ref, *refs):
    outs, (low_gate, low_up, hidden_ref, x_held, g_held) = refs[:-5], refs[-5:]
    if both:
        residual_ref, outs = outs[0], outs[1:]
    part_ref, dgate_ref, dup_ref, ddown_ref = outs[:4]
    at, steps = pl.program_id(0), pl.num_programs(0)
    chunks = steps // 2
    begin_jobs(jobs, at, steps)

    @pl.when(at < chunks)
    def _():
        rows = pl.ds(pl.multiple_of(at * CHUNK, CHUNK), CHUNK)
        x, g = x_ref[...], g_ref[...]
        x_held[rows, :] = x
        g_held[rows, :] = g
        gate, up, act, sig = ffn_parts(x, gate_ref, up_ref)
        hidden = (act * up).astype(BF16)
        hidden_ref[rows, :] = hidden
        if both:
            own = lax.axis_index("zl") * 2 + lax.axis_index("core")
            outs[4][...] = (
                mm(hidden, down_ref[...], NT) + jnp.where(at == own, residual_ref[lax.axis_index("zl")], 0.0)
            ).astype(BF16)
        dhidden = mm(g, down_ref[...])
        dgate = (dhidden * up * (sig * (1.0 + gate * (1.0 - sig)))).astype(BF16)
        dup = (dhidden * act).astype(BF16)
        low_gate[rows, :] = dgate
        low_up[rows, :] = dup
        part_ref[...] = (mm(dgate, gate_ref[...], NT) + mm(dup, up_ref[...], NT)).astype(BF16)

    @pl.when(at >= chunks)
    def _():
        columns = pl.ds(pl.multiple_of((at - chunks) * CHUNK, CHUNK), CHUNK)
        dgate_ref[...] = mm(x_held[:, columns], low_gate[...], TN).astype(BF16)
        dup_ref[...] = mm(x_held[:, columns], low_up[...], TN).astype(BF16)
        ddown_ref[...] = mm(g_held[:, columns], hidden_ref[...], TN).astype(BF16)

    end_jobs(jobs, at, steps)


def ffn_backward(x, g, weights, jobs, number, residual=None):
    both = residual is not None
    length, width = x.shape
    chunks = length // CHUNK
    units = weights[0].shape[1]
    assert length == width and (not both or residual.shape[1] == CHUNK)
    rows = pl.BlockSpec((CHUNK, width), lambda i: (jnp.minimum(i, chunks - 1), 0))
    late = pl.BlockSpec((CHUNK, units), lambda i: (jnp.maximum(i - chunks, 0), 0))
    out = lambda cols: jax.ShapeDtypeStruct((length, cols), BF16)
    return carry_call(
        functools.partial(ffn_backward_kernel, both), jobs, (2 * chunks,),
        [rows, rows] + [whole(weight.shape) for weight in weights] + [
            pl.BlockSpec((2, CHUNK, width), lambda i: (0, 0, 0), pipeline_mode=pl.Buffered(1))
        ] * both,
        [rows] + [late] * 3 + [rows] * both,
        [out(width)] + [out(units)] * 3 + [out(width)] * both,
        [pltpu.VMEM((length, units), BF16)] * 3 + [pltpu.VMEM((length, width), BF16)] * 2,
        (x, g, *weights) + ((residual,) if both else ()), number, "ffn_backward", 12 * 10**9,
    )


class Held:
    def __init__(self, at, sources, held, sems):
        self.at = at
        self.copies = [
            pltpu.make_async_copy(source, ref, sems.at[index])
            for index, (source, ref) in enumerate(zip(sources, held))
        ]

    def start(self):
        @pl.when(self.at == 0)
        def _():
            for copy in self.copies:
                copy.start()

    def ready(self, index):
        pl.when(self.at == 0)(self.copies[index].wait)


def held_scratch(weights):
    return [pltpu.VMEM(weight.shape, BF16) for weight in weights] + [
        pltpu.SemaphoreType.DMA((len(weights),))
    ]


def row_major(x):
    return with_layout_constraint(x, Layout(major_to_minor=tuple(range(x.ndim))))


def linear(sizes, index):
    place = 0
    for size, at in zip(sizes, index):
        place = place * size + at
    return place


class Roles:
    def __init__(self):
        self.sizes = tuple(lax.axis_size(name) for name in AXES)
        self.chips, self.cores, self.zps, self.zls = self.sizes
        assert self.cores == 2 and self.zps == 2 and self.zls == 2

    def every(self):
        for chip in range(self.chips):
            for core in range(2):
                for zp in range(2):
                    for zl in range(2):
                        yield chip, core, zp, zl

    def rows_pairs(self):
        pairs = []
        for chip, core, zp, zl in self.every():
            slot, part = chip * 2 + zp, zl * 2 + core
            source = linear(self.sizes, (slot // 2, slot % 2, part // 2, part % 2))
            pairs.append((source, linear(self.sizes, (chip, core, zp, zl))))
        return pairs

    def weight_pairs(self, which):
        pairs = []
        for chip, core, zp, zl in self.every():
            head = zp * 2 + zl
            to = (chip, head % 2, core ^ which, head // 2)
            pairs.append(
                (linear(self.sizes, (chip, core, zp, zl)), linear(self.sizes, to))
            )
        return pairs


def flipped(pairs):
    return [(b, a) for a, b in pairs]


def chip_gather(ordered):
    return lax.all_gather(ordered, "chip", axis=0, tiled=True)


def to_plane(pack, roles):
    halves = [lax.ppermute(pack, AXES, roles.weight_pairs(which)) for which in range(2)]
    swap = lax.axis_index("zp") == 1
    return jnp.concatenate(
        [jnp.where(swap, halves[1], halves[0]), jnp.where(swap, halves[0], halves[1])], axis=0
    )


def summed(parts, kind):
    return jnp.sum(parts.astype(F32), axis=0).astype(kind)


def deal(values, order):
    spread = lax.all_to_all(values, ("chip", "core"), split_axis=2, concat_axis=1, tiled=True)
    picked = jnp.take(spread, order, axis=1)
    return lax.all_to_all(picked, ("chip", "core"), split_axis=1, concat_axis=2, tiled=True)


def shards(
    tokens, lengths, order, norm_mix, w_query, w_key, w_value, w_gate, w_decay, conv_filter,
    log_rate, step_bias, norm_heads, w_out, norm_ffn, w_ffn_gate, w_ffn_up, w_ffn_down, cotangent,
):
    roles = Roles()
    layer_count = w_query.shape[0]
    assert layer_count == 2
    heads_total = log_rate.shape[1]
    chip, core, zp, zl = (lax.axis_index(name) for name in AXES)
    head = zl * 2 + core
    rows_local, slots_local, width = tokens.shape
    assert slots_local == 1 and w_decay.shape[2] == 1
    slot_total = order.shape[0]
    units = w_ffn_gate.shape[2]
    rows_part = w_query.shape[1]
    to_roles = roles.rows_pairs()

    def carry(*jobs):
        return Jobs(list(jobs), roles.chips)

    scalars = (log_rate, step_bias)
    kernel_deal = rows_local % (16 * slot_total) == 0
    if kernel_deal:
        turned = lambda w: w.transpose(0, 2, 1)
        raw = (
            w_query, w_key, w_value, w_gate, turned(w_decay[:, :, 0, :]), conv_filter[:, :, 0, :],
            w_out, turned(w_ffn_gate), turned(w_ffn_up), w_ffn_down,
        )
        (residual, rows_in, start, qkv_next, side_next, out_next, gate_next, up_first, up_next,
         down_first, down_next, qkv0, side0, _, _, out_wide, gate_wide) = deal_and_gather(
            order, lengths, tokens[:, 0, :], norm_mix, cotangent[:, 0, :], raw, roles.chips, 1
        )
    else:
        packs = []
        for layer in range(layer_count):
            aux = jnp.concatenate([w_decay[layer, :, 0, :], conv_filter[layer, :, 0, :].T], axis=1)
            aux = jnp.pad(aux, ((0, 0), (0, LANES - aux.shape[1])))
            packs.append(
                [
                    row_major(pack) for pack in (
                        jnp.concatenate([w_query[layer], w_key[layer], w_value[layer]], axis=1),
                        jnp.concatenate([w_gate[layer], aux], axis=1),
                        w_out[layer].T, w_ffn_gate[layer], w_ffn_up[layer], w_ffn_down[layer].T,
                    )
                ]
            )
        (qkv0, side0, out_wide, gate_wide, up_first, down_first) = packs[0]
        (qkv_next, side_next, out_next, gate_next, up_next, down_next) = packs[1]
        positions = (zp * 2 + zl) * rows_local + jnp.arange(rows_local)
        start = cotangent[:, 0, :] * (positions < lengths[order[chip * 2 + core]]).astype(BF16)[:, None]
        residual = lax.ppermute(deal(tokens, order)[:, 0, :], AXES, to_roles)
        (residual, rows_in), _ = first_gather(residual, norm_mix, 0, carry(), 1)
        qkv0, side0 = (chip_gather(to_plane(pack, roles)) for pack in (qkv0, side0))
        out_wide, gate_wide = (to_plane(pack, roles) for pack in (out_wide, gate_wide))

    (heads0, *kept0), (out0, gate0, up_wide, down_wide, qkv_wide) = mixer_forward(
        0, rows_in, qkv0, side0, norm_heads, scalars,
        carry((Spread, out_wide), (Spread, gate_wide), (ToPlane, up_first), (ToPlane, down_first),
              (ToPlane, qkv_next)),
        2,
    )
    rows_in0, residual0 = rows_in, residual
    (middle0, rows_ffn0), (up0, down0, side_wide, gradient) = mixer_bridge(
        heads0, out0, residual0, norm_ffn, 0,
        carry((Spread, up_wide), (Spread, down_wide), (ToPlane, side_next), (ToRole, start)), 3,
    )
    ffn0 = (gate0, up0, down0)
    (part,), _ = ffn_forward(rows_ffn0, ffn0, carry(), None)
    (residual1, rows_in1), (qkv1, side1, out_wide, down_wide) = forward_bridge(
        part, middle0, norm_mix, 1,
        carry((Spread, qkv_wide), (Spread, side_wide), (ToPlane, out_next), (ToPlane, down_next)), 4,
    )
    (heads1, *kept1), (out1, down1, gate_wide, up_wide, grad_rows) = mixer_forward(
        1, rows_in1, qkv1, side1, norm_heads, scalars,
        carry((Spread, out_wide), (Spread, down_wide), (ToPlane, gate_next), (ToPlane, up_next),
              (Share, gradient)),
        5,
    )
    (middle1, rows_ffn1), (gate1, up1) = mixer_bridge(
        heads1, out1, residual1, norm_ffn, 1, carry((Spread, gate_wide), (Spread, up_wide)), 6
    )
    ffn1 = (gate1, up1, down1)
    (part, dgate1, dup1, ddown1, part_out), _ = ffn_backward(
        rows_ffn1, grad_rows, ffn1, carry(), None, residual=middle1
    )

    (gradient, grad_rows, dgain_ffn1, dout1), (dgate1, dup1) = backward_bridge(
        part, middle1, norm_ffn, 1, grad_rows, carry((Reduce, dgate1), (Reduce, dup1)), 7, heads1
    )
    (part, din1, daux1, dgain1, dscalars1), jobs_results = mixer_backward(
        1, grad_rows, rows_in1, qkv1, side1, out1, norm_heads, scalars, kept1,
        carry((Reduce, ddown1), (Reduce, dout1), (FromPlane, dgate1), (FromPlane, dup1),
              (ShareSum, part_out)),
        8,
    )
    ddown1, dout1, gate_home1, up_home1, mixed = jobs_results
    (gradient, grad_rows, dgain_mix1), (dqkv1, daux1, mixed) = backward_bridge(
        part, residual1, norm_mix, 1, gradient,
        carry((Reduce, din1, (0, CONV_CH)), (Reduce, daux1), (FromRole, mixed)), 9,
    )
    (part, dgate0, dup0, ddown0), (side1, qkv_home1, aux_home1, down_home1) = ffn_backward(
        rows_ffn0, grad_rows, ffn0,
        carry((Reduce, din1, (CONV_CH, VAL)), (FromPlane, dqkv1), (FromPlane, daux1),
              (FromPlane, ddown1)),
        14,
    )
    (gradient, grad_rows, dgain_ffn0, dout0), (dgate0, dup0) = backward_bridge(
        part, middle0, norm_ffn, 0, gradient,
        carry((Reduce, dgate0), (Reduce, dup0)), 10, heads0,
    )
    (part, din0, daux0, dgain0, dscalars0), jobs_results = mixer_backward(
        0, grad_rows, rows_in0, qkv0, side0, out0, norm_heads, scalars, kept0,
        carry((Reduce, ddown0), (Reduce, dout0), (FromPlane, dgate0), (FromPlane, dup0),
              (FromPlane, side1), (FromPlane, dout1)),
        11,
    )
    ddown0, dout0, gate_home0, up_home0, side_home1, out_home1 = jobs_results
    terms = (dgain_mix1, dgain_ffn0, dgain_ffn1, dgain0, dgain1, dscalars0, dscalars1)
    last = (din0, daux0)
    last_jobs = carry((FromPlane, ddown0), (FromPlane, dout0))
    if kernel_deal:
        (home, flat, *last), results = final_step(
            order, part, residual0, norm_mix, gradient, terms, last, roles.chips, last_jobs, 12
        )
    else:
        (gradient, dgain_mix), results = backward_last(
            part, residual0, norm_mix, 0, gradient, last_jobs, 12
        )
        mine = (jnp.arange(heads_total) == head).astype(F32)
        flat = jnp.concatenate(
            [dgain_mix[0], *(term[0] for term in terms[:5])]
            + [mine * term[row, 0] for row in range(2) for term in terms[5:]]
        )
        flat = jnp.pad(flat, (0, small_rows(width) * LANES - flat.shape[0])).reshape(-1, LANES)
        flat = lax.psum(flat, AXES)
        dealt_grad = lax.ppermute(gradient, AXES, flipped(to_roles))
        places = jnp.arange(slot_total, dtype=jnp.int32)
        inverse = jnp.sum(jnp.where(order[None, :] == places[:, None], places[None, :], 0), axis=1)
        home = deal(dealt_grad[:, None, :], inverse)[:, 0, :]
        last = only_jobs(
            carry((Reduce, din0, (0, CONV_CH)), (Reduce, din0, (CONV_CH, VAL)), (Reduce, daux0)), 13
        )
        last = only_jobs(carry(*[(FromPlane, a) for a in last]), 15)
    down_home0, out_home0 = results
    qkv_home0, side_home0, aux_home0 = last
    first = (qkv_home0, side_home0, aux_home0, out_home0, gate_home0, up_home0, down_home0)
    second = (qkv_home1, side_home1, aux_home1, out_home1, gate_home1, up_home1, down_home1)
    if rows_part % LANES == 0:
        outs = weights_out(flat, home, first, second, heads_total)
    else:
        flat = flat.reshape(-1)
        small, at = [], 0
        for size in (width, width, VAL, heads_total, heads_total):
            small.append(flat[at : at + layer_count * size].reshape(layer_count, size))
            at += layer_count * size
        qkv, side, aux, out, gate, up, down = (
            jnp.stack([summed(a, F32), summed(b, F32)]) for a, b in zip(first, second)
        )
        turned = lambda a: a.transpose(0, 2, 1)
        outs = [
            qkv[:, :, :KEY], qkv[:, :, KEY : 2 * KEY], qkv[:, :, 2 * KEY :], side, turned(aux)[:, :2], turned(out), turned(gate), turned(up),
            turned(down), *small, turned(aux)[:, 2:6], home.astype(F32)[:, None, :],
        ]
    return (
        mixed[:, None, :],
        outs[15],
        outs[9],
        outs[0], outs[1], outs[2], outs[3],
        outs[4].transpose(0, 2, 1)[:, :, None, :],
        outs[14][:, :, None, :],
        outs[12],
        outs[13],
        outs[11],
        outs[5],
        outs[10],
        outs[6].transpose(0, 2, 1), outs[7].transpose(0, 2, 1), outs[8],
    )


def solution(mesh):
    dp, tensor = mesh.devices.shape
    mesh = Mesh(mesh.devices.reshape(dp // 2, 2, tensor // 2, 2), AXES)
    d, t = ("chip", "core"), ("zp", "zl")
    rows = P(t, d, None)
    by_rows, by_columns = P(None, d, t), P(None, t, d)
    heads, filters = P(None, d, t, None), P(None, None, t, d)
    return jax.shard_map(
        shards,
        mesh=mesh,
        in_specs=(
            rows, P(), P(), P(), by_rows, by_rows, by_rows, by_rows, heads, filters,
            P(), P(), P(), by_columns, P(), by_rows, by_rows, by_columns, rows,
        ),
        out_specs=(
            rows, rows, P(), by_rows, by_rows, by_rows, by_rows, heads, filters,
            P(), P(), P(), by_columns, P(), by_rows, by_rows, by_columns,
        ),
        check_vma=False,
    )
```

```python
import functools
import jax
import jax.numpy as jnp
from jax import lax
from jax.experimental import pallas as pl
from jax.experimental.layout import Layout, with_layout_constraint
from jax.experimental.pallas import tpu as pltpu
from jax.sharding import Mesh, PartitionSpec as P

CHUNK = 256
LANES = 128
KEY = 256
VAL = 512
CONV_CH = 2 * KEY + VAL
F32 = jnp.float32
BF16 = jnp.bfloat16
NN = (((1,), (0,)), ((), ()))
NT = (((1,), (1,)), ((), ()))
TN = (((0,), (0,)), ((), ()))


def mm(a, b, dims=NN):
    return lax.dot_general(
        a.astype(BF16), b.astype(BF16), dims, preferred_element_type=F32
    )


def split_low(a):
    high = a.astype(BF16)
    return high, (a - high.astype(F32)).astype(BF16)


def mm3(a, b, dims=NN):
    a_high, a_low = split_low(a)
    b_high, b_low = split_low(b)
    dot = functools.partial(
        lax.dot_general, dimension_numbers=dims, preferred_element_type=F32
    )
    return dot(a_high, b_high) + (dot(a_high, b_low) + dot(a_low, b_high))


def mm_exact_left(a, b, dims=NN):
    a = a.astype(BF16)
    high = b.astype(BF16)
    rest = b - high.astype(F32)
    mid = rest.astype(BF16)
    low = (rest - mid.astype(F32)).astype(BF16)
    dot = functools.partial(
        lax.dot_general, dimension_numbers=dims, preferred_element_type=F32
    )
    return dot(a, high) + (dot(a, mid) + dot(a, low))


def iotas():
    rows = lax.broadcasted_iota(jnp.int32, (CHUNK, CHUNK), 0)
    cols = lax.broadcasted_iota(jnp.int32, (CHUNK, CHUNK), 1)
    return rows, cols


def wide(col_block, width):
    return jnp.concatenate([col_block] * (width // LANES), axis=1)


def rates_of(rates, rate, bias):
    write = jax.nn.sigmoid(jnp.broadcast_to(rates[:, 0:1], (CHUNK, LANES)))
    logit = jnp.broadcast_to(rates[:, 1:2], (CHUNK, LANES)) + bias
    soft = jnp.maximum(logit, 0.0) + jnp.log1p(jnp.exp(-jnp.abs(logit)))
    return write, -rate * soft, jax.nn.sigmoid(logit)


def head_scalars(scalars_ref, layer):
    head = lax.axis_index("zl") * 2 + lax.axis_index("core")
    rate_ref, bias_ref = scalars_ref
    here = lax.broadcasted_iota(jnp.int32, (1, rate_ref.shape[1]), 1) == head
    pick = lambda ref: jnp.sum(
        jnp.where(here, ref[layer : layer + 1, :].astype(F32), 0.0), axis=1, keepdims=True
    )
    return jnp.exp(pick(rate_ref)), pick(bias_ref)


def decay_terms(step, rows, cols):
    inclusive = (rows >= cols).astype(BF16)
    total = mm_exact_left(inclusive, step)
    spread = wide(total, CHUNK) - jnp.concatenate([total.T] * (CHUNK // LANES), axis=0)
    decay = jnp.where(rows >= cols, jnp.exp(jnp.minimum(spread, 0.0)), 0.0)
    last = jnp.broadcast_to(total[CHUNK - 1 : CHUNK, :], (CHUNK, LANES))
    return decay, jnp.exp(total), jnp.exp(last - total), jnp.exp(last)


def solve_unit(coupling, rows, cols):
    unit = jnp.where(rows == cols, 1.0, 0.0)
    same = ((rows >> 1) == (cols >> 1)) & (rows != cols)
    inverse = unit - jnp.where(same, coupling, 0.0)
    for level in range(1, CHUNK.bit_length() - 1):
        between = ((rows >> (level + 1)) == (cols >> (level + 1))) & (
            (rows >> level) != (cols >> level)
        )
        part = jnp.where(between, coupling, 0.0)
        inverse = inverse - mm(mm(inverse, part), inverse)
    return inverse + mm(inverse, unit - inverse - mm3(coupling, inverse))


def silu_of(x):
    gate = jax.nn.sigmoid(x)
    return x * gate, gate


def conv_rows(padded_ref, taps_ref, start):
    result = padded_ref[pl.ds(start, CHUNK), :] * taps_ref[0:1, :]
    for j in range(1, 4):
        result = result + padded_ref[pl.ds(start + j, CHUNK), :] * taps_ref[j : j + 1, :]
    return result


def forward_kernel(
    layer, jobs, rate_ref, bias_ref, x_ref, qkv_hbm, side_hbm, gain_ref,
    heads_ref, proj_ref, conv_ref, gate_ref, rates_ref, inverse_ref, fresh_ref, o_ref, state_ref,
    padded, memory, taps_ref, w_qkv_ref, w_side_ref, sems,
):
    at = pl.program_id(0)
    held = Held(at, (qkv_hbm, side_hbm), (w_qkv_ref, w_side_ref), sems)
    held.start()
    begin_jobs(jobs, at, pl.num_programs(0), (pl.num_programs(0) - 1,) * 2)
    @pl.when(pl.program_id(0) == 0)
    def _():
        memory[...] = jnp.zeros_like(memory)
        padded[0:8, :] = jnp.zeros((8, CONV_CH), F32)

    x = x_ref[...]
    held.ready(0)
    qkv = mm(x, w_qkv_ref[...])
    held.ready(1)

    @pl.when(at == 0)
    def _():
        taps_ref[...] = w_side_ref[:, VAL:].astype(F32).T[2:6, :]

    rates = mm(x, w_side_ref[:, VAL:])
    rates_ref[...] = rates
    proj_ref[...] = qkv
    gate_in = mm(x, w_side_ref[:, :VAL])
    gate_ref[...] = gate_in
    padded[8 : 8 + CHUNK, :] = qkv
    conv = conv_rows(padded, taps_ref, 5)
    padded[0:8, :] = qkv[CHUNK - 8 :, :]
    conv_ref[...] = conv
    act, _ = silu_of(conv)
    q, k, v = act[:, :KEY], act[:, KEY : 2 * KEY], act[:, 2 * KEY :]
    q = q * (lax.rsqrt(jnp.sum(q * q, axis=1, keepdims=True) + 1e-6) * KEY**-0.5)
    k = k * lax.rsqrt(jnp.sum(k * k, axis=1, keepdims=True) + 1e-6)
    rows, cols = iotas()
    write, step, _ = rates_of(rates, *head_scalars((rate_ref, bias_ref), layer))
    decay, growth, rest, final = decay_terms(step, rows, cols)
    coupling = jnp.where(rows > cols, wide(write, CHUNK) * mm3(k, k, NT) * decay, 0.0)
    inverse = solve_unit(coupling, rows, cols)
    inverse_ref[...] = inverse.astype(BF16)
    within = mm(q, k, NT) * decay
    state = memory[...]
    state_ref[...] = state
    low_state = state.astype(BF16)
    source = wide(write, VAL) * (v - wide(growth, VAL) * mm(k, low_state))
    fresh = mm3(inverse, source)
    fresh_ref[...] = fresh
    o = wide(growth, VAL) * mm(q, low_state) + mm(within, fresh)
    o_ref[...] = o
    memory[...] = wide(final, VAL) * state + mm(k * wide(rest, KEY), fresh, TN)
    scaled = o * lax.rsqrt(jnp.mean(o * o, axis=1, keepdims=True) + 1e-5) * gain_ref[layer : layer + 1, :].astype(F32)
    heads = (scaled * silu_of(gate_in)[0]).astype(BF16)
    heads_ref[...] = heads
    end_jobs(jobs, pl.program_id(0), pl.num_programs(0))


def head_spec(value):
    return pl.BlockSpec(value.shape, lambda i: (0, 0))


def mixer_forward(layer, x, qkv, pack, gain, scalars, jobs, number):
    length, width = x.shape
    chunks = length // CHUNK
    row = lambda cols: pl.BlockSpec((CHUNK, cols), lambda i: (i, 0))
    out = lambda cols, kind: jax.ShapeDtypeStruct((length, cols), kind)
    return carry_call(
        functools.partial(forward_kernel, layer), jobs, (chunks,),
        [head_spec(scalars[0]), head_spec(scalars[1]), row(width), ANY_SPEC, ANY_SPEC, head_spec(gain)],
        [
            row(VAL), row(CONV_CH), row(CONV_CH), row(VAL), row(LANES), row(CHUNK), row(VAL), row(VAL),
            pl.BlockSpec((None, KEY, VAL), lambda i: (i, 0, 0)),
        ],
        [
            out(VAL, BF16), out(CONV_CH, F32), out(CONV_CH, F32), out(VAL, F32), out(LANES, F32),
            out(CHUNK, BF16), out(VAL, F32), out(VAL, F32),
            jax.ShapeDtypeStruct((chunks, KEY, VAL), F32),
        ],
        [
            pltpu.VMEM((CHUNK + 8, CONV_CH), F32), pltpu.VMEM((KEY, VAL), F32),
            pltpu.VMEM((4, CONV_CH), F32),
        ] + held_scratch((qkv, pack)),
        (*scalars, x, qkv, pack, gain), number, "mixer_forward", 16 * 10**9,
    )


def unit_back(grad, vector, scale):
    inv = lax.rsqrt(jnp.sum(vector * vector, axis=1, keepdims=True) + 1e-6)
    dot = jnp.sum(grad * vector, axis=1, keepdims=True)
    return (grad - vector * (inv * inv * dot)) * (inv * scale)


def backward_kernel(
    layer, jobs, rate_ref, bias_ref, g_ref, x_ref, out_hbm, qkv_hbm, side_hbm, gain_ref,
    proj_ref, halo_ref, conv_ref, gate_ref, rates_ref, inverse_ref, fresh_ref, o_ref, state_ref,
    part_ref, din_ref, daux_ref, dgain_ref, dscalars_ref,
    padded, dpadded, dmemory, taps_ref, dtaps_ref, daux_sum, x_held, dproj_ref,
    w_out_ref, w_qkv_ref, w_side_ref, sems,
):
    at, steps = pl.program_id(0), pl.num_programs(0)
    chunks = steps // 2
    last = chunks - 1
    held = Held(at, (out_hbm, qkv_hbm, side_hbm), (w_out_ref, w_qkv_ref, w_side_ref), sems)
    held.start()
    begin_jobs(jobs, at, steps, (chunks - 1, chunks // 2))

    @pl.when(at == 0)
    def _():
        dmemory[...] = jnp.zeros_like(dmemory)
        dpadded[CHUNK : CHUNK + 8, :] = jnp.zeros((8, CONV_CH), F32)
        dtaps_ref[...] = jnp.zeros_like(dtaps_ref)
        daux_sum[...] = jnp.zeros_like(daux_sum)
        dgain_ref[...] = jnp.zeros_like(dgain_ref)
        dscalars_ref[...] = jnp.zeros_like(dscalars_ref)

    @pl.when(at < chunks)
    def _():
        rows, cols = iotas()
        padded[8 : 8 + CHUNK, :] = proj_ref[...]
        padded[0:8, :] = jnp.where(at == last, 0.0, halo_ref[...])
        conv = conv_ref[...]
        act, sig = silu_of(conv)
        act_q, act_k, v = act[:, :KEY], act[:, KEY : 2 * KEY], act[:, 2 * KEY :]
        q = act_q * (lax.rsqrt(jnp.sum(act_q * act_q, axis=1, keepdims=True) + 1e-6) * KEY**-0.5)
        k = act_k * lax.rsqrt(jnp.sum(act_k * act_k, axis=1, keepdims=True) + 1e-6)
        rates = rates_ref[...]
        write, step, sig_decay = rates_of(rates, *head_scalars((rate_ref, bias_ref), layer))
        decay, growth, rest, final = decay_terms(step, rows, cols)
        growth_v = wide(growth, VAL)
        write_v = wide(write, VAL)
        low_q, low_k = q.astype(BF16), k.astype(BF16)
        below = rows > cols
        strict_decay = jnp.where(below, decay, 0.0)
        keys = mm(low_k, low_k, NT) * strict_decay * wide(write, CHUNK)
        within = mm(low_q, low_k, NT) * decay
        held.ready(0)
        dheads = mm(g_ref[...], w_out_ref[...])
        o = o_ref[...]
        gate_in = gate_ref[...]
        gate, gate_sig = silu_of(gate_in)
        inv = lax.rsqrt(jnp.mean(o * o, axis=1, keepdims=True) + 1e-5)
        normal = o * inv
        gain = gain_ref[layer : layer + 1, :].astype(F32)
        dgate = dheads * normal * gain * (gate_sig * (1.0 + gate_in * (1.0 - gate_sig)))
        dscaled = dheads * gate
        dgain_ref[...] += jnp.sum(dscaled * normal, axis=0, keepdims=True)
        dnormal = dscaled * gain
        do = inv * (dnormal - normal * jnp.mean(dnormal * normal, axis=1, keepdims=True))
        state = state_ref[...]
        low_state = state.astype(BF16)
        fresh = fresh_ref[...]
        low_fresh = fresh.astype(BF16)
        dstate = dmemory[...]
        low_dstate = dstate.astype(BF16)
        low_do = do.astype(BF16)
        k_rest = k * wide(rest, KEY)
        rest_dstate = mm(k_rest, low_dstate)
        dfresh = mm(within, low_do, TN) + rest_dstate
        dsource = mm(inverse_ref[...], dfresh, TN)
        low_dsource = dsource.astype(BF16)
        dv = write_v * dsource
        dread = -(growth_v * dv)
        low_dread = dread.astype(BF16)
        do_growth = growth_v * do
        low_do_growth = do_growth.astype(BF16)
        dwithin = mm(low_do, low_fresh, NT)
        dcoupling = -mm(low_dsource, low_fresh, NT)
        dkeys = dcoupling * strict_decay * wide(write, CHUNK)
        dpairs = dwithin * decay
        dq = mm(low_do_growth, low_state, NT) + mm(dpairs, low_k)
        dk = (
            mm(low_dread, low_state, NT)
            + mm(dpairs, low_q, TN)
            + mm(dkeys + dkeys.T, low_k)
            + wide(rest, KEY) * mm(low_fresh, low_dstate, NT)
        )
        dmemory[...] = (
            wide(final, VAL) * dstate + mm(low_q, low_do_growth, TN) + mm(low_k, low_dread, TN)
        )
        spread = dwithin * within + dcoupling * keys
        straddle = jnp.where(below, mm_exact_left((rows <= cols).astype(BF16), spread), 0.0)
        read_rows = jnp.sum(
            do_growth * mm(low_q, low_state) + dread * mm(low_k, low_state), axis=1, keepdims=True
        )
        rest_rows = jnp.sum(fresh * rest_dstate, axis=1, keepdims=True)
        carried = jnp.sum(dstate * state) * final[0:1, 0:1]
        suffix = mm_exact_left(
            (rows <= cols).astype(BF16), jnp.broadcast_to(read_rows, (CHUNK, LANES))
        ) + mm_exact_left((rows > cols).astype(BF16), jnp.broadcast_to(rest_rows, (CHUNK, LANES)))
        dstep = suffix + jnp.sum(straddle, axis=1, keepdims=True) + carried
        dlogit = dstep * (-head_scalars((rate_ref, bias_ref), layer)[0]) * sig_decay
        dwrite = (1.0 - write) * jnp.sum(dsource * fresh, axis=1, keepdims=True)
        lane = lax.broadcasted_iota(jnp.int32, (CHUNK, LANES), 1)
        drates = jnp.where(lane == 0, dwrite, jnp.where(lane == 1, dlogit, 0.0))
        low_drates = drates.astype(BF16)
        daux_sum[...] += mm(low_drates, x_ref[...], TN)
        dscalars_ref[0:1, :] += jnp.sum(dstep * step, axis=0, keepdims=True)
        dscalars_ref[1:2, :] += jnp.sum(dlogit, axis=0, keepdims=True)
        dact = jnp.concatenate(
            [unit_back(dq, act_q, KEY**-0.5), unit_back(dk, act_k, 1.0), dv], axis=1
        )
        dconv = dact * (sig * (1.0 + conv * (1.0 - sig)))
        dpadded[0:CHUNK, :] = dconv
        dtaps_ref[2:6, :] += jnp.concatenate(
            [
                jnp.sum(dconv * padded[5 + j : 5 + j + CHUNK, :], axis=0, keepdims=True)
                for j in range(4)
            ],
            axis=0,
        )
        held.ready(1)
        held.ready(2)

        @pl.when(at == 0)
        def _():
            taps_ref[...] = w_side_ref[:, VAL:].astype(F32).T[2:6, :]

        dqkv = dconv * taps_ref[3:4, :]
        for j in range(3):
            dqkv = dqkv + dpadded[pl.ds(3 - j, CHUNK), :] * taps_ref[j : j + 1, :]
        dpadded[CHUNK : CHUNK + 8, :] = dconv[0:8, :]
        low_dqkv, low_dgate = dqkv.astype(BF16), dgate.astype(BF16)
        place = block(last - at, CHUNK)
        dproj_ref[place, :CONV_CH] = low_dqkv
        dproj_ref[place, CONV_CH:] = low_dgate
        x_held[place, :] = x_ref[...]
        part_ref[...] = (
            mm(low_dqkv, w_qkv_ref[...], NT)
            + mm(low_dgate, w_side_ref[:, :VAL], NT)
            + mm(low_drates, w_side_ref[:, VAL:], NT)
        ).astype(BF16)

    @pl.when(at == last)
    def _():
        daux_ref[...] = (daux_sum[...] + dtaps_ref[...]).T.astype(BF16)

    @pl.when(at >= chunks)
    def _():
        columns = block(at - chunks, CHUNK)
        din_ref[...] = mm(x_held[:, columns], dproj_ref[...], TN).astype(BF16)

    end_jobs(jobs, at, steps)


def mixer_backward(layer, g, x, qkv, pack, w_out, gain, scalars, saved, jobs, number):
    proj, conv, gate_in, rates, inverse, fresh, o, states = saved
    length, width = g.shape
    chunks = length // CHUNK
    back = chunks - 1
    at = lambda i: jnp.maximum(back - i, 0)
    row = lambda cols: pl.BlockSpec((CHUNK, cols), lambda i: (at(i), 0))
    out = lambda cols, kind: jax.ShapeDtypeStruct((length, cols), kind)
    steps = CHUNK // 8
    return carry_call(
        functools.partial(backward_kernel, layer), jobs, (2 * chunks,),
        [head_spec(scalars[0]), head_spec(scalars[1]), row(width), row(width)]
        + [ANY_SPEC] * 3 + [head_spec(gain),
            row(CONV_CH),
            pl.BlockSpec((8, CONV_CH), lambda i: (jnp.maximum(at(i) * steps - 1, 0), 0)),
            row(CONV_CH), row(VAL), row(LANES), row(CHUNK), row(VAL), row(VAL),
            pl.BlockSpec((None, KEY, VAL), lambda i: (at(i), 0, 0)),
        ],
        [
            row(width),
            pl.BlockSpec((CHUNK, CONV_CH + VAL), lambda i: (jnp.maximum(i - chunks, 0), 0)),
            pl.BlockSpec((width, LANES), lambda i: (0, 0)),
            pl.BlockSpec((1, VAL), lambda i: (0, 0)),
            pl.BlockSpec((8, LANES), lambda i: (0, 0)),
        ],
        [
            out(width, BF16), jax.ShapeDtypeStruct((width, CONV_CH + VAL), BF16),
            jax.ShapeDtypeStruct((width, LANES), BF16),
            jax.ShapeDtypeStruct((1, VAL), F32),
            jax.ShapeDtypeStruct((8, LANES), F32),
        ],
        [
            pltpu.VMEM((CHUNK + 8, CONV_CH), F32),
            pltpu.VMEM((CHUNK + 8, CONV_CH), F32),
            pltpu.VMEM((KEY, VAL), F32),
            pltpu.VMEM((4, CONV_CH), F32),
            pltpu.VMEM((LANES, CONV_CH), F32),
            pltpu.VMEM((LANES, width), F32),
            pltpu.VMEM((length, width), BF16),
            pltpu.VMEM((length, CONV_CH + VAL), BF16),
        ] + held_scratch((w_out, qkv, pack)),
        (*scalars, g, x, w_out, qkv, pack, gain, proj, proj, conv, gate_in, rates, inverse, fresh, o,
         states),
        number, "mixer_backward", 16 * 10**9,
    )


PIECES = 4
TURN = (1, 2)
AXES = ("chip", "core", "zp", "zl")


def partners():
    core, zl = lax.axis_index("core"), lax.axis_index("zl")
    return core, zl, {"core": 1 - core}, {"zl": 1 - zl}


def remote(src, dst, send, recv, device):
    return pltpu.make_async_remote_copy(
        src_ref=src, dst_ref=dst, send_sem=send, recv_sem=recv,
        device_id=device, device_id_type=pl.DeviceIdType.MESH,
    )


class Block:
    def __init__(self, zl, core, rows):
        self.first = (zl * 2 + core) * rows
        self.size = rows // PIECES

    def piece(self, p):
        return pl.ds(pl.multiple_of(self.first + p * self.size, self.size), self.size)

    def rows(self):
        rows = self.size * PIECES
        return pl.ds(pl.multiple_of(self.first, rows), rows)


class Scatter:
    def __init__(self, partial, beside_far, beside_own, sums, far, send, recv, held=None):
        core, zl, beside, across = partners()
        self.held = held
        rows = far.shape[0]
        self.partial, self.beside_far, self.beside_own = partial, beside_far, beside_own
        self.sums, self.far = sums, far
        self.size = rows // PIECES
        self.own = Block(zl, core, rows)
        self.away = Block(1 - zl, core, rows)
        own_beside, away_beside = Block(zl, 1 - core, rows), Block(1 - zl, 1 - core, rows)
        self.to_far = [
            remote(partial.at[away_beside.piece(p)], beside_far.at[self.local(p)],
                   send.at[0, p], recv.at[0, p], beside)
            for p in range(PIECES)
        ]
        self.to_own = [
            remote(partial.at[own_beside.piece(p)], beside_own.at[self.local(p)],
                   send.at[1, p], recv.at[1, p], beside)
            for p in range(PIECES)
        ]
        self.cross = [
            remote(sums.at[self.local(p)], far.at[self.local(p)],
                   send.at[2, p], recv.at[2, p], across)
            for p in range(PIECES)
        ]

    def local(self, p):
        return pl.ds(p * self.size, self.size)

    def load(self):
        away, own, sems = self.held
        self.loads = [
            pltpu.make_async_copy(self.partial.at[block.rows()], ref, sems.at[at])
            for at, (block, ref) in enumerate(((self.away, away), (self.own, own)))
        ]
        for copy in self.loads:
            copy.start()

    def mine(self, which, p):
        if self.held is None:
            return self.partial[(self.away, self.own)[which].piece(p), :]
        if p == 0:
            self.loads[which].wait()
        return self.held[which][self.local(p), :]

    def start(self):
        for copy in self.to_far:
            copy.start()
        for copy in self.to_own:
            copy.start()
        for p in range(PIECES):
            self.to_far[p].wait_recv()
            at = self.local(p)
            self.sums[at, :] = (
                self.mine(0, p).astype(F32) + self.beside_far[at, :].astype(F32)
            ).astype(BF16)
            self.cross[p].start()

    def total(self, p):
        self.to_own[p].wait_recv()
        self.cross[p].wait_recv()
        at = self.local(p)
        return (
            self.mine(1, p).astype(F32)
            + self.beside_own[at, :].astype(F32)
            + self.far[at, :].astype(F32)
        )

    def finish(self):
        for copies in (self.to_far, self.to_own, self.cross):
            for copy in copies:
                copy.wait_send()


class Exchange:
    def __init__(self, partial, near, sums, far, send, recv):
        core, zl, beside, across = partners()
        rows = far.shape[1]
        self.near, self.sums, self.far = near, sums, far
        self.size = rows // PIECES
        self.blocks = [Block(l, core, rows) for l in range(2)]
        self.others = [Block(l, 1 - core, rows) for l in range(2)]
        self.order = [(l, p) for l in range(2) for p in range(PIECES)]
        self.beside = [
            [
                remote(partial.at[self.others[l].piece(p)], near.at[l, self.local(p)],
                       send.at[l, p], recv.at[l, p], beside)
                for p in range(PIECES)
            ]
            for l in range(2)
        ]
        self.across = [
            [
                remote(sums.at[l, self.local(p)], far.at[l, self.local(p)],
                       send.at[2 + l, p], recv.at[2 + l, p], across)
                for p in range(PIECES)
            ]
            for l in range(2)
        ]

    def local(self, p):
        return pl.ds(p * self.size, self.size)

    def send(self, l):
        for copy in self.beside[l]:
            copy.start()

    def pass_on(self, l, mine):
        for p in range(PIECES):
            self.beside[l][p].wait_recv()
            at = self.local(p)
            self.sums[l, at, :] = (
                mine(l, p).astype(F32) + self.near[l, at, :].astype(F32)
            ).astype(BF16)
            self.across[l][p].start()

    def total(self, l, p):
        self.across[l][p].wait_recv()
        at = self.local(p)
        return self.sums[l, at, :].astype(F32) + self.far[l, at, :].astype(F32)

    def finish(self):
        for l, p in self.order:
            self.beside[l][p].wait_send()
            self.across[l][p].wait_send()


class Sharing:
    def __init__(self, held, out, send, recv, stores):
        core, _, beside, _ = partners()
        rows = held.shape[0] // 4
        self.held = held
        self.blocks = [Block(l, core, rows) for l in range(2)]
        self.copies = [
            [
                remote(held.at[block.piece(p)], held.at[block.piece(p)], send.at[l, p], recv.at[l, p],
                       beside)
                for p in range(PIECES)
            ]
            for l, block in enumerate(self.blocks)
        ]
        others = [Block(l, 1 - core, rows) for l in range(2)]
        self.stores = [
            pltpu.make_async_copy(held.at[block.rows()], out.at[block.rows()], stores.at[at])
            for at, block in enumerate(self.blocks + others)
        ]

    def put(self, l, p, rows):
        self.held[self.blocks[l].piece(p), :] = rows
        self.copies[l][p].start()
        if p == PIECES - 1:
            self.stores[l].start()

    def arrive(self):
        for l in range(2):
            for copy in self.copies[l]:
                copy.wait_recv()
            self.stores[2 + l].start()

    def finish(self):
        for l in range(2):
            for copy in self.copies[l]:
                copy.wait_send()
        for store in self.stores:
            store.wait()


def normed_of(x, gain):
    return x * lax.rsqrt(jnp.mean(x * x, axis=1, keepdims=True) + 1e-6) * gain


def load_all(copies):
    for copy in copies:
        copy.start()


def first_kernel(row, jobs, x_ref, gain_ref, new_ref, out_ref, raw, held, cross_send, cross_recv, send,
                 recv, stores):
    _, zl, _, across = partners()
    wait_greetings(greet_group() + jobs.greet())
    swap = remote(raw.at[zl], raw.at[zl], cross_send.at[0], cross_recv.at[0], across)
    raw[zl] = x_ref[...]
    swap.start()
    jobs.start()
    sharing = Sharing(held, out_ref, send, recv, stores)
    swap.wait()
    size = raw.shape[1] // PIECES
    for l in range(2):
        for p in range(PIECES):
            x = raw[l, p * size : (p + 1) * size, :].astype(F32)
            sharing.put(l, p, normed_of(x, gain_ref[row : row + 1, :].astype(F32)).astype(BF16))
    new_ref[...] = raw[...]
    jobs.middle()
    sharing.arrive()
    sharing.finish()
    jobs.finish()


def forward_bridge_kernel(
    row, jobs, partial, x_ref, gain_ref, new_ref, out_ref, mine, near, sums, far, x, held, send, recv,
    share_send, share_recv, loads, stores
):
    exchange = Exchange(partial, near, sums, far, send, recv)
    sharing = Sharing(held, out_ref, share_send, share_recv, stores)
    own = [
        pltpu.make_async_copy(partial.at[exchange.blocks[l].rows()], mine.at[l], loads.at[l])
        for l in range(2)
    ]
    old = [pltpu.make_async_copy(x_ref.at[l], x.at[l], loads.at[2 + l]) for l in range(2)]
    new = [pltpu.make_async_copy(x.at[l], new_ref.at[l], stores.at[4 + l]) for l in range(2)]
    load_all(own + old)
    wait_greetings(greet_group() + jobs.greet())
    for l in range(2):
        exchange.send(l)
    jobs.start()
    for l in range(2):
        own[l].wait()
        exchange.pass_on(l, lambda l, p: mine[l, exchange.local(p), :])
    forward_rows(row, jobs, exchange, sharing, old, new, x, gain_ref)


def forward_rows(row, jobs, exchange, sharing, old, new, x, gain_ref):
    gain = gain_ref[row : row + 1, :].astype(F32)
    for l in range(2):
        old[l].wait()
        for p in range(PIECES):
            if (l, p) == TURN:
                jobs.middle()
            at = exchange.local(p)
            rows = x[l, at, :] + exchange.total(l, p)
            x[l, at, :] = rows
            sharing.put(l, p, normed_of(rows, gain).astype(BF16))
        new[l].start()
    sharing.arrive()
    exchange.finish()
    sharing.finish()
    for store in new:
        store.wait()
    jobs.finish()


def mixer_bridge_kernel(
    row, jobs, heads_ref, w_out_ref, x_ref, gain_ref, new_ref, out_ref, partial, raw, near, sums, far, x,
    held, send, recv, share_send, share_recv, loads, stores
):
    exchange = Exchange(partial, near, sums, far, send, recv)
    sharing = Sharing(held, out_ref, share_send, share_recv, stores)
    old = [pltpu.make_async_copy(x_ref.at[l], raw.at[l], loads.at[2 + l]) for l in range(2)]
    new = [pltpu.make_async_copy(x.at[l], new_ref.at[l], stores.at[4 + l]) for l in range(2)]
    load_all(old)
    wait_greetings(greet_group() + jobs.greet())

    def make(block):
        rows = block.rows()
        partial[rows, :] = mm(heads_ref[rows, :], w_out_ref[...], NT).astype(BF16)

    for l in range(2):
        make(exchange.others[l])
        exchange.send(l)
    jobs.start()
    for l in range(2):
        make(exchange.blocks[l])
        exchange.pass_on(l, lambda l, p: partial[exchange.blocks[l].piece(p), :])
    for l in range(2):
        old[l].wait()
        if x_ref.dtype != F32:
            x[l] = raw[l].astype(F32)
        old[l] = Done()
    forward_rows(row, jobs, exchange, sharing, old, new, x, gain_ref)


class Done:
    def wait(self):
        pass


def norm_back(total, x, gain):
    inv = lax.rsqrt(jnp.mean(x * x, axis=1, keepdims=True) + 1e-6)
    unit = x * inv
    scaled = total * gain
    grad = inv * (scaled - unit * jnp.mean(scaled * unit, axis=1, keepdims=True))
    return grad, jnp.sum(total * unit, axis=0, keepdims=True)


def backward_bridge_kernel(row, last, jobs, partial, x_ref, gain_ref, grad_ref, *refs):
    if last:
        heads_ref, new_ref, out_ref, dgain_ref, dout_ref, *refs = refs
    else:
        new_ref, out_ref, dgain_ref, *refs = refs
    (mine, near, sums, far, x, grad, new_rows, held, send, recv, share_send, share_recv, loads,
     stores) = refs
    exchange = Exchange(partial, near, sums, far, send, recv)
    sharing = Sharing(held, out_ref, share_send, share_recv, stores)
    zl = lax.axis_index("zl")
    place = lambda ref, l: ref.at[exchange.blocks[l].rows()] if len(ref.shape) == 2 else ref.at[l]
    own, old = [], []
    for l in range(2):
        own.append(
            pltpu.make_async_copy(partial.at[exchange.blocks[l].rows()], mine.at[l], loads.at[l])
        )
        old.append(
            (pltpu.make_async_copy(x_ref.at[l], x.at[l], loads.at[2 + l]),
             pltpu.make_async_copy(place(grad_ref, l), grad.at[l], loads.at[4 + l]))
        )
    new = [pltpu.make_async_copy(new_rows.at[l], new_ref.at[l], stores.at[4 + l]) for l in range(2)]
    load_all(own + [copy for pair in old for copy in pair])
    wait_greetings(greet_group() + jobs.greet())
    for l in range(2):
        exchange.send(l)
    jobs.start()
    for l in range(2):
        own[l].wait()
        exchange.pass_on(l, lambda l, p: mine[l, exchange.local(p), :])
    gain = gain_ref[row : row + 1, :].astype(F32)
    dgain = jnp.zeros(dgain_ref.shape, F32)
    for l in range(2):
        for copy in old[l]:
            copy.wait()
        for p in range(PIECES):
            if (l, p) == TURN:
                jobs.middle()
            at = exchange.local(p)
            rows, part = norm_back(exchange.total(l, p), x[l, at, :].astype(F32), gain)
            dgain = dgain + jnp.where(zl == l, part, 0.0)
            rows = rows + grad[l, at, :].astype(F32)
            new_rows[l, at, :] = rows
            sharing.put(l, p, rows.astype(BF16))
        new[l].start()
    dgain_ref[...] = dgain
    sharing.arrive()
    if last:
        for first in range(0, held.shape[1], 256):
            columns = slice(first, first + 256)
            dout_ref[columns, :] = mm(held[:, columns], heads_ref[...], TN).astype(BF16)
    exchange.finish()
    sharing.finish()
    for store in new:
        store.wait()
    jobs.finish()


def backward_last_kernel(
    row, jobs, partial, x_ref, gain_ref, grad_ref, new_ref, dgain_ref,
    beside_far, beside_own, sums, far, send, recv
):
    wait_greetings(greet_group() + jobs.greet())
    scatter = Scatter(partial, beside_far, beside_own, sums, far, send, recv)
    scatter.start()
    jobs.start()
    zl = lax.axis_index("zl")
    dgain = jnp.zeros(dgain_ref.shape, F32)
    for p in range(PIECES):
        at = scatter.local(p)
        grad, part = norm_back(
            scatter.total(p), x_ref[zl, at, :].astype(F32), gain_ref[row : row + 1, :].astype(F32)
        )
        dgain = dgain + part
        new_ref[at, :] = (grad + grad_ref[zl, at, :]).astype(BF16)
    dgain_ref[...] = dgain
    jobs.middle()
    scatter.finish()
    jobs.finish()


VMEM_SPEC = pl.BlockSpec(memory_space=pltpu.VMEM)
ANY_SPEC = pl.BlockSpec(memory_space=pl.ANY)


def pair_scratch(rows, width, kinds):
    return [pltpu.VMEM((2, rows, width), kind) for kind in kinds]


def bridge_sems():
    many = pltpu.SemaphoreType.DMA((4, PIECES))
    few = pltpu.SemaphoreType.DMA((2, PIECES))
    return [many, many, few, few, pltpu.SemaphoreType.DMA((6,)), pltpu.SemaphoreType.DMA((6,))]


def bridge_shapes(rows, width):
    return [
        jax.ShapeDtypeStruct((2, rows, width), F32),
        jax.ShapeDtypeStruct((4 * rows, width), BF16),
    ]


def first_gather(x, gain, row, jobs, number):
    rows, width = x.shape
    few = pltpu.SemaphoreType.DMA((2, PIECES))
    one = pltpu.SemaphoreType.DMA((1,))
    return carry_call(
        functools.partial(first_kernel, row), jobs, (), [VMEM_SPEC] * 2, [VMEM_SPEC, ANY_SPEC],
        [
            jax.ShapeDtypeStruct((2, rows, width), BF16),
            jax.ShapeDtypeStruct((4 * rows, width), BF16),
        ],
        [pltpu.VMEM((2, rows, width), BF16), pltpu.VMEM((4 * rows, width), BF16), one, one, few, few,
         pltpu.SemaphoreType.DMA((4,))],
        (x, gain), number, "first", rows * width * 20,
    )


def forward_bridge(partial, x, gain, row, jobs, number):
    _, rows, width = x.shape
    return carry_call(
        functools.partial(forward_bridge_kernel, row), jobs, (),
        [ANY_SPEC, ANY_SPEC, VMEM_SPEC], [ANY_SPEC] * 2, bridge_shapes(rows, width),
        pair_scratch(rows, width, [BF16] * 4 + [F32]) + [pltpu.VMEM((4 * rows, width), BF16)]
        + bridge_sems(),
        (partial, x, gain), number, "forward_bridge", rows * width * 20,
    )


def mixer_bridge(heads, w_out, x, gain, row, jobs, number):
    _, rows, width = x.shape
    kernel = functools.partial(
        mixer_bridge_kernel if x.dtype != F32 else mixer_bridge_kernel_f32, row
    )
    raw = pair_scratch(rows, width, [BF16]) if x.dtype != F32 else []
    return carry_call(
        kernel, jobs, (), [VMEM_SPEC, VMEM_SPEC, ANY_SPEC, VMEM_SPEC], [ANY_SPEC] * 2,
        bridge_shapes(rows, width),
        [pltpu.VMEM((4 * rows, width), BF16)] + raw + pair_scratch(rows, width, [BF16] * 3 + [F32])
        + [pltpu.VMEM((4 * rows, width), BF16)] + bridge_sems(),
        (heads, w_out, x, gain), number, "mixer_bridge", 10**9,
    )


def mixer_bridge_kernel_f32(row, jobs, heads_ref, w_out_ref, x_ref, gain_ref, new_ref, out_ref, partial,
                            near, sums, far, x, *refs):
    mixer_bridge_kernel(row, jobs, heads_ref, w_out_ref, x_ref, gain_ref, new_ref, out_ref, partial, x,
                        near, sums, far, x, *refs)


def backward_bridge(partial, x, gain, row, grad, jobs, number, heads=None):
    _, rows, width = x.shape
    last = heads is not None
    outs = bridge_shapes(rows, width) + [jax.ShapeDtypeStruct((1, width), F32)]
    if last:
        outs.append(jax.ShapeDtypeStruct((width, heads.shape[1]), BF16))
    return carry_call(
        functools.partial(backward_bridge_kernel, row, last), jobs, (),
        [ANY_SPEC, ANY_SPEC, VMEM_SPEC, ANY_SPEC] + [VMEM_SPEC] * last,
        [ANY_SPEC, ANY_SPEC, VMEM_SPEC] + [VMEM_SPEC] * last, outs,
        pair_scratch(rows, width, [BF16] * 4 + [x.dtype, grad.dtype, F32])
        + [pltpu.VMEM((4 * rows, width), BF16)] + bridge_sems(),
        (partial, x, gain, grad) + ((heads,) if last else ()), number, "backward_bridge",
        rows * width * 20,
    )


def backward_last(partial, x, gain, row, grad, jobs, number):
    _, rows, width = x.shape
    hops = pltpu.SemaphoreType.DMA((3, PIECES))
    return carry_call(
        functools.partial(backward_last_kernel, row), jobs, (), [VMEM_SPEC] * 4, [VMEM_SPEC] * 2,
        [jax.ShapeDtypeStruct((rows, width), BF16), jax.ShapeDtypeStruct((1, width), F32)],
        [pltpu.VMEM((rows, width), BF16) for _ in range(4)] + [hops, hops],
        (partial, x, gain, grad), number, "backward_last", rows * width * 20,
    )


class Job:
    in_vmem = False
    late = False

    @staticmethod
    def buffers(shape, chips):
        return []

    def __init__(self, source, target, send, recv, chips, buffers=()):
        self.source, self.target, self.send, self.recv = source, target, send, recv
        self.held = buffers
        self.chips = chips
        self.chip, self.core, self.zp, self.zl, self.own = place(chips)
        self.fixed = (self.zp == self.zl) & (self.zl == self.core)
        self.outward, self.inward, self.locals = [], [], []
        self.plan()

    def copy(self, src, dst, send, recv, device):
        return remote(src, dst, self.send.at[send], self.recv.at[recv], device)

    def local(self, src, dst, at, when=None, through=None):
        if through is None:
            self.locals.append((pltpu.make_async_copy(src, dst, self.send.at[at]), None, when))
        else:
            self.locals.append(
                (pltpu.make_async_copy(src, through, self.send.at[at]),
                 pltpu.make_async_copy(through, dst, self.send.at[at]), when)
            )

    def column(self, chip, core, zp, zl):
        return at_device(chip, core, zp, zl)

    def greet(self):
        count = 0
        for copy, device, mine in self.inward:
            if mine is None:
                signal(device)
            else:
                unless(mine, functools.partial(signal, device))
        for copy, mine in self.outward:
            count = count + (1 if mine is None else 1 - mine.astype(jnp.int32))
        return count

    def start(self):
        for copy, mine in self.outward:
            if mine is None:
                copy.start()
            else:
                unless(mine, copy.start)
        for load, _, when in self.locals:
            if when is None:
                load.start()
            else:
                pl.when(when)(load.start)

    def middle(self):
        for load, store, when in self.locals:
            def turn():
                load.wait()
                store.start()

            if store is not None and when is None:
                turn()
            elif store is not None:
                pl.when(when)(turn)

    def arrivals(self):
        for copy, device, mine in self.inward:
            if mine is None:
                copy.wait_recv()
            else:
                unless(mine, copy.wait_recv)

    def departures(self):
        for copy, mine in self.outward:
            if mine is None:
                copy.wait_send()
            else:
                unless(mine, copy.wait_send)
        for load, store, when in self.locals:
            last = load if store is None else store
            if when is None:
                last.wait()
            else:
                pl.when(when)(last.wait)

    def finish(self):
        self.arrivals()
        self.departures()


def block(index, size):
    return pl.ds(pl.multiple_of(index * size, size), size)


class ToPlane(Job):
    @staticmethod
    def result(shape, chips):
        return (2 * shape[0], shape[1])

    @staticmethod
    def buffers(shape, chips):
        return [pltpu.VMEM(shape, BF16)]

    def plan(self):
        rows = self.source.shape[0]
        at = block(self.core, rows)
        for to in range(2):
            self.outward.append(
                (self.copy(self.source, self.target.at[at], to, self.core,
                           at_device(self.chip, self.zl, to, self.zp)),
                 self.fixed & (self.zp == to))
            )
        for co in range(2):
            device = at_device(self.chip, co, self.zl, self.core)
            self.inward.append(
                (self.copy(self.source, self.target.at[block(co, rows)], 0, co, device), device,
                 self.fixed & (self.core == co))
            )
        self.local(self.source, self.target.at[at], 2, self.fixed, self.held[0] if self.held else None)


class FromPlane(Job):
    @staticmethod
    def result(shape, chips):
        return (2, shape[0] // 2, shape[1])

    @staticmethod
    def buffers(shape, chips):
        return [pltpu.VMEM((shape[0] // 2, shape[1]), BF16)]

    def plan(self):
        rows = self.source.shape[0] // 2
        for co in range(2):
            src, mine = self.source.at[block(co, rows)], self.fixed & (self.core == co)
            self.outward.append(
                (self.copy(src, self.target.at[self.zp], co, self.zp,
                           at_device(self.chip, co, self.zl, self.core)), mine)
            )
            self.local(src, self.target.at[self.zp], 2 + co, mine, self.held[0] if self.held else None)
        for at in range(2):
            device = at_device(self.chip, self.zl, at, self.zp)
            self.inward.append(
                (self.copy(self.source.at[block(0, rows)], self.target.at[at], 0, at, device), device,
                 self.fixed & (self.zp == at))
            )


class Spread(Job):
    @staticmethod
    def result(shape, chips):
        return (chips * shape[0], shape[1])

    @staticmethod
    def buffers(shape, chips):
        return [pltpu.VMEM(shape, BF16)]

    def to(self, chip):
        return at_device(chip, self.core, self.zp, self.zl)

    def plan(self):
        rows = self.source.shape[0]
        own = self.target.at[block(self.chip, rows)]
        self.local(self.source, own, 0, None, self.held[0])
        self.onward, self.later = [], []
        if self.chips != 4:
            for j in range(1, self.chips):
                to = lax.rem(self.chip + j, self.chips)
                source = lax.rem(self.chip + self.chips - j, self.chips)
                self.outward.append((self.copy(self.source, own, j, j, self.to(to)), None))
                self.inward.append(
                    (self.copy(self.source, self.target.at[block(source, rows)], j, j,
                               self.to(source)), self.to(source), None)
                )
            return
        y, x = self.chip // 2, lax.rem(self.chip, 2)
        sides = [y * 2 + (1 - x), (1 - y) * 2 + x]
        across = (1 - y) * 2 + (1 - x)
        half = rows // 2
        for side in range(2):
            device = self.to(sides[side])
            self.outward.append((self.copy(self.source, own, 1 + side, 1 + side, device), None))
            self.inward.append(
                (self.copy(self.source, self.target.at[block(sides[side], rows)], 1 + side, 1 + side,
                           device), device, None)
            )
        for side in range(2):
            part = pl.ds(pl.multiple_of(sides[side] * rows + side * half, half), half)
            self.onward.append(
                self.copy(self.target.at[part], self.target.at[part], 3 + side, 3 + side,
                          self.to(sides[1 - side]))
            )
            part = pl.ds(pl.multiple_of(across * rows + side * half, half), half)
            self.later.append(
                self.copy(self.target.at[part], self.target.at[part], 3 + side, 3 + side,
                          self.to(sides[1 - side]))
            )

    def middle(self):
        super().middle()
        if self.onward:
            self.arrivals()
            for copy in self.onward:
                copy.start()

    def finish(self):
        if not self.onward:
            self.arrivals()
        for copy in self.later:
            copy.wait_recv()
        for copy in self.onward:
            copy.wait_send()
        self.departures()


class Reduce(Job):
    in_vmem = True

    @staticmethod
    def result(shape, chips):
        return (shape[0] // chips, shape[1])

    @staticmethod
    def buffers(shape, chips):
        rows, cols = shape[0] // chips, shape[1]
        if chips != 4:
            return [pltpu.VMEM((chips, rows, cols), BF16)]
        return [pltpu.VMEM((rows // 2, cols), BF16)] * 4 + [pltpu.VMEM((rows, cols), BF16)] * 3

    def plan(self):
        rows = self.source.shape[0] // self.chips
        to = lambda chip: at_device(chip, self.core, self.zp, self.zl)
        if self.chips != 4:
            (parts,) = self.held
            self.local(self.source.at[block(self.chip, rows)], parts.at[self.chip], 0)
            for j in range(1, self.chips):
                target = lax.rem(self.chip + j, self.chips)
                source = lax.rem(self.chip + self.chips - j, self.chips)
                src = self.source.at[block(target, rows)]
                self.outward.append((self.copy(src, parts.at[self.chip], j, j, to(target)), None))
                self.inward.append(
                    (self.copy(src, parts.at[source], j, j, to(source)), to(source), None)
                )
            return
        half = rows // 2
        y, x = self.chip // 2, lax.rem(self.chip, 2)
        sides = [y * 2 + (1 - x), (1 - y) * 2 + x]
        across = (1 - y) * 2 + (1 - x)
        passing, staged, blocks, own = self.held[0:2], self.held[2:4], self.held[4:6], self.held[6]
        piece = lambda chip, at: self.source.at[
            pl.ds(pl.multiple_of(chip * rows + at * half, half), half)
        ]
        self.local(self.source.at[block(self.chip, rows)], own, 0)
        self.loads = []
        self.onward, self.later = [], []
        for side in range(2):
            device = to(sides[side])
            copy = self.copy(piece(across, side), passing[side], 1 + side, 1 + side, device)
            self.outward.append((copy, None))
            self.inward.append((copy, device, None))
        self.direct = []
        for side in range(2):
            device = to(sides[side])
            part = pl.ds(side * half, half)
            self.direct.append(
                self.copy(piece(sides[side], side), blocks[side].at[part], 3 + side, 3 + side, device)
            )
            self.loads.append(
                pltpu.make_async_copy(piece(sides[side], 1 - side), staged[side], self.send.at[5 + side])
            )
            part = pl.ds((1 - side) * half, half)
            self.onward.append(
                self.copy(staged[side], blocks[side].at[part], 7 + side, 5 + side, device)
            )

    def start(self):
        super().start()
        if self.chips == 4:
            for copy in self.direct + self.loads:
                copy.start()

    def middle(self):
        if self.chips == 4:
            for side in range(2):
                self.inward[1 - side][0].wait_recv()
                self.loads[side].wait()
                self.held[2 + side][...] = (
                    self.held[2 + side][...].astype(F32) + self.held[1 - side][...].astype(F32)
                ).astype(BF16)
                self.onward[side].start()

    def finish(self):
        if self.chips == 4:
            for copy in self.direct + self.onward:
                copy.wait_recv()
            self.departures()
            for copy in self.direct + self.onward:
                copy.wait_send()
            total = self.held[6][...].astype(F32) + (
                self.held[4][...].astype(F32) + self.held[5][...].astype(F32)
            )
        else:
            super().finish()
            total = self.held[0][0].astype(F32)
            for chip in range(1, self.chips):
                total = total + self.held[0][chip].astype(F32)
        self.target[...] = total.astype(BF16)


class ToRole(Job):
    @staticmethod
    def result(shape, chips):
        return shape

    @staticmethod
    def buffers(shape, chips):
        return [pltpu.VMEM(shape, BF16)]

    def ends(self):
        role = at_device(self.chip, self.zl, self.core, self.zp)
        home = at_device(self.chip, self.zp, self.zl, self.core)
        return role, home, self.fixed & (self.zp == self.core)

    def plan(self):
        to, source, mine = self.ends()
        self.outward.append((self.copy(self.source, self.target, 0, 0, to), mine))
        self.inward.append((self.copy(self.source, self.target, 0, 0, source), source, mine))
        self.local(self.source, self.target, 1, mine, self.held[0])


class FromRole(ToRole):
    def ends(self):
        role, home, mine = super().ends()
        return home, role, mine


class Share(Job):
    late = True
    @staticmethod
    def result(shape, chips):
        return (4 * shape[0], shape[1])

    @staticmethod
    def buffers(shape, chips):
        return [pltpu.VMEM(shape, BF16)]

    def plan(self):
        rows = self.source.shape[0]
        own = self.target.at[block(self.zl * 2 + self.core, rows)]
        beside = at_device(self.chip, 1 - self.core, self.zp, self.zl)
        across = at_device(self.chip, self.core, self.zp, 1 - self.zl)
        self.local(self.source, own, 0, None, self.held[0])
        for at, device, zl, core in ((1, beside, self.zl, 1 - self.core), (2, across, 1 - self.zl, self.core)):
            self.outward.append((self.copy(self.source, own, at, at, device), None))
            self.inward.append(
                (self.copy(self.source, self.target.at[block(zl * 2 + core, rows)], at, at, device),
                 device, None)
            )
        other = self.target.at[block((1 - self.zl) * 2 + self.core, rows)]
        self.onward = self.copy(other, other, 3, 3, beside)
        last = self.target.at[block((1 - self.zl) * 2 + 1 - self.core, rows)]
        self.later = self.copy(last, last, 3, 3, beside)

    def middle(self):
        super().middle()
        self.arrivals()
        self.onward.start()

    def finish(self):
        self.later.wait_recv()
        self.onward.wait_send()
        self.departures()


class ShareSum(Job):
    late = True
    in_vmem = True

    @staticmethod
    def result(shape, chips):
        return (shape[0] // 4, shape[1])

    @staticmethod
    def buffers(shape, chips):
        return [pltpu.VMEM((shape[0] // 4, shape[1]), BF16)] * 5

    def plan(self):
        rows = self.target.shape[0]
        beside = at_device(self.chip, 1 - self.core, self.zp, self.zl)
        across = at_device(self.chip, self.core, self.zp, 1 - self.zl)
        part = lambda zl, core: self.source.at[block(zl * 2 + core, rows)]
        self.far, self.near, self.staged, self.own, self.other = self.held
        for at, src, dst in (
            (0, part(1 - self.zl, 1 - self.core), self.far), (1, part(self.zl, 1 - self.core), self.near)
        ):
            copy = self.copy(src, dst, at, at, beside)
            self.outward.append((copy, None))
            self.inward.append((copy, beside, None))
        self.local(part(1 - self.zl, self.core), self.staged, 2)
        self.local(part(self.zl, self.core), self.own, 3)
        self.onward = self.copy(self.staged, self.other, 4, 2, across)
        self.across = across

    def greet(self):
        signal(self.across)
        return super().greet() + 1

    def middle(self):
        self.arrivals()
        for load, _, _ in self.locals:
            load.wait()
        self.staged[...] = (
            self.staged[...].astype(F32) + self.far[...].astype(F32)
        ).astype(BF16)
        self.onward.start()

    def finish(self):
        for copy, _ in self.outward:
            copy.wait_send()
        self.onward.wait()
        self.target[...] = (
            self.own[...].astype(F32) + self.near[...].astype(F32) + self.other[...].astype(F32)
        ).astype(BF16)


class Jobs:
    def __init__(self, jobs, chips):
        self.kinds = [job[0] for job in jobs]
        self.values = [job[1] for job in jobs]
        self.columns = [job[2] if len(job) > 2 else None for job in jobs]
        shapes = [
            value.shape if columns is None else (value.shape[0], columns[1])
            for value, columns in zip(self.values, self.columns)
        ]
        self.chips = chips
        count = max(9, chips + 1)
        any_space = pl.BlockSpec(memory_space=pl.ANY)
        self.in_specs = [any_space] * len(jobs)
        self.out_shape = [
            jax.ShapeDtypeStruct(kind.result(shape, chips), BF16)
            for kind, shape in zip(self.kinds, shapes)
        ]
        self.buffers = [kind.buffers(shape, chips) for kind, shape in zip(self.kinds, shapes)]
        self.scratch = [pltpu.SemaphoreType.DMA((count,))] * (2 * len(jobs))
        self.scratch += [buffer for buffers in self.buffers for buffer in buffers]

    def out_specs(self, grid):
        specs = []
        for kind, shape in zip(self.kinds, self.out_shape):
            if not kind.in_vmem:
                specs.append(pl.BlockSpec(memory_space=pl.ANY))
            elif grid:
                specs.append(pl.BlockSpec(shape.shape, lambda i: (0, 0)))
            else:
                specs.append(pl.BlockSpec(memory_space=pltpu.VMEM))
        return specs

    def bind(self, sources, targets, scratch):
        sems, scratch = scratch[: 2 * len(self.kinds)], scratch[2 * len(self.kinds) :]
        self.bound = []
        for at, (kind, source, target) in enumerate(zip(self.kinds, sources, targets)):
            if self.columns[at] is not None:
                source = source.at[:, pl.ds(*self.columns[at])]
            held, scratch = scratch[: len(self.buffers[at])], scratch[len(self.buffers[at]) :]
            self.bound.append(
                kind(source, target, sems[2 * at], sems[2 * at + 1], self.chips, held)
            )

    def greet(self):
        count = 0
        for job in self.bound:
            count = count + job.greet()
        return count

    def start(self):
        for job in self.bound:
            job.start()

    def middle(self, late=None):
        for job in self.bound:
            if late is None or job.late == late:
                job.middle()

    def finish(self):
        for job in self.bound:
            job.finish()


def carrying(body, jobs, ins, outs):
    extra = len(jobs.kinds)

    def kernel(*refs):
        operands, refs = refs[:ins], refs[ins:]
        sources, refs = refs[:extra], refs[extra:]
        results, refs = refs[:outs], refs[outs:]
        targets, refs = refs[:extra], refs[extra:]
        own = len(refs) - len(jobs.scratch)
        scratch = refs[:own]
        jobs.bind(sources, targets, refs[own:])
        body(jobs, *operands, *results, *scratch)

    return kernel


def carry_call(body, jobs, grid, in_specs, out_specs, out_shape, scratch, args, number, name, work):
    outs = len(out_shape)
    results = pl.pallas_call(
        carrying(body, jobs, len(args), outs),
        grid=grid,
        in_specs=list(in_specs) + jobs.in_specs,
        out_specs=list(out_specs) + jobs.out_specs(grid),
        out_shape=list(out_shape) + jobs.out_shape,
        scratch_shapes=list(scratch) + jobs.scratch,
        compiler_params=pltpu.CompilerParams(
            collective_id=number, has_side_effects=True, vmem_limit_bytes=56 * 1024 * 1024
        ),
        cost_estimate=pl.CostEstimate(
            flops=work, bytes_accessed=80 * 1024 * 1024, transcendentals=0
        ),
        name=name,
    )(*args, *jobs.values)
    return list(results[:outs]), list(results[outs:])


def place(chips):
    chip, core, zp, zl = (lax.axis_index(name) for name in AXES)
    return chip, core, zp, zl, chip * 2 + core


def at_device(chip, core, zp, zl):
    return {"chip": chip, "core": core, "zp": zp, "zl": zl}


def signal(device):
    pl.semaphore_signal(
        pltpu.get_barrier_semaphore(), inc=1, device_id=device,
        device_id_type=pl.DeviceIdType.MESH,
    )


def unless(condition, action):
    pl.when(jnp.logical_not(condition))(action)


class Plane:
    def __init__(self, chips):
        self.count = 2 * chips
        _, _, self.zp, self.zl, self.own = place(chips)

    def device(self, index):
        return at_device(index // 2, index % 2, self.zp, self.zl)

    def to(self, j):
        return lax.rem(self.own + j, self.count)

    def source(self, j):
        return lax.rem(self.own + self.count - j, self.count)

    def greet(self):
        for j in range(1, self.count):
            signal(self.device(self.to(j)))
        return self.count - 1


class Trade:
    def __init__(self, chips):
        self.chips, self.count = chips, 2 * chips
        self.chip, self.core, self.zp, self.zl, self.own = place(chips)
        self.fixed = (self.zp == self.zl) & (self.zl == self.core)
        self.slot = self.chip * 2 + self.zp

    def role(self, slot):
        return at_device(slot // 2, self.zl, slot % 2, self.zp)

    def role_mine(self, slot):
        return self.fixed & (self.slot == slot)

    def home(self, index):
        return at_device(index // 2, index % 2, self.zl, self.core)

    def home_mine(self, index):
        return self.fixed & (self.own == index)

    def greet_homes(self):
        for index in range(self.count):
            unless(self.home_mine(index), functools.partial(signal, self.home(index)))
        return self.count - self.fixed.astype(jnp.int32)

    def greet_roles(self):
        for slot in range(self.count):
            unless(self.role_mine(slot), functools.partial(signal, self.role(slot)))
        return self.count - self.fixed.astype(jnp.int32)


def greet_group():
    _, _, beside, across = partners()
    signal(beside)
    signal(across)
    return 2


def wait_greetings(count):
    pl.semaphore_wait(pltpu.get_barrier_semaphore(), count)


class Raw:
    def __init__(self, refs, square):
        (self.query, self.key, self.value, self.gate, self.decay, self.conv, self.out,
         self.ffn_gate, self.ffn_up, self.ffn_down) = refs
        self.square = square

    def qkv(self, layer, ref):
        ref[:, 0:KEY] = self.query[layer]
        ref[:, KEY : 2 * KEY] = self.key[layer]
        ref[:, 2 * KEY :] = self.value[layer]

    def side(self, layer, ref):
        ref[:, 0:VAL] = self.gate[layer]
        self.square[...] = jnp.zeros(self.square.shape, F32)
        self.square[0:2, :] = self.decay[layer].astype(F32)
        self.square[2:6, :] = self.conv[layer].astype(F32)
        ref[:, VAL:] = self.square[...].T.astype(BF16)

    def turn(self, value, ref):
        ref[...] = value.astype(F32).T.astype(BF16)


def deal_kernel(chips, jobs, order_ref, lengths_ref, x_ref, gain_ref, cotangent_ref, *refs):
    raw, refs = refs[:10], refs[10:]
    (new_ref, out_ref, start_ref, qkv_next, side_next, out_next, gate_next, up_ref, up_next, down_ref,
     down_next, first_full, second_full, first_wide, second_wide, third_wide, fourth_wide) = refs[:17]
    (spread, picked, square, first, second, third, fourth, held_first, held_other, held_second, held, send, recv,
     stores,     cross_send, cross_recv,
     plane_send, plane_recv, role_send, role_recv, *sems) = refs[17:]
    raw = Raw(raw, square)
    plane, trade = Plane(chips), Trade(chips)
    half = CONV_CH // 2
    halves = []
    for at, (own, four) in enumerate(((held_first, sems[0:4]), (held_other, sems[12:16]))):
        cut = pl.ds(at * half, half)
        wide = first_wide.at[:, cut]
        halves.append(
            (ToPlane(first.at[:, cut], wide, four[0], four[1], chips),
             Spread(wide, first_full.at[:, cut], four[2], four[3], chips, [own]))
        )
    second_column = ToPlane(second, second_wide, sems[4], sems[5], chips)
    second_across = Spread(second_wide, second_full, sems[6], sems[7], chips, [held_second])
    third_column = ToPlane(third, third_wide, sems[8], sems[9], chips)
    fourth_column = ToPlane(fourth, fourth_wide, sems[10], sems[11], chips)
    sharing = Sharing(held, out_ref, send, recv, stores)
    across = {"zl": 1 - trade.zl}
    count = plane.count
    part = x_ref.shape[0] // count
    rows = lambda index: pl.ds(pl.multiple_of(index * part, part), part)
    expected = plane.greet() + trade.greet_homes() + greet_group()
    for job in (*halves[0], *halves[1], second_column, second_across, third_column, fourth_column):
        expected = expected + job.greet()
    raw.qkv(0, first)
    raw.side(0, second)
    wait_greetings(expected)
    outward, inward = [], []
    for j in range(1, count):
        to, source = plane.to(j), plane.source(j)
        outward.append(
            remote(x_ref.at[rows(to)], spread.at[plane.own], plane_send.at[j], plane_recv.at[j],
                   plane.device(to))
        )
        inward.append(
            remote(x_ref.at[rows(to)], spread.at[source], plane_send.at[j], plane_recv.at[j],
                   plane.device(source))
        )
    for copy in outward:
        copy.start()
    for column, _ in halves:
        column.start()
    spread[plane.own] = x_ref[rows(plane.own), :]
    for copy in inward:
        copy.wait_recv()
    halves[0][0].finish()
    halves[0][1].start()
    to_roles = []
    for slot in range(count):
        picked[slot] = spread[order_ref[slot]]
        copy = remote(picked.at[slot], new_ref.at[trade.zp, rows(plane.own)], role_send.at[slot],
                      role_recv.at[plane.own], trade.role(slot))
        mine = trade.role_mine(slot)
        unless(mine, copy.start)

        @pl.when(mine)
        def _():
            new_ref[trade.zl, rows(plane.own), :] = picked[slot]

        to_roles.append((copy, mine))
    second_column.start()
    raw.turn(raw.out[0], third)
    raw.turn(raw.ffn_gate[0], fourth)
    halves[1][0].finish()
    halves[1][1].start()
    size = x_ref.shape[0] // PIECES
    parts = max(size // part, 1)
    swaps = []
    for p in range(PIECES):
        piece = new_ref.at[trade.zl, pl.ds(p * size, size)]
        swaps.append(remote(piece, piece, cross_send.at[p], cross_recv.at[p], across))
    for p in range(PIECES):
        for index in range(p * parts, (p + 1) * parts):
            arrival = remote(picked.at[0], new_ref.at[trade.zl, rows(index)], role_send.at[0],
                             role_recv.at[index], trade.home(index))
            unless(trade.home_mine(index), arrival.wait_recv)
        swaps[p].start()
    gain = gain_ref[0:1, :].astype(F32)

    def share(l):
        for p in range(PIECES):
            x = new_ref[l, p * size : (p + 1) * size, :].astype(F32)
            sharing.put(l, p, normed_of(x, gain).astype(BF16))

    for l in range(2):
        pl.when(trade.zl == l)(functools.partial(share, l))
    second_column.finish()
    second_across.start()
    third_column.start()
    fourth_column.start()
    for _, across_chips in halves:
        across_chips.middle()
    for swap in swaps:
        swap.wait_recv()
    for l in range(2):
        pl.when(trade.zl != l)(functools.partial(share, l))
    length = lengths_ref[order_ref[plane.own]]
    at = (trade.zp * 2 + trade.zl) * x_ref.shape[0]
    positions = lax.broadcasted_iota(jnp.int32, x_ref.shape, 0) + at
    start_ref[...] = jnp.where(positions < length, cotangent_ref[...], jnp.zeros(x_ref.shape, BF16))
    raw.qkv(1, qkv_next)
    raw.side(1, side_next)
    raw.turn(raw.out[1], out_next)
    raw.turn(raw.ffn_gate[1], gate_next)
    raw.turn(raw.ffn_up[0], up_ref)
    raw.turn(raw.ffn_up[1], up_next)
    raw.turn(raw.ffn_down[0], down_ref)
    raw.turn(raw.ffn_down[1], down_next)
    for copy in outward:
        copy.wait_send()
    for copy, mine in to_roles:
        unless(mine, copy.wait_send)
    for swap in swaps:
        swap.wait_send()
    sharing.arrive()
    sharing.finish()
    second_across.middle()
    for _, across_chips in halves:
        across_chips.finish()
    second_across.finish()
    third_column.finish()
    fourth_column.finish()


def deal_and_gather(order, lengths, x, gain, cotangent, raw, chips, number):
    rows, width = x.shape
    part, units = raw[0].shape[1], raw[7].shape[1]
    vmem = pl.BlockSpec(memory_space=pltpu.VMEM)
    smem = pl.BlockSpec(memory_space=pltpu.SMEM)
    hbm = pl.BlockSpec(memory_space=pl.ANY)
    count = 2 * chips
    buffer = pltpu.VMEM((count, rows // count, width), BF16)
    sems = lambda *shape: [pltpu.SemaphoreType.DMA(shape), pltpu.SemaphoreType.DMA(shape)]
    qkv, side = CONV_CH, VAL + LANES
    held = [(part, cols) for cols in (qkv, side, VAL, units, units, units, units, units)]
    spread = [(2 * chips * part, qkv), (2 * chips * part, side)]
    moved = [(2 * part, cols) for cols in (qkv, side, VAL, units)]
    shapes = [(2, rows, width), (4 * rows, width), (rows, width)] + held + spread + moved
    halved = (2 * part, qkv // 2)
    own = [(part, qkv), (part, side), (part, VAL), (part, units), halved, halved, moved[1]]
    return carry_call(
        functools.partial(deal_kernel, chips), Jobs([], chips), (),
        [smem, smem] + [vmem] * 13,
        [vmem, hbm] + [vmem] * 9 + [hbm] * 6,
        [jax.ShapeDtypeStruct(shape, BF16) for shape in shapes],
        [buffer, buffer, pltpu.VMEM((LANES, LANES), F32)]
        + [pltpu.VMEM(shape, BF16) for shape in own]
        + [pltpu.VMEM((4 * rows, width), BF16)] + sems(2, PIECES) + [pltpu.SemaphoreType.DMA((4,))]
        + sems(PIECES) + sems(count) + sems(count)
        + [pltpu.SemaphoreType.DMA((max(9, chips + 1),))] * 16,
        (order, lengths, x, gain, cotangent, *raw), number, "deal_and_gather", rows * width * 20,
    )[0]


def small_rows(width):
    rows = (4 * width + 2 * VAL) // LANES + 1
    return rows + -rows % 8


def assemble(small, mix0, mix1, ffn0, ffn1, heads0, heads1, scalars0, scalars1):
    small[...] = jnp.zeros(small.shape, F32)
    at = 0
    for term in (mix0, mix1, ffn0, ffn1, heads0, heads1):
        for r in range(term.shape[1] // LANES):
            small[at : at + 1, :] = term[:, r * LANES : (r + 1) * LANES]
            at += 1
    head = lax.axis_index("zl") * 2 + lax.axis_index("core")
    lane = lax.broadcasted_iota(jnp.int32, (1, LANES), 1)
    row = jnp.zeros((1, LANES), F32)
    values = (scalars0[0:1, :], scalars1[0:1, :], scalars0[1:2, :], scalars1[1:2, :])
    for place, value in enumerate(values):
        row = row + jnp.where(lane == place * 4 + head, value, 0.0)
    small[at : at + 1, :] = row


def final_kernel(
    chips, jobs, order_ref, partial, x_hbm, gain_ref, grad_hbm, *refs
):
    terms, refs = refs[:7], refs[7:]
    (in_ref, aux_ref), refs = refs[:2], refs[2:]
    home_ref, total_ref, *homes = refs[:5]
    refs = refs[5:]
    cut = [pl.ds(0, CONV_CH), pl.ds(CONV_CH, VAL)]
    grads = [in_ref.at[:, cut[0]], in_ref.at[:, cut[1]], aux_ref]
    (away_held, own_held, x_ref, grad_ref, loads, beside_far, beside_own, sums, far, last, back,
     picked, small, by_plane, by_z, plane_sum,
     send, recv, role_send, role_recv, plane_send, plane_recv, small_send, small_recv, z_send,
     z_recv), refs = refs[:26], refs[26:]
    reduces, returns = [], []
    for at in range(3):
        summed, four, refs = refs[0], refs[1:5], refs[5:]
        buffers = len(Reduce.buffers(grads[at].shape, chips))
        reduces.append(Reduce(grads[at], summed, four[0], four[1], chips, refs[:buffers]))
        returns.append(FromPlane(summed, homes[at], four[2], four[3], chips))
        refs = refs[buffers:]
    plane, trade = Plane(chips), Trade(chips)
    scatter = Scatter(
        partial, beside_far, beside_own, sums, far, send, recv, (away_held, own_held, loads)
    )
    scatter.load()
    rows_in = [
        pltpu.make_async_copy(x_hbm.at[trade.zl], x_ref, loads.at[2]),
        pltpu.make_async_copy(grad_hbm.at[trade.zl], grad_ref, loads.at[3]),
    ]
    load_all(rows_in)
    count = plane.count
    part = x_ref.shape[0] // count
    rows = lambda index: pl.ds(pl.multiple_of(index * part, part), part)
    tier = trade.zp * 2 + trade.zl
    tier_device = lambda at: at_device(trade.chip, trade.core, at // 2, at % 2)
    for k in range(1, 4):
        signal(tier_device(lax.rem(tier + k, 4)))
    expected = plane.greet() + trade.greet_roles() + greet_group() + jobs.greet() + 3
    for job in reduces + returns:
        expected = expected + job.greet()
    wait_greetings(expected)
    scatter.start()
    for job in reduces:
        job.start()
    jobs.start()
    dgain = jnp.zeros((1, x_ref.shape[1]), F32)
    for copy in rows_in:
        copy.wait()
    to_homes = []
    size = x_ref.shape[0] // PIECES
    parts = max(size // part, 1)
    for p in range(PIECES):
        at = scatter.local(p)
        grad, piece = norm_back(scatter.total(p), x_ref[at, :].astype(F32), gain_ref[0:1, :].astype(F32))
        dgain = dgain + piece
        last[at, :] = (grad + grad_ref[at, :]).astype(BF16)
        for index in range(p * parts, (p + 1) * parts):
            copy = remote(last.at[rows(index)], back.at[trade.slot], role_send.at[index],
                          role_recv.at[trade.slot], trade.home(index))
            mine = trade.home_mine(index)
            unless(mine, copy.start)

            @pl.when(mine)
            def _():
                back[trade.slot] = last[rows(index), :]

            to_homes.append((copy, mine))
    assemble(small, dgain, *terms)
    small_out, small_in = [], []
    for j in range(1, count):
        to, source = plane.to(j), plane.source(j)
        small_out.append(
            remote(small, by_plane.at[plane.own], small_send.at[j], small_recv.at[j], plane.device(to))
        )
        small_in.append(
            remote(small, by_plane.at[source], small_send.at[j], small_recv.at[j], plane.device(source))
        )
    for copy in small_out:
        copy.start()
    by_plane[plane.own] = small[...]
    for job in reduces:
        job.middle()
    reduces[0].finish()
    returns[0].start()
    for slot in range(count):
        arrival = remote(last.at[rows(0)], back.at[slot], role_send.at[0], role_recv.at[slot],
                         trade.role(slot))
        unless(trade.role_mine(slot), arrival.wait_recv)
    outward, inward = [], []
    for j in range(count):
        to, source = plane.to(j), plane.source(j)
        at = jnp.int32(0)
        for slot in range(count):
            at = jnp.where(order_ref[slot] == to, slot, at)
        picked[j] = back[at]
        if j == 0:
            home_ref[rows(plane.own), :] = picked[0]
            continue
        copy = remote(picked.at[j], home_ref.at[rows(plane.own)], plane_send.at[j], plane_recv.at[j],
                      plane.device(to))
        copy.start()
        outward.append(copy)
        inward.append(
            remote(picked.at[j], home_ref.at[rows(source)], plane_send.at[j], plane_recv.at[j],
                   plane.device(source))
        )
    jobs.middle()
    for reduce, back_home in zip(reduces[1:], returns[1:]):
        reduce.finish()
        back_home.start()
    for copy in small_in:
        copy.wait_recv()
    total = by_plane[0]
    for index in range(1, count):
        total = total + by_plane[index]
    plane_sum[...] = total
    z_out, z_in = [], []
    for k in range(1, 4):
        to, source = lax.rem(tier + k, 4), lax.rem(tier + 4 - k, 4)
        z_out.append(remote(plane_sum, by_z.at[tier], z_send.at[k], z_recv.at[k], tier_device(to)))
        z_in.append(remote(plane_sum, by_z.at[source], z_send.at[k], z_recv.at[k], tier_device(source)))
    for copy in z_out:
        copy.start()
    by_z[tier] = total
    for copy in z_in:
        copy.wait_recv()
    total_ref[...] = (by_z[0] + by_z[1]) + (by_z[2] + by_z[3])
    for copy in inward:
        copy.wait_recv()
    scatter.finish()
    for copy, mine in to_homes:
        unless(mine, copy.wait_send)
    for copy in small_out + z_out + outward:
        copy.wait_send()
    jobs.finish()
    for job in returns:
        job.finish()


def final_step(order, partial, x, gain, grad, terms, grads, chips, jobs, number):
    _, rows, width = x.shape
    small = jax.ShapeDtypeStruct((small_rows(width), LANES), F32)
    vmem = pl.BlockSpec(memory_space=pltpu.VMEM)
    count = 2 * chips
    block = pltpu.VMEM((rows, width), BF16)
    parted = pltpu.VMEM((count, rows // count, width), BF16)
    hbm = pl.BlockSpec(memory_space=pl.ANY)
    chained = []
    pieces = [(grads[0].shape[0], cols) for cols in (CONV_CH, VAL, LANES)]
    for a in pieces:
        chained.append(pltpu.VMEM(Reduce.result(a, chips), BF16))
        chained += [pltpu.SemaphoreType.DMA((max(9, chips + 1),))] * 4
        chained += Reduce.buffers(a, chips)
    sems = lambda *shape: [pltpu.SemaphoreType.DMA(shape), pltpu.SemaphoreType.DMA(shape)]
    return carry_call(
        functools.partial(final_kernel, chips), jobs, (),
        [pl.BlockSpec(memory_space=pltpu.SMEM), hbm, hbm, vmem, hbm] + [vmem] * 7 + [hbm] * 2,
        [vmem, vmem] + [hbm] * 3,
        [
            jax.ShapeDtypeStruct((rows, width), BF16),
            jax.ShapeDtypeStruct(small.shape, F32),
        ]
        + [
            jax.ShapeDtypeStruct(FromPlane.result(Reduce.result(a, chips), chips), BF16)
            for a in pieces
        ],
        [block] * 2 + [pltpu.VMEM((rows, width), x.dtype), pltpu.VMEM((rows, width), F32)]
        + [pltpu.SemaphoreType.DMA((4,))] + [block] * 5 + [parted] * 2
        + [
            pltpu.VMEM(small.shape, F32), pltpu.VMEM((count,) + small.shape, F32),
            pltpu.VMEM((4,) + small.shape, F32), pltpu.VMEM(small.shape, F32),
        ]
        + sems(3, PIECES) + sems(count) + sems(count) + sems(count) + sems(4) + chained,
        (order, partial, x, gain, grad, *terms, *grads), number, "final_step", rows * width * 20,
    )


def only_jobs_kernel(jobs):
    wait_greetings(jobs.greet())
    jobs.start()
    jobs.middle()
    jobs.finish()


def only_jobs(jobs, number):
    return carry_call(only_jobs_kernel, jobs, (), [], [], [], [], (), number, "weights_back", 0)[1]


def weights_out_kernel(small_ref, home_ref, *refs):
    ins, outs = refs[:14], refs[14:]
    for layer in range(2):
        total = lambda ref: ref[0].astype(F32) + ref[1].astype(F32)
        qkv, head_gate, aux, out, gate, up, down = (
            total(ref) for ref in ins[7 * layer : 7 * layer + 7]
        )
        outs[0][layer] = qkv[:, :KEY]
        outs[1][layer] = qkv[:, KEY : 2 * KEY]
        outs[2][layer] = qkv[:, 2 * KEY :]
        outs[3][layer] = head_gate
        turned = aux.T
        outs[4][layer] = turned[0:2, :]
        outs[14][layer] = turned[2:6, :]
        outs[5][layer] = out.T
        outs[6][layer] = gate.T
        outs[7][layer] = up.T
        outs[8][layer] = down.T
    outs[15][...] = home_ref[...].astype(F32)[:, None, :]
    at = 0
    for ref in outs[9:12]:
        for layer in range(2):
            for r in range(ref.shape[1] // LANES):
                ref[layer : layer + 1, r * LANES : (r + 1) * LANES] = small_ref[at : at + 1, :]
                at += 1
    heads = outs[12].shape[1]
    for member in range(2):
        for layer in range(2):
            first = (2 * member + layer) * heads
            outs[12 + member][layer : layer + 1, :] = small_ref[at : at + 1, first : first + heads]


def weights_out(small, home, first, second, heads):
    width = home.shape[1]
    rows, units = first[0].shape[1], first[6].shape[2]
    shapes = [
        (2, rows, KEY), (2, rows, KEY), (2, rows, VAL), (2, rows, VAL), (2, 2, rows), (2, VAL, rows),
        (2, units, rows), (2, units, rows), (2, units, rows),
        (2, width), (2, width), (2, VAL), (2, heads), (2, heads), (2, 4, rows),
        (home.shape[0], 1, width),
    ]
    vmem = pl.BlockSpec(memory_space=pltpu.VMEM)
    return pl.pallas_call(
        weights_out_kernel,
        in_specs=[vmem] * 16,
        out_specs=[vmem] * 16,
        out_shape=[jax.ShapeDtypeStruct(shape, F32) for shape in shapes],
        compiler_params=pltpu.CompilerParams(vmem_limit_bytes=56 * 1024 * 1024),
        name="weights_out",
    )(small, home, *first, *second)


def ffn_parts(x, gate_ref, up_ref):
    gate, up = mm(x, gate_ref[...]), mm(x, up_ref[...])
    act, sig = silu_of(gate)
    return gate, up, act, sig


def begin_jobs(jobs, at, steps, turns=None):
    if jobs.kinds:
        @pl.when(at == 0)
        def _():
            wait_greetings(jobs.greet())
            jobs.start()

        early, late = turns or (steps // 2, steps - 1)

        @pl.when(at == early)
        def _():
            jobs.middle(late=False)

        @pl.when(at == late)
        def _():
            jobs.middle(late=True)


def end_jobs(jobs, at, steps):
    if jobs.kinds:
        @pl.when(at == steps - 1)
        def _():
            jobs.finish()


def ffn_forward_kernel(jobs, x_ref, gate_ref, up_ref, down_ref, part_ref):
    at, steps = pl.program_id(0), pl.num_programs(0)
    begin_jobs(jobs, at, steps)
    _, up, act, _ = ffn_parts(x_ref[...], gate_ref, up_ref)
    part_ref[...] = mm((act * up).astype(BF16), down_ref[...], NT).astype(BF16)
    end_jobs(jobs, at, steps)


def whole(shape):
    return pl.BlockSpec(shape, lambda i: (0, 0), pipeline_mode=pl.Buffered(1))


def ffn_forward(x, weights, jobs, number):
    length, width = x.shape
    rows = pl.BlockSpec((CHUNK, width), lambda i: (i, 0))
    return carry_call(
        ffn_forward_kernel, jobs, (length // CHUNK,),
        [rows] + [whole(weight.shape) for weight in weights], [rows],
        [jax.ShapeDtypeStruct((length, width), BF16)], [], (x, *weights), number, "ffn_forward",
        4 * 10**9,
    )


def ffn_backward_kernel(both, jobs, x_ref, g_ref, gate_ref, up_ref, down_ref, *refs):
    outs, (low_gate, low_up, hidden_ref, x_held, g_held) = refs[:-5], refs[-5:]
    if both:
        residual_ref, outs = outs[0], outs[1:]
    part_ref, dgate_ref, dup_ref, ddown_ref = outs[:4]
    at, steps = pl.program_id(0), pl.num_programs(0)
    chunks = steps // 2
    begin_jobs(jobs, at, steps)

    @pl.when(at < chunks)
    def _():
        rows = pl.ds(pl.multiple_of(at * CHUNK, CHUNK), CHUNK)
        x, g = x_ref[...], g_ref[...]
        x_held[rows, :] = x
        g_held[rows, :] = g
        gate, up, act, sig = ffn_parts(x, gate_ref, up_ref)
        hidden = (act * up).astype(BF16)
        hidden_ref[rows, :] = hidden
        if both:
            own = lax.axis_index("zl") * 2 + lax.axis_index("core")
            outs[4][...] = (
                mm(hidden, down_ref[...], NT) + jnp.where(at == own, residual_ref[lax.axis_index("zl")], 0.0)
            ).astype(BF16)
        dhidden = mm(g, down_ref[...])
        dgate = (dhidden * up * (sig * (1.0 + gate * (1.0 - sig)))).astype(BF16)
        dup = (dhidden * act).astype(BF16)
        low_gate[rows, :] = dgate
        low_up[rows, :] = dup
        part_ref[...] = (mm(dgate, gate_ref[...], NT) + mm(dup, up_ref[...], NT)).astype(BF16)

    @pl.when(at >= chunks)
    def _():
        columns = pl.ds(pl.multiple_of((at - chunks) * CHUNK, CHUNK), CHUNK)
        dgate_ref[...] = mm(x_held[:, columns], low_gate[...], TN).astype(BF16)
        dup_ref[...] = mm(x_held[:, columns], low_up[...], TN).astype(BF16)
        ddown_ref[...] = mm(g_held[:, columns], hidden_ref[...], TN).astype(BF16)

    end_jobs(jobs, at, steps)


def ffn_backward(x, g, weights, jobs, number, residual=None):
    both = residual is not None
    length, width = x.shape
    chunks = length // CHUNK
    units = weights[0].shape[1]
    assert length == width and (not both or residual.shape[1] == CHUNK)
    rows = pl.BlockSpec((CHUNK, width), lambda i: (jnp.minimum(i, chunks - 1), 0))
    late = pl.BlockSpec((CHUNK, units), lambda i: (jnp.maximum(i - chunks, 0), 0))
    out = lambda cols: jax.ShapeDtypeStruct((length, cols), BF16)
    return carry_call(
        functools.partial(ffn_backward_kernel, both), jobs, (2 * chunks,),
        [rows, rows] + [whole(weight.shape) for weight in weights] + [
            pl.BlockSpec((2, CHUNK, width), lambda i: (0, 0, 0), pipeline_mode=pl.Buffered(1))
        ] * both,
        [rows] + [late] * 3 + [rows] * both,
        [out(width)] + [out(units)] * 3 + [out(width)] * both,
        [pltpu.VMEM((length, units), BF16)] * 3 + [pltpu.VMEM((length, width), BF16)] * 2,
        (x, g, *weights) + ((residual,) if both else ()), number, "ffn_backward", 12 * 10**9,
    )


class Held:
    def __init__(self, at, sources, held, sems):
        self.at = at
        self.copies = [
            pltpu.make_async_copy(source, ref, sems.at[index])
            for index, (source, ref) in enumerate(zip(sources, held))
        ]

    def start(self):
        @pl.when(self.at == 0)
        def _():
            for copy in self.copies:
                copy.start()

    def ready(self, index):
        pl.when(self.at == 0)(self.copies[index].wait)


def held_scratch(weights):
    return [pltpu.VMEM(weight.shape, BF16) for weight in weights] + [
        pltpu.SemaphoreType.DMA((len(weights),))
    ]


def row_major(x):
    return with_layout_constraint(x, Layout(major_to_minor=tuple(range(x.ndim))))


def linear(sizes, index):
    place = 0
    for size, at in zip(sizes, index):
        place = place * size + at
    return place


class Roles:
    def __init__(self):
        self.sizes = tuple(lax.axis_size(name) for name in AXES)
        self.chips, self.cores, self.zps, self.zls = self.sizes
        assert self.cores == 2 and self.zps == 2 and self.zls == 2

    def every(self):
        for chip in range(self.chips):
            for core in range(2):
                for zp in range(2):
                    for zl in range(2):
                        yield chip, core, zp, zl

    def rows_pairs(self):
        pairs = []
        for chip, core, zp, zl in self.every():
            slot, part = chip * 2 + zp, zl * 2 + core
            source = linear(self.sizes, (slot // 2, slot % 2, part // 2, part % 2))
            pairs.append((source, linear(self.sizes, (chip, core, zp, zl))))
        return pairs

    def weight_pairs(self, which):
        pairs = []
        for chip, core, zp, zl in self.every():
            head = zp * 2 + zl
            to = (chip, head % 2, core ^ which, head // 2)
            pairs.append(
                (linear(self.sizes, (chip, core, zp, zl)), linear(self.sizes, to))
            )
        return pairs


def flipped(pairs):
    return [(b, a) for a, b in pairs]


def chip_gather(ordered):
    return lax.all_gather(ordered, "chip", axis=0, tiled=True)


def to_plane(pack, roles):
    halves = [lax.ppermute(pack, AXES, roles.weight_pairs(which)) for which in range(2)]
    swap = lax.axis_index("zp") == 1
    return jnp.concatenate(
        [jnp.where(swap, halves[1], halves[0]), jnp.where(swap, halves[0], halves[1])], axis=0
    )


def summed(parts, kind):
    return jnp.sum(parts.astype(F32), axis=0).astype(kind)


def deal(values, order):
    spread = lax.all_to_all(values, ("chip", "core"), split_axis=2, concat_axis=1, tiled=True)
    picked = jnp.take(spread, order, axis=1)
    return lax.all_to_all(picked, ("chip", "core"), split_axis=1, concat_axis=2, tiled=True)


def shards(
    tokens, lengths, order, norm_mix, w_query, w_key, w_value, w_gate, w_decay, conv_filter,
    log_rate, step_bias, norm_heads, w_out, norm_ffn, w_ffn_gate, w_ffn_up, w_ffn_down, cotangent,
):
    roles = Roles()
    layer_count = w_query.shape[0]
    assert layer_count == 2
    heads_total = log_rate.shape[1]
    chip, core, zp, zl = (lax.axis_index(name) for name in AXES)
    head = zl * 2 + core
    rows_local, slots_local, width = tokens.shape
    assert slots_local == 1 and w_decay.shape[2] == 1
    slot_total = order.shape[0]
    units = w_ffn_gate.shape[2]
    rows_part = w_query.shape[1]
    to_roles = roles.rows_pairs()

    def carry(*jobs):
        return Jobs(list(jobs), roles.chips)

    scalars = (log_rate, step_bias)
    kernel_deal = rows_local % (16 * slot_total) == 0
    if kernel_deal:
        turned = lambda w: w.transpose(0, 2, 1)
        raw = (
            w_query, w_key, w_value, w_gate, turned(w_decay[:, :, 0, :]), conv_filter[:, :, 0, :],
            w_out, turned(w_ffn_gate), turned(w_ffn_up), w_ffn_down,
        )
        (residual, rows_in, start, qkv_next, side_next, out_next, gate_next, up_first, up_next,
         down_first, down_next, qkv0, side0, _, _, out_wide, gate_wide) = deal_and_gather(
            order, lengths, tokens[:, 0, :], norm_mix, cotangent[:, 0, :], raw, roles.chips, 1
        )
    else:
        packs = []
        for layer in range(layer_count):
            aux = jnp.concatenate([w_decay[layer, :, 0, :], conv_filter[layer, :, 0, :].T], axis=1)
            aux = jnp.pad(aux, ((0, 0), (0, LANES - aux.shape[1])))
            packs.append(
                [
                    row_major(pack) for pack in (
                        jnp.concatenate([w_query[layer], w_key[layer], w_value[layer]], axis=1),
                        jnp.concatenate([w_gate[layer], aux], axis=1),
                        w_out[layer].T, w_ffn_gate[layer], w_ffn_up[layer], w_ffn_down[layer].T,
                    )
                ]
            )
        (qkv0, side0, out_wide, gate_wide, up_first, down_first) = packs[0]
        (qkv_next, side_next, out_next, gate_next, up_next, down_next) = packs[1]
        positions = (zp * 2 + zl) * rows_local + jnp.arange(rows_local)
        start = cotangent[:, 0, :] * (positions < lengths[order[chip * 2 + core]]).astype(BF16)[:, None]
        residual = lax.ppermute(deal(tokens, order)[:, 0, :], AXES, to_roles)
        (residual, rows_in), _ = first_gather(residual, norm_mix, 0, carry(), 1)
        qkv0, side0 = (chip_gather(to_plane(pack, roles)) for pack in (qkv0, side0))
        out_wide, gate_wide = (to_plane(pack, roles) for pack in (out_wide, gate_wide))

    (heads0, *kept0), (out0, gate0, up_wide, down_wide, qkv_wide) = mixer_forward(
        0, rows_in, qkv0, side0, norm_heads, scalars,
        carry((Spread, out_wide), (Spread, gate_wide), (ToPlane, up_first), (ToPlane, down_first),
              (ToPlane, qkv_next)),
        2,
    )
    rows_in0, residual0 = rows_in, residual
    (middle0, rows_ffn0), (up0, down0, side_wide, gradient) = mixer_bridge(
        heads0, out0, residual0, norm_ffn, 0,
        carry((Spread, up_wide), (Spread, down_wide), (ToPlane, side_next), (ToRole, start)), 3,
    )
    ffn0 = (gate0, up0, down0)
    (part,), _ = ffn_forward(rows_ffn0, ffn0, carry(), None)
    (residual1, rows_in1), (qkv1, side1, out_wide, down_wide) = forward_bridge(
        part, middle0, norm_mix, 1,
        carry((Spread, qkv_wide), (Spread, side_wide), (ToPlane, out_next), (ToPlane, down_next)), 4,
    )
    (heads1, *kept1), (out1, down1, gate_wide, up_wide, grad_rows) = mixer_forward(
        1, rows_in1, qkv1, side1, norm_heads, scalars,
        carry((Spread, out_wide), (Spread, down_wide), (ToPlane, gate_next), (ToPlane, up_next),
              (Share, gradient)),
        5,
    )
    (middle1, rows_ffn1), (gate1, up1) = mixer_bridge(
        heads1, out1, residual1, norm_ffn, 1, carry((Spread, gate_wide), (Spread, up_wide)), 6
    )
    ffn1 = (gate1, up1, down1)
    (part, dgate1, dup1, ddown1, part_out), _ = ffn_backward(
        rows_ffn1, grad_rows, ffn1, carry(), None, residual=middle1
    )

    (gradient, grad_rows, dgain_ffn1, dout1), (dgate1, dup1) = backward_bridge(
        part, middle1, norm_ffn, 1, grad_rows, carry((Reduce, dgate1), (Reduce, dup1)), 7, heads1
    )
    (part, din1, daux1, dgain1, dscalars1), jobs_results = mixer_backward(
        1, grad_rows, rows_in1, qkv1, side1, out1, norm_heads, scalars, kept1,
        carry((Reduce, ddown1), (Reduce, dout1), (FromPlane, dgate1), (FromPlane, dup1),
              (ShareSum, part_out)),
        8,
    )
    ddown1, dout1, gate_home1, up_home1, mixed = jobs_results
    (gradient, grad_rows, dgain_mix1), (dqkv1, daux1, mixed) = backward_bridge(
        part, residual1, norm_mix, 1, gradient,
        carry((Reduce, din1, (0, CONV_CH)), (Reduce, daux1), (FromRole, mixed)), 9,
    )
    (part, dgate0, dup0, ddown0), (side1, qkv_home1, aux_home1, down_home1) = ffn_backward(
        rows_ffn0, grad_rows, ffn0,
        carry((Reduce, din1, (CONV_CH, VAL)), (FromPlane, dqkv1), (FromPlane, daux1),
              (FromPlane, ddown1)),
        14,
    )
    (gradient, grad_rows, dgain_ffn0, dout0), (dgate0, dup0) = backward_bridge(
        part, middle0, norm_ffn, 0, gradient,
        carry((Reduce, dgate0), (Reduce, dup0)), 10, heads0,
    )
    (part, din0, daux0, dgain0, dscalars0), jobs_results = mixer_backward(
        0, grad_rows, rows_in0, qkv0, side0, out0, norm_heads, scalars, kept0,
        carry((Reduce, ddown0), (Reduce, dout0), (FromPlane, dgate0), (FromPlane, dup0),
              (FromPlane, side1), (FromPlane, dout1)),
        11,
    )
    ddown0, dout0, gate_home0, up_home0, side_home1, out_home1 = jobs_results
    terms = (dgain_mix1, dgain_ffn0, dgain_ffn1, dgain0, dgain1, dscalars0, dscalars1)
    last = (din0, daux0)
    last_jobs = carry((FromPlane, ddown0), (FromPlane, dout0))
    if kernel_deal:
        (home, flat, *last), results = final_step(
            order, part, residual0, norm_mix, gradient, terms, last, roles.chips, last_jobs, 12
        )
    else:
        (gradient, dgain_mix), results = backward_last(
            part, residual0, norm_mix, 0, gradient, last_jobs, 12
        )
        mine = (jnp.arange(heads_total) == head).astype(F32)
        flat = jnp.concatenate(
            [dgain_mix[0], *(term[0] for term in terms[:5])]
            + [mine * term[row, 0] for row in range(2) for term in terms[5:]]
        )
        flat = jnp.pad(flat, (0, small_rows(width) * LANES - flat.shape[0])).reshape(-1, LANES)
        flat = lax.psum(flat, AXES)
        dealt_grad = lax.ppermute(gradient, AXES, flipped(to_roles))
        places = jnp.arange(slot_total, dtype=jnp.int32)
        inverse = jnp.sum(jnp.where(order[None, :] == places[:, None], places[None, :], 0), axis=1)
        home = deal(dealt_grad[:, None, :], inverse)[:, 0, :]
        last = only_jobs(
            carry((Reduce, din0, (0, CONV_CH)), (Reduce, din0, (CONV_CH, VAL)), (Reduce, daux0)), 13
        )
        last = only_jobs(carry(*[(FromPlane, a) for a in last]), 15)
    down_home0, out_home0 = results
    qkv_home0, side_home0, aux_home0 = last
    first = (qkv_home0, side_home0, aux_home0, out_home0, gate_home0, up_home0, down_home0)
    second = (qkv_home1, side_home1, aux_home1, out_home1, gate_home1, up_home1, down_home1)
    if rows_part % LANES == 0:
        outs = weights_out(flat, home, first, second, heads_total)
    else:
        flat = flat.reshape(-1)
        small, at = [], 0
        for size in (width, width, VAL, heads_total, heads_total):
            small.append(flat[at : at + layer_count * size].reshape(layer_count, size))
            at += layer_count * size
        qkv, side, aux, out, gate, up, down = (
            jnp.stack([summed(a, F32), summed(b, F32)]) for a, b in zip(first, second)
        )
        turned = lambda a: a.transpose(0, 2, 1)
        outs = [
            qkv[:, :, :KEY], qkv[:, :, KEY : 2 * KEY], qkv[:, :, 2 * KEY :], side, turned(aux)[:, :2], turned(out), turned(gate), turned(up),
            turned(down), *small, turned(aux)[:, 2:6], home.astype(F32)[:, None, :],
        ]
    return (
        mixed[:, None, :],
        outs[15],
        outs[9],
        outs[0], outs[1], outs[2], outs[3],
        outs[4].transpose(0, 2, 1)[:, :, None, :],
        outs[14][:, :, None, :],
        outs[12],
        outs[13],
        outs[11],
        outs[5],
        outs[10],
        outs[6].transpose(0, 2, 1), outs[7].transpose(0, 2, 1), outs[8],
    )


def solution(mesh):
    dp, tensor = mesh.devices.shape
    mesh = Mesh(mesh.devices.reshape(dp // 2, 2, tensor // 2, 2), AXES)
    d, t = ("chip", "core"), ("zp", "zl")
    rows = P(t, d, None)
    by_rows, by_columns = P(None, d, t), P(None, t, d)
    heads, filters = P(None, d, t, None), P(None, None, t, d)
    return jax.shard_map(
        shards,
        mesh=mesh,
        in_specs=(
            rows, P(), P(), P(), by_rows, by_rows, by_rows, by_rows, heads, filters,
            P(), P(), P(), by_columns, P(), by_rows, by_rows, by_columns, rows,
        ),
        out_specs=(
            rows, rows, P(), by_rows, by_rows, by_rows, by_rows, heads, filters,
            P(), P(), P(), by_columns, P(), by_rows, by_rows, by_columns,
        ),
        check_vma=False,
    )
```

```python
import functools
import jax
import jax.numpy as jnp
from jax import lax
from jax.experimental import pallas as pl
from jax.experimental.layout import Layout, with_layout_constraint
from jax.experimental.pallas import tpu as pltpu
from jax.sharding import Mesh, PartitionSpec as P

CHUNK = 256
LANES = 128
KEY = 256
VAL = 512
CONV_CH = 2 * KEY + VAL
F32 = jnp.float32
BF16 = jnp.bfloat16
NN = (((1,), (0,)), ((), ()))
NT = (((1,), (1,)), ((), ()))
TN = (((0,), (0,)), ((), ()))


def mm(a, b, dims=NN):
    return lax.dot_general(
        a.astype(BF16), b.astype(BF16), dims, preferred_element_type=F32
    )


def split_low(a):
    high = a.astype(BF16)
    return high, (a - high.astype(F32)).astype(BF16)


def mm3(a, b, dims=NN):
    a_high, a_low = split_low(a)
    b_high, b_low = split_low(b)
    dot = functools.partial(
        lax.dot_general, dimension_numbers=dims, preferred_element_type=F32
    )
    return dot(a_high, b_high) + (dot(a_high, b_low) + dot(a_low, b_high))


def mm_exact_left(a, b, dims=NN):
    a = a.astype(BF16)
    high = b.astype(BF16)
    rest = b - high.astype(F32)
    mid = rest.astype(BF16)
    low = (rest - mid.astype(F32)).astype(BF16)
    dot = functools.partial(
        lax.dot_general, dimension_numbers=dims, preferred_element_type=F32
    )
    return dot(a, high) + (dot(a, mid) + dot(a, low))


def iotas():
    rows = lax.broadcasted_iota(jnp.int32, (CHUNK, CHUNK), 0)
    cols = lax.broadcasted_iota(jnp.int32, (CHUNK, CHUNK), 1)
    return rows, cols


def wide(col_block, width):
    return jnp.concatenate([col_block] * (width // LANES), axis=1)


def rates_of(rates, rate, bias):
    write = jax.nn.sigmoid(jnp.broadcast_to(rates[:, 0:1], (CHUNK, LANES)))
    logit = jnp.broadcast_to(rates[:, 1:2], (CHUNK, LANES)) + bias
    soft = jnp.maximum(logit, 0.0) + jnp.log1p(jnp.exp(-jnp.abs(logit)))
    return write, -rate * soft, jax.nn.sigmoid(logit)


def head_scalars(scalars_ref, layer):
    head = lax.axis_index("zl") * 2 + lax.axis_index("core")
    rate_ref, bias_ref = scalars_ref
    here = lax.broadcasted_iota(jnp.int32, (1, rate_ref.shape[1]), 1) == head
    pick = lambda ref: jnp.sum(
        jnp.where(here, ref[layer : layer + 1, :].astype(F32), 0.0), axis=1, keepdims=True
    )
    return jnp.exp(pick(rate_ref)), pick(bias_ref)


def decay_terms(step, rows, cols):
    inclusive = (rows >= cols).astype(BF16)
    total = mm_exact_left(inclusive, step)
    spread = wide(total, CHUNK) - jnp.concatenate([total.T] * (CHUNK // LANES), axis=0)
    decay = jnp.where(rows >= cols, jnp.exp(jnp.minimum(spread, 0.0)), 0.0)
    last = jnp.broadcast_to(total[CHUNK - 1 : CHUNK, :], (CHUNK, LANES))
    return decay, jnp.exp(total), jnp.exp(last - total), jnp.exp(last)


def solve_unit(coupling, rows, cols):
    unit = jnp.where(rows == cols, 1.0, 0.0)
    same = ((rows >> 1) == (cols >> 1)) & (rows != cols)
    inverse = unit - jnp.where(same, coupling, 0.0)
    for level in range(1, CHUNK.bit_length() - 1):
        between = ((rows >> (level + 1)) == (cols >> (level + 1))) & (
            (rows >> level) != (cols >> level)
        )
        part = jnp.where(between, coupling, 0.0)
        inverse = inverse - mm(mm(inverse, part), inverse)
    return inverse + mm(inverse, unit - inverse - mm3(coupling, inverse))


def silu_of(x):
    gate = jax.nn.sigmoid(x)
    return x * gate, gate


def conv_rows(padded_ref, taps_ref, start):
    result = padded_ref[pl.ds(start, CHUNK), :] * taps_ref[0:1, :]
    for j in range(1, 4):
        result = result + padded_ref[pl.ds(start + j, CHUNK), :] * taps_ref[j : j + 1, :]
    return result


def forward_kernel(
    layer, jobs, rate_ref, bias_ref, x_ref, qkv_hbm, side_hbm, gain_ref,
    heads_ref, proj_ref, conv_ref, gate_ref, rates_ref, inverse_ref, fresh_ref, o_ref, state_ref,
    padded, memory, taps_ref, w_qkv_ref, w_side_ref, sems,
):
    at = pl.program_id(0)
    held = Held(at, (qkv_hbm, side_hbm), (w_qkv_ref, w_side_ref), sems)
    held.start()
    begin_jobs(jobs, at, pl.num_programs(0), (pl.num_programs(0) - 1,) * 2)
    @pl.when(pl.program_id(0) == 0)
    def _():
        memory[...] = jnp.zeros_like(memory)
        padded[0:8, :] = jnp.zeros((8, CONV_CH), F32)

    x = x_ref[...]
    held.ready(0)
    qkv = mm(x, w_qkv_ref[...])
    held.ready(1)

    @pl.when(at == 0)
    def _():
        taps_ref[...] = w_side_ref[:, VAL:].astype(F32).T[2:6, :]

    rates = mm(x, w_side_ref[:, VAL:])
    rates_ref[...] = rates
    proj_ref[...] = qkv
    gate_in = mm(x, w_side_ref[:, :VAL])
    gate_ref[...] = gate_in
    padded[8 : 8 + CHUNK, :] = qkv
    conv = conv_rows(padded, taps_ref, 5)
    padded[0:8, :] = qkv[CHUNK - 8 :, :]
    conv_ref[...] = conv
    act, _ = silu_of(conv)
    q, k, v = act[:, :KEY], act[:, KEY : 2 * KEY], act[:, 2 * KEY :]
    q = q * (lax.rsqrt(jnp.sum(q * q, axis=1, keepdims=True) + 1e-6) * KEY**-0.5)
    k = k * lax.rsqrt(jnp.sum(k * k, axis=1, keepdims=True) + 1e-6)
    rows, cols = iotas()
    write, step, _ = rates_of(rates, *head_scalars((rate_ref, bias_ref), layer))
    decay, growth, rest, final = decay_terms(step, rows, cols)
    coupling = jnp.where(rows > cols, wide(write, CHUNK) * mm3(k, k, NT) * decay, 0.0)
    inverse = solve_unit(coupling, rows, cols)
    inverse_ref[...] = inverse.astype(BF16)
    within = mm(q, k, NT) * decay
    state = memory[...]
    state_ref[...] = state
    low_state = state.astype(BF16)
    source = wide(write, VAL) * (v - wide(growth, VAL) * mm(k, low_state))
    fresh = mm3(inverse, source)
    fresh_ref[...] = fresh
    o = wide(growth, VAL) * mm(q, low_state) + mm(within, fresh)
    o_ref[...] = o
    memory[...] = wide(final, VAL) * state + mm(k * wide(rest, KEY), fresh, TN)
    scaled = o * lax.rsqrt(jnp.mean(o * o, axis=1, keepdims=True) + 1e-5) * gain_ref[layer : layer + 1, :].astype(F32)
    heads = (scaled * silu_of(gate_in)[0]).astype(BF16)
    heads_ref[...] = heads
    end_jobs(jobs, pl.program_id(0), pl.num_programs(0))


def head_spec(value):
    return pl.BlockSpec(value.shape, lambda i: (0, 0))


def mixer_forward(layer, x, qkv, pack, gain, scalars, jobs, number):
    length, width = x.shape
    chunks = length // CHUNK
    row = lambda cols: pl.BlockSpec((CHUNK, cols), lambda i: (i, 0))
    out = lambda cols, kind: jax.ShapeDtypeStruct((length, cols), kind)
    return carry_call(
        functools.partial(forward_kernel, layer), jobs, (chunks,),
        [head_spec(scalars[0]), head_spec(scalars[1]), row(width), ANY_SPEC, ANY_SPEC, head_spec(gain)],
        [
            row(VAL), row(CONV_CH), row(CONV_CH), row(VAL), row(LANES), row(CHUNK), row(VAL), row(VAL),
            pl.BlockSpec((None, KEY, VAL), lambda i: (i, 0, 0)),
        ],
        [
            out(VAL, BF16), out(CONV_CH, F32), out(CONV_CH, F32), out(VAL, F32), out(LANES, F32),
            out(CHUNK, BF16), out(VAL, F32), out(VAL, F32),
            jax.ShapeDtypeStruct((chunks, KEY, VAL), F32),
        ],
        [
            pltpu.VMEM((CHUNK + 8, CONV_CH), F32), pltpu.VMEM((KEY, VAL), F32),
            pltpu.VMEM((4, CONV_CH), F32),
        ] + held_scratch((qkv, pack)),
        (*scalars, x, qkv, pack, gain), number, "mixer_forward", 16 * 10**9,
    )


def unit_back(grad, vector, scale):
    inv = lax.rsqrt(jnp.sum(vector * vector, axis=1, keepdims=True) + 1e-6)
    dot = jnp.sum(grad * vector, axis=1, keepdims=True)
    return (grad - vector * (inv * inv * dot)) * (inv * scale)


def backward_kernel(
    layer, jobs, rate_ref, bias_ref, g_ref, x_ref, out_hbm, qkv_hbm, side_hbm, gain_ref,
    proj_ref, halo_ref, conv_ref, gate_ref, rates_ref, inverse_ref, fresh_ref, o_ref, state_ref,
    part_ref, din_ref, daux_ref, dgain_ref, dscalars_ref,
    padded, dpadded, dmemory, taps_ref, dtaps_ref, daux_sum, x_held, dproj_ref,
    w_out_ref, w_qkv_ref, w_side_ref, sems,
):
    at, steps = pl.program_id(0), pl.num_programs(0)
    chunks = steps // 2
    last = chunks - 1
    held = Held(at, (out_hbm, qkv_hbm, side_hbm), (w_out_ref, w_qkv_ref, w_side_ref), sems)
    held.start()
    begin_jobs(jobs, at, steps, (chunks - 1, chunks // 2))

    @pl.when(at == 0)
    def _():
        dmemory[...] = jnp.zeros_like(dmemory)
        dpadded[CHUNK : CHUNK + 8, :] = jnp.zeros((8, CONV_CH), F32)
        dtaps_ref[...] = jnp.zeros_like(dtaps_ref)
        daux_sum[...] = jnp.zeros_like(daux_sum)
        dgain_ref[...] = jnp.zeros_like(dgain_ref)
        dscalars_ref[...] = jnp.zeros_like(dscalars_ref)

    @pl.when(at < chunks)
    def _():
        rows, cols = iotas()
        padded[8 : 8 + CHUNK, :] = proj_ref[...]
        padded[0:8, :] = jnp.where(at == last, 0.0, halo_ref[...])
        conv = conv_ref[...]
        act, sig = silu_of(conv)
        act_q, act_k, v = act[:, :KEY], act[:, KEY : 2 * KEY], act[:, 2 * KEY :]
        q = act_q * (lax.rsqrt(jnp.sum(act_q * act_q, axis=1, keepdims=True) + 1e-6) * KEY**-0.5)
        k = act_k * lax.rsqrt(jnp.sum(act_k * act_k, axis=1, keepdims=True) + 1e-6)
        rates = rates_ref[...]
        write, step, sig_decay = rates_of(rates, *head_scalars((rate_ref, bias_ref), layer))
        decay, growth, rest, final = decay_terms(step, rows, cols)
        growth_v = wide(growth, VAL)
        write_v = wide(write, VAL)
        low_q, low_k = q.astype(BF16), k.astype(BF16)
        below = rows > cols
        strict_decay = jnp.where(below, decay, 0.0)
        keys = mm(low_k, low_k, NT) * strict_decay * wide(write, CHUNK)
        within = mm(low_q, low_k, NT) * decay
        held.ready(0)
        dheads = mm(g_ref[...], w_out_ref[...])
        o = o_ref[...]
        gate_in = gate_ref[...]
        gate, gate_sig = silu_of(gate_in)
        inv = lax.rsqrt(jnp.mean(o * o, axis=1, keepdims=True) + 1e-5)
        normal = o * inv
        gain = gain_ref[layer : layer + 1, :].astype(F32)
        dgate = dheads * normal * gain * (gate_sig * (1.0 + gate_in * (1.0 - gate_sig)))
        dscaled = dheads * gate
        dgain_ref[...] += jnp.sum(dscaled * normal, axis=0, keepdims=True)
        dnormal = dscaled * gain
        do = inv * (dnormal - normal * jnp.mean(dnormal * normal, axis=1, keepdims=True))
        state = state_ref[...]
        low_state = state.astype(BF16)
        fresh = fresh_ref[...]
        low_fresh = fresh.astype(BF16)
        dstate = dmemory[...]
        low_dstate = dstate.astype(BF16)
        low_do = do.astype(BF16)
        k_rest = k * wide(rest, KEY)
        rest_dstate = mm(k_rest, low_dstate)
        dfresh = mm(within, low_do, TN) + rest_dstate
        dsource = mm(inverse_ref[...], dfresh, TN)
        low_dsource = dsource.astype(BF16)
        dv = write_v * dsource
        dread = -(growth_v * dv)
        low_dread = dread.astype(BF16)
        do_growth = growth_v * do
        low_do_growth = do_growth.astype(BF16)
        dwithin = mm(low_do, low_fresh, NT)
        dcoupling = -mm(low_dsource, low_fresh, NT)
        dkeys = dcoupling * strict_decay * wide(write, CHUNK)
        dpairs = dwithin * decay
        dq = mm(low_do_growth, low_state, NT) + mm(dpairs, low_k)
        dk = (
            mm(low_dread, low_state, NT)
            + mm(dpairs, low_q, TN)
            + mm(dkeys + dkeys.T, low_k)
            + wide(rest, KEY) * mm(low_fresh, low_dstate, NT)
        )
        dmemory[...] = (
            wide(final, VAL) * dstate + mm(low_q, low_do_growth, TN) + mm(low_k, low_dread, TN)
        )
        spread = dwithin * within + dcoupling * keys
        straddle = jnp.where(below, mm_exact_left((rows <= cols).astype(BF16), spread), 0.0)
        read_rows = jnp.sum(
            do_growth * mm(low_q, low_state) + dread * mm(low_k, low_state), axis=1, keepdims=True
        )
        rest_rows = jnp.sum(fresh * rest_dstate, axis=1, keepdims=True)
        carried = jnp.sum(dstate * state) * final[0:1, 0:1]
        suffix = mm_exact_left(
            (rows <= cols).astype(BF16), jnp.broadcast_to(read_rows, (CHUNK, LANES))
        ) + mm_exact_left((rows > cols).astype(BF16), jnp.broadcast_to(rest_rows, (CHUNK, LANES)))
        dstep = suffix + jnp.sum(straddle, axis=1, keepdims=True) + carried
        dlogit = dstep * (-head_scalars((rate_ref, bias_ref), layer)[0]) * sig_decay
        dwrite = (1.0 - write) * jnp.sum(dsource * fresh, axis=1, keepdims=True)
        lane = lax.broadcasted_iota(jnp.int32, (CHUNK, LANES), 1)
        drates = jnp.where(lane == 0, dwrite, jnp.where(lane == 1, dlogit, 0.0))
        low_drates = drates.astype(BF16)
        daux_sum[...] += mm(low_drates, x_ref[...], TN)
        dscalars_ref[0:1, :] += jnp.sum(dstep * step, axis=0, keepdims=True)
        dscalars_ref[1:2, :] += jnp.sum(dlogit, axis=0, keepdims=True)
        dact = jnp.concatenate(
            [unit_back(dq, act_q, KEY**-0.5), unit_back(dk, act_k, 1.0), dv], axis=1
        )
        dconv = dact * (sig * (1.0 + conv * (1.0 - sig)))
        dpadded[0:CHUNK, :] = dconv
        dtaps_ref[2:6, :] += jnp.concatenate(
            [
                jnp.sum(dconv * padded[5 + j : 5 + j + CHUNK, :], axis=0, keepdims=True)
                for j in range(4)
            ],
            axis=0,
        )
        held.ready(1)
        held.ready(2)

        @pl.when(at == 0)
        def _():
            taps_ref[...] = w_side_ref[:, VAL:].astype(F32).T[2:6, :]

        dqkv = dconv * taps_ref[3:4, :]
        for j in range(3):
            dqkv = dqkv + dpadded[pl.ds(3 - j, CHUNK), :] * taps_ref[j : j + 1, :]
        dpadded[CHUNK : CHUNK + 8, :] = dconv[0:8, :]
        low_dqkv, low_dgate = dqkv.astype(BF16), dgate.astype(BF16)
        place = block(last - at, CHUNK)
        dproj_ref[place, :CONV_CH] = low_dqkv
        dproj_ref[place, CONV_CH:] = low_dgate
        x_held[place, :] = x_ref[...]
        part_ref[...] = (
            mm(low_dqkv, w_qkv_ref[...], NT)
            + mm(low_dgate, w_side_ref[:, :VAL], NT)
            + mm(low_drates, w_side_ref[:, VAL:], NT)
        ).astype(BF16)

    @pl.when(at == last)
    def _():
        daux_ref[...] = (daux_sum[...] + dtaps_ref[...]).T.astype(BF16)

    @pl.when(at >= chunks)
    def _():
        columns = block(at - chunks, CHUNK)
        din_ref[...] = mm(x_held[:, columns], dproj_ref[...], TN).astype(BF16)

    end_jobs(jobs, at, steps)


def mixer_backward(layer, g, x, qkv, pack, w_out, gain, scalars, saved, jobs, number):
    proj, conv, gate_in, rates, inverse, fresh, o, states = saved
    length, width = g.shape
    chunks = length // CHUNK
    back = chunks - 1
    at = lambda i: jnp.maximum(back - i, 0)
    row = lambda cols: pl.BlockSpec((CHUNK, cols), lambda i: (at(i), 0))
    out = lambda cols, kind: jax.ShapeDtypeStruct((length, cols), kind)
    steps = CHUNK // 8
    return carry_call(
        functools.partial(backward_kernel, layer), jobs, (2 * chunks,),
        [head_spec(scalars[0]), head_spec(scalars[1]), row(width), row(width)]
        + [ANY_SPEC] * 3 + [head_spec(gain),
            row(CONV_CH),
            pl.BlockSpec((8, CONV_CH), lambda i: (jnp.maximum(at(i) * steps - 1, 0), 0)),
            row(CONV_CH), row(VAL), row(LANES), row(CHUNK), row(VAL), row(VAL),
            pl.BlockSpec((None, KEY, VAL), lambda i: (at(i), 0, 0)),
        ],
        [
            row(width),
            pl.BlockSpec((CHUNK, CONV_CH + VAL), lambda i: (jnp.maximum(i - chunks, 0), 0)),
            pl.BlockSpec((width, LANES), lambda i: (0, 0)),
            pl.BlockSpec((1, VAL), lambda i: (0, 0)),
            pl.BlockSpec((8, LANES), lambda i: (0, 0)),
        ],
        [
            out(width, BF16), jax.ShapeDtypeStruct((width, CONV_CH + VAL), BF16),
            jax.ShapeDtypeStruct((width, LANES), BF16),
            jax.ShapeDtypeStruct((1, VAL), F32),
            jax.ShapeDtypeStruct((8, LANES), F32),
        ],
        [
            pltpu.VMEM((CHUNK + 8, CONV_CH), F32),
            pltpu.VMEM((CHUNK + 8, CONV_CH), F32),
            pltpu.VMEM((KEY, VAL), F32),
            pltpu.VMEM((4, CONV_CH), F32),
            pltpu.VMEM((LANES, CONV_CH), F32),
            pltpu.VMEM((LANES, width), F32),
            pltpu.VMEM((length, width), BF16),
            pltpu.VMEM((length, CONV_CH + VAL), BF16),
        ] + held_scratch((w_out, qkv, pack)),
        (*scalars, g, x, w_out, qkv, pack, gain, proj, proj, conv, gate_in, rates, inverse, fresh, o,
         states),
        number, "mixer_backward", 16 * 10**9,
    )


PIECES = 4
TURN = (1, 2)
AXES = ("chip", "core", "zp", "zl")


def partners():
    core, zl = lax.axis_index("core"), lax.axis_index("zl")
    return core, zl, {"core": 1 - core}, {"zl": 1 - zl}


def remote(src, dst, send, recv, device):
    return pltpu.make_async_remote_copy(
        src_ref=src, dst_ref=dst, send_sem=send, recv_sem=recv,
        device_id=device, device_id_type=pl.DeviceIdType.MESH,
    )


class Block:
    def __init__(self, zl, core, rows):
        self.first = (zl * 2 + core) * rows
        self.size = rows // PIECES

    def piece(self, p):
        return pl.ds(pl.multiple_of(self.first + p * self.size, self.size), self.size)

    def rows(self):
        rows = self.size * PIECES
        return pl.ds(pl.multiple_of(self.first, rows), rows)


class Scatter:
    def __init__(self, partial, beside_far, beside_own, sums, far, send, recv, held=None):
        core, zl, beside, across = partners()
        self.held = held
        rows = far.shape[0]
        self.partial, self.beside_far, self.beside_own = partial, beside_far, beside_own
        self.sums, self.far = sums, far
        self.size = rows // PIECES
        self.own = Block(zl, core, rows)
        self.away = Block(1 - zl, core, rows)
        own_beside, away_beside = Block(zl, 1 - core, rows), Block(1 - zl, 1 - core, rows)
        self.to_far = [
            remote(partial.at[away_beside.piece(p)], beside_far.at[self.local(p)],
                   send.at[0, p], recv.at[0, p], beside)
            for p in range(PIECES)
        ]
        self.to_own = [
            remote(partial.at[own_beside.piece(p)], beside_own.at[self.local(p)],
                   send.at[1, p], recv.at[1, p], beside)
            for p in range(PIECES)
        ]
        self.cross = [
            remote(sums.at[self.local(p)], far.at[self.local(p)],
                   send.at[2, p], recv.at[2, p], across)
            for p in range(PIECES)
        ]

    def local(self, p):
        return pl.ds(p * self.size, self.size)

    def load(self):
        away, own, sems = self.held
        self.loads = [
            pltpu.make_async_copy(self.partial.at[block.rows()], ref, sems.at[at])
            for at, (block, ref) in enumerate(((self.away, away), (self.own, own)))
        ]
        for copy in self.loads:
            copy.start()

    def mine(self, which, p):
        if self.held is None:
            return self.partial[(self.away, self.own)[which].piece(p), :]
        if p == 0:
            self.loads[which].wait()
        return self.held[which][self.local(p), :]

    def start(self):
        for copy in self.to_far:
            copy.start()
        for copy in self.to_own:
            copy.start()
        for p in range(PIECES):
            self.to_far[p].wait_recv()
            at = self.local(p)
            self.sums[at, :] = (
                self.mine(0, p).astype(F32) + self.beside_far[at, :].astype(F32)
            ).astype(BF16)
            self.cross[p].start()

    def total(self, p):
        self.to_own[p].wait_recv()
        self.cross[p].wait_recv()
        at = self.local(p)
        return (
            self.mine(1, p).astype(F32)
            + self.beside_own[at, :].astype(F32)
            + self.far[at, :].astype(F32)
        )

    def finish(self):
        for copies in (self.to_far, self.to_own, self.cross):
            for copy in copies:
                copy.wait_send()


class Exchange:
    def __init__(self, partial, near, sums, far, send, recv):
        core, zl, beside, across = partners()
        rows = far.shape[1]
        self.near, self.sums, self.far = near, sums, far
        self.size = rows // PIECES
        self.blocks = [Block(l, core, rows) for l in range(2)]
        self.others = [Block(l, 1 - core, rows) for l in range(2)]
        self.order = [(l, p) for l in range(2) for p in range(PIECES)]
        self.beside = [
            [
                remote(partial.at[self.others[l].piece(p)], near.at[l, self.local(p)],
                       send.at[l, p], recv.at[l, p], beside)
                for p in range(PIECES)
            ]
            for l in range(2)
        ]
        self.across = [
            [
                remote(sums.at[l, self.local(p)], far.at[l, self.local(p)],
                       send.at[2 + l, p], recv.at[2 + l, p], across)
                for p in range(PIECES)
            ]
            for l in range(2)
        ]

    def local(self, p):
        return pl.ds(p * self.size, self.size)

    def send(self, l):
        for copy in self.beside[l]:
            copy.start()

    def pass_on(self, l, mine):
        for p in range(PIECES):
            self.beside[l][p].wait_recv()
            at = self.local(p)
            self.sums[l, at, :] = (
                mine(l, p).astype(F32) + self.near[l, at, :].astype(F32)
            ).astype(BF16)
            self.across[l][p].start()

    def total(self, l, p):
        self.across[l][p].wait_recv()
        at = self.local(p)
        return self.sums[l, at, :].astype(F32) + self.far[l, at, :].astype(F32)

    def finish(self):
        for l, p in self.order:
            self.beside[l][p].wait_send()
            self.across[l][p].wait_send()


class Sharing:
    def __init__(self, held, out, send, recv, stores):
        core, _, beside, _ = partners()
        rows = held.shape[0] // 4
        self.held = held
        self.blocks = [Block(l, core, rows) for l in range(2)]
        self.copies = [
            [
                remote(held.at[block.piece(p)], held.at[block.piece(p)], send.at[l, p], recv.at[l, p],
                       beside)
                for p in range(PIECES)
            ]
            for l, block in enumerate(self.blocks)
        ]
        others = [Block(l, 1 - core, rows) for l in range(2)]
        self.stores = [
            pltpu.make_async_copy(held.at[block.rows()], out.at[block.rows()], stores.at[at])
            for at, block in enumerate(self.blocks + others)
        ]

    def put(self, l, p, rows):
        self.held[self.blocks[l].piece(p), :] = rows
        self.copies[l][p].start()
        if p == PIECES - 1:
            self.stores[l].start()

    def arrive(self):
        for l in range(2):
            for copy in self.copies[l]:
                copy.wait_recv()
            self.stores[2 + l].start()

    def finish(self):
        for l in range(2):
            for copy in self.copies[l]:
                copy.wait_send()
        for store in self.stores:
            store.wait()


def normed_of(x, gain):
    return x * lax.rsqrt(jnp.mean(x * x, axis=1, keepdims=True) + 1e-6) * gain


def load_all(copies):
    for copy in copies:
        copy.start()


def first_kernel(row, jobs, x_ref, gain_ref, new_ref, out_ref, raw, held, cross_send, cross_recv, send,
                 recv, stores):
    _, zl, _, across = partners()
    wait_greetings(greet_group() + jobs.greet())
    swap = remote(raw.at[zl], raw.at[zl], cross_send.at[0], cross_recv.at[0], across)
    raw[zl] = x_ref[...]
    swap.start()
    jobs.start()
    sharing = Sharing(held, out_ref, send, recv, stores)
    swap.wait()
    size = raw.shape[1] // PIECES
    for l in range(2):
        for p in range(PIECES):
            x = raw[l, p * size : (p + 1) * size, :].astype(F32)
            sharing.put(l, p, normed_of(x, gain_ref[row : row + 1, :].astype(F32)).astype(BF16))
    new_ref[...] = raw[...]
    jobs.middle()
    sharing.arrive()
    sharing.finish()
    jobs.finish()


def forward_bridge_kernel(
    row, jobs, partial, x_ref, gain_ref, new_ref, out_ref, mine, near, sums, far, x, held, send, recv,
    share_send, share_recv, loads, stores
):
    exchange = Exchange(partial, near, sums, far, send, recv)
    sharing = Sharing(held, out_ref, share_send, share_recv, stores)
    own = [
        pltpu.make_async_copy(partial.at[exchange.blocks[l].rows()], mine.at[l], loads.at[l])
        for l in range(2)
    ]
    old = [pltpu.make_async_copy(x_ref.at[l], x.at[l], loads.at[2 + l]) for l in range(2)]
    new = [pltpu.make_async_copy(x.at[l], new_ref.at[l], stores.at[4 + l]) for l in range(2)]
    load_all(own + old)
    wait_greetings(greet_group() + jobs.greet())
    for l in range(2):
        exchange.send(l)
    jobs.start()
    for l in range(2):
        own[l].wait()
        exchange.pass_on(l, lambda l, p: mine[l, exchange.local(p), :])
    forward_rows(row, jobs, exchange, sharing, old, new, x, gain_ref)


def forward_rows(row, jobs, exchange, sharing, old, new, x, gain_ref):
    gain = gain_ref[row : row + 1, :].astype(F32)
    for l in range(2):
        old[l].wait()
        for p in range(PIECES):
            if (l, p) == TURN:
                jobs.middle()
            at = exchange.local(p)
            rows = x[l, at, :] + exchange.total(l, p)
            x[l, at, :] = rows
            sharing.put(l, p, normed_of(rows, gain).astype(BF16))
        new[l].start()
    sharing.arrive()
    exchange.finish()
    sharing.finish()
    for store in new:
        store.wait()
    jobs.finish()


def mixer_bridge_kernel(
    row, jobs, heads_hbm, w_out_hbm, x_ref, gain_ref, new_ref, out_ref, partial, raw, near, sums, far, x,
    held, heads_ref, w_out_ref, fetch, send, recv, share_send, share_recv, loads, stores
):
    fetches = [
        pltpu.make_async_copy(w_out_hbm, w_out_ref, fetch.at[0]),
        pltpu.make_async_copy(heads_hbm, heads_ref, fetch.at[1]),
    ]
    load_all(fetches)
    exchange = Exchange(partial, near, sums, far, send, recv)
    sharing = Sharing(held, out_ref, share_send, share_recv, stores)
    old = [pltpu.make_async_copy(x_ref.at[l], raw.at[l], loads.at[2 + l]) for l in range(2)]
    new = [pltpu.make_async_copy(x.at[l], new_ref.at[l], stores.at[4 + l]) for l in range(2)]
    load_all(old)
    wait_greetings(greet_group() + jobs.greet())

    for copy in fetches:
        copy.wait()

    def make(block):
        rows = block.rows()
        partial[rows, :] = mm(heads_ref[rows, :], w_out_ref[...], NT).astype(BF16)

    for l in range(2):
        make(exchange.others[l])
        exchange.send(l)
    jobs.start()
    for l in range(2):
        make(exchange.blocks[l])
        exchange.pass_on(l, lambda l, p: partial[exchange.blocks[l].piece(p), :])
    for l in range(2):
        old[l].wait()
        if x_ref.dtype != F32:
            x[l] = raw[l].astype(F32)
        old[l] = Done()
    forward_rows(row, jobs, exchange, sharing, old, new, x, gain_ref)


class Done:
    def wait(self):
        pass


def norm_back(total, x, gain):
    inv = lax.rsqrt(jnp.mean(x * x, axis=1, keepdims=True) + 1e-6)
    unit = x * inv
    scaled = total * gain
    grad = inv * (scaled - unit * jnp.mean(scaled * unit, axis=1, keepdims=True))
    return grad, jnp.sum(total * unit, axis=0, keepdims=True)


def backward_bridge_kernel(row, last, jobs, partial, x_ref, gain_ref, grad_ref, *refs):
    if last:
        heads_hbm, new_ref, out_ref, dgain_ref, dout_ref, *refs = refs
        heads_ref, fetch, *refs = refs
        heads_copy = pltpu.make_async_copy(heads_hbm, heads_ref, fetch.at[0])
        heads_copy.start()
    else:
        new_ref, out_ref, dgain_ref, *refs = refs
    (mine, near, sums, far, x, grad, new_rows, held, send, recv, share_send, share_recv, loads,
     stores) = refs
    exchange = Exchange(partial, near, sums, far, send, recv)
    sharing = Sharing(held, out_ref, share_send, share_recv, stores)
    zl = lax.axis_index("zl")
    place = lambda ref, l: ref.at[exchange.blocks[l].rows()] if len(ref.shape) == 2 else ref.at[l]
    own, old = [], []
    for l in range(2):
        own.append(
            pltpu.make_async_copy(partial.at[exchange.blocks[l].rows()], mine.at[l], loads.at[l])
        )
        old.append(
            (pltpu.make_async_copy(x_ref.at[l], x.at[l], loads.at[2 + l]),
             pltpu.make_async_copy(place(grad_ref, l), grad.at[l], loads.at[4 + l]))
        )
    new = [pltpu.make_async_copy(new_rows.at[l], new_ref.at[l], stores.at[4 + l]) for l in range(2)]
    load_all(own + [copy for pair in old for copy in pair])
    wait_greetings(greet_group() + jobs.greet())
    for l in range(2):
        exchange.send(l)
    jobs.start()
    for l in range(2):
        own[l].wait()
        exchange.pass_on(l, lambda l, p: mine[l, exchange.local(p), :])
    gain = gain_ref[row : row + 1, :].astype(F32)
    dgain = jnp.zeros(dgain_ref.shape, F32)
    for l in range(2):
        for copy in old[l]:
            copy.wait()
        for p in range(PIECES):
            if (l, p) == TURN:
                jobs.middle()
            at = exchange.local(p)
            rows, part = norm_back(exchange.total(l, p), x[l, at, :].astype(F32), gain)
            dgain = dgain + jnp.where(zl == l, part, 0.0)
            rows = rows + grad[l, at, :].astype(F32)
            new_rows[l, at, :] = rows
            sharing.put(l, p, rows.astype(BF16))
        new[l].start()
    dgain_ref[...] = dgain
    sharing.arrive()
    if last:
        heads_copy.wait()
        for first in range(0, held.shape[1], 256):
            columns = slice(first, first + 256)
            dout_ref[columns, :] = mm(held[:, columns], heads_ref[...], TN).astype(BF16)
    exchange.finish()
    sharing.finish()
    for store in new:
        store.wait()
    jobs.finish()


def backward_last_kernel(
    row, jobs, partial, x_ref, gain_ref, grad_ref, new_ref, dgain_ref,
    beside_far, beside_own, sums, far, send, recv
):
    wait_greetings(greet_group() + jobs.greet())
    scatter = Scatter(partial, beside_far, beside_own, sums, far, send, recv)
    scatter.start()
    jobs.start()
    zl = lax.axis_index("zl")
    dgain = jnp.zeros(dgain_ref.shape, F32)
    for p in range(PIECES):
        at = scatter.local(p)
        grad, part = norm_back(
            scatter.total(p), x_ref[zl, at, :].astype(F32), gain_ref[row : row + 1, :].astype(F32)
        )
        dgain = dgain + part
        new_ref[at, :] = (grad + grad_ref[zl, at, :]).astype(BF16)
    dgain_ref[...] = dgain
    jobs.middle()
    scatter.finish()
    jobs.finish()


VMEM_SPEC = pl.BlockSpec(memory_space=pltpu.VMEM)
ANY_SPEC = pl.BlockSpec(memory_space=pl.ANY)


def pair_scratch(rows, width, kinds):
    return [pltpu.VMEM((2, rows, width), kind) for kind in kinds]


def bridge_sems():
    many = pltpu.SemaphoreType.DMA((4, PIECES))
    few = pltpu.SemaphoreType.DMA((2, PIECES))
    return [many, many, few, few, pltpu.SemaphoreType.DMA((6,)), pltpu.SemaphoreType.DMA((6,))]


def bridge_shapes(rows, width):
    return [
        jax.ShapeDtypeStruct((2, rows, width), F32),
        jax.ShapeDtypeStruct((4 * rows, width), BF16),
    ]


def first_gather(x, gain, row, jobs, number):
    rows, width = x.shape
    few = pltpu.SemaphoreType.DMA((2, PIECES))
    one = pltpu.SemaphoreType.DMA((1,))
    return carry_call(
        functools.partial(first_kernel, row), jobs, (), [VMEM_SPEC] * 2, [VMEM_SPEC, ANY_SPEC],
        [
            jax.ShapeDtypeStruct((2, rows, width), BF16),
            jax.ShapeDtypeStruct((4 * rows, width), BF16),
        ],
        [pltpu.VMEM((2, rows, width), BF16), pltpu.VMEM((4 * rows, width), BF16), one, one, few, few,
         pltpu.SemaphoreType.DMA((4,))],
        (x, gain), number, "first", rows * width * 20,
    )


def forward_bridge(partial, x, gain, row, jobs, number):
    _, rows, width = x.shape
    return carry_call(
        functools.partial(forward_bridge_kernel, row), jobs, (),
        [ANY_SPEC, ANY_SPEC, VMEM_SPEC], [ANY_SPEC] * 2, bridge_shapes(rows, width),
        pair_scratch(rows, width, [BF16] * 4 + [F32]) + [pltpu.VMEM((4 * rows, width), BF16)]
        + bridge_sems(),
        (partial, x, gain), number, "forward_bridge", rows * width * 20,
    )


def mixer_bridge(heads, w_out, x, gain, row, jobs, number):
    _, rows, width = x.shape
    kernel = functools.partial(
        mixer_bridge_kernel if x.dtype != F32 else mixer_bridge_kernel_f32, row
    )
    raw = pair_scratch(rows, width, [BF16]) if x.dtype != F32 else []
    return carry_call(
        kernel, jobs, (), [ANY_SPEC, ANY_SPEC, ANY_SPEC, VMEM_SPEC], [ANY_SPEC] * 2,
        bridge_shapes(rows, width),
        [pltpu.VMEM((4 * rows, width), BF16)] + raw + pair_scratch(rows, width, [BF16] * 3 + [F32])
        + [pltpu.VMEM((4 * rows, width), BF16), pltpu.VMEM(heads.shape, BF16),
           pltpu.VMEM(w_out.shape, BF16), pltpu.SemaphoreType.DMA((2,))] + bridge_sems(),
        (heads, w_out, x, gain), number, "mixer_bridge", 10**9,
    )


def mixer_bridge_kernel_f32(row, jobs, heads_ref, w_out_ref, x_ref, gain_ref, new_ref, out_ref, partial,
                            near, sums, far, x, *refs):
    mixer_bridge_kernel(row, jobs, heads_ref, w_out_ref, x_ref, gain_ref, new_ref, out_ref, partial, x,
                        near, sums, far, x, *refs)


def backward_bridge(partial, x, gain, row, grad, jobs, number, heads=None):
    _, rows, width = x.shape
    last = heads is not None
    outs = bridge_shapes(rows, width) + [jax.ShapeDtypeStruct((1, width), F32)]
    if last:
        outs.append(jax.ShapeDtypeStruct((width, heads.shape[1]), BF16))
    return carry_call(
        functools.partial(backward_bridge_kernel, row, last), jobs, (),
        [ANY_SPEC, ANY_SPEC, VMEM_SPEC, ANY_SPEC] + [ANY_SPEC] * last,
        [ANY_SPEC, ANY_SPEC, VMEM_SPEC] + [VMEM_SPEC] * last, outs,
        ([pltpu.VMEM(heads.shape, BF16), pltpu.SemaphoreType.DMA((1,))] if last else [])
        + pair_scratch(rows, width, [BF16] * 4 + [x.dtype, grad.dtype, F32])
        + [pltpu.VMEM((4 * rows, width), BF16)] + bridge_sems(),
        (partial, x, gain, grad) + ((heads,) if last else ()), number, "backward_bridge",
        rows * width * 20,
    )


def backward_last(partial, x, gain, row, grad, jobs, number):
    _, rows, width = x.shape
    hops = pltpu.SemaphoreType.DMA((3, PIECES))
    return carry_call(
        functools.partial(backward_last_kernel, row), jobs, (), [VMEM_SPEC] * 4, [VMEM_SPEC] * 2,
        [jax.ShapeDtypeStruct((rows, width), BF16), jax.ShapeDtypeStruct((1, width), F32)],
        [pltpu.VMEM((rows, width), BF16) for _ in range(4)] + [hops, hops],
        (partial, x, gain, grad), number, "backward_last", rows * width * 20,
    )


class Job:
    in_vmem = False
    late = False

    @staticmethod
    def buffers(shape, chips):
        return []

    def __init__(self, source, target, send, recv, chips, buffers=()):
        self.source, self.target, self.send, self.recv = source, target, send, recv
        self.held = buffers
        self.chips = chips
        self.chip, self.core, self.zp, self.zl, self.own = place(chips)
        self.fixed = (self.zp == self.zl) & (self.zl == self.core)
        self.outward, self.inward, self.locals = [], [], []
        self.plan()

    def copy(self, src, dst, send, recv, device):
        return remote(src, dst, self.send.at[send], self.recv.at[recv], device)

    def local(self, src, dst, at, when=None, through=None):
        if through is None:
            self.locals.append((pltpu.make_async_copy(src, dst, self.send.at[at]), None, when))
        else:
            self.locals.append(
                (pltpu.make_async_copy(src, through, self.send.at[at]),
                 pltpu.make_async_copy(through, dst, self.send.at[at]), when)
            )

    def column(self, chip, core, zp, zl):
        return at_device(chip, core, zp, zl)

    def greet(self):
        count = 0
        for copy, device, mine in self.inward:
            if mine is None:
                signal(device)
            else:
                unless(mine, functools.partial(signal, device))
        for copy, mine in self.outward:
            count = count + (1 if mine is None else 1 - mine.astype(jnp.int32))
        return count

    def start(self):
        for copy, mine in self.outward:
            if mine is None:
                copy.start()
            else:
                unless(mine, copy.start)
        for load, _, when in self.locals:
            if when is None:
                load.start()
            else:
                pl.when(when)(load.start)

    def middle(self):
        for load, store, when in self.locals:
            def turn():
                load.wait()
                store.start()

            if store is not None and when is None:
                turn()
            elif store is not None:
                pl.when(when)(turn)

    def arrivals(self):
        for copy, device, mine in self.inward:
            if mine is None:
                copy.wait_recv()
            else:
                unless(mine, copy.wait_recv)

    def departures(self):
        for copy, mine in self.outward:
            if mine is None:
                copy.wait_send()
            else:
                unless(mine, copy.wait_send)
        for load, store, when in self.locals:
            last = load if store is None else store
            if when is None:
                last.wait()
            else:
                pl.when(when)(last.wait)

    def finish(self):
        self.arrivals()
        self.departures()


def block(index, size):
    return pl.ds(pl.multiple_of(index * size, size), size)


class ToPlane(Job):
    @staticmethod
    def result(shape, chips):
        return (2 * shape[0], shape[1])

    @staticmethod
    def buffers(shape, chips):
        return [pltpu.VMEM(shape, BF16)]

    def plan(self):
        rows = self.source.shape[0]
        at = block(self.core, rows)
        for to in range(2):
            self.outward.append(
                (self.copy(self.source, self.target.at[at], to, self.core,
                           at_device(self.chip, self.zl, to, self.zp)),
                 self.fixed & (self.zp == to))
            )
        for co in range(2):
            device = at_device(self.chip, co, self.zl, self.core)
            self.inward.append(
                (self.copy(self.source, self.target.at[block(co, rows)], 0, co, device), device,
                 self.fixed & (self.core == co))
            )
        self.local(self.source, self.target.at[at], 2, self.fixed, self.held[0] if self.held else None)


class FromPlane(Job):
    @staticmethod
    def result(shape, chips):
        return (2, shape[0] // 2, shape[1])

    @staticmethod
    def buffers(shape, chips):
        return [pltpu.VMEM((shape[0] // 2, shape[1]), BF16)]

    def plan(self):
        rows = self.source.shape[0] // 2
        for co in range(2):
            src, mine = self.source.at[block(co, rows)], self.fixed & (self.core == co)
            self.outward.append(
                (self.copy(src, self.target.at[self.zp], co, self.zp,
                           at_device(self.chip, co, self.zl, self.core)), mine)
            )
            self.local(src, self.target.at[self.zp], 2 + co, mine, self.held[0] if self.held else None)
        for at in range(2):
            device = at_device(self.chip, self.zl, at, self.zp)
            self.inward.append(
                (self.copy(self.source.at[block(0, rows)], self.target.at[at], 0, at, device), device,
                 self.fixed & (self.zp == at))
            )


class Spread(Job):
    @staticmethod
    def result(shape, chips):
        return (chips * shape[0], shape[1])

    @staticmethod
    def buffers(shape, chips):
        return [pltpu.VMEM(shape, BF16)]

    def to(self, chip):
        return at_device(chip, self.core, self.zp, self.zl)

    def plan(self):
        rows = self.source.shape[0]
        own = self.target.at[block(self.chip, rows)]
        self.local(self.source, own, 0, None, self.held[0])
        self.onward, self.later = [], []
        if self.chips != 4:
            for j in range(1, self.chips):
                to = lax.rem(self.chip + j, self.chips)
                source = lax.rem(self.chip + self.chips - j, self.chips)
                self.outward.append((self.copy(self.source, own, j, j, self.to(to)), None))
                self.inward.append(
                    (self.copy(self.source, self.target.at[block(source, rows)], j, j,
                               self.to(source)), self.to(source), None)
                )
            return
        y, x = self.chip // 2, lax.rem(self.chip, 2)
        sides = [y * 2 + (1 - x), (1 - y) * 2 + x]
        across = (1 - y) * 2 + (1 - x)
        half = rows // 2
        for side in range(2):
            device = self.to(sides[side])
            self.outward.append((self.copy(self.source, own, 1 + side, 1 + side, device), None))
            self.inward.append(
                (self.copy(self.source, self.target.at[block(sides[side], rows)], 1 + side, 1 + side,
                           device), device, None)
            )
        for side in range(2):
            part = pl.ds(pl.multiple_of(sides[side] * rows + side * half, half), half)
            self.onward.append(
                self.copy(self.target.at[part], self.target.at[part], 3 + side, 3 + side,
                          self.to(sides[1 - side]))
            )
            part = pl.ds(pl.multiple_of(across * rows + side * half, half), half)
            self.later.append(
                self.copy(self.target.at[part], self.target.at[part], 3 + side, 3 + side,
                          self.to(sides[1 - side]))
            )

    def middle(self):
        super().middle()
        if self.onward:
            self.arrivals()
            for copy in self.onward:
                copy.start()

    def finish(self):
        if not self.onward:
            self.arrivals()
        for copy in self.later:
            copy.wait_recv()
        for copy in self.onward:
            copy.wait_send()
        self.departures()


class Reduce(Job):
    in_vmem = True

    @staticmethod
    def result(shape, chips):
        return (shape[0] // chips, shape[1])

    @staticmethod
    def buffers(shape, chips):
        rows, cols = shape[0] // chips, shape[1]
        if chips != 4:
            return [pltpu.VMEM((chips, rows, cols), BF16)]
        return [pltpu.VMEM((rows // 2, cols), BF16)] * 4 + [pltpu.VMEM((rows, cols), BF16)] * 3

    def plan(self):
        rows = self.source.shape[0] // self.chips
        to = lambda chip: at_device(chip, self.core, self.zp, self.zl)
        if self.chips != 4:
            (parts,) = self.held
            self.local(self.source.at[block(self.chip, rows)], parts.at[self.chip], 0)
            for j in range(1, self.chips):
                target = lax.rem(self.chip + j, self.chips)
                source = lax.rem(self.chip + self.chips - j, self.chips)
                src = self.source.at[block(target, rows)]
                self.outward.append((self.copy(src, parts.at[self.chip], j, j, to(target)), None))
                self.inward.append(
                    (self.copy(src, parts.at[source], j, j, to(source)), to(source), None)
                )
            return
        half = rows // 2
        y, x = self.chip // 2, lax.rem(self.chip, 2)
        sides = [y * 2 + (1 - x), (1 - y) * 2 + x]
        across = (1 - y) * 2 + (1 - x)
        passing, staged, blocks, own = self.held[0:2], self.held[2:4], self.held[4:6], self.held[6]
        piece = lambda chip, at: self.source.at[
            pl.ds(pl.multiple_of(chip * rows + at * half, half), half)
        ]
        self.local(self.source.at[block(self.chip, rows)], own, 0)
        self.loads = []
        self.onward, self.later = [], []
        for side in range(2):
            device = to(sides[side])
            copy = self.copy(piece(across, side), passing[side], 1 + side, 1 + side, device)
            self.outward.append((copy, None))
            self.inward.append((copy, device, None))
        self.direct = []
        for side in range(2):
            device = to(sides[side])
            part = pl.ds(side * half, half)
            self.direct.append(
                self.copy(piece(sides[side], side), blocks[side].at[part], 3 + side, 3 + side, device)
            )
            self.loads.append(
                pltpu.make_async_copy(piece(sides[side], 1 - side), staged[side], self.send.at[5 + side])
            )
            part = pl.ds((1 - side) * half, half)
            self.onward.append(
                self.copy(staged[side], blocks[side].at[part], 7 + side, 5 + side, device)
            )

    def start(self):
        super().start()
        if self.chips == 4:
            for copy in self.direct + self.loads:
                copy.start()

    def middle(self):
        if self.chips == 4:
            for side in range(2):
                self.inward[1 - side][0].wait_recv()
                self.loads[side].wait()
                self.held[2 + side][...] = (
                    self.held[2 + side][...].astype(F32) + self.held[1 - side][...].astype(F32)
                ).astype(BF16)
                self.onward[side].start()

    def finish(self):
        if self.chips == 4:
            for copy in self.direct + self.onward:
                copy.wait_recv()
            self.departures()
            for copy in self.direct + self.onward:
                copy.wait_send()
            total = self.held[6][...].astype(F32) + (
                self.held[4][...].astype(F32) + self.held[5][...].astype(F32)
            )
        else:
            super().finish()
            total = self.held[0][0].astype(F32)
            for chip in range(1, self.chips):
                total = total + self.held[0][chip].astype(F32)
        self.target[...] = total.astype(BF16)


class ToRole(Job):
    @staticmethod
    def result(shape, chips):
        return shape

    @staticmethod
    def buffers(shape, chips):
        return [pltpu.VMEM(shape, BF16)]

    def ends(self):
        role = at_device(self.chip, self.zl, self.core, self.zp)
        home = at_device(self.chip, self.zp, self.zl, self.core)
        return role, home, self.fixed & (self.zp == self.core)

    def plan(self):
        to, source, mine = self.ends()
        self.outward.append((self.copy(self.source, self.target, 0, 0, to), mine))
        self.inward.append((self.copy(self.source, self.target, 0, 0, source), source, mine))
        self.local(self.source, self.target, 1, mine, self.held[0])


class FromRole(ToRole):
    def ends(self):
        role, home, mine = super().ends()
        return home, role, mine


class Share(Job):
    late = True
    @staticmethod
    def result(shape, chips):
        return (4 * shape[0], shape[1])

    @staticmethod
    def buffers(shape, chips):
        return [pltpu.VMEM(shape, BF16)]

    def plan(self):
        rows = self.source.shape[0]
        own = self.target.at[block(self.zl * 2 + self.core, rows)]
        beside = at_device(self.chip, 1 - self.core, self.zp, self.zl)
        across = at_device(self.chip, self.core, self.zp, 1 - self.zl)
        self.local(self.source, own, 0, None, self.held[0])
        for at, device, zl, core in ((1, beside, self.zl, 1 - self.core), (2, across, 1 - self.zl, self.core)):
            self.outward.append((self.copy(self.source, own, at, at, device), None))
            self.inward.append(
                (self.copy(self.source, self.target.at[block(zl * 2 + core, rows)], at, at, device),
                 device, None)
            )
        other = self.target.at[block((1 - self.zl) * 2 + self.core, rows)]
        self.onward = self.copy(other, other, 3, 3, beside)
        last = self.target.at[block((1 - self.zl) * 2 + 1 - self.core, rows)]
        self.later = self.copy(last, last, 3, 3, beside)

    def middle(self):
        super().middle()
        self.arrivals()
        self.onward.start()

    def finish(self):
        self.later.wait_recv()
        self.onward.wait_send()
        self.departures()


class ShareSum(Job):
    late = True
    in_vmem = True

    @staticmethod
    def result(shape, chips):
        return (shape[0] // 4, shape[1])

    @staticmethod
    def buffers(shape, chips):
        return [pltpu.VMEM((shape[0] // 4, shape[1]), BF16)] * 5

    def plan(self):
        rows = self.target.shape[0]
        beside = at_device(self.chip, 1 - self.core, self.zp, self.zl)
        across = at_device(self.chip, self.core, self.zp, 1 - self.zl)
        part = lambda zl, core: self.source.at[block(zl * 2 + core, rows)]
        self.far, self.near, self.staged, self.own, self.other = self.held
        for at, src, dst in (
            (0, part(1 - self.zl, 1 - self.core), self.far), (1, part(self.zl, 1 - self.core), self.near)
        ):
            copy = self.copy(src, dst, at, at, beside)
            self.outward.append((copy, None))
            self.inward.append((copy, beside, None))
        self.local(part(1 - self.zl, self.core), self.staged, 2)
        self.local(part(self.zl, self.core), self.own, 3)
        self.onward = self.copy(self.staged, self.other, 4, 2, across)
        self.across = across

    def greet(self):
        signal(self.across)
        return super().greet() + 1

    def middle(self):
        self.arrivals()
        for load, _, _ in self.locals:
            load.wait()
        self.staged[...] = (
            self.staged[...].astype(F32) + self.far[...].astype(F32)
        ).astype(BF16)
        self.onward.start()

    def finish(self):
        for copy, _ in self.outward:
            copy.wait_send()
        self.onward.wait()
        self.target[...] = (
            self.own[...].astype(F32) + self.near[...].astype(F32) + self.other[...].astype(F32)
        ).astype(BF16)


class Jobs:
    def __init__(self, jobs, chips):
        self.kinds = [job[0] for job in jobs]
        self.values = [job[1] for job in jobs]
        self.columns = [job[2] if len(job) > 2 else None for job in jobs]
        shapes = [
            value.shape if columns is None else (value.shape[0], columns[1])
            for value, columns in zip(self.values, self.columns)
        ]
        self.chips = chips
        count = max(9, chips + 1)
        any_space = pl.BlockSpec(memory_space=pl.ANY)
        self.in_specs = [any_space] * len(jobs)
        self.out_shape = [
            jax.ShapeDtypeStruct(kind.result(shape, chips), BF16)
            for kind, shape in zip(self.kinds, shapes)
        ]
        self.buffers = [kind.buffers(shape, chips) for kind, shape in zip(self.kinds, shapes)]
        self.scratch = [pltpu.SemaphoreType.DMA((count,))] * (2 * len(jobs))
        self.scratch += [buffer for buffers in self.buffers for buffer in buffers]

    def out_specs(self, grid):
        specs = []
        for kind, shape in zip(self.kinds, self.out_shape):
            if not kind.in_vmem:
                specs.append(pl.BlockSpec(memory_space=pl.ANY))
            elif grid:
                specs.append(pl.BlockSpec(shape.shape, lambda i: (0, 0)))
            else:
                specs.append(pl.BlockSpec(memory_space=pltpu.VMEM))
        return specs

    def bind(self, sources, targets, scratch):
        sems, scratch = scratch[: 2 * len(self.kinds)], scratch[2 * len(self.kinds) :]
        self.bound = []
        for at, (kind, source, target) in enumerate(zip(self.kinds, sources, targets)):
            if self.columns[at] is not None:
                source = source.at[:, pl.ds(*self.columns[at])]
            held, scratch = scratch[: len(self.buffers[at])], scratch[len(self.buffers[at]) :]
            self.bound.append(
                kind(source, target, sems[2 * at], sems[2 * at + 1], self.chips, held)
            )

    def greet(self):
        count = 0
        for job in self.bound:
            count = count + job.greet()
        return count

    def start(self):
        for job in self.bound:
            job.start()

    def middle(self, late=None):
        for job in self.bound:
            if late is None or job.late == late:
                job.middle()

    def finish(self):
        for job in self.bound:
            job.finish()


def carrying(body, jobs, ins, outs):
    extra = len(jobs.kinds)

    def kernel(*refs):
        operands, refs = refs[:ins], refs[ins:]
        sources, refs = refs[:extra], refs[extra:]
        results, refs = refs[:outs], refs[outs:]
        targets, refs = refs[:extra], refs[extra:]
        own = len(refs) - len(jobs.scratch)
        scratch = refs[:own]
        jobs.bind(sources, targets, refs[own:])
        body(jobs, *operands, *results, *scratch)

    return kernel


def carry_call(body, jobs, grid, in_specs, out_specs, out_shape, scratch, args, number, name, work):
    outs = len(out_shape)
    results = pl.pallas_call(
        carrying(body, jobs, len(args), outs),
        grid=grid,
        in_specs=list(in_specs) + jobs.in_specs,
        out_specs=list(out_specs) + jobs.out_specs(grid),
        out_shape=list(out_shape) + jobs.out_shape,
        scratch_shapes=list(scratch) + jobs.scratch,
        compiler_params=pltpu.CompilerParams(
            collective_id=number, has_side_effects=True, vmem_limit_bytes=56 * 1024 * 1024
        ),
        cost_estimate=pl.CostEstimate(
            flops=work, bytes_accessed=80 * 1024 * 1024, transcendentals=0
        ),
        name=name,
    )(*args, *jobs.values)
    return list(results[:outs]), list(results[outs:])


def place(chips):
    chip, core, zp, zl = (lax.axis_index(name) for name in AXES)
    return chip, core, zp, zl, chip * 2 + core


def at_device(chip, core, zp, zl):
    return {"chip": chip, "core": core, "zp": zp, "zl": zl}


def signal(device):
    pl.semaphore_signal(
        pltpu.get_barrier_semaphore(), inc=1, device_id=device,
        device_id_type=pl.DeviceIdType.MESH,
    )


def unless(condition, action):
    pl.when(jnp.logical_not(condition))(action)


class Plane:
    def __init__(self, chips):
        self.count = 2 * chips
        _, _, self.zp, self.zl, self.own = place(chips)

    def device(self, index):
        return at_device(index // 2, index % 2, self.zp, self.zl)

    def to(self, j):
        return lax.rem(self.own + j, self.count)

    def source(self, j):
        return lax.rem(self.own + self.count - j, self.count)

    def greet(self):
        for j in range(1, self.count):
            signal(self.device(self.to(j)))
        return self.count - 1


class Trade:
    def __init__(self, chips):
        self.chips, self.count = chips, 2 * chips
        self.chip, self.core, self.zp, self.zl, self.own = place(chips)
        self.fixed = (self.zp == self.zl) & (self.zl == self.core)
        self.slot = self.chip * 2 + self.zp

    def role(self, slot):
        return at_device(slot // 2, self.zl, slot % 2, self.zp)

    def role_mine(self, slot):
        return self.fixed & (self.slot == slot)

    def home(self, index):
        return at_device(index // 2, index % 2, self.zl, self.core)

    def home_mine(self, index):
        return self.fixed & (self.own == index)

    def greet_homes(self):
        for index in range(self.count):
            unless(self.home_mine(index), functools.partial(signal, self.home(index)))
        return self.count - self.fixed.astype(jnp.int32)

    def greet_roles(self):
        for slot in range(self.count):
            unless(self.role_mine(slot), functools.partial(signal, self.role(slot)))
        return self.count - self.fixed.astype(jnp.int32)


def greet_group():
    _, _, beside, across = partners()
    signal(beside)
    signal(across)
    return 2


def wait_greetings(count):
    pl.semaphore_wait(pltpu.get_barrier_semaphore(), count)


class Raw:
    def __init__(self, refs, square):
        (self.query, self.key, self.value, self.gate, self.decay, self.conv, self.out,
         self.ffn_gate, self.ffn_up, self.ffn_down) = refs
        self.square = square

    def qkv(self, layer, ref):
        ref[:, 0:KEY] = self.query[layer]
        ref[:, KEY : 2 * KEY] = self.key[layer]
        ref[:, 2 * KEY :] = self.value[layer]

    def side(self, layer, ref):
        ref[:, 0:VAL] = self.gate[layer]
        self.square[...] = jnp.zeros(self.square.shape, F32)
        self.square[0:2, :] = self.decay[layer].astype(F32)
        self.square[2:6, :] = self.conv[layer].astype(F32)
        ref[:, VAL:] = self.square[...].T.astype(BF16)

    def turn(self, value, ref):
        ref[...] = value.astype(F32).T.astype(BF16)


def deal_kernel(chips, jobs, order_ref, lengths_ref, x_ref, gain_ref, cotangent_ref, *refs):
    raw, refs = list(refs[:10]), refs[10:]
    (new_ref, out_ref, start_ref, qkv_next, side_next, out_next, gate_next, up_ref, up_next, down_ref,
     down_next, first_full, second_full, first_wide, second_wide, third_wide, fourth_wide) = refs[:17]
    (late_out, late_gate, late_up, late_down, cotangent, fetch, spread, picked, square, first, second,
     third, fourth, held_first, held_other, held_second, held, send, recv,
     stores,     cross_send, cross_recv,
     plane_send, plane_recv, role_send, role_recv, *sems) = refs[17:]
    fetches = [
        pltpu.make_async_copy(source, ref, fetch.at[at])
        for at, (source, ref) in enumerate(
            zip(raw[6:] + [cotangent_ref], (late_out, late_gate, late_up, late_down, cotangent))
        )
    ]
    raw = Raw(raw[:6] + [late_out, late_gate, late_up, late_down], square)
    plane, trade = Plane(chips), Trade(chips)
    half = CONV_CH // 2
    halves = []
    for at, (own, four) in enumerate(((held_first, sems[0:4]), (held_other, sems[12:16]))):
        cut = pl.ds(at * half, half)
        wide = first_wide.at[:, cut]
        halves.append(
            (ToPlane(first.at[:, cut], wide, four[0], four[1], chips),
             Spread(wide, first_full.at[:, cut], four[2], four[3], chips, [own]))
        )
    second_column = ToPlane(second, second_wide, sems[4], sems[5], chips)
    second_across = Spread(second_wide, second_full, sems[6], sems[7], chips, [held_second])
    third_column = ToPlane(third, third_wide, sems[8], sems[9], chips)
    fourth_column = ToPlane(fourth, fourth_wide, sems[10], sems[11], chips)
    sharing = Sharing(held, out_ref, send, recv, stores)
    across = {"zl": 1 - trade.zl}
    count = plane.count
    part = x_ref.shape[0] // count
    rows = lambda index: pl.ds(pl.multiple_of(index * part, part), part)
    expected = plane.greet() + trade.greet_homes() + greet_group()
    for job in (*halves[0], *halves[1], second_column, second_across, third_column, fourth_column):
        expected = expected + job.greet()
    raw.qkv(0, first)
    raw.side(0, second)
    load_all(fetches)
    wait_greetings(expected)
    outward, inward = [], []
    for j in range(1, count):
        to, source = plane.to(j), plane.source(j)
        outward.append(
            remote(x_ref.at[rows(to)], spread.at[plane.own], plane_send.at[j], plane_recv.at[j],
                   plane.device(to))
        )
        inward.append(
            remote(x_ref.at[rows(to)], spread.at[source], plane_send.at[j], plane_recv.at[j],
                   plane.device(source))
        )
    for copy in outward:
        copy.start()
    for column, _ in halves:
        column.start()
    spread[plane.own] = x_ref[rows(plane.own), :]
    for copy in inward:
        copy.wait_recv()
    halves[0][0].finish()
    halves[0][1].start()
    to_roles = []
    for slot in range(count):
        picked[slot] = spread[order_ref[slot]]
        copy = remote(picked.at[slot], new_ref.at[trade.zp, rows(plane.own)], role_send.at[slot],
                      role_recv.at[plane.own], trade.role(slot))
        mine = trade.role_mine(slot)
        unless(mine, copy.start)

        @pl.when(mine)
        def _():
            new_ref[trade.zl, rows(plane.own), :] = picked[slot]

        to_roles.append((copy, mine))
    second_column.start()
    for copy in fetches:
        copy.wait()
    raw.turn(raw.out[0], third)
    raw.turn(raw.ffn_gate[0], fourth)
    halves[1][0].finish()
    halves[1][1].start()
    size = x_ref.shape[0] // PIECES
    parts = max(size // part, 1)
    swaps = []
    for p in range(PIECES):
        piece = new_ref.at[trade.zl, pl.ds(p * size, size)]
        swaps.append(remote(piece, piece, cross_send.at[p], cross_recv.at[p], across))
    for p in range(PIECES):
        for index in range(p * parts, (p + 1) * parts):
            arrival = remote(picked.at[0], new_ref.at[trade.zl, rows(index)], role_send.at[0],
                             role_recv.at[index], trade.home(index))
            unless(trade.home_mine(index), arrival.wait_recv)
        swaps[p].start()
    gain = gain_ref[0:1, :].astype(F32)

    def share(l):
        for p in range(PIECES):
            x = new_ref[l, p * size : (p + 1) * size, :].astype(F32)
            sharing.put(l, p, normed_of(x, gain).astype(BF16))

    for l in range(2):
        pl.when(trade.zl == l)(functools.partial(share, l))
    second_column.finish()
    second_across.start()
    third_column.start()
    fourth_column.start()
    for _, across_chips in halves:
        across_chips.middle()
    for swap in swaps:
        swap.wait_recv()
    for l in range(2):
        pl.when(trade.zl != l)(functools.partial(share, l))
    length = lengths_ref[order_ref[plane.own]]
    at = (trade.zp * 2 + trade.zl) * x_ref.shape[0]
    positions = lax.broadcasted_iota(jnp.int32, x_ref.shape, 0) + at
    start_ref[...] = jnp.where(positions < length, cotangent[...], jnp.zeros(x_ref.shape, BF16))
    raw.qkv(1, qkv_next)
    raw.side(1, side_next)
    raw.turn(raw.out[1], out_next)
    raw.turn(raw.ffn_gate[1], gate_next)
    raw.turn(raw.ffn_up[0], up_ref)
    raw.turn(raw.ffn_up[1], up_next)
    raw.turn(raw.ffn_down[0], down_ref)
    raw.turn(raw.ffn_down[1], down_next)
    for copy in outward:
        copy.wait_send()
    for copy, mine in to_roles:
        unless(mine, copy.wait_send)
    for swap in swaps:
        swap.wait_send()
    sharing.arrive()
    sharing.finish()
    second_across.middle()
    for _, across_chips in halves:
        across_chips.finish()
    second_across.finish()
    third_column.finish()
    fourth_column.finish()


def deal_and_gather(order, lengths, x, gain, cotangent, raw, chips, number):
    rows, width = x.shape
    part, units = raw[0].shape[1], raw[7].shape[1]
    vmem = pl.BlockSpec(memory_space=pltpu.VMEM)
    smem = pl.BlockSpec(memory_space=pltpu.SMEM)
    hbm = pl.BlockSpec(memory_space=pl.ANY)
    count = 2 * chips
    buffer = pltpu.VMEM((count, rows // count, width), BF16)
    sems = lambda *shape: [pltpu.SemaphoreType.DMA(shape), pltpu.SemaphoreType.DMA(shape)]
    qkv, side = CONV_CH, VAL + LANES
    held = [(part, cols) for cols in (qkv, side, VAL, units, units, units, units, units)]
    spread = [(2 * chips * part, qkv), (2 * chips * part, side)]
    moved = [(2 * part, cols) for cols in (qkv, side, VAL, units)]
    shapes = [(2, rows, width), (4 * rows, width), (rows, width)] + held + spread + moved
    halved = (2 * part, qkv // 2)
    own = [(part, qkv), (part, side), (part, VAL), (part, units), halved, halved, moved[1]]
    return carry_call(
        functools.partial(deal_kernel, chips), Jobs([], chips), (),
        [smem, smem, vmem, vmem, hbm] + [vmem] * 6 + [hbm] * 4,
        [vmem, hbm] + [vmem] * 9 + [hbm] * 6,
        [jax.ShapeDtypeStruct(shape, BF16) for shape in shapes],
        [pltpu.VMEM(value.shape, BF16) for value in (*raw[6:], cotangent)]
        + [pltpu.SemaphoreType.DMA((5,))]
        + [buffer, buffer, pltpu.VMEM((LANES, LANES), F32)]
        + [pltpu.VMEM(shape, BF16) for shape in own]
        + [pltpu.VMEM((4 * rows, width), BF16)] + sems(2, PIECES) + [pltpu.SemaphoreType.DMA((4,))]
        + sems(PIECES) + sems(count) + sems(count)
        + [pltpu.SemaphoreType.DMA((max(9, chips + 1),))] * 16,
        (order, lengths, x, gain, cotangent, *raw), number, "deal_and_gather", rows * width * 20,
    )[0]


def small_rows(width):
    rows = (4 * width + 2 * VAL) // LANES + 1
    return rows + -rows % 8


def assemble(small, mix0, mix1, ffn0, ffn1, heads0, heads1, scalars0, scalars1):
    small[...] = jnp.zeros(small.shape, F32)
    at = 0
    for term in (mix0, mix1, ffn0, ffn1, heads0, heads1):
        for r in range(term.shape[1] // LANES):
            small[at : at + 1, :] = term[:, r * LANES : (r + 1) * LANES]
            at += 1
    head = lax.axis_index("zl") * 2 + lax.axis_index("core")
    lane = lax.broadcasted_iota(jnp.int32, (1, LANES), 1)
    row = jnp.zeros((1, LANES), F32)
    values = (scalars0[0:1, :], scalars1[0:1, :], scalars0[1:2, :], scalars1[1:2, :])
    for place, value in enumerate(values):
        row = row + jnp.where(lane == place * 4 + head, value, 0.0)
    small[at : at + 1, :] = row


def final_kernel(
    chips, jobs, order_ref, partial, x_hbm, gain_ref, grad_hbm, *refs
):
    terms, refs = refs[:7], refs[7:]
    (in_ref, aux_ref), refs = refs[:2], refs[2:]
    home_ref, total_ref, *homes = refs[:5]
    refs = refs[5:]
    cut = [pl.ds(0, CONV_CH), pl.ds(CONV_CH, VAL)]
    grads = [in_ref.at[:, cut[0]], in_ref.at[:, cut[1]], aux_ref]
    (away_held, own_held, x_ref, grad_ref, loads, beside_far, beside_own, sums, far, last, back,
     picked, small, by_plane, by_z, plane_sum,
     send, recv, role_send, role_recv, plane_send, plane_recv, small_send, small_recv, z_send,
     z_recv), refs = refs[:26], refs[26:]
    reduces, returns = [], []
    for at in range(3):
        summed, four, refs = refs[0], refs[1:5], refs[5:]
        buffers = len(Reduce.buffers(grads[at].shape, chips))
        reduces.append(Reduce(grads[at], summed, four[0], four[1], chips, refs[:buffers]))
        returns.append(FromPlane(summed, homes[at], four[2], four[3], chips))
        refs = refs[buffers:]
    plane, trade = Plane(chips), Trade(chips)
    scatter = Scatter(
        partial, beside_far, beside_own, sums, far, send, recv, (away_held, own_held, loads)
    )
    scatter.load()
    rows_in = [
        pltpu.make_async_copy(x_hbm.at[trade.zl], x_ref, loads.at[2]),
        pltpu.make_async_copy(grad_hbm.at[trade.zl], grad_ref, loads.at[3]),
    ]
    load_all(rows_in)
    count = plane.count
    part = x_ref.shape[0] // count
    rows = lambda index: pl.ds(pl.multiple_of(index * part, part), part)
    tier = trade.zp * 2 + trade.zl
    tier_device = lambda at: at_device(trade.chip, trade.core, at // 2, at % 2)
    for k in range(1, 4):
        signal(tier_device(lax.rem(tier + k, 4)))
    expected = plane.greet() + trade.greet_roles() + greet_group() + jobs.greet() + 3
    for job in reduces + returns:
        expected = expected + job.greet()
    wait_greetings(expected)
    scatter.start()
    for job in reduces:
        job.start()
    jobs.start()
    dgain = jnp.zeros((1, x_ref.shape[1]), F32)
    for copy in rows_in:
        copy.wait()
    to_homes = []
    size = x_ref.shape[0] // PIECES
    parts = max(size // part, 1)
    for p in range(PIECES):
        at = scatter.local(p)
        grad, piece = norm_back(scatter.total(p), x_ref[at, :].astype(F32), gain_ref[0:1, :].astype(F32))
        dgain = dgain + piece
        last[at, :] = (grad + grad_ref[at, :]).astype(BF16)
        for index in range(p * parts, (p + 1) * parts):
            copy = remote(last.at[rows(index)], back.at[trade.slot], role_send.at[index],
                          role_recv.at[trade.slot], trade.home(index))
            mine = trade.home_mine(index)
            unless(mine, copy.start)

            @pl.when(mine)
            def _():
                back[trade.slot] = last[rows(index), :]

            to_homes.append((copy, mine))
    assemble(small, dgain, *terms)
    small_out, small_in = [], []
    for j in range(1, count):
        to, source = plane.to(j), plane.source(j)
        small_out.append(
            remote(small, by_plane.at[plane.own], small_send.at[j], small_recv.at[j], plane.device(to))
        )
        small_in.append(
            remote(small, by_plane.at[source], small_send.at[j], small_recv.at[j], plane.device(source))
        )
    for copy in small_out:
        copy.start()
    by_plane[plane.own] = small[...]
    for job in reduces:
        job.middle()
    reduces[0].finish()
    returns[0].start()
    for slot in range(count):
        arrival = remote(last.at[rows(0)], back.at[slot], role_send.at[0], role_recv.at[slot],
                         trade.role(slot))
        unless(trade.role_mine(slot), arrival.wait_recv)
    outward, inward = [], []
    for j in range(count):
        to, source = plane.to(j), plane.source(j)
        at = jnp.int32(0)
        for slot in range(count):
            at = jnp.where(order_ref[slot] == to, slot, at)
        picked[j] = back[at]
        if j == 0:
            home_ref[rows(plane.own), :] = picked[0]
            continue
        copy = remote(picked.at[j], home_ref.at[rows(plane.own)], plane_send.at[j], plane_recv.at[j],
                      plane.device(to))
        copy.start()
        outward.append(copy)
        inward.append(
            remote(picked.at[j], home_ref.at[rows(source)], plane_send.at[j], plane_recv.at[j],
                   plane.device(source))
        )
    jobs.middle()
    for reduce, back_home in zip(reduces[1:], returns[1:]):
        reduce.finish()
        back_home.start()
    for copy in small_in:
        copy.wait_recv()
    total = by_plane[0]
    for index in range(1, count):
        total = total + by_plane[index]
    plane_sum[...] = total
    z_out, z_in = [], []
    for k in range(1, 4):
        to, source = lax.rem(tier + k, 4), lax.rem(tier + 4 - k, 4)
        z_out.append(remote(plane_sum, by_z.at[tier], z_send.at[k], z_recv.at[k], tier_device(to)))
        z_in.append(remote(plane_sum, by_z.at[source], z_send.at[k], z_recv.at[k], tier_device(source)))
    for copy in z_out:
        copy.start()
    by_z[tier] = total
    for copy in z_in:
        copy.wait_recv()
    total_ref[...] = (by_z[0] + by_z[1]) + (by_z[2] + by_z[3])
    for copy in inward:
        copy.wait_recv()
    scatter.finish()
    for copy, mine in to_homes:
        unless(mine, copy.wait_send)
    for copy in small_out + z_out + outward:
        copy.wait_send()
    jobs.finish()
    for job in returns:
        job.finish()


def final_step(order, partial, x, gain, grad, terms, grads, chips, jobs, number):
    _, rows, width = x.shape
    small = jax.ShapeDtypeStruct((small_rows(width), LANES), F32)
    vmem = pl.BlockSpec(memory_space=pltpu.VMEM)
    count = 2 * chips
    block = pltpu.VMEM((rows, width), BF16)
    parted = pltpu.VMEM((count, rows // count, width), BF16)
    hbm = pl.BlockSpec(memory_space=pl.ANY)
    chained = []
    pieces = [(grads[0].shape[0], cols) for cols in (CONV_CH, VAL, LANES)]
    for a in pieces:
        chained.append(pltpu.VMEM(Reduce.result(a, chips), BF16))
        chained += [pltpu.SemaphoreType.DMA((max(9, chips + 1),))] * 4
        chained += Reduce.buffers(a, chips)
    sems = lambda *shape: [pltpu.SemaphoreType.DMA(shape), pltpu.SemaphoreType.DMA(shape)]
    return carry_call(
        functools.partial(final_kernel, chips), jobs, (),
        [pl.BlockSpec(memory_space=pltpu.SMEM), hbm, hbm, vmem, hbm] + [vmem] * 7 + [hbm] * 2,
        [vmem, vmem] + [hbm] * 3,
        [
            jax.ShapeDtypeStruct((rows, width), BF16),
            jax.ShapeDtypeStruct(small.shape, F32),
        ]
        + [
            jax.ShapeDtypeStruct(FromPlane.result(Reduce.result(a, chips), chips), BF16)
            for a in pieces
        ],
        [block] * 2 + [pltpu.VMEM((rows, width), x.dtype), pltpu.VMEM((rows, width), F32)]
        + [pltpu.SemaphoreType.DMA((4,))] + [block] * 5 + [parted] * 2
        + [
            pltpu.VMEM(small.shape, F32), pltpu.VMEM((count,) + small.shape, F32),
            pltpu.VMEM((4,) + small.shape, F32), pltpu.VMEM(small.shape, F32),
        ]
        + sems(3, PIECES) + sems(count) + sems(count) + sems(count) + sems(4) + chained,
        (order, partial, x, gain, grad, *terms, *grads), number, "final_step", rows * width * 20,
    )


def only_jobs_kernel(jobs):
    wait_greetings(jobs.greet())
    jobs.start()
    jobs.middle()
    jobs.finish()


def only_jobs(jobs, number):
    return carry_call(only_jobs_kernel, jobs, (), [], [], [], [], (), number, "weights_back", 0)[1]


def weights_out_kernel(small_ref, home_ref, *refs):
    ins, outs = refs[:14], refs[14:]
    for layer in range(2):
        total = lambda ref: ref[0].astype(F32) + ref[1].astype(F32)
        qkv, head_gate, aux, out, gate, up, down = (
            total(ref) for ref in ins[7 * layer : 7 * layer + 7]
        )
        outs[0][layer] = qkv[:, :KEY]
        outs[1][layer] = qkv[:, KEY : 2 * KEY]
        outs[2][layer] = qkv[:, 2 * KEY :]
        outs[3][layer] = head_gate
        turned = aux.T
        outs[4][layer] = turned[0:2, :]
        outs[14][layer] = turned[2:6, :]
        outs[5][layer] = out.T
        outs[6][layer] = gate.T
        outs[7][layer] = up.T
        outs[8][layer] = down.T
    outs[15][...] = home_ref[...].astype(F32)[:, None, :]
    at = 0
    for ref in outs[9:12]:
        for layer in range(2):
            for r in range(ref.shape[1] // LANES):
                ref[layer : layer + 1, r * LANES : (r + 1) * LANES] = small_ref[at : at + 1, :]
                at += 1
    heads = outs[12].shape[1]
    for member in range(2):
        for layer in range(2):
            first = (2 * member + layer) * heads
            outs[12 + member][layer : layer + 1, :] = small_ref[at : at + 1, first : first + heads]


def weights_out(small, home, first, second, heads):
    width = home.shape[1]
    rows, units = first[0].shape[1], first[6].shape[2]
    shapes = [
        (2, rows, KEY), (2, rows, KEY), (2, rows, VAL), (2, rows, VAL), (2, 2, rows), (2, VAL, rows),
        (2, units, rows), (2, units, rows), (2, units, rows),
        (2, width), (2, width), (2, VAL), (2, heads), (2, heads), (2, 4, rows),
        (home.shape[0], 1, width),
    ]
    vmem = pl.BlockSpec(memory_space=pltpu.VMEM)
    return pl.pallas_call(
        weights_out_kernel,
        in_specs=[vmem] * 16,
        out_specs=[vmem] * 16,
        out_shape=[jax.ShapeDtypeStruct(shape, F32) for shape in shapes],
        compiler_params=pltpu.CompilerParams(vmem_limit_bytes=56 * 1024 * 1024),
        name="weights_out",
    )(small, home, *first, *second)


def ffn_parts(x, gate_ref, up_ref):
    gate, up = mm(x, gate_ref[...]), mm(x, up_ref[...])
    act, sig = silu_of(gate)
    return gate, up, act, sig


def begin_jobs(jobs, at, steps, turns=None):
    if jobs.kinds:
        @pl.when(at == 0)
        def _():
            wait_greetings(jobs.greet())
            jobs.start()

        early, late = turns or (steps // 2, steps - 1)

        @pl.when(at == early)
        def _():
            jobs.middle(late=False)

        @pl.when(at == late)
        def _():
            jobs.middle(late=True)


def end_jobs(jobs, at, steps):
    if jobs.kinds:
        @pl.when(at == steps - 1)
        def _():
            jobs.finish()


def ffn_forward_kernel(jobs, x_ref, gate_ref, up_ref, down_ref, part_ref):
    at, steps = pl.program_id(0), pl.num_programs(0)
    begin_jobs(jobs, at, steps)
    _, up, act, _ = ffn_parts(x_ref[...], gate_ref, up_ref)
    part_ref[...] = mm((act * up).astype(BF16), down_ref[...], NT).astype(BF16)
    end_jobs(jobs, at, steps)


def whole(shape):
    return pl.BlockSpec(shape, lambda i: (0, 0), pipeline_mode=pl.Buffered(1))


def ffn_forward(x, weights, jobs, number):
    length, width = x.shape
    rows = pl.BlockSpec((CHUNK, width), lambda i: (i, 0))
    return carry_call(
        ffn_forward_kernel, jobs, (length // CHUNK,),
        [rows] + [whole(weight.shape) for weight in weights], [rows],
        [jax.ShapeDtypeStruct((length, width), BF16)], [], (x, *weights), number, "ffn_forward",
        4 * 10**9,
    )


def ffn_backward_kernel(both, jobs, x_ref, g_ref, gate_ref, up_ref, down_ref, *refs):
    outs, (low_gate, low_up, hidden_ref, x_held, g_held) = refs[:-5], refs[-5:]
    if both:
        residual_ref, outs = outs[0], outs[1:]
    part_ref, dgate_ref, dup_ref, ddown_ref = outs[:4]
    at, steps = pl.program_id(0), pl.num_programs(0)
    chunks = steps // 2
    begin_jobs(jobs, at, steps)

    @pl.when(at < chunks)
    def _():
        rows = pl.ds(pl.multiple_of(at * CHUNK, CHUNK), CHUNK)
        x, g = x_ref[...], g_ref[...]
        x_held[rows, :] = x
        g_held[rows, :] = g
        gate, up, act, sig = ffn_parts(x, gate_ref, up_ref)
        hidden = (act * up).astype(BF16)
        hidden_ref[rows, :] = hidden
        if both:
            own = lax.axis_index("zl") * 2 + lax.axis_index("core")
            outs[4][...] = (
                mm(hidden, down_ref[...], NT) + jnp.where(at == own, residual_ref[lax.axis_index("zl")], 0.0)
            ).astype(BF16)
        dhidden = mm(g, down_ref[...])
        dgate = (dhidden * up * (sig * (1.0 + gate * (1.0 - sig)))).astype(BF16)
        dup = (dhidden * act).astype(BF16)
        low_gate[rows, :] = dgate
        low_up[rows, :] = dup
        part_ref[...] = (mm(dgate, gate_ref[...], NT) + mm(dup, up_ref[...], NT)).astype(BF16)

    @pl.when(at >= chunks)
    def _():
        columns = pl.ds(pl.multiple_of((at - chunks) * CHUNK, CHUNK), CHUNK)
        dgate_ref[...] = mm(x_held[:, columns], low_gate[...], TN).astype(BF16)
        dup_ref[...] = mm(x_held[:, columns], low_up[...], TN).astype(BF16)
        ddown_ref[...] = mm(g_held[:, columns], hidden_ref[...], TN).astype(BF16)

    end_jobs(jobs, at, steps)


def ffn_backward(x, g, weights, jobs, number, residual=None):
    both = residual is not None
    length, width = x.shape
    chunks = length // CHUNK
    units = weights[0].shape[1]
    assert length == width and (not both or residual.shape[1] == CHUNK)
    rows = pl.BlockSpec((CHUNK, width), lambda i: (jnp.minimum(i, chunks - 1), 0))
    late = pl.BlockSpec((CHUNK, units), lambda i: (jnp.maximum(i - chunks, 0), 0))
    out = lambda cols: jax.ShapeDtypeStruct((length, cols), BF16)
    return carry_call(
        functools.partial(ffn_backward_kernel, both), jobs, (2 * chunks,),
        [rows, rows] + [whole(weight.shape) for weight in weights] + [
            pl.BlockSpec((2, CHUNK, width), lambda i: (0, 0, 0), pipeline_mode=pl.Buffered(1))
        ] * both,
        [rows] + [late] * 3 + [rows] * both,
        [out(width)] + [out(units)] * 3 + [out(width)] * both,
        [pltpu.VMEM((length, units), BF16)] * 3 + [pltpu.VMEM((length, width), BF16)] * 2,
        (x, g, *weights) + ((residual,) if both else ()), number, "ffn_backward", 12 * 10**9,
    )


class Held:
    def __init__(self, at, sources, held, sems):
        self.at = at
        self.copies = [
            pltpu.make_async_copy(source, ref, sems.at[index])
            for index, (source, ref) in enumerate(zip(sources, held))
        ]

    def start(self):
        @pl.when(self.at == 0)
        def _():
            for copy in self.copies:
                copy.start()

    def ready(self, index):
        pl.when(self.at == 0)(self.copies[index].wait)


def held_scratch(weights):
    return [pltpu.VMEM(weight.shape, BF16) for weight in weights] + [
        pltpu.SemaphoreType.DMA((len(weights),))
    ]


def row_major(x):
    return with_layout_constraint(x, Layout(major_to_minor=tuple(range(x.ndim))))


def linear(sizes, index):
    place = 0
    for size, at in zip(sizes, index):
        place = place * size + at
    return place


class Roles:
    def __init__(self):
        self.sizes = tuple(lax.axis_size(name) for name in AXES)
        self.chips, self.cores, self.zps, self.zls = self.sizes
        assert self.cores == 2 and self.zps == 2 and self.zls == 2

    def every(self):
        for chip in range(self.chips):
            for core in range(2):
                for zp in range(2):
                    for zl in range(2):
                        yield chip, core, zp, zl

    def rows_pairs(self):
        pairs = []
        for chip, core, zp, zl in self.every():
            slot, part = chip * 2 + zp, zl * 2 + core
            source = linear(self.sizes, (slot // 2, slot % 2, part // 2, part % 2))
            pairs.append((source, linear(self.sizes, (chip, core, zp, zl))))
        return pairs

    def weight_pairs(self, which):
        pairs = []
        for chip, core, zp, zl in self.every():
            head = zp * 2 + zl
            to = (chip, head % 2, core ^ which, head // 2)
            pairs.append(
                (linear(self.sizes, (chip, core, zp, zl)), linear(self.sizes, to))
            )
        return pairs


def flipped(pairs):
    return [(b, a) for a, b in pairs]


def chip_gather(ordered):
    return lax.all_gather(ordered, "chip", axis=0, tiled=True)


def to_plane(pack, roles):
    halves = [lax.ppermute(pack, AXES, roles.weight_pairs(which)) for which in range(2)]
    swap = lax.axis_index("zp") == 1
    return jnp.concatenate(
        [jnp.where(swap, halves[1], halves[0]), jnp.where(swap, halves[0], halves[1])], axis=0
    )


def summed(parts, kind):
    return jnp.sum(parts.astype(F32), axis=0).astype(kind)


def deal(values, order):
    spread = lax.all_to_all(values, ("chip", "core"), split_axis=2, concat_axis=1, tiled=True)
    picked = jnp.take(spread, order, axis=1)
    return lax.all_to_all(picked, ("chip", "core"), split_axis=1, concat_axis=2, tiled=True)


def shards(
    tokens, lengths, order, norm_mix, w_query, w_key, w_value, w_gate, w_decay, conv_filter,
    log_rate, step_bias, norm_heads, w_out, norm_ffn, w_ffn_gate, w_ffn_up, w_ffn_down, cotangent,
):
    roles = Roles()
    layer_count = w_query.shape[0]
    assert layer_count == 2
    heads_total = log_rate.shape[1]
    chip, core, zp, zl = (lax.axis_index(name) for name in AXES)
    head = zl * 2 + core
    rows_local, slots_local, width = tokens.shape
    assert slots_local == 1 and w_decay.shape[2] == 1
    slot_total = order.shape[0]
    units = w_ffn_gate.shape[2]
    rows_part = w_query.shape[1]
    to_roles = roles.rows_pairs()

    def carry(*jobs):
        return Jobs(list(jobs), roles.chips)

    scalars = (log_rate, step_bias)
    kernel_deal = rows_local % (16 * slot_total) == 0
    if kernel_deal:
        turned = lambda w: w.transpose(0, 2, 1)
        raw = (
            w_query, w_key, w_value, w_gate, turned(w_decay[:, :, 0, :]), conv_filter[:, :, 0, :],
            w_out, turned(w_ffn_gate), turned(w_ffn_up), w_ffn_down,
        )
        (residual, rows_in, start, qkv_next, side_next, out_next, gate_next, up_first, up_next,
         down_first, down_next, qkv0, side0, _, _, out_wide, gate_wide) = deal_and_gather(
            order, lengths, tokens[:, 0, :], norm_mix, cotangent[:, 0, :], raw, roles.chips, 1
        )
    else:
        packs = []
        for layer in range(layer_count):
            aux = jnp.concatenate([w_decay[layer, :, 0, :], conv_filter[layer, :, 0, :].T], axis=1)
            aux = jnp.pad(aux, ((0, 0), (0, LANES - aux.shape[1])))
            packs.append(
                [
                    row_major(pack) for pack in (
                        jnp.concatenate([w_query[layer], w_key[layer], w_value[layer]], axis=1),
                        jnp.concatenate([w_gate[layer], aux], axis=1),
                        w_out[layer].T, w_ffn_gate[layer], w_ffn_up[layer], w_ffn_down[layer].T,
                    )
                ]
            )
        (qkv0, side0, out_wide, gate_wide, up_first, down_first) = packs[0]
        (qkv_next, side_next, out_next, gate_next, up_next, down_next) = packs[1]
        positions = (zp * 2 + zl) * rows_local + jnp.arange(rows_local)
        start = cotangent[:, 0, :] * (positions < lengths[order[chip * 2 + core]]).astype(BF16)[:, None]
        residual = lax.ppermute(deal(tokens, order)[:, 0, :], AXES, to_roles)
        (residual, rows_in), _ = first_gather(residual, norm_mix, 0, carry(), 1)
        qkv0, side0 = (chip_gather(to_plane(pack, roles)) for pack in (qkv0, side0))
        out_wide, gate_wide = (to_plane(pack, roles) for pack in (out_wide, gate_wide))

    (heads0, *kept0), (out0, gate0, up_wide, down_wide, qkv_wide) = mixer_forward(
        0, rows_in, qkv0, side0, norm_heads, scalars,
        carry((Spread, out_wide), (Spread, gate_wide), (ToPlane, up_first), (ToPlane, down_first),
              (ToPlane, qkv_next)),
        2,
    )
    rows_in0, residual0 = rows_in, residual
    (middle0, rows_ffn0), (up0, down0, side_wide, gradient) = mixer_bridge(
        heads0, out0, residual0, norm_ffn, 0,
        carry((Spread, up_wide), (Spread, down_wide), (ToPlane, side_next), (ToRole, start)), 3,
    )
    ffn0 = (gate0, up0, down0)
    (part,), _ = ffn_forward(rows_ffn0, ffn0, carry(), None)
    (residual1, rows_in1), (qkv1, side1, out_wide, down_wide) = forward_bridge(
        part, middle0, norm_mix, 1,
        carry((Spread, qkv_wide), (Spread, side_wide), (ToPlane, out_next), (ToPlane, down_next)), 4,
    )
    (heads1, *kept1), (out1, down1, gate_wide, up_wide, grad_rows) = mixer_forward(
        1, rows_in1, qkv1, side1, norm_heads, scalars,
        carry((Spread, out_wide), (Spread, down_wide), (ToPlane, gate_next), (ToPlane, up_next),
              (Share, gradient)),
        5,
    )
    (middle1, rows_ffn1), (gate1, up1) = mixer_bridge(
        heads1, out1, residual1, norm_ffn, 1, carry((Spread, gate_wide), (Spread, up_wide)), 6
    )
    ffn1 = (gate1, up1, down1)
    (part, dgate1, dup1, ddown1, part_out), _ = ffn_backward(
        rows_ffn1, grad_rows, ffn1, carry(), None, residual=middle1
    )

    (gradient, grad_rows, dgain_ffn1, dout1), (dgate1, dup1) = backward_bridge(
        part, middle1, norm_ffn, 1, grad_rows, carry((Reduce, dgate1), (Reduce, dup1)), 7, heads1
    )
    (part, din1, daux1, dgain1, dscalars1), jobs_results = mixer_backward(
        1, grad_rows, rows_in1, qkv1, side1, out1, norm_heads, scalars, kept1,
        carry((Reduce, ddown1), (Reduce, dout1), (FromPlane, dgate1), (FromPlane, dup1),
              (ShareSum, part_out)),
        8,
    )
    ddown1, dout1, gate_home1, up_home1, mixed = jobs_results
    (gradient, grad_rows, dgain_mix1), (dqkv1, daux1, mixed) = backward_bridge(
        part, residual1, norm_mix, 1, gradient,
        carry((Reduce, din1, (0, CONV_CH)), (Reduce, daux1), (FromRole, mixed)), 9,
    )
    (part, dgate0, dup0, ddown0), (side1, qkv_home1, aux_home1, down_home1) = ffn_backward(
        rows_ffn0, grad_rows, ffn0,
        carry((Reduce, din1, (CONV_CH, VAL)), (FromPlane, dqkv1), (FromPlane, daux1),
              (FromPlane, ddown1)),
        14,
    )
    (gradient, grad_rows, dgain_ffn0, dout0), (dgate0, dup0) = backward_bridge(
        part, middle0, norm_ffn, 0, gradient,
        carry((Reduce, dgate0), (Reduce, dup0)), 10, heads0,
    )
    (part, din0, daux0, dgain0, dscalars0), jobs_results = mixer_backward(
        0, grad_rows, rows_in0, qkv0, side0, out0, norm_heads, scalars, kept0,
        carry((Reduce, ddown0), (Reduce, dout0), (FromPlane, dgate0), (FromPlane, dup0),
              (FromPlane, side1), (FromPlane, dout1)),
        11,
    )
    ddown0, dout0, gate_home0, up_home0, side_home1, out_home1 = jobs_results
    terms = (dgain_mix1, dgain_ffn0, dgain_ffn1, dgain0, dgain1, dscalars0, dscalars1)
    last = (din0, daux0)
    last_jobs = carry((FromPlane, ddown0), (FromPlane, dout0))
    if kernel_deal:
        (home, flat, *last), results = final_step(
            order, part, residual0, norm_mix, gradient, terms, last, roles.chips, last_jobs, 12
        )
    else:
        (gradient, dgain_mix), results = backward_last(
            part, residual0, norm_mix, 0, gradient, last_jobs, 12
        )
        mine = (jnp.arange(heads_total) == head).astype(F32)
        flat = jnp.concatenate(
            [dgain_mix[0], *(term[0] for term in terms[:5])]
            + [mine * term[row, 0] for row in range(2) for term in terms[5:]]
        )
        flat = jnp.pad(flat, (0, small_rows(width) * LANES - flat.shape[0])).reshape(-1, LANES)
        flat = lax.psum(flat, AXES)
        dealt_grad = lax.ppermute(gradient, AXES, flipped(to_roles))
        places = jnp.arange(slot_total, dtype=jnp.int32)
        inverse = jnp.sum(jnp.where(order[None, :] == places[:, None], places[None, :], 0), axis=1)
        home = deal(dealt_grad[:, None, :], inverse)[:, 0, :]
        last = only_jobs(
            carry((Reduce, din0, (0, CONV_CH)), (Reduce, din0, (CONV_CH, VAL)), (Reduce, daux0)), 13
        )
        last = only_jobs(carry(*[(FromPlane, a) for a in last]), 15)
    down_home0, out_home0 = results
    qkv_home0, side_home0, aux_home0 = last
    first = (qkv_home0, side_home0, aux_home0, out_home0, gate_home0, up_home0, down_home0)
    second = (qkv_home1, side_home1, aux_home1, out_home1, gate_home1, up_home1, down_home1)
    if rows_part % LANES == 0:
        outs = weights_out(flat, home, first, second, heads_total)
    else:
        flat = flat.reshape(-1)
        small, at = [], 0
        for size in (width, width, VAL, heads_total, heads_total):
            small.append(flat[at : at + layer_count * size].reshape(layer_count, size))
            at += layer_count * size
        qkv, side, aux, out, gate, up, down = (
            jnp.stack([summed(a, F32), summed(b, F32)]) for a, b in zip(first, second)
        )
        turned = lambda a: a.transpose(0, 2, 1)
        outs = [
            qkv[:, :, :KEY], qkv[:, :, KEY : 2 * KEY], qkv[:, :, 2 * KEY :], side, turned(aux)[:, :2], turned(out), turned(gate), turned(up),
            turned(down), *small, turned(aux)[:, 2:6], home.astype(F32)[:, None, :],
        ]
    return (
        mixed[:, None, :],
        outs[15],
        outs[9],
        outs[0], outs[1], outs[2], outs[3],
        outs[4].transpose(0, 2, 1)[:, :, None, :],
        outs[14][:, :, None, :],
        outs[12],
        outs[13],
        outs[11],
        outs[5],
        outs[10],
        outs[6].transpose(0, 2, 1), outs[7].transpose(0, 2, 1), outs[8],
    )


def solution(mesh):
    dp, tensor = mesh.devices.shape
    mesh = Mesh(mesh.devices.reshape(dp // 2, 2, tensor // 2, 2), AXES)
    d, t = ("chip", "core"), ("zp", "zl")
    rows = P(t, d, None)
    by_rows, by_columns = P(None, d, t), P(None, t, d)
    heads, filters = P(None, d, t, None), P(None, None, t, d)
    return jax.shard_map(
        shards,
        mesh=mesh,
        in_specs=(
            rows, P(), P(), P(), by_rows, by_rows, by_rows, by_rows, heads, filters,
            P(), P(), P(), by_columns, P(), by_rows, by_rows, by_columns, rows,
        ),
        out_specs=(
            rows, rows, P(), by_rows, by_rows, by_rows, by_rows, heads, filters,
            P(), P(), P(), by_columns, P(), by_rows, by_rows, by_columns,
        ),
        check_vma=False,
    )
```
